32 devices in a mesh: sub: 2 (over core), row: 4 (over y, x), col: 4 (over z).
Axes of the slice: x: 2, y: 2, z: 4, core: 2. Of those that a mesh axis runs over, the one named last changes fastest.
Arguments:
- front_entries: bfloat16 [5, 2, 4, 128, 10, 4, 128], P(None, 'sub', 'row', None, None, 'col'), may hold values from -6 to 6
- block_pattern: int32 [5, 2, 4, 10, 4], P(None, 'sub', 'row', None, 'col'), may hold values 0 or 1
- child_update: bfloat16 [2, 6, 4, 128, 6, 4, 128], P('sub', None, 'row', None, None, 'col'), may hold values from -6 to 6
- child_map: int32 [2, 6, 4], replicated, may hold values from 0 to 9, as said below
- diag_inverse: bfloat16 [1024, 1024], P('col'), may hold values from -0.0390625 to 0.0390625
Outputs:
- trailing: bfloat16 [5, 2, 4, 128, 10, 4, 128], P(None, 'sub', 'row', None, None, 'col')
The draws below stay inside these ranges and needn't reach their ends.
Inputs may be any that keep to these rules, and one draw needn't show every extreme that they name: For each child s and each r, the 6 values child_map[s, :, r] are distinct; exactly 3 of them are even and 3 odd.
All inputs are finite; a program needn't handle non-finite values. No bound on the sum of `block_pattern` on one device may be relied on, other than what follows from the above.
Results may differ from the reference program's by a relative error of at most 0.0057.
Values may be sent and summed in bfloat16 or wider, within the bound.
No kernel may reach another device: no remote copies, remote signals or barrier semaphores. Data moves between devices by JAX's collectives and lax.ppermute only.
A program may use at most 64 MiB of HBM per device.

```python
import jax
import jax.numpy as jnp
from jax import lax

BLK = 128
PANEL = 1024
RBK = 5
CBK = 6
GRID = 4


def pick_targets(key):
    key_even, key_odd, key_order = jax.random.split(key, 3)
    even_slots = jax.random.permutation(key_even, RBK)[:CBK // 2] * 2
    odd_slots = jax.random.permutation(key_odd, RBK)[:CBK // 2] * 2 + 1
    joined = jnp.concatenate([even_slots, odd_slots]).astype(jnp.int32)
    return jax.random.permutation(key_order, joined)


def draw_child_map(key, part):
    key_list = jax.random.split(jax.random.fold_in(key, 7), 2 * GRID)
    slot_table = jax.vmap(pick_targets)(key_list)
    return slot_table.reshape(2, GRID, CBK).transpose(0, 2, 1).astype(jnp.int32)


def set_ends(values, rng, low, largest):
    index_at = [jax.random.randint(jax.random.fold_in(rng, axis), (), 0, length) for axis, length in enumerate(values.shape)]
    longest = values.shape.index(max(values.shape))
    beside = index_at[:longest] + [(index_at[longest] + 1) % values.shape[longest]] + index_at[longest + 1:]
    return values.at[tuple(index_at)].set(low).at[tuple(beside)].set(largest)


def block_scale(rng, shape, cuts, least, high):
    gain = 1.0
    for dim, parts in cuts:
        draws = jax.random.uniform(jax.random.fold_in(jax.random.fold_in(rng, 6), dim), (parts,), jnp.float32, least / len(cuts), high / len(cuts))
        gain = gain * jnp.repeat(jnp.exp(draws), shape[dim] // parts).reshape((-1,) + (1,) * (len(shape) - 1 - dim))
    return gain


def bell_draw(own_key, shape, width, reach, cuts=(), kind=jnp.bfloat16):
    drawn = jax.random.normal(own_key, shape, jnp.float32) * width
    if len(cuts) > 0:
        drawn = block_scale(own_key, shape, cuts, -0.22, 0.18) * drawn
    return jnp.clip(drawn, min=-reach, max=reach).astype(kind)


def setup_inputs(seed: int = 0) -> dict:
    arg_keys = jax.random.split(jax.random.key(seed), 6)
    return {
        "front_entries": bell_draw(arg_keys[0], (RBK, 2, GRID, BLK, 2 * RBK, GRID, BLK), 1.0, 6.0, ((1, 2), (2, 4), (5, 4))),
        "block_pattern": set_ends((jax.random.randint(arg_keys[1], (RBK, 2, GRID, 2 * RBK, GRID), 0, 2) < 1).astype(jnp.int32), jax.random.fold_in(arg_keys[1], 1), 0, 1),
        "child_update": bell_draw(arg_keys[2], (2, CBK, GRID, BLK, CBK, GRID, BLK), 1.0, 6.0, ((0, 2), (2, 4), (5, 4))),
        "child_map": draw_child_map(jax.random.fold_in(arg_keys[5], 71), 0),
        "diag_inverse": bell_draw(arg_keys[4], (PANEL, PANEL), (PANEL * PANEL // 45) ** -0.5, 0.0390625, ((0, 4),)),
    }


def reference(front_entries, block_pattern, child_update, child_map, diag_inverse):
    nblocks = 2 * RBK * GRID
    front_order = nblocks * BLK
    child_blocks = CBK * GRID
    blocks = front_entries.reshape(nblocks, BLK, nblocks, BLK).transpose(0, 2, 1, 3).astype(jnp.float32)
    blocks = blocks * block_pattern.reshape(nblocks, nblocks)[:, :, None, None].astype(jnp.float32)
    positions = jnp.arange(GRID, dtype=jnp.int32)
    for child_index in range(2):
        targets = (child_map[child_index] * GRID + positions[None, :]).reshape(child_blocks).astype(jnp.int32)
        update = child_update[child_index].reshape(child_blocks, BLK, child_blocks, BLK).transpose(0, 2, 1, 3).astype(jnp.float32)
        blocks = blocks.at[targets[:, None], targets[None, :]].add(update)
    front = blocks.transpose(0, 2, 1, 3).reshape(front_order, front_order).astype(jnp.bfloat16)
    lower_inverse = jnp.tril(diag_inverse)
    contract = (((1,), (1,)), ((), ()))
    factor = lax.dot_general(front[:, :PANEL], lower_inverse, contract, preferred_element_type=jnp.float32).astype(jnp.bfloat16)

    def one_block(block_index):
        row_block = lax.dynamic_slice_in_dim(front, block_index * BLK, BLK, 0)
        left_rows = lax.dynamic_slice_in_dim(factor, block_index * BLK, BLK, 0)
        product = lax.dot_general(left_rows, factor, contract, preferred_element_type=jnp.float32)
        return (row_block.astype(jnp.float32) - product).astype(jnp.bfloat16)

    trailing = lax.map(one_block, jnp.arange(nblocks, dtype=jnp.int32))
    return trailing.reshape(RBK, 2, GRID, BLK, 2 * RBK, GRID, BLK)
```

```python
import jax
import jax.numpy as jnp
from jax import lax
from jax.sharding import PartitionSpec as P

PANEL = 1024
PLANE = ("row", "col")


def from_partner(block, axis, apart):
    count = lax.axis_size(axis)
    route = []
    for low in range(count):
        high = low | 1 << apart
        if high != low and high < count:
            route += [(low, high), (high, low)]
    return lax.ppermute(block, axis, route)


def shifted(block, axis, apart):
    count = lax.axis_size(axis)
    return lax.ppermute(block, axis, [(i, (i + apart) % count) for i in range(count)])


def flipped(block, axis, mask):
    count = lax.axis_size(axis)
    return lax.ppermute(block, axis, [(i, i ^ mask) for i in range(count)])


def plane_route(col_size, source, target):
    return [((c ^ source) * col_size + c, (c ^ target) * col_size + c) for c in range(col_size)]


def plane_spread(block, row_size, col_size, offset):
    half = block.shape[0] // 2
    held = {0: block}
    total = jnp.where(offset == 0, block, jnp.zeros_like(block))
    for mask in sorted(range(1, row_size), key=lambda m: (m.bit_count(), m)):
        low_parent = mask & (mask - 1)
        high_parent = mask ^ (1 << (mask.bit_length() - 1))
        if low_parent == high_parent:
            got = lax.ppermute(held[low_parent], PLANE, plane_route(col_size, low_parent, mask))
        else:
            top = lax.ppermute(held[low_parent][:half], PLANE, plane_route(col_size, low_parent, mask))
            bottom = lax.ppermute(held[high_parent][half:], PLANE, plane_route(col_size, high_parent, mask))
            got = jnp.concatenate([top, bottom], axis=0)
        held[mask] = got
        total = total + got
    return total


def place_update(update, row_targets, col_targets, sub_index, slot_count, column_count):
    wanted_rows = jnp.arange(slot_count, dtype=jnp.int32) * 2 + sub_index
    row_pick = (row_targets[None, :] == wanted_rows[:, None]).astype(jnp.bfloat16)
    col_pick = (col_targets[None, :] == jnp.arange(column_count, dtype=jnp.int32)[:, None]).astype(
        jnp.bfloat16
    )
    return jnp.einsum(
        "ak,kxly,bl->axby", row_pick, update, col_pick, preferred_element_type=jnp.float32
    )


def gather_inverse(diag_inverse, block_size, panel_slots):
    sub_size, row_size, col_size = (lax.axis_size(name) for name in ("sub", "row", "col"))
    sub_index, row_index, col_index = (lax.axis_index(name) for name in ("sub", "row", "col"))
    width_share = diag_inverse.shape[0]
    part = width_share // (sub_size * row_size)
    first = (sub_index * row_size + row_index) * part
    share = lax.dynamic_slice_in_dim(diag_inverse, first, part, 0)
    row_numbers = col_index * width_share + first + jnp.arange(part, dtype=jnp.int32)
    below = jnp.arange(PANEL, dtype=jnp.int32)[None, :] <= row_numbers[:, None]
    share = jnp.where(below, share, jnp.zeros((), jnp.bfloat16))
    line = jnp.concatenate([share] + [shifted(share, "col", t) for t in range(1, col_size)], axis=0)
    padded = panel_slots * col_size * block_size
    line = jnp.pad(line, ((0, 0), (0, padded - PANEL)))
    line = line.reshape(line.shape[0], panel_slots, col_size, block_size)
    doubled = jnp.concatenate([line[:, :, ::-1]] * 2, axis=2)
    line = lax.dynamic_slice_in_dim(doubled, col_size - 1 - col_index, col_size, 2)
    line = line.transpose(0, 2, 1, 3).reshape(line.shape[0], padded)
    plane = jnp.concatenate([line] + [flipped(line, "row", m) for m in range(1, row_size)], axis=0)
    return jnp.concatenate([plane, from_partner(plane, "sub", 0)], axis=0)


def body(front_entries, block_pattern, child_update, child_map, diag_inverse):
    slot_count = front_entries.shape[0]
    block_size = front_entries.shape[3]
    column_count = front_entries.shape[4]
    child_count = child_update.shape[1]
    sub_index = lax.axis_index("sub")
    row_index = lax.axis_index("row")
    col_index = lax.axis_index("col")
    row_size = lax.axis_size("row")
    col_size = lax.axis_size("col")
    panel_slots = -(-(PANEL // block_size) // col_size)
    partner = 1 - sub_index
    own_update = child_update.reshape(child_count, block_size, child_count, block_size)
    own_maps = lax.dynamic_index_in_dim(child_map, sub_index, 0, keepdims=False)
    other_maps = lax.dynamic_index_in_dim(child_map, partner, 0, keepdims=False)
    own_rows = lax.dynamic_index_in_dim(own_maps, row_index, 1, keepdims=False)
    own_cols = lax.dynamic_index_in_dim(own_maps, col_index, 1, keepdims=False)
    other_rows = lax.dynamic_index_in_dim(other_maps, row_index, 1, keepdims=False)
    other_cols = lax.dynamic_index_in_dim(other_maps, col_index, 1, keepdims=False)
    inverse = gather_inverse(diag_inverse, block_size, panel_slots)
    masked = front_entries.reshape(slot_count, block_size, column_count, block_size).astype(
        jnp.float32
    )
    masked = masked * block_pattern.reshape(slot_count, 1, column_count, 1).astype(jnp.float32)
    own_part = place_update(own_update, own_rows, own_cols, sub_index, slot_count, column_count)
    received = from_partner(own_update, "sub", 0)
    partner_part = place_update(
        received, other_rows, other_cols, sub_index, slot_count, column_count
    )
    front = (masked + own_part + partner_part).astype(jnp.bfloat16)
    row_total = slot_count * block_size
    piece = front[:, :, :panel_slots, :].reshape(row_total, panel_slots * block_size)

    offset = row_index ^ col_index
    pieces = [piece] + [shifted(piece, "col", t) for t in range(1, col_size)]
    group = max(1, col_size // 4)
    spread = []
    for start in range(0, col_size, group):
        bundle = jnp.concatenate(pieces[start:start + group], axis=1)
        spread.append(plane_spread(bundle, row_size, col_size, offset))
    row_panel = jnp.concatenate(pieces, axis=1)
    own_panel = jnp.concatenate(spread, axis=1)
    other_panel = from_partner(own_panel, "sub", 0)
    low_half = jnp.where(sub_index == 0, own_panel, other_panel)
    high_half = jnp.where(sub_index == 0, other_panel, own_panel)
    both = jnp.stack(
        [half.reshape(slot_count, block_size, -1) for half in (low_half, high_half)], axis=1
    ).reshape(column_count * block_size, -1)

    contract = (((1,), (1,)), ((), ()))
    factor = lax.dot_general(
        row_panel, inverse, contract, preferred_element_type=jnp.float32
    ).astype(jnp.bfloat16)
    column_rows = lax.dot_general(
        both, inverse, contract, preferred_element_type=jnp.float32
    ).astype(jnp.bfloat16)
    product = lax.dot_general(factor, column_rows, contract, preferred_element_type=jnp.float32)
    trailing = front.reshape(row_total, column_count * block_size).astype(jnp.float32) - product
    return trailing.astype(jnp.bfloat16).reshape(
        slot_count, 1, 1, block_size, column_count, 1, block_size
    )


def solution(mesh):
    return jax.shard_map(
        body,
        mesh=mesh,
        in_specs=(
            P(None, "sub", "row", None, None, "col", None),
            P(None, "sub", "row", None, "col"),
            P("sub", None, "row", None, None, "col", None),
            P(),
            P("col", None),
        ),
        out_specs=P(None, "sub", "row", None, None, "col", None),
        check_vma=False,
    )
```

```python
import functools

import jax
import jax.numpy as jnp
from jax import lax
from jax.experimental import pallas as pl
from jax.experimental.pallas import tpu as pltpu
from jax.sharding import PartitionSpec as P

PANEL = 1024
ROW_TILE = 16
VMEM_BYTES = 48 * 1024 * 1024
CONTRACT = (((1,), (1,)), ((), ()))
ON_CHIP = pl.BlockSpec(memory_space=pltpu.VMEM)
SCALARS = pl.BlockSpec(memory_space=pltpu.SMEM)


def call(kernel, out_shape, in_specs, flops=0, moved=1 << 19):
    single = not isinstance(out_shape, (list, tuple))
    return pl.pallas_call(
        kernel,
        out_shape=out_shape,
        in_specs=in_specs,
        out_specs=ON_CHIP if single else [ON_CHIP] * len(out_shape),
        compiler_params=pltpu.CompilerParams(vmem_limit_bytes=VMEM_BYTES),
        cost_estimate=pl.CostEstimate(flops=flops, bytes_accessed=moved, transcendentals=0),
    )


def bf16(*shape):
    return jax.ShapeDtypeStruct(shape, jnp.bfloat16)


def f32(*shape):
    return jax.ShapeDtypeStruct(shape, jnp.float32)


def flipped(block, axis, mask):
    count = lax.axis_size(axis)
    return lax.ppermute(block, axis, [(i, i ^ mask) for i in range(count)])


def swap_even(i, count):
    return i ^ 1 if i ^ 1 < count else i


def swap_odd(i, count):
    j = ((i + 1) ^ 1) - 1
    return j if 0 <= j < count else i


@functools.cache
def line_plan(count):
    streams = ([list(range(count))], [list(range(count))])
    seen = [[(0, 0, i)] for i in range(count)]
    step = 0
    while min(len(s) for s in seen) < count:
        step += 1
        for stream in (0, 1):
            swap = swap_even if (step + stream) % 2 == 1 else swap_odd
            last = streams[stream][-1]
            streams[stream].append([last[swap(i, count)] for i in range(count)])
            for i in range(count):
                origin = streams[stream][-1][i]
                if all(origin != o for _, _, o in seen[i]):
                    seen[i].append((stream, step, origin))
    used = [max([k for s in seen for st, k, _ in s if st == stream]) for stream in (0, 1)]
    origins = [[seen[i][j][2] for i in range(count)] for j in range(count)]
    places = [[seen[i][j][:2] for i in range(count)] for j in range(count)]
    return used, origins, places


def line_swaps(block, axis):
    count = lax.axis_size(axis)
    used, _, places = line_plan(count)
    held = {(0, 0): block}
    for step in range(1, max(used) + 1):
        for stream in (0, 1):
            if step <= used[stream]:
                swap = swap_even if (step + stream) % 2 == 1 else swap_odd
                before = held[(stream, step - 1)] if step > 1 else block
                held[(stream, step)] = lax.ppermute(
                    before, axis, [(i, swap(i, count)) for i in range(count)]
                )
    slots = []
    for row in places:
        kinds = sorted(set(row))
        slots.append([(held[k], tuple(i for i in range(count) if row[i] == k)) for k in kinds])
    return slots


def among(index, members):
    found = index == members[0]
    for member in members[1:]:
        found = jnp.logical_or(found, index == member)
    return found


def looked_up(index, table):
    value = jnp.int32(table[0])
    for i, entry in enumerate(table[1:], 1):
        value = jnp.where(index == i, jnp.int32(entry), value)
    return value


def chosen(slot, index):
    value = slot[0][0]
    for array, members in slot[1:]:
        value = jnp.where(among(index, members), array, value)
    return value


def front_blocks(columns, first, map_ref, pattern_ref, entries_ref, own_ref, received_ref, store):
    sub_index = lax.axis_index("sub")
    row_index = lax.axis_index("row")
    col_index = lax.axis_index("col")
    slot_count = entries_ref.shape[0]
    child_count = own_ref.shape[0]

    def find(child, place, wanted):
        at = jnp.int32(0)
        found = jnp.float32(0)
        for k in range(child_count):
            same = map_ref[child, k, place] == wanted
            at = jnp.where(same, jnp.int32(k), at)
            found = jnp.where(same, jnp.float32(1), found)
        return at, found

    children = (sub_index, 1 - sub_index)
    rows = [[find(child, row_index, 2 * a + sub_index) for child in children] for a in range(slot_count)]
    cols = [[find(child, col_index, b) for child in children] for b in columns]
    for a in range(slot_count):
        for n, b in enumerate(columns):
            total = entries_ref[a, b - first].astype(jnp.float32)
            total = total * pattern_ref[a, b].astype(jnp.float32)
            for (k, k_found), (m, m_found), ref in zip(rows[a], cols[n], (own_ref, received_ref)):
                total = total + ref[k, m].astype(jnp.float32) * (k_found * m_found)
            store(a, n, total.astype(jnp.bfloat16))


def panel_kernel(columns, map_ref, pattern_ref, entries_ref, own_ref, received_ref, *out_refs):
    size = entries_ref.shape[2]

    def store(a, n, block):
        out_refs[n][pl.ds(a * size, size), :] = block

    front_blocks(columns, 0, map_ref, pattern_ref, entries_ref, own_ref, received_ref, store)


def rest_kernel(columns, map_ref, pattern_ref, entries_ref, own_ref, received_ref, out_ref):
    def store(a, n, block):
        out_ref[a, n] = block

    front_blocks(columns, 0, map_ref, pattern_ref, entries_ref, own_ref, received_ref, store)


def inverse_kernel(origins, part, size, *refs):
    *in_refs, out_ref = refs
    sub_index = lax.axis_index("sub")
    row_index = lax.axis_index("row")
    col_index = lax.axis_index("col")
    count = len(origins)
    row_size = lax.axis_size("row")
    share = part * len(in_refs)
    groups = out_ref.shape[1] // (count * size)
    width = in_refs[0].shape[1]
    homes = [looked_up(col_index, table) for table in origins]
    for n, ref in enumerate(in_refs):
        sub_at = sub_index if n < row_size else 1 - sub_index
        row_at = row_index ^ (n % row_size)
        inside = (sub_at * row_size + row_at) * part
        for j in range(count):
            top = homes[j] * share + inside
            for g in range(groups):
                for i in range(count):
                    left = (g * count + homes[i]) * size
                    block = ref[pl.ds(j * part, part), pl.ds(pl.multiple_of(left, size), size)]
                    row_at_w = top + lax.broadcasted_iota(jnp.int32, (part, size), 0)
                    col_at_w = left + lax.broadcasted_iota(jnp.int32, (part, size), 1)
                    block = jnp.where(col_at_w <= row_at_w, block.astype(jnp.float32), 0.0)
                    out_ref[
                        pl.ds(pl.multiple_of(top, part), part), pl.ds((g * count + i) * size, size)
                    ] = block.astype(jnp.bfloat16)


def ordered_kernel(origins, size, in_ref, out_ref):
    col_index = lax.axis_index("col")
    count = len(origins)
    width = in_ref.shape[1]
    groups = out_ref.shape[1] // (count * size)
    rows = in_ref.shape[0]
    homes = [looked_up(col_index, table) for table in origins]
    for g in range(groups):
        for i in range(count):
            left = (g * count + homes[i]) * size
            inside = jnp.minimum(left, width - size)
            block = in_ref[:, pl.ds(pl.multiple_of(inside, size), size)]
            row_at_w = lax.broadcasted_iota(jnp.int32, (rows, size), 0)
            col_at_w = left + lax.broadcasted_iota(jnp.int32, (rows, size), 1)
            block = jnp.where(col_at_w <= row_at_w, block.astype(jnp.float32), 0.0)
            out_ref[:, pl.ds((g * count + i) * size, size)] = block.astype(jnp.bfloat16)


def gather_inverse(diag_inverse, size, groups):
    sub_size, row_size, col_size = (lax.axis_size(name) for name in ("sub", "row", "col"))
    sub_index, row_index, col_index = (lax.axis_index(name) for name in ("sub", "row", "col"))
    share, width = diag_inverse.shape
    part = share // (sub_size * row_size)
    _, origins, _ = line_plan(col_size)
    out_shape = bf16(share * col_size, groups * col_size * size)
    if part % ROW_TILE:
        whole = lax.all_gather(diag_inverse, "col", axis=0, tiled=True)
        return call(functools.partial(ordered_kernel, origins, size), out_shape, [ON_CHIP])(whole)
    mine = lax.dynamic_slice_in_dim(diag_inverse, (sub_index * row_size + row_index) * part, part, 0)
    slots = [chosen(slot, col_index) for slot in line_swaps(mine, "col")]
    line = jnp.concatenate(slots, axis=0)
    plane = [line] + [flipped(line, "row", mask) for mask in range(1, row_size)]
    plane += [flipped(block, "sub", 1) for block in plane]
    return call(
        functools.partial(inverse_kernel, origins, part, size),
        out_shape,
        [ON_CHIP] * len(plane),
        moved=4 << 20,
    )(*plane)


def tick_kernel(members, has_item, has_last, finish, *refs):
    refs = list(refs)
    outs = refs[len(refs) - (2 * has_item + (finish is not None)):]
    row_index = lax.axis_index("row")
    col_index = lax.axis_index("col")
    role = row_index ^ col_index
    ins = refs[: len(refs) - len(outs)]
    taken = [ins.pop(0) for _ in members]
    if has_item:
        send_x, send_y = outs[:2]
        half = send_x.shape[0]
        for ref, kept in zip(taken, members):

            @pl.when(jnp.logical_and(role == 0, among(col_index, kept)))
            def _():
                send_x[...] = ref[:half]
                send_y[...] = ref[half:]

        if has_last:
            last_x, last_y = ins.pop(0), ins.pop(0)

            @pl.when(role != 0)
            def _():
                send_x[...] = last_y[...]
                send_y[...] = last_x[...]


def spread_pieces(items, row_size):
    row_index = lax.axis_index("row")
    col_index = lax.axis_index("col")
    role = row_index ^ col_index
    count = len(items)
    got_x, got_y = [], []
    for tick in range(count + 2):
        item = items[min(tick, count - 1)]
        arrays = [array for array, _ in item]
        members = [kept for _, kept in item]
        half = arrays[0].shape[0] // 2
        shape = bf16(half, arrays[0].shape[1])
        last = [got_x[-1], got_y[-1]] if tick else []
        send_x, send_y = call(
            functools.partial(tick_kernel, members, 1, len(last) > 0, None),
            [shape, shape],
            [ON_CHIP] * (len(arrays) + len(last)),
        )(*arrays, *last)
        got_x.append(flipped(send_x, "row", 1))
        got_y.append(flipped(send_y, "row", 2))
    whole = []
    for n, item in enumerate(items):
        arrays = [array for array, _ in item]
        members = [kept for _, kept in item]
        landed = [got_x[n], got_x[n + 1], got_x[n + 2], got_y[n], got_y[n + 1], got_y[n + 2]]
        whole.append(
            call(
                functools.partial(join_kernel, members), bf16(*arrays[0].shape),
                [ON_CHIP] * (len(arrays) + len(landed)),
            )(*arrays, *landed)
        )
    return whole


def join_kernel(members, *refs):
    *ins, out_ref = refs
    row_index = lax.axis_index("row")
    col_index = lax.axis_index("col")
    role = row_index ^ col_index
    half = out_ref.shape[0] // 2
    x0, x1, x2, y0, y1, y2 = ins[len(members):]
    for ref, kept in zip(ins, members):

        @pl.when(jnp.logical_and(role == 0, among(col_index, kept)))
        def _():
            out_ref[...] = ref[...]

    for wanted, top, bottom in ((1, x0, y2), (2, x2, y0), (3, y1, x1)):

        @pl.when(role == wanted)
        def _():
            out_ref[pl.ds(0, half), :] = top[...]
            out_ref[pl.ds(half, half), :] = bottom[...]


def spread_doubling(items, row_size):
    role = lax.axis_index("row") ^ lax.axis_index("col")
    col_index = lax.axis_index("col")
    held = jnp.concatenate([chosen(item, col_index) for item in items], axis=0)
    for bit in range(row_size.bit_length() - 1):
        got = flipped(held, "row", 1 << bit)
        held = jnp.where((role >> bit) == 1, got, held)
    return jnp.split(held, len(items), axis=0)


def joined(refs):
    return jnp.concatenate([ref[...] for ref in refs], axis=1)


def factor_kernel(count, group, width, inverse_ref, *refs):
    pieces, outs = refs[:count], refs[count:]
    panel = joined(pieces)
    depth = panel.shape[1]
    cols = pl.ds(group * depth, depth)
    outs[0][...] = lax.dot_general(
        panel, inverse_ref[pl.ds(group * width, width), cols], CONTRACT, preferred_element_type=jnp.float32
    ).astype(jnp.bfloat16)
    if len(outs) > 1:
        rows = outs[1].shape[1]
        outs[1][...] = lax.dot_general(
            panel, inverse_ref[pl.ds((group + 1) * width, rows), cols], CONTRACT,
            preferred_element_type=jnp.float32,
        )


def late_factor_kernel(count, group, width, inverse_ref, sum_ref, *refs):
    pieces, out_ref = refs[:count], refs[count]
    panel = joined(pieces)
    depth = panel.shape[1]
    out_ref[...] = (
        sum_ref[...]
        + lax.dot_general(
            panel,
            inverse_ref[pl.ds(group * width, width), pl.ds(group * depth, depth)],
            CONTRACT,
            preferred_element_type=jnp.float32,
        )
    ).astype(jnp.bfloat16)


def first_product_kernel(panel_count, size, rows_ref, own_ref, other_ref, rest_ref, *refs):
    front_refs, out_ref = refs[:panel_count], refs[panel_count]
    sub_index = lax.axis_index("sub")
    slot_count = rows_ref.shape[0] // size
    rows = rows_ref[...]
    for a in range(slot_count):
        for mine, ref in ((True, own_ref), (False, other_ref)):
            at = 2 * a + (sub_index if mine else 1 - sub_index)
            product = lax.dot_general(
                rows, ref[pl.ds(a * size, size), :], CONTRACT, preferred_element_type=jnp.float32
            )
            for m in range(slot_count):
                out_ref[m, at] = product[m * size:(m + 1) * size]
    for m in range(slot_count):
        for b in range(2 * slot_count):
            if b < panel_count:
                block = front_refs[b][pl.ds(m * size, size), :]
            else:
                block = rest_ref[m, b - panel_count]
            out_ref[m, b] = block.astype(jnp.float32) - out_ref[m, b]


def last_product_kernel(count, group, width, size, rows_ref, inverse_ref, left_ref, *refs):
    out_ref = refs[-1]
    own_pieces, other_pieces = refs[:count], refs[count:2 * count]
    sums = refs[2 * count:-1]
    sub_index = lax.axis_index("sub")
    slot_count = rows_ref.shape[0] // size
    rows = rows_ref[...]
    depth = count * size
    tail = inverse_ref[pl.ds(group * width, width), pl.ds(group * depth, depth)]
    for n, (mine, pieces) in enumerate(((True, own_pieces), (False, other_pieces))):
        factor = lax.dot_general(joined(pieces), tail, CONTRACT, preferred_element_type=jnp.float32)
        if sums:
            factor = factor + sums[n][...]
        factor = factor.astype(jnp.bfloat16)
        product = lax.dot_general(rows, factor, CONTRACT, preferred_element_type=jnp.float32)
        for a in range(slot_count):
            at = 2 * a + (sub_index if mine else 1 - sub_index)
            for m in range(slot_count):
                block = product[m * size:(m + 1) * size, a * size:(a + 1) * size]
                out_ref[m, at] = (left_ref[m, at].astype(jnp.float32) - block).astype(jnp.bfloat16)


def body(front_entries, block_pattern, child_update, child_map, diag_inverse):
    slot_count = front_entries.shape[0]
    size = front_entries.shape[3]
    column_count = front_entries.shape[4]
    child_count = child_update.shape[1]
    row_size = lax.axis_size("row")
    col_size = lax.axis_size("col")
    col_index = lax.axis_index("col")
    groups = -(-(PANEL // size) // col_size)
    width = min(PANEL, col_size * size)
    rows = slot_count * size
    entries = front_entries.reshape(slot_count, size, column_count, size).transpose(0, 2, 1, 3)
    pattern = block_pattern.reshape(slot_count, column_count)
    own = child_update.reshape(child_count, size, child_count, size).transpose(0, 2, 1, 3)

    received = flipped(own, "sub", 1)
    inverse = gather_inverse(diag_inverse, size, groups)
    specs = [SCALARS, SCALARS, ON_CHIP, ON_CHIP, ON_CHIP]
    panel = call(
        functools.partial(panel_kernel, tuple(range(groups))), [bf16(rows, size)] * groups, specs
    )(child_map, pattern, entries[:, :groups], own, received)
    rest = call(
        functools.partial(rest_kernel, tuple(range(groups, column_count))),
        bf16(slot_count, column_count - groups, size, size),
        specs,
        moved=6 << 20,
    )(child_map, pattern, entries, own, received)

    slots = [line_swaps(panel[g], "col") for g in range(groups)]
    items = [item for group in slots for item in group]
    spread = spread_pieces if row_size == 4 else spread_doubling
    own_items = spread(items, row_size)
    other_items = [flipped(item, "sub", 1) for item in own_items]
    row_items = [chosen(item, col_index) for item in items]

    def group_of(pieces, g):
        return pieces[g * col_size:(g + 1) * col_size]

    last = groups - 1
    depth = col_size * size
    factors = {}
    sums = {}
    for name, pieces in (("row", row_items), ("own", own_items), ("other", other_items)):
        factors[name], sums[name] = [], None
        for g in range(groups):
            if g == 0:
                if last == 0 and name != "row":
                    continue
                out = [bf16(rows, width)]
                if last > 0:
                    out.append(f32(rows, PANEL - width))
                got = call(
                    functools.partial(factor_kernel, col_size, 0, width), out,
                    [ON_CHIP] * (1 + col_size), flops=2 * rows * depth * PANEL,
                )(inverse, *group_of(pieces, 0))
                factors[name].append(got[0])
                sums[name] = got[1] if last > 0 else None
            elif name == "row":
                factors[name].append(
                    call(
                        functools.partial(late_factor_kernel, col_size, g, width), bf16(rows, width),
                        [ON_CHIP] * (2 + col_size), flops=2 * rows * depth * width,
                    )(inverse, sums[name], *group_of(pieces, g))
                )
    if last > 0:
        left = call(
            functools.partial(first_product_kernel, groups, size),
            f32(slot_count, column_count, size, size),
            [ON_CHIP] * (4 + groups),
            flops=2 * rows * rows * 2 * width,
        )(factors["row"][0], factors["own"][0], factors["other"][0], rest, *panel)
    else:
        left = jnp.concatenate([p.reshape(slot_count, 1, size, size) for p in panel] + [rest], axis=1)
    late = [sums["own"], sums["other"]] if last > 0 else []
    trailing = call(
        functools.partial(last_product_kernel, col_size, last, width, size),
        bf16(slot_count, column_count, size, size),
        [ON_CHIP] * (3 + 2 * col_size + len(late)),
        flops=2 * rows * rows * 2 * width,
    )(factors["row"][last], inverse, left, *group_of(own_items, last), *group_of(other_items, last), *late)
    return trailing.transpose(0, 2, 1, 3).reshape(
        slot_count, 1, 1, size, column_count, 1, size
    )


def solution(mesh):
    return jax.shard_map(
        body,
        mesh=mesh,
        in_specs=(
            P(None, "sub", "row", None, None, "col", None),
            P(None, "sub", "row", None, "col"),
            P("sub", None, "row", None, None, "col", None),
            P(),
            P("col", None),
        ),
        out_specs=P(None, "sub", "row", None, None, "col", None),
        check_vma=False,
    )
```

```python
import functools

import jax
import jax.numpy as jnp
from jax import lax
from jax.experimental import pallas as pl
from jax.experimental.pallas import tpu as pltpu
from jax.sharding import PartitionSpec as P

PANEL = 1024
ROW_TILE = 16
VMEM_BYTES = 24 * 1024 * 1024
CONTRACT = (((1,), (1,)), ((), ()))
ON_CHIP = pl.BlockSpec(memory_space=pltpu.VMEM)
SCALARS = pl.BlockSpec(memory_space=pltpu.SMEM)


def call(kernel, out_shape, in_specs, flops=0, moved=1 << 19, **more):
    single = not isinstance(out_shape, (list, tuple))
    return pl.pallas_call(
        kernel,
        out_shape=out_shape,
        in_specs=in_specs,
        out_specs=more.pop("out_specs", ON_CHIP if single else [ON_CHIP] * len(out_shape)),
        compiler_params=pltpu.CompilerParams(vmem_limit_bytes=VMEM_BYTES),
        cost_estimate=pl.CostEstimate(flops=flops, bytes_accessed=moved, transcendentals=0),
        **more,
    )


def bf16(*shape):
    return jax.ShapeDtypeStruct(shape, jnp.bfloat16)


def f32(*shape):
    return jax.ShapeDtypeStruct(shape, jnp.float32)


def flipped(block, axis, mask):
    count = lax.axis_size(axis)
    return lax.ppermute(block, axis, [(i, i ^ mask) for i in range(count)])


def shifted(block, axis, apart):
    count = lax.axis_size(axis)
    return lax.ppermute(block, axis, [(i, (i + apart) % count) for i in range(count)])


def swap_even(i, count):
    return i ^ 1 if i ^ 1 < count else i


def swap_odd(i, count):
    j = ((i + 1) ^ 1) - 1
    return j if 0 <= j < count else i


@functools.cache
def line_plan(count):
    streams = ([list(range(count))], [list(range(count))])
    seen = [[(0, 0, i)] for i in range(count)]
    step = 0
    while min(len(s) for s in seen) < count:
        step += 1
        for stream in (0, 1):
            swap = swap_even if (step + stream) % 2 == 1 else swap_odd
            last = streams[stream][-1]
            streams[stream].append([last[swap(i, count)] for i in range(count)])
            for i in range(count):
                origin = streams[stream][-1][i]
                if all(origin != o for _, _, o in seen[i]):
                    seen[i].append((stream, step, origin))
    used = [max([k for s in seen for st, k, _ in s if st == stream]) for stream in (0, 1)]
    origins = [[seen[i][j][2] for i in range(count)] for j in range(count)]
    places = [[seen[i][j][:2] for i in range(count)] for j in range(count)]
    return used, origins, places


def line_swaps(block, axis):
    count = lax.axis_size(axis)
    used, _, places = line_plan(count)
    held = {(0, 0): block}
    for step in range(1, max(used) + 1):
        for stream in (0, 1):
            if step <= used[stream]:
                swap = swap_even if (step + stream) % 2 == 1 else swap_odd
                before = held[(stream, step - 1)] if step > 1 else block
                held[(stream, step)] = lax.ppermute(
                    before, axis, [(i, swap(i, count)) for i in range(count)]
                )
    kinds = sorted({kind for row in places for kind in row})
    return [(kind, held[kind]) for kind in kinds]


def among(index, members):
    found = index == members[0]
    for member in members[1:]:
        found = jnp.logical_or(found, index == member)
    return found


def looked_up(index, table):
    value = jnp.int32(table[0])
    for i, entry in enumerate(table[1:], 1):
        value = jnp.where(index == i, jnp.int32(entry), value)
    return value


def front_blocks(columns, first, map_ref, pattern_ref, entries_ref, own_ref, received_ref, store):
    sub_index = lax.axis_index("sub")
    row_index = lax.axis_index("row")
    col_index = lax.axis_index("col")
    slot_count = entries_ref.shape[0]
    child_count = own_ref.shape[0]

    def find(child, place, wanted):
        at = jnp.int32(0)
        found = jnp.float32(0)
        for k in range(child_count):
            same = map_ref[child, k, place] == wanted
            at = jnp.where(same, jnp.int32(k), at)
            found = jnp.where(same, jnp.float32(1), found)
        return at, found

    children = (sub_index, 1 - sub_index)
    rows = [[find(child, row_index, 2 * a + sub_index) for child in children] for a in range(slot_count)]
    cols = [[find(child, col_index, b) for child in children] for b in columns]
    for a in range(slot_count):
        for n, b in enumerate(columns):
            total = entries_ref[a, b - first].astype(jnp.float32)
            total = total * pattern_ref[a, b].astype(jnp.float32)
            for (k, k_found), (m, m_found), ref in zip(rows[a], cols[n], (own_ref, received_ref)):
                total = total + ref[k, m].astype(jnp.float32) * (k_found * m_found)
            store(a, n, total.astype(jnp.bfloat16))


def panel_kernel(columns, part, map_ref, pattern_ref, entries_ref, own_ref, received_ref, piece_ref, *part_refs):
    size = entries_ref.shape[2]

    def store(a, n, block):
        piece_ref[pl.ds(a * size, size), pl.ds(n * size, size)] = block

    front_blocks(columns, 0, map_ref, pattern_ref, entries_ref, own_ref, received_ref, store)
    used = entries_ref.shape[0] * size
    if used < piece_ref.shape[0]:
        piece_ref[pl.ds(used, piece_ref.shape[0] - used), :] = jnp.zeros(
            (piece_ref.shape[0] - used, piece_ref.shape[1]), piece_ref.dtype
        )
    row_index = lax.axis_index("row")
    for mask, ref in enumerate(part_refs):
        ref[...] = piece_ref[pl.ds(pl.multiple_of((row_index ^ mask) * part, ROW_TILE), part), :]


def front_kernel(columns, map_ref, pattern_ref, entries_ref, own_ref, received_ref, piece_ref, out_ref):
    size = entries_ref.shape[2]
    panel_count = columns[0]

    def store(a, n, block):
        out_ref[a, columns[n]] = block

    front_blocks(columns, 0, map_ref, pattern_ref, entries_ref, own_ref, received_ref, store)
    for a in range(entries_ref.shape[0]):
        for n in range(panel_count):
            out_ref[a, n] = piece_ref[pl.ds(a * size, size), pl.ds(n * size, size)]


def inverse_kernel(part, row_size, in_ref, out_ref):
    rows, width = in_ref.shape
    blocks = rows // part
    col_size = lax.axis_size("col")
    for n in range(blocks):
        plane, col = divmod(n, col_size)
        top = (col * (blocks // col_size) + plane) * part
        block = in_ref[pl.ds(n * part, part), :].astype(jnp.float32)
        row_at = top + lax.broadcasted_iota(jnp.int32, (part, width), 0)
        col_at = lax.broadcasted_iota(jnp.int32, (part, width), 1)
        out_ref[pl.ds(top, part), :] = jnp.where(col_at <= row_at, block, 0.0).astype(jnp.bfloat16)


def gather_inverse(diag_inverse):
    sub_size, row_size = lax.axis_size("sub"), lax.axis_size("row")
    sub_index, row_index = lax.axis_index("sub"), lax.axis_index("row")
    share, width = diag_inverse.shape
    part = share // (sub_size * row_size)
    if part % ROW_TILE:
        part = share
        whole = lax.all_gather(diag_inverse, "col", axis=0, tiled=True)
    else:
        mine = lax.dynamic_slice_in_dim(diag_inverse, (sub_index * row_size + row_index) * part, part, 0)
        line = lax.all_gather(mine, "col", axis=0, tiled=True)
        whole = lax.all_gather(line, ("sub", "row"), axis=0, tiled=True)
    return call(
        functools.partial(inverse_kernel, part, row_size), bf16(*whole.shape), [ON_CHIP], moved=4 << 20
    )(whole)


def turn_kernel(*refs):
    count = lax.axis_size("col")
    held, outs = refs[: len(refs) - count], refs[len(refs) - count:]
    row_index = lax.axis_index("row")
    col_index = lax.axis_index("col")
    for apart, out_ref in enumerate(outs):
        wanted = row_index ^ lax.rem(col_index + apart, count)
        for mask, ref in enumerate(held):

            @pl.when(wanted == mask)
            def _():
                out_ref[...] = ref[...]


def place_piece(panel_ref, rows, block, origin, count, size):
    for g in range(block.shape[1] // size):
        left = pl.multiple_of((g * count + origin) * size, size)
        panel_ref[rows, pl.ds(left, size)] = block[:, g * size:(g + 1) * size]


def factor_from(panel_ref, inverse_ref, rows, tile, store):
    width = inverse_ref.shape[0]
    for first in range(0, width, tile):
        store(
            first,
            lax.dot_general(
                panel_ref[pl.ds(0, rows), pl.ds(0, first + tile)],
                inverse_ref[pl.ds(first, tile), pl.ds(0, first + tile)],
                CONTRACT,
                preferred_element_type=jnp.float32,
            ).astype(jnp.bfloat16),
        )


def row_factor_kernel(places, origins, kinds, size, tile, inverse_ref, *refs):
    arrays, out_ref, panel_ref = refs[: len(kinds)], refs[-2], refs[-1]
    col_index = lax.axis_index("col")
    count = len(origins)
    rows = out_ref.shape[0]
    for slot in range(count):
        origin = looked_up(col_index, origins[slot])
        for kind, ref in zip(kinds, arrays):
            members = tuple(i for i in range(count) if places[slot][i] == kind)
            if members:

                @pl.when(among(col_index, members))
                def _():
                    place_piece(panel_ref, pl.ds(0, rows), ref[pl.ds(0, rows), :], origin, count, size)

    def store(first, block):
        out_ref[:, pl.ds(first, tile)] = block

    factor_from(panel_ref, inverse_ref, rows, tile, store)


def column_factor_kernel(size, tile, part, inverse_ref, *refs):
    near, far, out_ref, panel_ref = refs[: len(refs) // 2 - 1], refs[len(refs) // 2 - 1:-2], refs[-2], refs[-1]
    row_index = lax.axis_index("row")
    col_index = lax.axis_index("col")
    count = lax.axis_size("col")
    rows = out_ref.shape[0]
    for mask in range(len(near)):
        at = pl.ds(pl.multiple_of((row_index ^ mask) * part, ROW_TILE), part)
        place_piece(panel_ref, at, near[mask][...], col_index, count, size)
        for apart in range(1, count):
            origin = lax.rem(col_index + count - apart, count)
            place_piece(
                panel_ref, at, far[mask][pl.ds((apart - 1) * part, part), :], origin, count, size
            )

    def store(first, block):
        out_ref[:, pl.ds(first, tile)] = block

    factor_from(panel_ref, inverse_ref, rows, tile, store)


def product_kernel(rows_ref, own_ref, other_ref, front_ref, out_ref):
    sub_index = lax.axis_index("sub")
    size = out_ref.shape[2]
    slot_count = out_ref.shape[0]
    at = pl.ds(pl.multiple_of(pl.program_id(0) * size, size), size)
    columns = jnp.concatenate([own_ref[at, :], other_ref[at, :]], axis=0)
    product = lax.dot_general(rows_ref[...], columns, CONTRACT, preferred_element_type=jnp.float32)
    for m in range(slot_count):
        for n in range(2):
            home = sub_index if n == 0 else 1 - sub_index
            block = product[m * size:(m + 1) * size, n * size:(n + 1) * size]
            out_ref[m, home] = (front_ref[m, home].astype(jnp.float32) - block).astype(jnp.bfloat16)


def body(front_entries, block_pattern, child_update, child_map, diag_inverse):
    slot_count = front_entries.shape[0]
    size = front_entries.shape[3]
    column_count = front_entries.shape[4]
    child_count = child_update.shape[1]
    row_size = lax.axis_size("row")
    col_size = lax.axis_size("col")
    groups = -(-(PANEL // size) // col_size)
    tile = 2 * size
    rows = slot_count * size
    part = -(-rows // (row_size * ROW_TILE)) * ROW_TILE
    padded = part * row_size
    depth = groups * col_size * size
    entries = front_entries.reshape(slot_count, size, column_count, size).transpose(0, 2, 1, 3)
    pattern = block_pattern.reshape(slot_count, column_count)
    own = child_update.reshape(child_count, size, child_count, size).transpose(0, 2, 1, 3)

    received = flipped(own, "sub", 1)
    inverse = gather_inverse(diag_inverse)
    piece, *parts = call(
        functools.partial(panel_kernel, tuple(range(groups)), part),
        [bf16(padded, groups * size)] + [bf16(part, groups * size)] * row_size,
        [
            SCALARS,
            SCALARS,
            pl.BlockSpec((slot_count, groups, size, size), lambda i: (0, 0, 0, 0)),
            pl.BlockSpec(own.shape, lambda i: (0, 0, 0, 0)),
            ON_CHIP,
        ],
        grid=(1,),
    )(child_map, pattern, entries, own, received)

    held = [parts[0]] + [flipped(parts[mask], "row", mask) for mask in range(1, row_size)]
    near, *sends = call(turn_kernel, [bf16(part, groups * size)] * col_size, [ON_CHIP] * row_size)(*held)
    used, origins, places = line_plan(col_size)
    line = line_swaps(piece, "col")
    turned = [shifted(block, "col", apart) for apart, block in enumerate(sends, 1)]
    far = jnp.concatenate(turned, axis=0)
    near_all = [near] + [flipped(near, "row", mask) for mask in range(1, row_size)]
    far_all = [far] + [flipped(far, "row", mask) for mask in range(1, row_size)]
    other_near = [flipped(block, "sub", 1) for block in near_all]
    other_far = [flipped(block, "sub", 1) for block in far_all]

    front = call(
        functools.partial(front_kernel, tuple(range(groups, column_count))),
        bf16(slot_count, column_count, size, size),
        [SCALARS, SCALARS] + [ON_CHIP] * 4,
        moved=6 << 20,
    )(child_map, pattern, entries, own, received, piece)

    kinds, arrays = [], []
    for kind, array in line:
        kinds.append(kind)
        arrays.append(array)
    scratch = [pltpu.VMEM((padded, depth), jnp.bfloat16)]
    flops = 2 * rows * PANEL * PANEL * 5 // 8
    row_factor = call(
        functools.partial(row_factor_kernel, places, origins, kinds, size, tile),
        bf16(rows, PANEL), [ON_CHIP] * (1 + len(arrays)), flops=flops, scratch_shapes=scratch,
    )(inverse, *arrays)
    halves = [
        call(
            functools.partial(column_factor_kernel, size, tile, part),
            bf16(rows, PANEL), [ON_CHIP] * (1 + 2 * row_size), flops=flops, scratch_shapes=scratch,
        )(inverse, *near_set, *far_set)
        for near_set, far_set in ((near_all, far_all), (other_near, other_far))
    ]
    pair = pl.BlockSpec((slot_count, 2, size, size), lambda i: (0, i, 0, 0))
    trailing = call(
        product_kernel,
        bf16(slot_count, column_count, size, size),
        [ON_CHIP] * 3 + [pair],
        flops=2 * rows * rows * 2 * PANEL,
        grid=(slot_count,),
        out_specs=pair,
    )(row_factor, *halves, front)
    return trailing.transpose(0, 2, 1, 3).reshape(
        slot_count, 1, 1, size, column_count, 1, size
    )


def solution(mesh):
    return jax.shard_map(
        body,
        mesh=mesh,
        in_specs=(
            P(None, "sub", "row", None, None, "col", None),
            P(None, "sub", "row", None, "col"),
            P("sub", None, "row", None, None, "col", None),
            P(),
            P("col", None),
        ),
        out_specs=P(None, "sub", "row", None, None, "col", None),
        check_vma=False,
    )
```

```python
import functools

import jax
import jax.numpy as jnp
from jax import lax
from jax.experimental import pallas as pl
from jax.experimental.pallas import tpu as pltpu
from jax.sharding import PartitionSpec as P

PANEL = 1024
ROW_TILE = 16
VMEM_BYTES = 16 * 1024 * 1024
CONTRACT = (((1,), (1,)), ((), ()))
ON_CHIP = pl.BlockSpec(memory_space=pltpu.VMEM)
SCALARS = pl.BlockSpec(memory_space=pltpu.SMEM)


def call(kernel, out_shape, in_specs, flops=0, moved=1 << 19, **more):
    single = not isinstance(out_shape, (list, tuple))
    return pl.pallas_call(
        kernel,
        out_shape=out_shape,
        in_specs=in_specs,
        out_specs=more.pop("out_specs", ON_CHIP if single else [ON_CHIP] * len(out_shape)),
        compiler_params=pltpu.CompilerParams(vmem_limit_bytes=VMEM_BYTES),
        cost_estimate=pl.CostEstimate(flops=flops, bytes_accessed=moved, transcendentals=0),
        **more,
    )


def bf16(*shape):
    return jax.ShapeDtypeStruct(shape, jnp.bfloat16)


def f32(*shape):
    return jax.ShapeDtypeStruct(shape, jnp.float32)


def flipped(block, axis, mask):
    count = lax.axis_size(axis)
    return lax.ppermute(block, axis, [(i, i ^ mask) for i in range(count)])


def shifted(block, axis, apart):
    count = lax.axis_size(axis)
    return lax.ppermute(block, axis, [(i, (i + apart) % count) for i in range(count)])


def swap_even(i, count):
    return i ^ 1 if i ^ 1 < count else i


def swap_odd(i, count):
    j = ((i + 1) ^ 1) - 1
    return j if 0 <= j < count else i


@functools.cache
def line_plan(count):
    streams = ([list(range(count))], [list(range(count))])
    seen = [[(0, 0, i)] for i in range(count)]
    step = 0
    while min(len(s) for s in seen) < count:
        step += 1
        for stream in (0, 1):
            swap = swap_even if (step + stream) % 2 == 1 else swap_odd
            last = streams[stream][-1]
            streams[stream].append([last[swap(i, count)] for i in range(count)])
            for i in range(count):
                origin = streams[stream][-1][i]
                if all(origin != o for _, _, o in seen[i]):
                    seen[i].append((stream, step, origin))
    used = [max([k for s in seen for st, k, _ in s if st == stream]) for stream in (0, 1)]
    origins = [[seen[i][j][2] for i in range(count)] for j in range(count)]
    places = [[seen[i][j][:2] for i in range(count)] for j in range(count)]
    return used, origins, places


def line_swaps(block, axis):
    count = lax.axis_size(axis)
    used, _, places = line_plan(count)
    held = {(0, 0): block}
    for step in range(1, max(used) + 1):
        for stream in (0, 1):
            if step <= used[stream]:
                swap = swap_even if (step + stream) % 2 == 1 else swap_odd
                before = held[(stream, step - 1)] if step > 1 else block
                held[(stream, step)] = lax.ppermute(
                    before, axis, [(i, swap(i, count)) for i in range(count)]
                )
    kinds = sorted({kind for row in places for kind in row})
    return [(kind, held[kind]) for kind in kinds]


def among(index, members):
    found = index == members[0]
    for member in members[1:]:
        found = jnp.logical_or(found, index == member)
    return found


def looked_up(index, table):
    value = jnp.int32(table[0])
    for i, entry in enumerate(table[1:], 1):
        value = jnp.where(index == i, jnp.int32(entry), value)
    return value


def found_at(map_ref, child, place, wanted, child_count):
    at = jnp.int32(0)
    found = jnp.float32(0)
    for k in range(child_count):
        same = map_ref[child, k, place] == wanted
        at = jnp.where(same, jnp.int32(k), at)
        found = jnp.where(same, jnp.float32(1), found)
    return at, found


def block_places(map_ref, child, columns, slot_count, child_count):
    sub_index, row_index, col_index = (lax.axis_index(name) for name in ("sub", "row", "col"))
    rows = [
        found_at(map_ref, child, row_index, 2 * a + sub_index, child_count) for a in range(slot_count)
    ]
    cols = [found_at(map_ref, child, col_index, b, child_count) for b in columns]
    return rows, cols


def child_block(ref, row, col):
    return ref[row[0], col[0]].astype(jnp.float32) * (row[1] * col[1])


def base_kernel(map_ref, pattern_ref, entries_hbm, own_hbm, base_ref, entries_ref, own_ref, sems):
    slot_count, groups, size, _ = entries_ref.shape
    copies = [
        pltpu.make_async_copy(entries_hbm.at[:, pl.ds(0, groups)], entries_ref, sems.at[0]),
        pltpu.make_async_copy(own_hbm, own_ref, sems.at[1]),
    ]
    for copy in copies:
        copy.start()
    rows, cols = block_places(
        map_ref, lax.axis_index("sub"), range(groups), slot_count, own_ref.shape[0]
    )
    for copy in copies:
        copy.wait()
    for a in range(slot_count):
        for b in range(groups):
            block = entries_ref[a, b].astype(jnp.float32) * pattern_ref[a, b].astype(jnp.float32)
            base_ref[pl.ds(a * size, size), pl.ds(b * size, size)] = block + child_block(
                own_ref, rows[a], cols[b]
            )


def panel_kernel(slot_count, map_ref, base_ref, received_ref, piece_ref):
    size = received_ref.shape[2]
    groups = base_ref.shape[1] // size
    rows, cols = block_places(
        map_ref, 1 - lax.axis_index("sub"), range(groups), slot_count, received_ref.shape[0]
    )
    for a in range(slot_count):
        for b in range(groups):
            at = (pl.ds(a * size, size), pl.ds(b * size, size))
            block = base_ref[at] + child_block(received_ref, rows[a], cols[b])
            piece_ref[at] = block.astype(jnp.bfloat16)
    used = slot_count * size
    if used < piece_ref.shape[0]:
        piece_ref[pl.ds(used, piece_ref.shape[0] - used), :] = jnp.zeros(
            (piece_ref.shape[0] - used, piece_ref.shape[1]), piece_ref.dtype
        )


def front_kernel(groups, map_ref, pattern_ref, entries_ref, own_ref, received_ref, piece_ref, out_ref):
    slot_count, column_count, size, _ = entries_ref.shape
    child_count = own_ref.shape[0]
    sub_index = lax.axis_index("sub")
    columns = range(groups, column_count)
    places = [
        block_places(map_ref, child, columns, slot_count, child_count)
        for child in (sub_index, 1 - sub_index)
    ]
    for a in range(slot_count):
        for b in range(groups):
            out_ref[a, b] = piece_ref[pl.ds(a * size, size), pl.ds(b * size, size)]
        for n, b in enumerate(columns):
            total = entries_ref[a, b].astype(jnp.float32) * pattern_ref[a, b].astype(jnp.float32)
            for (rows, cols), ref in zip(places, (own_ref, received_ref)):
                total = total + child_block(ref, rows[a], cols[n])
            out_ref[a, b] = total.astype(jnp.bfloat16)


def inverse_kernel(part, in_ref, out_ref):
    rows, width = in_ref.shape
    blocks = rows // part
    col_size = lax.axis_size("col")
    for n in range(blocks):
        plane, col = divmod(n, col_size)
        top = (col * (blocks // col_size) + plane) * part
        block = in_ref[pl.ds(n * part, part), :].astype(jnp.float32)
        row_at = top + lax.broadcasted_iota(jnp.int32, (part, width), 0)
        col_at = lax.broadcasted_iota(jnp.int32, (part, width), 1)
        out_ref[pl.ds(top, part), :] = jnp.where(col_at <= row_at, block, 0.0).astype(jnp.bfloat16)


def gather_inverse(diag_inverse):
    sub_size, row_size = lax.axis_size("sub"), lax.axis_size("row")
    sub_index, row_index = lax.axis_index("sub"), lax.axis_index("row")
    share, width = diag_inverse.shape
    part = share // (sub_size * row_size)
    if part % ROW_TILE:
        part = share
        whole = lax.all_gather(diag_inverse, "col", axis=0, tiled=True)
    else:
        mine = lax.dynamic_slice_in_dim(diag_inverse, (sub_index * row_size + row_index) * part, part, 0)
        whole = lax.all_gather(mine, ("sub", "row", "col"), axis=0, tiled=True)
    return call(functools.partial(inverse_kernel, part), bf16(*whole.shape), [ON_CHIP], moved=4 << 20)(whole)


def place_piece(panel_ref, rows, block, origin, count, size):
    for g in range(block.shape[1] // size):
        left = (g * count + origin) * size
        if not isinstance(origin, int):
            left = pl.multiple_of(left, size)
        panel_ref[rows, pl.ds(left, size)] = block[:, g * size:(g + 1) * size]


def factor_from(panel_ref, inverse_ref, out_ref, tile):
    rows, width = out_ref.shape
    for first in range(0, width, tile):
        out_ref[:, pl.ds(first, tile)] = lax.dot_general(
            panel_ref[pl.ds(0, rows), pl.ds(0, first + tile)],
            inverse_ref[pl.ds(first, tile), pl.ds(0, first + tile)],
            CONTRACT,
            preferred_element_type=jnp.float32,
        ).astype(jnp.bfloat16)


def row_factor_kernel(places, origins, kinds, size, tile, inverse_ref, *refs):
    arrays, out_ref, panel_ref = refs[: len(kinds)], refs[-2], refs[-1]
    col_index = lax.axis_index("col")
    count = len(origins)
    rows = out_ref.shape[0]
    for slot in range(count):
        origin = looked_up(col_index, origins[slot])
        for kind, ref in zip(kinds, arrays):
            members = tuple(i for i in range(count) if places[slot][i] == kind)
            if members:

                @pl.when(among(col_index, members))
                def _():
                    place_piece(panel_ref, pl.ds(0, rows), ref[pl.ds(0, rows), :], origin, count, size)

    factor_from(panel_ref, inverse_ref, out_ref, tile)


def column_factor_kernel(size, tile, inverse_ref, *refs):
    parts, out_ref, panel_ref = refs[:-2], refs[-2], refs[-1]
    row_index = lax.axis_index("row")
    count = lax.axis_size("col")
    part = parts[0].shape[0] // count
    for mask, ref in enumerate(parts):
        at = pl.ds(pl.multiple_of((row_index ^ mask) * part, ROW_TILE), part)
        for col in range(count):
            place_piece(panel_ref, at, ref[pl.ds(col * part, part), :], col, count, size)
    factor_from(panel_ref, inverse_ref, out_ref, tile)


def product_kernel(mine, rows_ref, columns_ref, front_ref, *refs):
    out_hbm, out_ref, sem = refs[-3:]
    sub_index = lax.axis_index("sub")
    half = sub_index if mine else 1 - sub_index
    slot_count, _, size, _ = out_ref.shape
    product = lax.dot_general(
        rows_ref[...], columns_ref[...], CONTRACT, preferred_element_type=jnp.float32
    )
    for m in range(slot_count):
        for a in range(slot_count):
            block = product[m * size:(m + 1) * size, a * size:(a + 1) * size]
            out_ref[m, a] = (front_ref[m, a, half].astype(jnp.float32) - block).astype(jnp.bfloat16)
    copy = pltpu.make_async_copy(out_ref, out_hbm.at[:, :, half], sem)
    copy.start()
    copy.wait()


def body(front_entries, block_pattern, child_update, child_map, diag_inverse):
    slot_count = front_entries.shape[0]
    size = front_entries.shape[3]
    column_count = front_entries.shape[4]
    child_count = child_update.shape[1]
    row_size = lax.axis_size("row")
    col_size = lax.axis_size("col")
    groups = -(-(PANEL // size) // col_size)
    tile = PANEL // 2
    rows = slot_count * size
    part = -(-rows // (row_size * ROW_TILE)) * ROW_TILE
    padded = part * row_size
    depth = groups * col_size * size
    in_hbm = pl.BlockSpec(memory_space=pltpu.HBM)
    entries = front_entries.reshape(slot_count, size, column_count, size).transpose(0, 2, 1, 3)
    pattern = block_pattern.reshape(slot_count, column_count)
    own = child_update.reshape(child_count, size, child_count, size).transpose(0, 2, 1, 3)

    received = flipped(own, "sub", 1)
    inverse = gather_inverse(diag_inverse)
    base = call(
        base_kernel,
        f32(rows, groups * size),
        [SCALARS, SCALARS, in_hbm, in_hbm],
        scratch_shapes=[
            pltpu.VMEM((slot_count, groups, size, size), jnp.bfloat16),
            pltpu.VMEM(own.shape, jnp.bfloat16),
            pltpu.SemaphoreType.DMA((2,)),
        ],
    )(child_map, pattern, entries, own)
    piece = call(
        functools.partial(panel_kernel, slot_count), bf16(padded, groups * size), [SCALARS, ON_CHIP, ON_CHIP]
    )(child_map, base, received)

    used, origins, places = line_plan(col_size)
    line = line_swaps(piece, "col")
    scattered = lax.all_to_all(piece.reshape(row_size, part, groups * size), "row", 0, 0, tiled=True)
    turned = lax.all_to_all(scattered, "col", 0, 0, tiled=True)
    turned = turned.reshape(col_size * part, groups * size)
    parts = [turned] + [flipped(turned, "row", mask) for mask in range(1, row_size)]

    front = call(
        functools.partial(front_kernel, groups),
        bf16(slot_count, column_count, size, size),
        [SCALARS, SCALARS] + [ON_CHIP] * 4,
        moved=6 << 20,
    )(child_map, pattern, entries, own, received, piece)
    front = front.reshape(slot_count, slot_count, 2, size, size)

    kinds = [kind for kind, _ in line]
    arrays = [array for _, array in line]
    scratch = [pltpu.VMEM((padded, depth), jnp.bfloat16)]
    flops = 2 * rows * PANEL * PANEL * 3 // 4
    column_factor = call(
        functools.partial(column_factor_kernel, size, tile),
        bf16(rows, PANEL), [ON_CHIP] * (1 + row_size), flops=flops, scratch_shapes=scratch,
    )(inverse, *parts)
    other_factor = flipped(column_factor, "sub", 1)
    row_factor = call(
        functools.partial(row_factor_kernel, places, origins, kinds, size, tile),
        bf16(rows, PANEL), [ON_CHIP] * (1 + len(arrays)), flops=flops, scratch_shapes=scratch,
    )(inverse, *arrays)
    product = functools.partial(
        call,
        out_shape=bf16(slot_count, slot_count, 2, size, size),
        flops=2 * rows * rows * PANEL,
        out_specs=in_hbm,
        scratch_shapes=[
            pltpu.VMEM((slot_count, slot_count, size, size), jnp.bfloat16),
            pltpu.SemaphoreType.DMA,
        ],
    )
    trailing = product(functools.partial(product_kernel, True), in_specs=[ON_CHIP] * 3)(
        row_factor, column_factor, front
    )
    trailing = product(
        functools.partial(product_kernel, False), in_specs=[ON_CHIP] * 3 + [in_hbm],
        input_output_aliases={3: 0},
    )(row_factor, other_factor, front, trailing)
    return trailing.reshape(slot_count, column_count, size, size).transpose(0, 2, 1, 3).reshape(
        slot_count, 1, 1, size, column_count, 1, size
    )


def solution(mesh):
    return jax.shard_map(
        body,
        mesh=mesh,
        in_specs=(
            P(None, "sub", "row", None, None, "col", None),
            P(None, "sub", "row", None, "col"),
            P("sub", None, "row", None, None, "col", None),
            P(),
            P("col", None),
        ),
        out_specs=P(None, "sub", "row", None, None, "col", None),
        check_vma=False,
    )
```

```python
import functools

import jax
import jax.numpy as jnp
from jax import lax
from jax.experimental import pallas as pl
from jax.experimental.pallas import tpu as pltpu
from jax.sharding import PartitionSpec as P

PANEL = 1024
ROW_TILE = 16
VMEM_BYTES = 12 * 1024 * 1024
MOST_VMEM_BYTES = 61 * 1024 * 1024
CONTRACT = (((1,), (1,)), ((), ()))
ON_CHIP = pl.BlockSpec(memory_space=pltpu.VMEM)
SCALARS = pl.BlockSpec(memory_space=pltpu.SMEM)


def call(kernel, out_shape, in_specs, flops=0, moved=1 << 19, limit=VMEM_BYTES, **more):
    single = not isinstance(out_shape, (list, tuple))
    return pl.pallas_call(
        kernel,
        out_shape=out_shape,
        in_specs=in_specs,
        out_specs=more.pop("out_specs", ON_CHIP if single else [ON_CHIP] * len(out_shape)),
        compiler_params=pltpu.CompilerParams(vmem_limit_bytes=limit),
        cost_estimate=pl.CostEstimate(flops=flops, bytes_accessed=moved, transcendentals=0),
        **more,
    )


def bf16(*shape):
    return jax.ShapeDtypeStruct(shape, jnp.bfloat16)


def f32(*shape):
    return jax.ShapeDtypeStruct(shape, jnp.float32)


def flipped(block, axis, mask):
    count = lax.axis_size(axis)
    return lax.ppermute(block, axis, [(i, i ^ mask) for i in range(count)])


def shifted(block, axis, apart):
    count = lax.axis_size(axis)
    return lax.ppermute(block, axis, [(i, (i + apart) % count) for i in range(count)])


def swap_even(i, count):
    return i ^ 1 if i ^ 1 < count else i


def swap_odd(i, count):
    j = ((i + 1) ^ 1) - 1
    return j if 0 <= j < count else i


@functools.cache
def line_plan(count):
    even = [swap_even(i, count) for i in range(count)]
    odd = [swap_odd(i, count) for i in range(count)]
    if count == 4:
        levels = [[(1, 0, even), (2, 0, odd)], [(3, 2, [2, 0, 3, 1]), (4, 1, [1, 3, 0, 2])]]
    else:
        levels, last = [], [0, 0]
        for step in range(count - 1):
            level = []
            for stream in (0, 1):
                level.append((1 + 2 * step + stream, last[stream], odd if (step + stream) % 2 else even))
                last[stream] = level[-1][0]
            levels.append(level)
    whose = {0: list(range(count))}
    seen = [[(0, i)] for i in range(count)]
    for level in levels:
        for array, source, to in level:
            whose[array] = [None] * count
            for i in range(count):
                whose[array][to[i]] = whose[source][i]
            for i in range(count):
                if all(whose[array][i] != origin for _, origin in seen[i]):
                    seen[i].append((array, whose[array][i]))
    origins = [[seen[i][j][1] for i in range(count)] for j in range(count)]
    places = [[seen[i][j][0] for i in range(count)] for j in range(count)]
    return levels, origins, places


class Line:
    def __init__(self, block, axis):
        self.axis = axis
        self.levels, _, self.places = line_plan(lax.axis_size(axis))
        self.held = {0: block}
        self.at = 0

    def step(self):
        for array, source, to in self.levels[self.at]:
            self.held[array] = lax.ppermute(self.held[source], self.axis, list(enumerate(to)))
        self.at += 1
        return self.at < len(self.levels)

    def fenced(self, *values):
        last = [array for array, _, _ in self.levels[self.at - 1]]
        out = fence(*values, *(self.held[array] for array in last))
        self.held.update(zip(last, out[len(values):]))
        return out[: len(values)]

    def taken(self):
        kinds = sorted({kind for row in self.places for kind in row})
        return kinds, [self.held[kind] for kind in kinds]


def among(index, members):
    found = index == members[0]
    for member in members[1:]:
        found = jnp.logical_or(found, index == member)
    return found


def looked_up(index, table):
    value = jnp.int32(table[0])
    for i, entry in enumerate(table[1:], 1):
        value = jnp.where(index == i, jnp.int32(entry), value)
    return value


def fence_kernel(*refs):
    pass


def fence(*values):
    place = pl.BlockSpec(memory_space=pl.ANY)
    return pl.pallas_call(
        fence_kernel,
        out_shape=[jax.ShapeDtypeStruct(v.shape, v.dtype) for v in values],
        in_specs=[place] * len(values),
        out_specs=[place] * len(values),
        input_output_aliases={n: n for n in range(len(values))},
    )(*values)


def found_at(map_ref, child, place, wanted, child_count):
    at = jnp.int32(0)
    found = jnp.float32(0)
    for k in range(child_count):
        same = map_ref[child, place, k] == wanted
        at = jnp.where(same, jnp.int32(k), at)
        found = jnp.where(same, jnp.float32(1), found)
    return at, found


def block_places(map_ref, child, columns, slot_count, child_count):
    sub_index, row_index, col_index = (lax.axis_index(name) for name in ("sub", "row", "col"))
    rows = [
        found_at(map_ref, child, row_index, 2 * a + sub_index, child_count) for a in range(slot_count)
    ]
    cols = [found_at(map_ref, child, col_index, b, child_count) for b in columns]
    return rows, cols


def child_block(ref, row, col):
    return ref[row[0], col[0]].astype(jnp.float32) * (row[1] * col[1])


def base_kernel(
    map_ref, pattern_ref, entries_hbm, own_hbm, inverse_hbm, base_ref, share_ref, entries_ref, own_ref, sems
):
    slot_count, groups, size, _ = entries_ref.shape
    sub_index, row_index = lax.axis_index("sub"), lax.axis_index("row")
    part = share_ref.shape[0]
    first = (sub_index * lax.axis_size("row") + row_index) * part if part < inverse_hbm.shape[0] else 0
    copies = [
        pltpu.make_async_copy(inverse_hbm.at[pl.ds(first, part)], share_ref, sems.at[2]),
        pltpu.make_async_copy(entries_hbm.at[:, pl.ds(0, groups)], entries_ref, sems.at[0]),
        pltpu.make_async_copy(own_hbm, own_ref, sems.at[1]),
    ]
    for copy in copies:
        copy.start()
    rows, cols = block_places(map_ref, sub_index, range(groups), slot_count, own_ref.shape[0])
    for copy in copies:
        copy.wait()
    for a in range(slot_count):
        for b in range(groups):
            block = entries_ref[a, b].astype(jnp.float32) * pattern_ref[a, 0, b].astype(jnp.float32)
            base_ref[pl.ds(a * size, size), pl.ds(b * size, size)] = block + child_block(
                own_ref, rows[a], cols[b]
            )


def panel_kernel(slot_count, part, map_ref, base_ref, received_ref, piece_ref, *part_refs):
    size = received_ref.shape[2]
    groups = base_ref.shape[1] // size
    rows, cols = block_places(
        map_ref, 1 - lax.axis_index("sub"), range(groups), slot_count, received_ref.shape[0]
    )
    for a in range(slot_count):
        for b in range(groups):
            at = (pl.ds(a * size, size), pl.ds(b * size, size))
            block = base_ref[at] + child_block(received_ref, rows[a], cols[b])
            piece_ref[at] = block.astype(jnp.bfloat16)
    used = slot_count * size
    if used < piece_ref.shape[0]:
        piece_ref[pl.ds(used, piece_ref.shape[0] - used), :] = jnp.zeros(
            (piece_ref.shape[0] - used, piece_ref.shape[1]), piece_ref.dtype
        )
    row_index = lax.axis_index("row")
    for mask, ref in enumerate(part_refs):
        ref[...] = piece_ref[pl.ds(pl.multiple_of((row_index ^ mask) * part, ROW_TILE), part), :]


def front_kernel(groups, map_ref, pattern_ref, entries_ref, own_ref, received_ref, piece_ref, out_ref):
    slot_count, column_count, size, _ = entries_ref.shape
    child_count = own_ref.shape[0]
    sub_index = lax.axis_index("sub")
    columns = range(groups, column_count)
    places = [
        block_places(map_ref, child, columns, slot_count, child_count)
        for child in (sub_index, 1 - sub_index)
    ]
    for a in range(slot_count):
        for b in range(groups):
            out_ref[a, b] = piece_ref[pl.ds(a * size, size), pl.ds(b * size, size)]
        for n, b in enumerate(columns):
            total = entries_ref[a, b].astype(jnp.float32) * pattern_ref[a, 0, b].astype(jnp.float32)
            for (rows, cols), ref in zip(places, (own_ref, received_ref)):
                total = total + child_block(ref, rows[a], cols[n])
            out_ref[a, b] = total.astype(jnp.bfloat16)


def inverse_kernel(part, *refs):
    *in_refs, out_ref = refs
    sub_index, col_index = lax.axis_index("sub"), lax.axis_index("col")
    row_size, col_size = lax.axis_size("row"), lax.axis_size("col")
    width = out_ref.shape[1]
    share = part * row_size * len(in_refs)
    for n, ref in enumerate(in_refs):
        sub_at = sub_index if n == 0 else 1 - sub_index
        for row in range(row_size):
            for apart in range(col_size):
                col = lax.rem(col_index + col_size - apart, col_size)
                top = pl.multiple_of(col * share + (sub_at * row_size + row) * part, ROW_TILE)
                block = ref[pl.ds((row * col_size + apart) * part, part), :].astype(jnp.float32)
                row_at = top + lax.broadcasted_iota(jnp.int32, (part, width), 0)
                col_at = lax.broadcasted_iota(jnp.int32, (part, width), 1)
                out_ref[pl.ds(top, part), :] = jnp.where(col_at <= row_at, block, 0.0).astype(
                    jnp.bfloat16
                )


def lower_kernel(in_ref, out_ref):
    row_at = lax.broadcasted_iota(jnp.int32, in_ref.shape, 0)
    col_at = lax.broadcasted_iota(jnp.int32, in_ref.shape, 1)
    out_ref[...] = jnp.where(col_at <= row_at, in_ref[...].astype(jnp.float32), 0.0).astype(jnp.bfloat16)


def join_kernel(*refs):
    *in_refs, out_ref = refs
    rows = in_refs[0].shape[0]
    for n, ref in enumerate(in_refs):
        out_ref[pl.ds(n * rows, rows), :] = ref[...]


def joined(blocks):
    rows, width = blocks[0].shape
    return call(join_kernel, bf16(rows * len(blocks), width), [ON_CHIP] * len(blocks))(*blocks)


def inverse_line(share, whole):
    if whole:
        return lax.all_gather(share, "col", axis=0, tiled=True)
    return joined([share] + [shifted(share, "col", apart) for apart in range(1, lax.axis_size("col"))])


def whole_inverse(plane, part, whole):
    width = plane.shape[1]
    if whole:
        return call(lower_kernel, bf16(width, width), [ON_CHIP], moved=4 << 20)(plane)
    return call(
        functools.partial(inverse_kernel, part), bf16(width, width), [ON_CHIP] * 2, moved=4 << 20
    )(plane, flipped(plane, "sub", 1))


def place_piece(panel_ref, rows, block, origin, count, size):
    for g in range(block.shape[1] // size):
        left = (g * count + origin) * size
        if not isinstance(origin, int):
            left = pl.multiple_of(left, size)
        panel_ref[rows, pl.ds(left, size)] = block[:, g * size:(g + 1) * size]


def factor_from(panel_ref, inverse_ref, out_ref, tile):
    rows, width = out_ref.shape
    for first in range(0, width, tile):
        out_ref[:, pl.ds(first, tile)] = lax.dot_general(
            panel_ref[pl.ds(0, rows), pl.ds(0, first + tile)],
            inverse_ref[pl.ds(first, tile), pl.ds(0, first + tile)],
            CONTRACT,
            preferred_element_type=jnp.float32,
        ).astype(jnp.bfloat16)


def row_factor_kernel(places, origins, kinds, size, tile, inverse_ref, *refs):
    arrays, out_ref, panel_ref = refs[: len(kinds)], refs[-2], refs[-1]
    col_index = lax.axis_index("col")
    count = len(origins)
    rows = out_ref.shape[0]
    for slot in range(count):
        origin = looked_up(col_index, origins[slot])
        for kind, ref in zip(kinds, arrays):
            members = tuple(i for i in range(count) if places[slot][i] == kind)
            if members:

                @pl.when(among(col_index, members))
                def _():
                    place_piece(panel_ref, pl.ds(0, rows), ref[pl.ds(0, rows), :], origin, count, size)

    factor_from(panel_ref, inverse_ref, out_ref, tile)


def column_factor_kernel(size, tile, inverse_ref, *refs):
    parts, out_ref, panel_ref = refs[:-2], refs[-2], refs[-1]
    row_index = lax.axis_index("row")
    count = lax.axis_size("col")
    part = parts[0].shape[0] // count
    for mask, ref in enumerate(parts):
        at = pl.ds(pl.multiple_of((row_index ^ mask) * part, ROW_TILE), part)
        for col in range(count):
            place_piece(panel_ref, at, ref[pl.ds(col * part, part), :], col, count, size)
    factor_from(panel_ref, inverse_ref, out_ref, tile)


def product_kernel(mine, rows_ref, columns_ref, front_ref, *refs):
    out_hbm, out_ref, sem = refs[-3:]
    sub_index = lax.axis_index("sub")
    half = sub_index if mine else 1 - sub_index
    slot_count, _, size, _ = out_ref.shape
    product = lax.dot_general(
        rows_ref[...], columns_ref[...], CONTRACT, preferred_element_type=jnp.float32
    )
    for m in range(slot_count):
        for a in range(slot_count):
            block = product[m * size:(m + 1) * size, a * size:(a + 1) * size]
            out_ref[m, a] = (front_ref[m, a, half].astype(jnp.float32) - block).astype(jnp.bfloat16)
    copy = pltpu.make_async_copy(out_ref, out_hbm.at[:, :, half], sem)
    copy.start()
    copy.wait()


def body(front_entries, block_pattern, child_update, child_map, diag_inverse):
    slot_count = front_entries.shape[0]
    size = front_entries.shape[3]
    column_count = front_entries.shape[4]
    child_count = child_update.shape[1]
    row_size = lax.axis_size("row")
    col_size = lax.axis_size("col")
    groups = -(-(PANEL // size) // col_size)
    tile = PANEL // 2
    rows = slot_count * size
    part = -(-rows // (row_size * ROW_TILE)) * ROW_TILE
    padded = part * row_size
    depth = groups * col_size * size
    in_hbm = pl.BlockSpec(memory_space=pltpu.HBM)
    entries = front_entries.reshape(slot_count, size, column_count, size).transpose(0, 2, 1, 3)
    pattern = block_pattern.reshape(slot_count, 1, column_count)
    slots = child_map.transpose(0, 2, 1)
    own = child_update.reshape(child_count, size, child_count, size).transpose(0, 2, 1, 3)
    share = diag_inverse.shape[0]
    even = share // (lax.axis_size("sub") * row_size)
    whole = even % ROW_TILE > 0
    share = share if whole else even

    received = flipped(own, "sub", 1)
    base, inverse_share = call(
        base_kernel,
        [f32(rows, groups * size), bf16(share, PANEL)],
        [SCALARS, SCALARS] + [in_hbm] * 3,
        limit=MOST_VMEM_BYTES,
        scratch_shapes=[
            pltpu.VMEM((slot_count, groups, size, size), jnp.bfloat16),
            pltpu.VMEM(own.shape, jnp.bfloat16),
            pltpu.SemaphoreType.DMA((3,)),
        ],
    )(slots, pattern, entries, own, diag_inverse)
    piece = call(
        functools.partial(panel_kernel, slot_count, part), bf16(padded, groups * size), [SCALARS, ON_CHIP, ON_CHIP]
    )(slots, base, received)
    line = inverse_line(inverse_share, whole)
    piece, line = fence(piece, line)
    plane = line if whole else lax.all_gather(line, "row", axis=0, tiled=True)

    _, origins, places = line_plan(col_size)
    pieces = Line(piece, "col")
    pieces.step()
    scattered = lax.all_to_all(piece.reshape(row_size, part, groups * size), "row", 0, 0, tiled=True)
    (scattered,) = pieces.fenced(scattered)
    turned = lax.all_to_all(scattered, "col", 0, 0, tiled=True).reshape(col_size * part, groups * size)
    turned, plane = pieces.fenced(turned, plane)
    inverse = whole_inverse(plane, share, whole)
    while pieces.step():
        pass
    parts = pieces.fenced(turned, *(flipped(turned, "row", mask) for mask in range(1, row_size)))

    front = call(
        functools.partial(front_kernel, groups),
        bf16(slot_count, column_count, size, size),
        [SCALARS, SCALARS] + [ON_CHIP] * 4,
        moved=6 << 20,
    )(slots, pattern, entries, own, received, piece)
    front = front.reshape(slot_count, slot_count, 2, size, size)

    kinds, arrays = pieces.taken()
    scratch = [pltpu.VMEM((padded, depth), jnp.bfloat16)]
    flops = 2 * rows * PANEL * PANEL * 3 // 4
    column_factor = call(
        functools.partial(column_factor_kernel, size, tile),
        bf16(rows, PANEL), [ON_CHIP] * (1 + row_size), flops=flops, scratch_shapes=scratch,
    )(inverse, *parts)
    other_factor = flipped(column_factor, "sub", 1)
    row_factor = call(
        functools.partial(row_factor_kernel, places, origins, kinds, size, tile),
        bf16(rows, PANEL), [ON_CHIP] * (1 + len(arrays)), flops=flops, scratch_shapes=scratch,
    )(inverse, *arrays)
    product = functools.partial(
        call,
        out_shape=bf16(slot_count, slot_count, 2, size, size),
        flops=2 * rows * rows * PANEL,
        out_specs=in_hbm,
        scratch_shapes=[
            pltpu.VMEM((slot_count, slot_count, size, size), jnp.bfloat16),
            pltpu.SemaphoreType.DMA,
        ],
    )
    trailing = product(functools.partial(product_kernel, True), in_specs=[ON_CHIP] * 3)(
        row_factor, column_factor, front
    )
    trailing = product(
        functools.partial(product_kernel, False), in_specs=[ON_CHIP] * 3 + [in_hbm],
        input_output_aliases={3: 0},
    )(row_factor, other_factor, front, trailing)
    return trailing.reshape(slot_count, column_count, size, size).transpose(0, 2, 1, 3).reshape(
        slot_count, 1, 1, size, column_count, 1, size
    )


def solution(mesh):
    return jax.shard_map(
        body,
        mesh=mesh,
        in_specs=(
            P(None, "sub", "row", None, None, "col", None),
            P(None, "sub", "row", None, "col"),
            P("sub", None, "row", None, None, "col", None),
            P(),
            P("col", None),
        ),
        out_specs=P(None, "sub", "row", None, None, "col", None),
        check_vma=False,
    )
```

```python
import functools

import jax
import jax.numpy as jnp
from jax import lax
from jax.experimental import pallas as pl
from jax.experimental.pallas import tpu as pltpu
from jax.sharding import PartitionSpec as P

PANEL = 1024
ROW_TILE = 16
VMEM_BYTES = 12 * 1024 * 1024
CONTRACT = (((1,), (1,)), ((), ()))
ON_CHIP = pl.BlockSpec(memory_space=pltpu.VMEM)
SCALARS = pl.BlockSpec(memory_space=pltpu.SMEM)


def call(kernel, out_shape, in_specs, flops=0, moved=1 << 19, **more):
    single = not isinstance(out_shape, (list, tuple))
    return pl.pallas_call(
        kernel,
        out_shape=out_shape,
        in_specs=in_specs,
        out_specs=more.pop("out_specs", ON_CHIP if single else [ON_CHIP] * len(out_shape)),
        compiler_params=pltpu.CompilerParams(vmem_limit_bytes=VMEM_BYTES),
        cost_estimate=pl.CostEstimate(flops=flops, bytes_accessed=moved, transcendentals=0),
        **more,
    )


def bf16(*shape):
    return jax.ShapeDtypeStruct(shape, jnp.bfloat16)


def f32(*shape):
    return jax.ShapeDtypeStruct(shape, jnp.float32)


def flipped(block, axis, mask):
    count = lax.axis_size(axis)
    return lax.ppermute(block, axis, [(i, i ^ mask) for i in range(count)])


def shifted(block, axis, apart):
    count = lax.axis_size(axis)
    return lax.ppermute(block, axis, [(i, (i + apart) % count) for i in range(count)])


def swap_even(i, count):
    return i ^ 1 if i ^ 1 < count else i


def swap_odd(i, count):
    j = ((i + 1) ^ 1) - 1
    return j if 0 <= j < count else i


@functools.cache
def line_plan(count):
    even = [swap_even(i, count) for i in range(count)]
    odd = [swap_odd(i, count) for i in range(count)]
    if count == 4:
        levels = [[(1, 0, even), (2, 0, odd)], [(3, 2, [2, 0, 3, 1]), (4, 1, [1, 3, 0, 2])]]
    else:
        levels, last = [], [0, 0]
        for step in range(count - 1):
            level = []
            for stream in (0, 1):
                level.append((1 + 2 * step + stream, last[stream], odd if (step + stream) % 2 else even))
                last[stream] = level[-1][0]
            levels.append(level)
    whose = {0: list(range(count))}
    seen = [[(0, i)] for i in range(count)]
    for level in levels:
        for array, source, to in level:
            whose[array] = [None] * count
            for i in range(count):
                whose[array][to[i]] = whose[source][i]
            for i in range(count):
                if all(whose[array][i] != origin for _, origin in seen[i]):
                    seen[i].append((array, whose[array][i]))
    origins = [[seen[i][j][1] for i in range(count)] for j in range(count)]
    places = [[seen[i][j][0] for i in range(count)] for j in range(count)]
    return levels, origins, places


class Line:
    def __init__(self, block, axis):
        self.axis = axis
        self.levels, _, self.places = line_plan(lax.axis_size(axis))
        self.held = {0: block}
        self.at = 0

    def step(self):
        for array, source, to in self.levels[self.at]:
            self.held[array] = lax.ppermute(self.held[source], self.axis, list(enumerate(to)))
        self.at += 1
        return self.at < len(self.levels)

    def fenced(self, *values):
        last = [array for array, _, _ in self.levels[self.at - 1]]
        out = fence(*values, *(self.held[array] for array in last))
        self.held.update(zip(last, out[len(values):]))
        return out[: len(values)]

    def taken(self):
        kinds = sorted({kind for row in self.places for kind in row})
        return kinds, [self.held[kind] for kind in kinds]


def among(index, members):
    found = index == members[0]
    for member in members[1:]:
        found = jnp.logical_or(found, index == member)
    return found


def looked_up(index, table):
    value = jnp.int32(table[0])
    for i, entry in enumerate(table[1:], 1):
        value = jnp.where(index == i, jnp.int32(entry), value)
    return value


def fence_kernel(*refs):
    pass


def fence(*values):
    place = pl.BlockSpec(memory_space=pl.ANY)
    return pl.pallas_call(
        fence_kernel,
        out_shape=[jax.ShapeDtypeStruct(v.shape, v.dtype) for v in values],
        in_specs=[place] * len(values),
        out_specs=[place] * len(values),
        input_output_aliases={n: n for n in range(len(values))},
        compiler_params=pltpu.CompilerParams(vmem_limit_bytes=1 << 20),
    )(*values)


def found_at(map_ref, child, place, wanted, child_count):
    at = jnp.int32(0)
    found = jnp.float32(0)
    for k in range(child_count):
        same = map_ref[child, place, k] == wanted
        at = jnp.where(same, jnp.int32(k), at)
        found = jnp.where(same, jnp.float32(1), found)
    return at, found


def block_places(map_ref, child, columns, slot_count, child_count):
    sub_index, row_index, col_index = (lax.axis_index(name) for name in ("sub", "row", "col"))
    rows = [
        found_at(map_ref, child, row_index, 2 * a + sub_index, child_count) for a in range(slot_count)
    ]
    cols = [found_at(map_ref, child, col_index, b, child_count) for b in columns]
    return rows, cols


def child_block(ref, row, col):
    return ref[row[0], col[0]].astype(jnp.float32) * (row[1] * col[1])


def base_kernel(map_ref, pattern_ref, entries_ref, own_ref, base_ref):
    slot_count, groups, size, _ = entries_ref.shape
    rows, cols = block_places(
        map_ref, lax.axis_index("sub"), range(groups), slot_count, own_ref.shape[0]
    )
    for a in range(slot_count):
        for b in range(groups):
            block = entries_ref[a, b].astype(jnp.float32) * pattern_ref[a, 0, b].astype(jnp.float32)
            base_ref[pl.ds(a * size, size), pl.ds(b * size, size)] = block + child_block(
                own_ref, rows[a], cols[b]
            )


def panel_kernel(slot_count, part, map_ref, base_ref, received_ref, piece_ref, *part_refs):
    size = received_ref.shape[2]
    groups = base_ref.shape[1] // size
    rows, cols = block_places(
        map_ref, 1 - lax.axis_index("sub"), range(groups), slot_count, received_ref.shape[0]
    )
    for a in range(slot_count):
        for b in range(groups):
            at = (pl.ds(a * size, size), pl.ds(b * size, size))
            block = base_ref[at] + child_block(received_ref, rows[a], cols[b])
            piece_ref[at] = block.astype(jnp.bfloat16)
    used = slot_count * size
    if used < piece_ref.shape[0]:
        piece_ref[pl.ds(used, piece_ref.shape[0] - used), :] = jnp.zeros(
            (piece_ref.shape[0] - used, piece_ref.shape[1]), piece_ref.dtype
        )
    row_index = lax.axis_index("row")
    for mask, ref in enumerate(part_refs):
        ref[...] = piece_ref[pl.ds(pl.multiple_of((row_index ^ mask) * part, ROW_TILE), part), :]


def front_kernel(groups, map_ref, pattern_ref, entries_ref, own_ref, received_ref, piece_ref, out_ref):
    slot_count, column_count, size, _ = entries_ref.shape
    child_count = own_ref.shape[0]
    sub_index = lax.axis_index("sub")
    columns = range(groups, column_count)
    places = [
        block_places(map_ref, child, columns, slot_count, child_count)
        for child in (sub_index, 1 - sub_index)
    ]
    for a in range(slot_count):
        for b in range(groups):
            out_ref[a, b] = piece_ref[pl.ds(a * size, size), pl.ds(b * size, size)]
        for n, b in enumerate(columns):
            total = entries_ref[a, b].astype(jnp.float32) * pattern_ref[a, 0, b].astype(jnp.float32)
            for (rows, cols), ref in zip(places, (own_ref, received_ref)):
                total = total + child_block(ref, rows[a], cols[n])
            out_ref[a, b] = total.astype(jnp.bfloat16)


def inverse_kernel(part, *refs):
    *in_refs, out_ref = refs
    sub_index = lax.axis_index("sub")
    row_size, col_size = lax.axis_size("row"), lax.axis_size("col")
    width = out_ref.shape[1]
    share = part * row_size * len(in_refs)
    for n, ref in enumerate(in_refs):
        sub_at = sub_index if n == 0 else 1 - sub_index
        for row in range(row_size):
            for col in range(col_size):
                top = pl.multiple_of(col * share + (sub_at * row_size + row) * part, ROW_TILE)
                block = ref[pl.ds((row * col_size + col) * part, part), :].astype(jnp.float32)
                row_at = top + lax.broadcasted_iota(jnp.int32, (part, width), 0)
                col_at = lax.broadcasted_iota(jnp.int32, (part, width), 1)
                out_ref[pl.ds(top, part), :] = jnp.where(col_at <= row_at, block, 0.0).astype(
                    jnp.bfloat16
                )


def lower_kernel(in_ref, out_ref):
    row_at = lax.broadcasted_iota(jnp.int32, in_ref.shape, 0)
    col_at = lax.broadcasted_iota(jnp.int32, in_ref.shape, 1)
    out_ref[...] = jnp.where(col_at <= row_at, in_ref[...].astype(jnp.float32), 0.0).astype(jnp.bfloat16)


def inverse_rows(diag_inverse):
    sub_size, row_size = lax.axis_size("sub"), lax.axis_size("row")
    part = diag_inverse.shape[0] // (sub_size * row_size)
    if part % ROW_TILE:
        return lax.all_gather(diag_inverse, "col", axis=0, tiled=True), None
    first = (lax.axis_index("sub") * row_size + lax.axis_index("row")) * part
    mine = lax.dynamic_slice_in_dim(diag_inverse, first, part, 0)
    return lax.all_gather(mine, ("row", "col"), axis=0, tiled=True), part


def whole_inverse(rows, part):
    width = rows.shape[1]
    if part is None:
        return call(lower_kernel, bf16(width, width), [ON_CHIP], moved=4 << 20)(rows)
    return call(
        functools.partial(inverse_kernel, part), bf16(width, width), [ON_CHIP] * 2, moved=4 << 20
    )(rows, flipped(rows, "sub", 1))


def join_kernel(*refs):
    *in_refs, out_ref = refs
    rows = in_refs[0].shape[0]
    for n, ref in enumerate(in_refs):
        out_ref[pl.ds(n * rows, rows), :] = ref[...]


def joined(blocks):
    rows, width = blocks[0].shape
    return call(join_kernel, bf16(rows * len(blocks), width), [ON_CHIP] * len(blocks))(*blocks)


def turn_kernel(*refs):
    count = lax.axis_size("col")
    held, outs = refs[: len(refs) - count], refs[len(refs) - count:]
    row_index, col_index = lax.axis_index("row"), lax.axis_index("col")
    for apart, out_ref in enumerate(outs):
        wanted = row_index ^ lax.rem(col_index + apart, count)
        for mask, ref in enumerate(held):

            @pl.when(wanted == mask)
            def _():
                out_ref[...] = ref[...]


def place_piece(panel_ref, rows, block, origin, count, size):
    for g in range(block.shape[1] // size):
        left = (g * count + origin) * size
        if not isinstance(origin, int):
            left = pl.multiple_of(left, size)
        panel_ref[rows, pl.ds(left, size)] = block[:, g * size:(g + 1) * size]


def factor_from(panel_ref, inverse_ref, out_ref, tile):
    rows, width = out_ref.shape
    for first in range(0, width, tile):
        out_ref[:, pl.ds(first, tile)] = lax.dot_general(
            panel_ref[pl.ds(0, rows), pl.ds(0, first + tile)],
            inverse_ref[pl.ds(first, tile), pl.ds(0, first + tile)],
            CONTRACT,
            preferred_element_type=jnp.float32,
        ).astype(jnp.bfloat16)


def row_factor_kernel(places, origins, kinds, size, tile, inverse_ref, *refs):
    arrays, out_ref, panel_ref = refs[: len(kinds)], refs[-2], refs[-1]
    col_index = lax.axis_index("col")
    count = len(origins)
    rows = out_ref.shape[0]
    for slot in range(count):
        origin = looked_up(col_index, origins[slot])
        for kind, ref in zip(kinds, arrays):
            members = tuple(i for i in range(count) if places[slot][i] == kind)
            if members:

                @pl.when(among(col_index, members))
                def _():
                    for top in range(0, rows, size):
                        at = pl.ds(top, size)
                        place_piece(panel_ref, at, ref[at, :], origin, count, size)

    factor_from(panel_ref, inverse_ref, out_ref, tile)


def column_factor_kernel(size, tile, inverse_ref, *refs):
    parts, out_ref, panel_ref = refs[:-2], refs[-2], refs[-1]
    row_index, col_index = lax.axis_index("row"), lax.axis_index("col")
    count = lax.axis_size("col")
    part = parts[0].shape[0] // count
    for mask, ref in enumerate(parts):
        at = pl.ds(pl.multiple_of((row_index ^ mask) * part, ROW_TILE), part)
        for apart in range(count):
            origin = lax.rem(col_index + count - apart, count)
            place_piece(panel_ref, at, ref[pl.ds(apart * part, part), :], origin, count, size)
    factor_from(panel_ref, inverse_ref, out_ref, tile)


def product_kernel(mine, rows_ref, columns_ref, front_ref, *refs):
    out_hbm, out_ref, sem = refs[-3:]
    sub_index = lax.axis_index("sub")
    half = sub_index if mine else 1 - sub_index
    slot_count, _, size, _ = out_ref.shape
    product = lax.dot_general(
        rows_ref[...], columns_ref[...], CONTRACT, preferred_element_type=jnp.float32
    )
    for m in range(slot_count):
        for a in range(slot_count):
            block = product[m * size:(m + 1) * size, a * size:(a + 1) * size]
            out_ref[m, a] = (front_ref[m, a, half].astype(jnp.float32) - block).astype(jnp.bfloat16)
    copy = pltpu.make_async_copy(out_ref, out_hbm.at[:, :, half], sem)
    copy.start()
    copy.wait()


def body(front_entries, block_pattern, child_update, child_map, diag_inverse):
    slot_count = front_entries.shape[0]
    size = front_entries.shape[3]
    column_count = front_entries.shape[4]
    child_count = child_update.shape[1]
    row_size = lax.axis_size("row")
    col_size = lax.axis_size("col")
    groups = -(-(PANEL // size) // col_size)
    tile = PANEL // 2
    rows = slot_count * size
    part = -(-rows // (row_size * ROW_TILE)) * ROW_TILE
    padded = part * row_size
    depth = groups * col_size * size
    in_hbm = pl.BlockSpec(memory_space=pltpu.HBM)
    entries = front_entries.reshape(slot_count, size, column_count, size).transpose(0, 2, 1, 3)
    pattern = block_pattern.reshape(slot_count, 1, column_count)
    slots = child_map.transpose(0, 2, 1)
    own = child_update.reshape(child_count, size, child_count, size).transpose(0, 2, 1, 3)

    received = flipped(own, "sub", 1)
    inverse_part, part_rows = inverse_rows(diag_inverse)
    base = call(base_kernel, f32(rows, groups * size), [SCALARS, SCALARS, ON_CHIP, ON_CHIP])(
        slots, pattern, entries[:, :groups], own
    )
    piece, *parts = call(
        functools.partial(panel_kernel, slot_count, part),
        [bf16(padded, groups * size)] + [bf16(part, groups * size)] * row_size,
        [SCALARS, ON_CHIP, ON_CHIP],
    )(slots, base, received)

    _, origins, places = line_plan(col_size)
    pieces = Line(piece, "col")
    pieces.step()
    held = [parts[0]] + [flipped(parts[mask], "row", mask) for mask in range(1, row_size)]
    turned = call(turn_kernel, [bf16(part, groups * size)] * col_size, [ON_CHIP] * row_size)(*held)
    turned = joined(
        [turned[0]] + [shifted(turned[apart], "col", apart) for apart in range(1, col_size)]
    )
    turned, inverse_part = pieces.fenced(turned, inverse_part)
    while pieces.step():
        pass
    front = call(
        functools.partial(front_kernel, groups),
        bf16(slot_count, column_count, size, size),
        [SCALARS, SCALARS] + [ON_CHIP] * 4,
        moved=6 << 20,
    )(slots, pattern, entries, own, received, piece)
    inverse = whole_inverse(inverse_part, part_rows)
    front, inverse, *parts = pieces.fenced(
        front, inverse, turned, *(flipped(turned, "row", mask) for mask in range(1, row_size))
    )
    front = front.reshape(slot_count, slot_count, 2, size, size)

    kinds, arrays = pieces.taken()
    scratch = [pltpu.VMEM((padded, depth), jnp.bfloat16)]
    flops = 2 * rows * PANEL * PANEL * 3 // 4
    column_factor = call(
        functools.partial(column_factor_kernel, size, tile),
        bf16(rows, PANEL), [ON_CHIP] * (1 + row_size), flops=flops, scratch_shapes=scratch,
    )(inverse, *parts)
    other_factor = flipped(column_factor, "sub", 1)
    row_factor = call(
        functools.partial(row_factor_kernel, places, origins, kinds, size, tile),
        bf16(rows, PANEL), [ON_CHIP] * (1 + len(arrays)), flops=flops, scratch_shapes=scratch,
    )(inverse, *arrays)
    product = functools.partial(
        call,
        out_shape=bf16(slot_count, slot_count, 2, size, size),
        flops=2 * rows * rows * PANEL,
        out_specs=in_hbm,
        scratch_shapes=[
            pltpu.VMEM((slot_count, slot_count, size, size), jnp.bfloat16),
            pltpu.SemaphoreType.DMA,
        ],
    )
    trailing = product(functools.partial(product_kernel, True), in_specs=[ON_CHIP] * 3)(
        row_factor, column_factor, front
    )
    trailing = product(
        functools.partial(product_kernel, False), in_specs=[ON_CHIP] * 3 + [in_hbm],
        input_output_aliases={3: 0},
    )(row_factor, other_factor, front, trailing)
    return trailing.reshape(slot_count, column_count, size, size).transpose(0, 2, 1, 3).reshape(
        slot_count, 1, 1, size, column_count, 1, size
    )


def solution(mesh):
    return jax.shard_map(
        body,
        mesh=mesh,
        in_specs=(
            P(None, "sub", "row", None, None, "col", None),
            P(None, "sub", "row", None, "col"),
            P("sub", None, "row", None, None, "col", None),
            P(),
            P("col", None),
        ),
        out_specs=P(None, "sub", "row", None, None, "col", None),
        check_vma=False,
    )
```

```python
import functools

import jax
import jax.numpy as jnp
from jax import lax
from jax.experimental import pallas as pl
from jax.experimental.pallas import tpu as pltpu
from jax.sharding import PartitionSpec as P

PANEL = 1024
ROW_TILE = 16
VMEM_BYTES = 12 * 1024 * 1024
CONTRACT = (((1,), (1,)), ((), ()))
ON_CHIP = pl.BlockSpec(memory_space=pltpu.VMEM)
SCALARS = pl.BlockSpec(memory_space=pltpu.SMEM)


def call(kernel, out_shape, in_specs, flops=0, moved=1 << 19, **more):
    single = not isinstance(out_shape, (list, tuple))
    return pl.pallas_call(
        kernel,
        out_shape=out_shape,
        in_specs=in_specs,
        out_specs=more.pop("out_specs", ON_CHIP if single else [ON_CHIP] * len(out_shape)),
        compiler_params=pltpu.CompilerParams(vmem_limit_bytes=VMEM_BYTES),
        cost_estimate=pl.CostEstimate(flops=flops, bytes_accessed=moved, transcendentals=0),
        **more,
    )


def bf16(*shape):
    return jax.ShapeDtypeStruct(shape, jnp.bfloat16)


def f32(*shape):
    return jax.ShapeDtypeStruct(shape, jnp.float32)


def flipped(block, axis, mask):
    count = lax.axis_size(axis)
    return lax.ppermute(block, axis, [(i, i ^ mask) for i in range(count)])


def shifted(block, axis, apart):
    count = lax.axis_size(axis)
    return lax.ppermute(block, axis, [(i, (i + apart) % count) for i in range(count)])


def swap_even(i, count):
    return i ^ 1 if i ^ 1 < count else i


def swap_odd(i, count):
    j = ((i + 1) ^ 1) - 1
    return j if 0 <= j < count else i


@functools.cache
def line_plan(count):
    even = [swap_even(i, count) for i in range(count)]
    odd = [swap_odd(i, count) for i in range(count)]
    if count == 4:
        levels = [[(1, 0, even), (2, 0, odd)], [(3, 2, [2, 0, 3, 1]), (4, 1, [1, 3, 0, 2])]]
    else:
        levels, last = [], [0, 0]
        for step in range(count - 1):
            level = []
            for stream in (0, 1):
                level.append((1 + 2 * step + stream, last[stream], odd if (step + stream) % 2 else even))
                last[stream] = level[-1][0]
            levels.append(level)
    whose = {0: list(range(count))}
    seen = [[(0, i)] for i in range(count)]
    for level in levels:
        for array, source, to in level:
            whose[array] = [None] * count
            for i in range(count):
                whose[array][to[i]] = whose[source][i]
            for i in range(count):
                if all(whose[array][i] != origin for _, origin in seen[i]):
                    seen[i].append((array, whose[array][i]))
    origins = [[seen[i][j][1] for i in range(count)] for j in range(count)]
    places = [[seen[i][j][0] for i in range(count)] for j in range(count)]
    return levels, origins, places


class Line:
    def __init__(self, block, axis):
        self.axis = axis
        self.levels, _, self.places = line_plan(lax.axis_size(axis))
        self.held = {0: block}
        self.at = 0

    def step(self):
        for array, source, to in self.levels[self.at]:
            self.held[array] = lax.ppermute(self.held[source], self.axis, list(enumerate(to)))
        self.at += 1
        return self.at < len(self.levels)

    def fenced(self, *values):
        last = [array for array, _, _ in self.levels[self.at - 1]]
        out = fence(*values, *(self.held[array] for array in last))
        self.held.update(zip(last, out[len(values):]))
        return out[: len(values)]

    def taken(self):
        kinds = sorted({kind for row in self.places for kind in row})
        return kinds, [self.held[kind] for kind in kinds]


def among(index, members):
    found = index == members[0]
    for member in members[1:]:
        found = jnp.logical_or(found, index == member)
    return found


def looked_up(index, table):
    value = jnp.int32(table[0])
    for i, entry in enumerate(table[1:], 1):
        value = jnp.where(index == i, jnp.int32(entry), value)
    return value


def fence_kernel(*refs):
    pass


def fence(*values):
    place = pl.BlockSpec(memory_space=pl.ANY)
    return pl.pallas_call(
        fence_kernel,
        out_shape=[jax.ShapeDtypeStruct(v.shape, v.dtype) for v in values],
        in_specs=[place] * len(values),
        out_specs=[place] * len(values),
        input_output_aliases={n: n for n in range(len(values))},
        compiler_params=pltpu.CompilerParams(vmem_limit_bytes=1 << 20),
    )(*values)


def found_at(map_ref, child, place, wanted, child_count):
    at = jnp.int32(0)
    found = jnp.float32(0)
    for k in range(child_count):
        same = map_ref[child, place, k] == wanted
        at = jnp.where(same, jnp.int32(k), at)
        found = jnp.where(same, jnp.float32(1), found)
    return at, found


def block_places(map_ref, child, columns, slot_count, child_count):
    sub_index, row_index, col_index = (lax.axis_index(name) for name in ("sub", "row", "col"))
    rows = [
        found_at(map_ref, child, row_index, 2 * a + sub_index, child_count) for a in range(slot_count)
    ]
    cols = [found_at(map_ref, child, col_index, b, child_count) for b in columns]
    return rows, cols


def child_block(ref, row, col):
    return ref[row[0], col[0]].astype(jnp.float32) * (row[1] * col[1])


def base_kernel(map_ref, pattern_ref, entries_ref, own_ref, base_ref):
    slot_count, groups, size, _ = entries_ref.shape
    rows, cols = block_places(
        map_ref, lax.axis_index("sub"), range(groups), slot_count, own_ref.shape[0]
    )
    for a in range(slot_count):
        for b in range(groups):
            block = entries_ref[a, b].astype(jnp.float32) * pattern_ref[a, 0, b].astype(jnp.float32)
            base_ref[pl.ds(a * size, size), pl.ds(b * size, size)] = block + child_block(
                own_ref, rows[a], cols[b]
            )


def panel_kernel(slot_count, part, map_ref, base_ref, received_ref, piece_ref, *part_refs):
    size = received_ref.shape[2]
    groups = base_ref.shape[1] // size
    rows, cols = block_places(
        map_ref, 1 - lax.axis_index("sub"), range(groups), slot_count, received_ref.shape[0]
    )
    for a in range(slot_count):
        for b in range(groups):
            at = (pl.ds(a * size, size), pl.ds(b * size, size))
            block = base_ref[at] + child_block(received_ref, rows[a], cols[b])
            piece_ref[at] = block.astype(jnp.bfloat16)
    used = slot_count * size
    if used < piece_ref.shape[0]:
        piece_ref[pl.ds(used, piece_ref.shape[0] - used), :] = jnp.zeros(
            (piece_ref.shape[0] - used, piece_ref.shape[1]), piece_ref.dtype
        )
    row_index = lax.axis_index("row")
    for mask, ref in enumerate(part_refs):
        ref[...] = piece_ref[pl.ds(pl.multiple_of((row_index ^ mask) * part, ROW_TILE), part), :]


def front_kernel(groups, map_ref, pattern_ref, entries_ref, own_ref, received_ref, piece_ref, out_ref):
    slot_count, column_count, size, _ = entries_ref.shape
    child_count = own_ref.shape[0]
    sub_index = lax.axis_index("sub")
    columns = range(groups, column_count)
    places = [
        block_places(map_ref, child, columns, slot_count, child_count)
        for child in (sub_index, 1 - sub_index)
    ]
    for a in range(slot_count):
        for b in range(groups):
            out_ref[a, b] = piece_ref[pl.ds(a * size, size), pl.ds(b * size, size)]
        for n, b in enumerate(columns):
            total = entries_ref[a, b].astype(jnp.float32) * pattern_ref[a, 0, b].astype(jnp.float32)
            for (rows, cols), ref in zip(places, (own_ref, received_ref)):
                total = total + child_block(ref, rows[a], cols[n])
            out_ref[a, b] = total.astype(jnp.bfloat16)


def inverse_kernel(part, *refs):
    *in_refs, out_ref = refs
    sub_index, row_index, col_index = (lax.axis_index(name) for name in ("sub", "row", "col"))
    row_size, col_size = lax.axis_size("row"), lax.axis_size("col")
    width = out_ref.shape[1]
    share = part * row_size * len(in_refs)
    for n, ref in enumerate(in_refs):
        sub_at = sub_index if n == 0 else 1 - sub_index
        for mask in range(row_size):
            for apart in range(col_size):
                col = lax.rem(col_index + col_size - apart, col_size)
                top = col * share + (sub_at * row_size + (row_index ^ mask)) * part
                top = pl.multiple_of(top, ROW_TILE)
                block = ref[pl.ds((mask * col_size + apart) * part, part), :].astype(jnp.float32)
                row_at = top + lax.broadcasted_iota(jnp.int32, (part, width), 0)
                col_at = lax.broadcasted_iota(jnp.int32, (part, width), 1)
                out_ref[pl.ds(top, part), :] = jnp.where(col_at <= row_at, block, 0.0).astype(
                    jnp.bfloat16
                )


def lower_kernel(in_ref, out_ref):
    row_at = lax.broadcasted_iota(jnp.int32, in_ref.shape, 0)
    col_at = lax.broadcasted_iota(jnp.int32, in_ref.shape, 1)
    out_ref[...] = jnp.where(col_at <= row_at, in_ref[...].astype(jnp.float32), 0.0).astype(jnp.bfloat16)


def join_kernel(*refs):
    *in_refs, out_ref = refs
    rows = in_refs[0].shape[0]
    for n, ref in enumerate(in_refs):
        out_ref[pl.ds(n * rows, rows), :] = ref[...]


def joined(blocks):
    rows, width = blocks[0].shape
    return call(join_kernel, bf16(rows * len(blocks), width), [ON_CHIP] * len(blocks))(*blocks)


def inverse_line(diag_inverse):
    sub_size, row_size = lax.axis_size("sub"), lax.axis_size("row")
    part = diag_inverse.shape[0] // (sub_size * row_size)
    if part % ROW_TILE:
        return lax.all_gather(diag_inverse, "col", axis=0, tiled=True), None
    first = (lax.axis_index("sub") * row_size + lax.axis_index("row")) * part
    mine = lax.dynamic_slice_in_dim(diag_inverse, first, part, 0)
    return joined([mine] + [shifted(mine, "col", apart) for apart in range(1, lax.axis_size("col"))]), part


def inverse_plane(line, part):
    if part is None:
        return line
    return joined([line] + [flipped(line, "row", mask) for mask in range(1, lax.axis_size("row"))])


def whole_inverse(plane, part):
    width = plane.shape[1]
    if part is None:
        return call(lower_kernel, bf16(width, width), [ON_CHIP], moved=4 << 20)(plane)
    return call(
        functools.partial(inverse_kernel, part), bf16(width, width), [ON_CHIP] * 2, moved=4 << 20
    )(plane, flipped(plane, "sub", 1))


def turn_kernel(*refs):
    count = lax.axis_size("col")
    held, outs = refs[: len(refs) - count], refs[len(refs) - count:]
    row_index, col_index = lax.axis_index("row"), lax.axis_index("col")
    for apart, out_ref in enumerate(outs):
        wanted = row_index ^ lax.rem(col_index + apart, count)
        for mask, ref in enumerate(held):

            @pl.when(wanted == mask)
            def _():
                out_ref[...] = ref[...]


def place_piece(panel_ref, rows, block, origin, count, size):
    for g in range(block.shape[1] // size):
        left = (g * count + origin) * size
        if not isinstance(origin, int):
            left = pl.multiple_of(left, size)
        panel_ref[rows, pl.ds(left, size)] = block[:, g * size:(g + 1) * size]


def factor_from(panel_ref, inverse_ref, out_ref, tile):
    rows, width = out_ref.shape
    for first in range(0, width, tile):
        out_ref[:, pl.ds(first, tile)] = lax.dot_general(
            panel_ref[pl.ds(0, rows), pl.ds(0, first + tile)],
            inverse_ref[pl.ds(first, tile), pl.ds(0, first + tile)],
            CONTRACT,
            preferred_element_type=jnp.float32,
        ).astype(jnp.bfloat16)


def row_factor_kernel(places, origins, kinds, size, tile, inverse_ref, *refs):
    arrays, out_ref, panel_ref = refs[: len(kinds)], refs[-2], refs[-1]
    col_index = lax.axis_index("col")
    count = len(origins)
    rows = out_ref.shape[0]
    for slot in range(count):
        origin = looked_up(col_index, origins[slot])
        for kind, ref in zip(kinds, arrays):
            members = tuple(i for i in range(count) if places[slot][i] == kind)
            if members:

                @pl.when(among(col_index, members))
                def _():
                    for top in range(0, rows, size):
                        at = pl.ds(top, size)
                        place_piece(panel_ref, at, ref[at, :], origin, count, size)

    factor_from(panel_ref, inverse_ref, out_ref, tile)


def column_factor_kernel(size, tile, inverse_ref, *refs):
    parts, out_ref, panel_ref = refs[:-2], refs[-2], refs[-1]
    row_index, col_index = lax.axis_index("row"), lax.axis_index("col")
    count = lax.axis_size("col")
    part = parts[0].shape[0] // count
    for mask, ref in enumerate(parts):
        at = pl.ds(pl.multiple_of((row_index ^ mask) * part, ROW_TILE), part)
        for apart in range(count):
            origin = lax.rem(col_index + count - apart, count)
            place_piece(panel_ref, at, ref[pl.ds(apart * part, part), :], origin, count, size)
    factor_from(panel_ref, inverse_ref, out_ref, tile)


def product_kernel(mine, rows_ref, columns_ref, front_ref, *refs):
    out_hbm, out_ref, sem = refs[-3:]
    sub_index = lax.axis_index("sub")
    half = sub_index if mine else 1 - sub_index
    slot_count, _, size, _ = out_ref.shape
    product = lax.dot_general(
        rows_ref[...], columns_ref[...], CONTRACT, preferred_element_type=jnp.float32
    )
    for m in range(slot_count):
        for a in range(slot_count):
            block = product[m * size:(m + 1) * size, a * size:(a + 1) * size]
            out_ref[m, a] = (front_ref[m, a, half].astype(jnp.float32) - block).astype(jnp.bfloat16)
    copy = pltpu.make_async_copy(out_ref, out_hbm.at[:, :, half], sem)
    copy.start()
    copy.wait()


def body(front_entries, block_pattern, child_update, child_map, diag_inverse):
    slot_count = front_entries.shape[0]
    size = front_entries.shape[3]
    column_count = front_entries.shape[4]
    child_count = child_update.shape[1]
    row_size = lax.axis_size("row")
    col_size = lax.axis_size("col")
    groups = -(-(PANEL // size) // col_size)
    tile = PANEL // 2
    rows = slot_count * size
    part = -(-rows // (row_size * ROW_TILE)) * ROW_TILE
    padded = part * row_size
    depth = groups * col_size * size
    in_hbm = pl.BlockSpec(memory_space=pltpu.HBM)
    entries = front_entries.reshape(slot_count, size, column_count, size).transpose(0, 2, 1, 3)
    pattern = block_pattern.reshape(slot_count, 1, column_count)
    slots = child_map.transpose(0, 2, 1)
    own = child_update.reshape(child_count, size, child_count, size).transpose(0, 2, 1, 3)

    received = flipped(own, "sub", 1)
    line, part_rows = inverse_line(diag_inverse)
    base = call(base_kernel, f32(rows, groups * size), [SCALARS, SCALARS, ON_CHIP, ON_CHIP])(
        slots, pattern, entries[:, :groups], own
    )
    base, line = fence(base, line)
    piece, *parts = call(
        functools.partial(panel_kernel, slot_count, part),
        [bf16(padded, groups * size)] + [bf16(part, groups * size)] * row_size,
        [SCALARS, ON_CHIP, ON_CHIP],
    )(slots, base, received)

    _, origins, places = line_plan(col_size)
    pieces = Line(piece, "col")
    pieces.step()
    held = [parts[0]] + [flipped(parts[mask], "row", mask) for mask in range(1, row_size)]
    near, *sends = call(turn_kernel, [bf16(part, groups * size)] * col_size, [ON_CHIP] * row_size)(*held)
    line, near, *sends = pieces.fenced(line, near, *sends)
    plane = inverse_plane(line, part_rows)
    turned = joined(
        [near] + [shifted(block, "col", apart) for apart, block in enumerate(sends, 1)]
    )
    turned, plane = pieces.fenced(turned, plane)
    while pieces.step():
        pass
    front = call(
        functools.partial(front_kernel, groups),
        bf16(slot_count, column_count, size, size),
        [SCALARS, SCALARS] + [ON_CHIP] * 4,
        moved=6 << 20,
    )(slots, pattern, entries, own, received, piece)
    inverse = whole_inverse(plane, part_rows)
    front, inverse, *parts = pieces.fenced(
        front, inverse, turned, *(flipped(turned, "row", mask) for mask in range(1, row_size))
    )
    front = front.reshape(slot_count, slot_count, 2, size, size)

    kinds, arrays = pieces.taken()
    scratch = [pltpu.VMEM((padded, depth), jnp.bfloat16)]
    flops = 2 * rows * PANEL * PANEL * 3 // 4
    column_factor = call(
        functools.partial(column_factor_kernel, size, tile),
        bf16(rows, PANEL), [ON_CHIP] * (1 + row_size), flops=flops, scratch_shapes=scratch,
    )(inverse, *parts)
    other_factor = flipped(column_factor, "sub", 1)
    row_factor = call(
        functools.partial(row_factor_kernel, places, origins, kinds, size, tile),
        bf16(rows, PANEL), [ON_CHIP] * (1 + len(arrays)), flops=flops, scratch_shapes=scratch,
    )(inverse, *arrays)
    product = functools.partial(
        call,
        out_shape=bf16(slot_count, slot_count, 2, size, size),
        flops=2 * rows * rows * PANEL,
        out_specs=in_hbm,
        scratch_shapes=[
            pltpu.VMEM((slot_count, slot_count, size, size), jnp.bfloat16),
            pltpu.SemaphoreType.DMA,
        ],
    )
    trailing = product(functools.partial(product_kernel, True), in_specs=[ON_CHIP] * 3)(
        row_factor, column_factor, front
    )
    trailing = product(
        functools.partial(product_kernel, False), in_specs=[ON_CHIP] * 3 + [in_hbm],
        input_output_aliases={3: 0},
    )(row_factor, other_factor, front, trailing)
    return trailing.reshape(slot_count, column_count, size, size).transpose(0, 2, 1, 3).reshape(
        slot_count, 1, 1, size, column_count, 1, size
    )


def solution(mesh):
    return jax.shard_map(
        body,
        mesh=mesh,
        in_specs=(
            P(None, "sub", "row", None, None, "col", None),
            P(None, "sub", "row", None, "col"),
            P("sub", None, "row", None, None, "col", None),
            P(),
            P("col", None),
        ),
        out_specs=P(None, "sub", "row", None, None, "col", None),
        check_vma=False,
    )
```

```python
import functools

import jax
import jax.numpy as jnp
from jax import lax
from jax.experimental import pallas as pl
from jax.experimental.pallas import tpu as pltpu
from jax.sharding import PartitionSpec as P

PANEL = 1024
ROW_TILE = 16
VMEM_BYTES = 12 * 1024 * 1024
CONTRACT = (((1,), (1,)), ((), ()))
ON_CHIP = pl.BlockSpec(memory_space=pltpu.VMEM)
SCALARS = pl.BlockSpec(memory_space=pltpu.SMEM)


def call(kernel, out_shape, in_specs, flops=0, moved=1 << 19, **more):
    single = not isinstance(out_shape, (list, tuple))
    return pl.pallas_call(
        kernel,
        out_shape=out_shape,
        in_specs=in_specs,
        out_specs=more.pop("out_specs", ON_CHIP if single else [ON_CHIP] * len(out_shape)),
        compiler_params=pltpu.CompilerParams(vmem_limit_bytes=VMEM_BYTES),
        cost_estimate=pl.CostEstimate(flops=flops, bytes_accessed=moved, transcendentals=0),
        **more,
    )


def bf16(*shape):
    return jax.ShapeDtypeStruct(shape, jnp.bfloat16)


def f32(*shape):
    return jax.ShapeDtypeStruct(shape, jnp.float32)


def flipped(block, axis, mask):
    count = lax.axis_size(axis)
    return lax.ppermute(block, axis, [(i, i ^ mask) for i in range(count)])


def shifted(block, axis, apart):
    count = lax.axis_size(axis)
    return lax.ppermute(block, axis, [(i, (i + apart) % count) for i in range(count)])


def swap_even(i, count):
    return i ^ 1 if i ^ 1 < count else i


def swap_odd(i, count):
    j = ((i + 1) ^ 1) - 1
    return j if 0 <= j < count else i


@functools.cache
def line_plan(count):
    even = [swap_even(i, count) for i in range(count)]
    odd = [swap_odd(i, count) for i in range(count)]
    if count == 4:
        levels = [[(1, 0, even), (2, 0, odd)], [(3, 2, [2, 0, 3, 1]), (4, 1, [1, 3, 0, 2])]]
    else:
        levels, last = [], [0, 0]
        for step in range(count - 1):
            level = []
            for stream in (0, 1):
                level.append((1 + 2 * step + stream, last[stream], odd if (step + stream) % 2 else even))
                last[stream] = level[-1][0]
            levels.append(level)
    whose = {0: list(range(count))}
    seen = [[(0, i)] for i in range(count)]
    for level in levels:
        for array, source, to in level:
            whose[array] = [None] * count
            for i in range(count):
                whose[array][to[i]] = whose[source][i]
            for i in range(count):
                if all(whose[array][i] != origin for _, origin in seen[i]):
                    seen[i].append((array, whose[array][i]))
    origins = [[seen[i][j][1] for i in range(count)] for j in range(count)]
    places = [[seen[i][j][0] for i in range(count)] for j in range(count)]
    return levels, origins, places


class Line:
    def __init__(self, block, axis):
        self.axis = axis
        self.levels, _, self.places = line_plan(lax.axis_size(axis))
        self.held = {0: block}
        self.at = 0

    def step(self):
        for array, source, to in self.levels[self.at]:
            self.held[array] = lax.ppermute(self.held[source], self.axis, list(enumerate(to)))
        self.at += 1
        return self.at < len(self.levels)

    def fenced(self, *values):
        last = [array for array, _, _ in self.levels[self.at - 1]]
        out = fence(*values, *(self.held[array] for array in last))
        self.held.update(zip(last, out[len(values):]))
        return out[: len(values)]

    def taken(self):
        kinds = sorted({kind for row in self.places for kind in row})
        return kinds, [self.held[kind] for kind in kinds]


def among(index, members):
    found = index == members[0]
    for member in members[1:]:
        found = jnp.logical_or(found, index == member)
    return found


def looked_up(index, table):
    value = jnp.int32(table[0])
    for i, entry in enumerate(table[1:], 1):
        value = jnp.where(index == i, jnp.int32(entry), value)
    return value


def fence_kernel(*refs):
    pass


def fence(*values):
    place = pl.BlockSpec(memory_space=pl.ANY)
    return pl.pallas_call(
        fence_kernel,
        out_shape=[jax.ShapeDtypeStruct(v.shape, v.dtype) for v in values],
        in_specs=[place] * len(values),
        out_specs=[place] * len(values),
        input_output_aliases={n: n for n in range(len(values))},
        compiler_params=pltpu.CompilerParams(vmem_limit_bytes=1 << 20),
    )(*values)


def found_at(map_ref, child, place, wanted, child_count):
    at = jnp.int32(0)
    found = jnp.float32(0)
    for k in range(child_count):
        same = map_ref[child, place, k] == wanted
        at = jnp.where(same, jnp.int32(k), at)
        found = jnp.where(same, jnp.float32(1), found)
    return at, found


def block_places(map_ref, child, columns, slot_count, child_count):
    sub_index, row_index, col_index = (lax.axis_index(name) for name in ("sub", "row", "col"))
    rows = [
        found_at(map_ref, child, row_index, 2 * a + sub_index, child_count) for a in range(slot_count)
    ]
    cols = [found_at(map_ref, child, col_index, b, child_count) for b in columns]
    return rows, cols


def child_block(ref, row, col):
    return ref[row[0], col[0]].astype(jnp.float32) * (row[1] * col[1])


def panel_kernel(part, map_ref, pattern_ref, entries_ref, own_ref, received_ref, piece_ref, *part_refs):
    slot_count, groups, size, _ = entries_ref.shape
    child_count = own_ref.shape[0]
    sub_index, row_index = lax.axis_index("sub"), lax.axis_index("row")
    places = [
        block_places(map_ref, child, range(groups), slot_count, child_count)
        for child in (sub_index, 1 - sub_index)
    ]
    for a in range(slot_count):
        for b in range(groups):
            total = entries_ref[a, b].astype(jnp.float32) * pattern_ref[a, 0, b].astype(jnp.float32)
            for (rows, cols), ref in zip(places, (own_ref, received_ref)):
                total = total + child_block(ref, rows[a], cols[b])
            piece_ref[pl.ds(a * size, size), pl.ds(b * size, size)] = total.astype(jnp.bfloat16)
    used = slot_count * size
    if used < piece_ref.shape[0]:
        piece_ref[pl.ds(used, piece_ref.shape[0] - used), :] = jnp.zeros(
            (piece_ref.shape[0] - used, piece_ref.shape[1]), piece_ref.dtype
        )
    for mask, ref in enumerate(part_refs):
        ref[...] = piece_ref[pl.ds(pl.multiple_of((row_index ^ mask) * part, ROW_TILE), part), :]


def front_kernel(groups, map_ref, pattern_ref, entries_ref, own_ref, received_ref, piece_ref, out_ref):
    slot_count, column_count, size, _ = entries_ref.shape
    child_count = own_ref.shape[0]
    sub_index = lax.axis_index("sub")
    columns = range(groups, column_count)
    places = [
        block_places(map_ref, child, columns, slot_count, child_count)
        for child in (sub_index, 1 - sub_index)
    ]
    for a in range(slot_count):
        for b in range(groups):
            out_ref[a, b] = piece_ref[pl.ds(a * size, size), pl.ds(b * size, size)]
        for n, b in enumerate(columns):
            total = entries_ref[a, b].astype(jnp.float32) * pattern_ref[a, 0, b].astype(jnp.float32)
            for (rows, cols), ref in zip(places, (own_ref, received_ref)):
                total = total + child_block(ref, rows[a], cols[n])
            out_ref[a, b] = total.astype(jnp.bfloat16)


def inverse_kernel(part, *refs):
    *in_refs, out_ref = refs
    sub_index, col_index = lax.axis_index("sub"), lax.axis_index("col")
    row_size, col_size = lax.axis_size("row"), lax.axis_size("col")
    half = lax.axis_index("row") // (row_size // 2)
    width = out_ref.shape[1]
    for n, ref in enumerate(in_refs):
        sub_at = sub_index if n == 0 else 1 - sub_index
        for mask in range(2):
            for apart in range(col_size):
                col = lax.rem(col_index + col_size - apart, col_size)
                top = ((col * len(in_refs) + sub_at) * 2 + (half ^ mask)) * part
                top = pl.multiple_of(top, ROW_TILE)
                block = ref[pl.ds((mask * col_size + apart) * part, part), :].astype(jnp.float32)
                row_at = top + lax.broadcasted_iota(jnp.int32, (part, width), 0)
                col_at = lax.broadcasted_iota(jnp.int32, (part, width), 1)
                out_ref[pl.ds(top, part), :] = jnp.where(col_at <= row_at, block, 0.0).astype(
                    jnp.bfloat16
                )


def lower_kernel(in_ref, out_ref):
    row_at = lax.broadcasted_iota(jnp.int32, in_ref.shape, 0)
    col_at = lax.broadcasted_iota(jnp.int32, in_ref.shape, 1)
    out_ref[...] = jnp.where(col_at <= row_at, in_ref[...].astype(jnp.float32), 0.0).astype(jnp.bfloat16)


def join_kernel(*refs):
    *in_refs, out_ref = refs
    rows = in_refs[0].shape[0]
    for n, ref in enumerate(in_refs):
        out_ref[pl.ds(n * rows, rows), :] = ref[...]


def joined(blocks):
    rows, width = blocks[0].shape
    return call(join_kernel, bf16(rows * len(blocks), width), [ON_CHIP] * len(blocks))(*blocks)


def inverse_line(diag_inverse):
    part = diag_inverse.shape[0] // (2 * lax.axis_size("sub"))
    if part % ROW_TILE:
        return lax.all_gather(diag_inverse, "col", axis=0, tiled=True), None
    half = lax.axis_index("row") // (lax.axis_size("row") // 2)
    first = (lax.axis_index("sub") * 2 + half) * part
    mine = lax.dynamic_slice_in_dim(diag_inverse, first, part, 0)
    return joined([mine] + [shifted(mine, "col", apart) for apart in range(1, lax.axis_size("col"))]), part


def whole_inverse(plane, part):
    width = plane.shape[1]
    if part is None:
        return call(lower_kernel, bf16(width, width), [ON_CHIP], moved=4 << 20)(plane)
    return call(
        functools.partial(inverse_kernel, part), bf16(width, width), [ON_CHIP] * 2, moved=4 << 20
    )(plane, flipped(plane, "sub", 1))


def turn_kernel(*refs):
    count = lax.axis_size("col")
    held, outs = refs[: len(refs) - count], refs[len(refs) - count:]
    row_index, col_index = lax.axis_index("row"), lax.axis_index("col")
    for apart, out_ref in enumerate(outs):
        wanted = row_index ^ lax.rem(col_index + apart, count)
        for mask, ref in enumerate(held):

            @pl.when(wanted == mask)
            def _():
                out_ref[...] = ref[...]


def place_piece(panel_ref, rows, block, origin, count, size):
    for g in range(block.shape[1] // size):
        left = (g * count + origin) * size
        if not isinstance(origin, int):
            left = pl.multiple_of(left, size)
        panel_ref[rows, pl.ds(left, size)] = block[:, g * size:(g + 1) * size]


def factor_from(panel_ref, inverse_ref, out_ref, tile):
    rows, width = out_ref.shape
    for first in range(0, width, tile):
        out_ref[:, pl.ds(first, tile)] = lax.dot_general(
            panel_ref[pl.ds(0, rows), pl.ds(0, first + tile)],
            inverse_ref[pl.ds(first, tile), pl.ds(0, first + tile)],
            CONTRACT,
            preferred_element_type=jnp.float32,
        ).astype(jnp.bfloat16)


def row_factor_kernel(places, origins, kinds, size, tile, inverse_ref, *refs):
    arrays, out_ref, panel_ref = refs[: len(kinds)], refs[-2], refs[-1]
    col_index = lax.axis_index("col")
    count = len(origins)
    rows = out_ref.shape[0]
    for slot in range(count):
        origin = looked_up(col_index, origins[slot])
        for kind, ref in zip(kinds, arrays):
            members = tuple(i for i in range(count) if places[slot][i] == kind)
            if members:

                @pl.when(among(col_index, members))
                def _():
                    for top in range(0, rows, size):
                        at = pl.ds(top, size)
                        place_piece(panel_ref, at, ref[at, :], origin, count, size)

    factor_from(panel_ref, inverse_ref, out_ref, tile)


def column_factor_kernel(size, tile, inverse_ref, *refs):
    parts, out_ref, panel_ref = refs[:-2], refs[-2], refs[-1]
    row_index, col_index = lax.axis_index("row"), lax.axis_index("col")
    count = lax.axis_size("col")
    part = parts[0].shape[0] // count
    for mask, ref in enumerate(parts):
        at = pl.ds(pl.multiple_of((row_index ^ mask) * part, ROW_TILE), part)
        for apart in range(count):
            origin = lax.rem(col_index + count - apart, count)
            place_piece(panel_ref, at, ref[pl.ds(apart * part, part), :], origin, count, size)
    factor_from(panel_ref, inverse_ref, out_ref, tile)


def product_kernel(mine, rows_ref, columns_ref, front_ref, *refs):
    out_hbm, out_ref, sem = refs[-3:]
    sub_index = lax.axis_index("sub")
    half = sub_index if mine else 1 - sub_index
    slot_count, _, size, _ = out_ref.shape
    product = lax.dot_general(
        rows_ref[...], columns_ref[...], CONTRACT, preferred_element_type=jnp.float32
    )
    for m in range(slot_count):
        for a in range(slot_count):
            block = product[m * size:(m + 1) * size, a * size:(a + 1) * size]
            out_ref[m, a] = (front_ref[m, a, half].astype(jnp.float32) - block).astype(jnp.bfloat16)
    copy = pltpu.make_async_copy(out_ref, out_hbm.at[:, :, half], sem)
    copy.start()
    copy.wait()


def body(front_entries, block_pattern, child_update, child_map, diag_inverse):
    slot_count = front_entries.shape[0]
    size = front_entries.shape[3]
    column_count = front_entries.shape[4]
    child_count = child_update.shape[1]
    row_size = lax.axis_size("row")
    col_size = lax.axis_size("col")
    groups = -(-(PANEL // size) // col_size)
    tile = PANEL // 2
    rows = slot_count * size
    part = -(-rows // (row_size * ROW_TILE)) * ROW_TILE
    padded = part * row_size
    depth = groups * col_size * size
    in_hbm = pl.BlockSpec(memory_space=pltpu.HBM)
    entries = front_entries.reshape(slot_count, size, column_count, size).transpose(0, 2, 1, 3)
    pattern = block_pattern.reshape(slot_count, 1, column_count)
    slots = child_map.transpose(0, 2, 1)
    own = child_update.reshape(child_count, size, child_count, size).transpose(0, 2, 1, 3)

    received = flipped(own, "sub", 1)
    line, part_rows = inverse_line(diag_inverse)
    received, line = fence(received, line)
    piece, *parts = call(
        functools.partial(panel_kernel, part),
        [bf16(padded, groups * size)] + [bf16(part, groups * size)] * row_size,
        [SCALARS, SCALARS] + [ON_CHIP] * 3,
    )(slots, pattern, entries[:, :groups], own, received)

    _, origins, places = line_plan(col_size)
    pieces = Line(piece, "col")
    pieces.step()
    held = [parts[0]] + [flipped(parts[mask], "row", mask) for mask in range(1, row_size)]
    near, *sends = call(turn_kernel, [bf16(part, groups * size)] * col_size, [ON_CHIP] * row_size)(*held)
    line, near, *sends = pieces.fenced(line, near, *sends)
    if part_rows:
        line = joined([line, flipped(line, "row", row_size // 2)])
    turned = joined(
        [near] + [shifted(block, "col", apart) for apart, block in enumerate(sends, 1)]
    )
    turned, plane = pieces.fenced(turned, line)
    while pieces.at < len(pieces.levels):
        pieces.step()
    parts = [turned] + [flipped(turned, "row", mask) for mask in range(1, row_size)]
    front = call(
        functools.partial(front_kernel, groups),
        bf16(slot_count, column_count, size, size),
        [SCALARS, SCALARS] + [ON_CHIP] * 4,
        moved=6 << 20,
    )(slots, pattern, entries, own, received, piece)
    inverse = whole_inverse(plane, part_rows)
    front, inverse, *parts = pieces.fenced(
        front, inverse, *parts
    )
    front = front.reshape(slot_count, slot_count, 2, size, size)

    kinds, arrays = pieces.taken()
    scratch = [pltpu.VMEM((padded, depth), jnp.bfloat16)]
    flops = 2 * rows * PANEL * PANEL * 3 // 4
    column_factor = call(
        functools.partial(column_factor_kernel, size, tile),
        bf16(rows, PANEL), [ON_CHIP] * (1 + row_size), flops=flops, scratch_shapes=scratch,
    )(inverse, *parts)
    other_factor = flipped(column_factor, "sub", 1)
    row_factor = call(
        functools.partial(row_factor_kernel, places, origins, kinds, size, tile),
        bf16(rows, PANEL), [ON_CHIP] * (1 + len(arrays)), flops=flops, scratch_shapes=scratch,
    )(inverse, *arrays)
    product = functools.partial(
        call,
        out_shape=bf16(slot_count, slot_count, 2, size, size),
        flops=2 * rows * rows * PANEL,
        out_specs=in_hbm,
        scratch_shapes=[
            pltpu.VMEM((slot_count, slot_count, size, size), jnp.bfloat16),
            pltpu.SemaphoreType.DMA,
        ],
    )
    trailing = product(functools.partial(product_kernel, True), in_specs=[ON_CHIP] * 3)(
        row_factor, column_factor, front
    )
    trailing = product(
        functools.partial(product_kernel, False), in_specs=[ON_CHIP] * 3 + [in_hbm],
        input_output_aliases={3: 0},
    )(row_factor, other_factor, front, trailing)
    return trailing.reshape(slot_count, column_count, size, size).transpose(0, 2, 1, 3).reshape(
        slot_count, 1, 1, size, column_count, 1, size
    )


def solution(mesh):
    return jax.shard_map(
        body,
        mesh=mesh,
        in_specs=(
            P(None, "sub", "row", None, None, "col", None),
            P(None, "sub", "row", None, "col"),
            P("sub", None, "row", None, None, "col", None),
            P(),
            P("col", None),
        ),
        out_specs=P(None, "sub", "row", None, None, "col", None),
        check_vma=False,
    )
```

```python
import functools

import jax
import jax.numpy as jnp
from jax import lax
from jax.experimental import pallas as pl
from jax.experimental.pallas import tpu as pltpu
from jax.sharding import PartitionSpec as P

PANEL = 1024
ROW_TILE = 16
VMEM_BYTES = 12 * 1024 * 1024
CONTRACT = (((1,), (1,)), ((), ()))
ON_CHIP = pl.BlockSpec(memory_space=pltpu.VMEM)
SCALARS = pl.BlockSpec(memory_space=pltpu.SMEM)


def call(kernel, out_shape, in_specs, flops=0, moved=1 << 19, **more):
    single = not isinstance(out_shape, (list, tuple))
    return pl.pallas_call(
        kernel,
        out_shape=out_shape,
        in_specs=in_specs,
        out_specs=more.pop("out_specs", ON_CHIP if single else [ON_CHIP] * len(out_shape)),
        compiler_params=pltpu.CompilerParams(vmem_limit_bytes=VMEM_BYTES),
        cost_estimate=pl.CostEstimate(flops=flops, bytes_accessed=moved, transcendentals=0),
        **more,
    )


def bf16(*shape):
    return jax.ShapeDtypeStruct(shape, jnp.bfloat16)


def f32(*shape):
    return jax.ShapeDtypeStruct(shape, jnp.float32)


def flipped(block, axis, mask):
    count = lax.axis_size(axis)
    return lax.ppermute(block, axis, [(i, i ^ mask) for i in range(count)])


def shifted(block, axis, apart):
    count = lax.axis_size(axis)
    return lax.ppermute(block, axis, [(i, (i + apart) % count) for i in range(count)])


def swap_even(i, count):
    return i ^ 1 if i ^ 1 < count else i


def swap_odd(i, count):
    j = ((i + 1) ^ 1) - 1
    return j if 0 <= j < count else i


@functools.cache
def line_plan(count):
    even = [swap_even(i, count) for i in range(count)]
    odd = [swap_odd(i, count) for i in range(count)]
    if count == 4:
        levels = [[(1, 0, even), (2, 0, odd)], [(3, 2, [2, 0, 3, 1]), (4, 1, [1, 3, 0, 2])]]
    else:
        levels, last = [], [0, 0]
        for step in range(count - 1):
            level = []
            for stream in (0, 1):
                level.append((1 + 2 * step + stream, last[stream], odd if (step + stream) % 2 else even))
                last[stream] = level[-1][0]
            levels.append(level)
    whose = {0: list(range(count))}
    seen = [[(0, i)] for i in range(count)]
    for level in levels:
        for array, source, to in level:
            whose[array] = [None] * count
            for i in range(count):
                whose[array][to[i]] = whose[source][i]
            for i in range(count):
                if all(whose[array][i] != origin for _, origin in seen[i]):
                    seen[i].append((array, whose[array][i]))
    origins = [[seen[i][j][1] for i in range(count)] for j in range(count)]
    places = [[seen[i][j][0] for i in range(count)] for j in range(count)]
    return levels, origins, places


class Line:
    def __init__(self, block, axis):
        self.axis = axis
        self.levels, _, self.places = line_plan(lax.axis_size(axis))
        self.held = {0: block}
        self.at = 0

    def step(self):
        for array, source, to in self.levels[self.at]:
            self.held[array] = lax.ppermute(self.held[source], self.axis, list(enumerate(to)))
        self.at += 1
        return self.at < len(self.levels)

    def fenced(self, *values):
        last = [array for array, _, _ in self.levels[self.at - 1]]
        out = fence(*values, *(self.held[array] for array in last))
        self.held.update(zip(last, out[len(values):]))
        return out[: len(values)]

    def taken(self):
        kinds = sorted({kind for row in self.places for kind in row})
        return kinds, [self.held[kind] for kind in kinds]


def among(index, members):
    found = index == members[0]
    for member in members[1:]:
        found = jnp.logical_or(found, index == member)
    return found


def looked_up(index, table):
    value = jnp.int32(table[0])
    for i, entry in enumerate(table[1:], 1):
        value = jnp.where(index == i, jnp.int32(entry), value)
    return value


def fence_kernel(*refs):
    pass


def fence(*values):
    place = pl.BlockSpec(memory_space=pl.ANY)
    return pl.pallas_call(
        fence_kernel,
        out_shape=[jax.ShapeDtypeStruct(v.shape, v.dtype) for v in values],
        in_specs=[place] * len(values),
        out_specs=[place] * len(values),
        input_output_aliases={n: n for n in range(len(values))},
        compiler_params=pltpu.CompilerParams(vmem_limit_bytes=1 << 20),
    )(*values)


def found_at(map_ref, child, place, wanted, child_count):
    at = jnp.int32(0)
    found = jnp.float32(0)
    for k in range(child_count):
        same = map_ref[child, place, k] == wanted
        at = jnp.where(same, jnp.int32(k), at)
        found = jnp.where(same, jnp.float32(1), found)
    return at, found


def block_places(map_ref, child, columns, slot_count, child_count):
    sub_index, row_index, col_index = (lax.axis_index(name) for name in ("sub", "row", "col"))
    rows = [
        found_at(map_ref, child, row_index, 2 * a + sub_index, child_count) for a in range(slot_count)
    ]
    cols = [found_at(map_ref, child, col_index, b, child_count) for b in columns]
    return rows, cols


def child_block(ref, row, col):
    return ref[row[0], col[0]].astype(jnp.float32) * (row[1] * col[1])


def panel_kernel(part, map_ref, pattern_ref, entries_ref, own_ref, received_ref, piece_ref, *part_refs):
    slot_count, groups, size, _ = entries_ref.shape
    child_count = own_ref.shape[0]
    sub_index, row_index = lax.axis_index("sub"), lax.axis_index("row")
    places = [
        block_places(map_ref, child, range(groups), slot_count, child_count)
        for child in (sub_index, 1 - sub_index)
    ]
    for a in range(slot_count):
        for b in range(groups):
            total = entries_ref[a, b].astype(jnp.float32) * pattern_ref[a, 0, b].astype(jnp.float32)
            for (rows, cols), ref in zip(places, (own_ref, received_ref)):
                total = total + child_block(ref, rows[a], cols[b])
            piece_ref[pl.ds(a * size, size), pl.ds(b * size, size)] = total.astype(jnp.bfloat16)
    used = slot_count * size
    if used < piece_ref.shape[0]:
        piece_ref[pl.ds(used, piece_ref.shape[0] - used), :] = jnp.zeros(
            (piece_ref.shape[0] - used, piece_ref.shape[1]), piece_ref.dtype
        )
    for mask, ref in enumerate(part_refs):
        ref[...] = piece_ref[pl.ds(pl.multiple_of((row_index ^ mask) * part, ROW_TILE), part), :]


def front_kernel(groups, map_ref, pattern_ref, entries_ref, own_ref, received_ref, piece_ref, out_ref):
    slot_count, column_count, size, _ = entries_ref.shape
    child_count = own_ref.shape[0]
    sub_index = lax.axis_index("sub")
    columns = range(groups, column_count)
    places = [
        block_places(map_ref, child, columns, slot_count, child_count)
        for child in (sub_index, 1 - sub_index)
    ]
    for a in range(slot_count):
        for b in range(groups):
            out_ref[a, b] = piece_ref[pl.ds(a * size, size), pl.ds(b * size, size)]
        for n, b in enumerate(columns):
            total = entries_ref[a, b].astype(jnp.float32) * pattern_ref[a, 0, b].astype(jnp.float32)
            for (rows, cols), ref in zip(places, (own_ref, received_ref)):
                total = total + child_block(ref, rows[a], cols[n])
            out_ref[a, b] = total.astype(jnp.bfloat16)


def inverse_kernel(part, *refs):
    *in_refs, out_ref = refs
    sub_index, row_index, col_index = (lax.axis_index(name) for name in ("sub", "row", "col"))
    row_size, col_size = lax.axis_size("row"), lax.axis_size("col")
    width = out_ref.shape[1]
    for n, ref in enumerate(in_refs):
        sub_at = sub_index if n == 0 else 1 - sub_index
        for mask in range(row_size):
            for apart in range(col_size):
                col = lax.rem(col_index + col_size - apart, col_size)
                top = ((col * len(in_refs) + sub_at) * row_size + (row_index ^ mask)) * part
                top = pl.multiple_of(top, ROW_TILE)
                block = ref[pl.ds((mask * col_size + apart) * part, part), :].astype(jnp.float32)
                row_at = top + lax.broadcasted_iota(jnp.int32, (part, width), 0)
                col_at = lax.broadcasted_iota(jnp.int32, (part, width), 1)
                out_ref[pl.ds(top, part), :] = jnp.where(col_at <= row_at, block, 0.0).astype(
                    jnp.bfloat16
                )


def lower_kernel(in_ref, out_ref):
    row_at = lax.broadcasted_iota(jnp.int32, in_ref.shape, 0)
    col_at = lax.broadcasted_iota(jnp.int32, in_ref.shape, 1)
    out_ref[...] = jnp.where(col_at <= row_at, in_ref[...].astype(jnp.float32), 0.0).astype(jnp.bfloat16)


def join_kernel(*refs):
    *in_refs, out_ref = refs
    rows = in_refs[0].shape[0]
    for n, ref in enumerate(in_refs):
        out_ref[pl.ds(n * rows, rows), :] = ref[...]


def joined(blocks):
    rows, width = blocks[0].shape
    return call(join_kernel, bf16(rows * len(blocks), width), [ON_CHIP] * len(blocks))(*blocks)


def inverse_line(diag_inverse):
    part = diag_inverse.shape[0] // (lax.axis_size("sub") * lax.axis_size("row"))
    if part % ROW_TILE:
        return lax.all_gather(diag_inverse, "col", axis=0, tiled=True), None
    first = (lax.axis_index("sub") * lax.axis_size("row") + lax.axis_index("row")) * part
    mine = lax.dynamic_slice_in_dim(diag_inverse, first, part, 0)
    return joined([mine] + [shifted(mine, "col", apart) for apart in range(1, lax.axis_size("col"))]), part


def plane_step(lines, bit, part):
    return lines if part is None else joined([lines, flipped(lines, "row", 1 << bit)])


def whole_inverse(plane, other, part):
    width = plane.shape[1]
    if part is None:
        return call(lower_kernel, bf16(width, width), [ON_CHIP], moved=4 << 20)(plane)
    return call(
        functools.partial(inverse_kernel, part), bf16(width, width), [ON_CHIP] * 2, moved=4 << 20
    )(plane, other)


def turn_kernel(*refs):
    count = lax.axis_size("col")
    held, outs = refs[: len(refs) - count], refs[len(refs) - count:]
    row_index, col_index = lax.axis_index("row"), lax.axis_index("col")
    for apart, out_ref in enumerate(outs):
        wanted = row_index ^ lax.rem(col_index + apart, count)
        for mask, ref in enumerate(held):

            @pl.when(wanted == mask)
            def _():
                out_ref[...] = ref[...]


def place_piece(panel_ref, rows, block, origin, count, size):
    for g in range(block.shape[1] // size):
        left = (g * count + origin) * size
        if not isinstance(origin, int):
            left = pl.multiple_of(left, size)
        panel_ref[rows, pl.ds(left, size)] = block[:, g * size:(g + 1) * size]


def factor_from(panel_ref, inverse_ref, out_ref, tile):
    rows, width = out_ref.shape
    for first in range(0, width, tile):
        out_ref[:, pl.ds(first, tile)] = lax.dot_general(
            panel_ref[pl.ds(0, rows), pl.ds(0, first + tile)],
            inverse_ref[pl.ds(first, tile), pl.ds(0, first + tile)],
            CONTRACT,
            preferred_element_type=jnp.float32,
        ).astype(jnp.bfloat16)


def row_factor_kernel(places, origins, kinds, size, tile, inverse_ref, *refs):
    arrays, out_ref, panel_ref = refs[: len(kinds)], refs[-2], refs[-1]
    col_index = lax.axis_index("col")
    count = len(origins)
    rows = out_ref.shape[0]
    for slot in range(count):
        origin = looked_up(col_index, origins[slot])
        for kind, ref in zip(kinds, arrays):
            members = tuple(i for i in range(count) if places[slot][i] == kind)
            if members:

                @pl.when(among(col_index, members))
                def _():
                    for top in range(0, rows, size):
                        at = pl.ds(top, size)
                        place_piece(panel_ref, at, ref[at, :], origin, count, size)

    factor_from(panel_ref, inverse_ref, out_ref, tile)


def column_factor_kernel(size, tile, inverse_ref, *refs):
    parts, out_ref, panel_ref = refs[:-2], refs[-2], refs[-1]
    row_index, col_index = lax.axis_index("row"), lax.axis_index("col")
    count = lax.axis_size("col")
    part = parts[0].shape[0] // count
    for mask, ref in enumerate(parts):
        at = pl.ds(pl.multiple_of((row_index ^ mask) * part, ROW_TILE), part)
        for apart in range(count):
            origin = lax.rem(col_index + count - apart, count)
            place_piece(panel_ref, at, ref[pl.ds(apart * part, part), :], origin, count, size)
    factor_from(panel_ref, inverse_ref, out_ref, tile)


def product_kernel(mine, rows_ref, columns_ref, front_ref, *refs):
    out_hbm, out_ref, sem = refs[-3:]
    sub_index = lax.axis_index("sub")
    half = sub_index if mine else 1 - sub_index
    slot_count, _, size, _ = out_ref.shape
    product = lax.dot_general(
        rows_ref[...], columns_ref[...], CONTRACT, preferred_element_type=jnp.float32
    )
    for m in range(slot_count):
        for a in range(slot_count):
            block = product[m * size:(m + 1) * size, a * size:(a + 1) * size]
            out_ref[m, a] = (front_ref[m, a, half].astype(jnp.float32) - block).astype(jnp.bfloat16)
    copy = pltpu.make_async_copy(out_ref, out_hbm.at[:, :, half], sem)
    copy.start()
    copy.wait()


def body(front_entries, block_pattern, child_update, child_map, diag_inverse):
    slot_count = front_entries.shape[0]
    size = front_entries.shape[3]
    column_count = front_entries.shape[4]
    child_count = child_update.shape[1]
    row_size = lax.axis_size("row")
    col_size = lax.axis_size("col")
    groups = -(-(PANEL // size) // col_size)
    tile = PANEL // 2
    rows = slot_count * size
    part = -(-rows // (row_size * ROW_TILE)) * ROW_TILE
    padded = part * row_size
    depth = groups * col_size * size
    in_hbm = pl.BlockSpec(memory_space=pltpu.HBM)
    entries = front_entries.reshape(slot_count, size, column_count, size).transpose(0, 2, 1, 3)
    pattern = block_pattern.reshape(slot_count, 1, column_count)
    slots = child_map.transpose(0, 2, 1)
    own = child_update.reshape(child_count, size, child_count, size).transpose(0, 2, 1, 3)

    received = flipped(own, "sub", 1)
    line, part_rows = inverse_line(diag_inverse)
    received, line = fence(received, line)
    piece, *parts = call(
        functools.partial(panel_kernel, part),
        [bf16(padded, groups * size)] + [bf16(part, groups * size)] * row_size,
        [SCALARS, SCALARS] + [ON_CHIP] * 3,
    )(slots, pattern, entries[:, :groups], own, received)

    _, origins, places = line_plan(col_size)
    pieces = Line(piece, "col")
    pieces.step()
    held = [parts[0]] + [flipped(parts[mask], "row", mask) for mask in range(1, row_size)]
    near, *sends = call(turn_kernel, [bf16(part, groups * size)] * col_size, [ON_CHIP] * row_size)(*held)
    line = plane_step(line, 0, part_rows)
    line, near, *sends = pieces.fenced(line, near, *sends)
    for bit in range(1, row_size.bit_length() - 1):
        line = plane_step(line, bit, part_rows)
    turned = joined(
        [near] + [shifted(block, "col", apart) for apart, block in enumerate(sends, 1)]
    )
    turned, line = pieces.fenced(turned, line)
    other = flipped(line, "sub", 1)
    parts = [turned] + [flipped(turned, "row", mask) for mask in range(1, row_size)]
    while pieces.at < len(pieces.levels):
        pieces.step()
    front = call(
        functools.partial(front_kernel, groups),
        bf16(slot_count, column_count, size, size),
        [SCALARS, SCALARS] + [ON_CHIP] * 4,
        moved=6 << 20,
    )(slots, pattern, entries, own, received, piece)
    inverse = whole_inverse(line, other, part_rows)
    front, inverse, *parts = pieces.fenced(front, inverse, *parts)
    front = front.reshape(slot_count, slot_count, 2, size, size)

    kinds, arrays = pieces.taken()
    scratch = [pltpu.VMEM((padded, depth), jnp.bfloat16)]
    flops = 2 * rows * PANEL * PANEL * 3 // 4
    column_factor = call(
        functools.partial(column_factor_kernel, size, tile),
        bf16(rows, PANEL), [ON_CHIP] * (1 + row_size), flops=flops, scratch_shapes=scratch,
    )(inverse, *parts)
    other_factor = flipped(column_factor, "sub", 1)
    row_factor = call(
        functools.partial(row_factor_kernel, places, origins, kinds, size, tile),
        bf16(rows, PANEL), [ON_CHIP] * (1 + len(arrays)), flops=flops, scratch_shapes=scratch,
    )(inverse, *arrays)
    product = functools.partial(
        call,
        out_shape=bf16(slot_count, slot_count, 2, size, size),
        flops=2 * rows * rows * PANEL,
        out_specs=in_hbm,
        scratch_shapes=[
            pltpu.VMEM((slot_count, slot_count, size, size), jnp.bfloat16),
            pltpu.SemaphoreType.DMA,
        ],
    )
    trailing = product(functools.partial(product_kernel, True), in_specs=[ON_CHIP] * 3)(
        row_factor, column_factor, front
    )
    trailing = product(
        functools.partial(product_kernel, False), in_specs=[ON_CHIP] * 3 + [in_hbm],
        input_output_aliases={3: 0},
    )(row_factor, other_factor, front, trailing)
    return trailing.reshape(slot_count, column_count, size, size).transpose(0, 2, 1, 3).reshape(
        slot_count, 1, 1, size, column_count, 1, size
    )


def solution(mesh):
    return jax.shard_map(
        body,
        mesh=mesh,
        in_specs=(
            P(None, "sub", "row", None, None, "col", None),
            P(None, "sub", "row", None, "col"),
            P("sub", None, "row", None, None, "col", None),
            P(),
            P("col", None),
        ),
        out_specs=P(None, "sub", "row", None, None, "col", None),
        check_vma=False,
    )
```

```python
import functools

import jax
import jax.numpy as jnp
from jax import lax
from jax.experimental import pallas as pl
from jax.experimental.pallas import tpu as pltpu
from jax.sharding import PartitionSpec as P

PANEL = 1024
ROW_TILE = 16
VMEM_BYTES = 12 * 1024 * 1024
CONTRACT = (((1,), (1,)), ((), ()))
ON_CHIP = pl.BlockSpec(memory_space=pltpu.VMEM)
SCALARS = pl.BlockSpec(memory_space=pltpu.SMEM)


def call(kernel, out_shape, in_specs, flops=0, moved=1 << 19, **more):
    single = not isinstance(out_shape, (list, tuple))
    return pl.pallas_call(
        kernel,
        out_shape=out_shape,
        in_specs=in_specs,
        out_specs=more.pop("out_specs", ON_CHIP if single else [ON_CHIP] * len(out_shape)),
        compiler_params=pltpu.CompilerParams(vmem_limit_bytes=VMEM_BYTES),
        cost_estimate=pl.CostEstimate(flops=flops, bytes_accessed=moved, transcendentals=0),
        **more,
    )


def bf16(*shape):
    return jax.ShapeDtypeStruct(shape, jnp.bfloat16)


def f32(*shape):
    return jax.ShapeDtypeStruct(shape, jnp.float32)


def flipped(block, axis, mask):
    count = lax.axis_size(axis)
    return lax.ppermute(block, axis, [(i, i ^ mask) for i in range(count)])


def shifted(block, axis, apart):
    count = lax.axis_size(axis)
    return lax.ppermute(block, axis, [(i, (i + apart) % count) for i in range(count)])


def swap_even(i, count):
    return i ^ 1 if i ^ 1 < count else i


def swap_odd(i, count):
    j = ((i + 1) ^ 1) - 1
    return j if 0 <= j < count else i


@functools.cache
def line_plan(count):
    even = [swap_even(i, count) for i in range(count)]
    odd = [swap_odd(i, count) for i in range(count)]
    if count == 4:
        levels = [[(1, 0, even), (2, 0, odd)], [(3, 2, [2, 0, 3, 1]), (4, 1, [1, 3, 0, 2])]]
    else:
        levels, last = [], [0, 0]
        for step in range(count - 1):
            level = []
            for stream in (0, 1):
                level.append((1 + 2 * step + stream, last[stream], odd if (step + stream) % 2 else even))
                last[stream] = level[-1][0]
            levels.append(level)
    whose = {0: list(range(count))}
    seen = [[(0, i)] for i in range(count)]
    for level in levels:
        for array, source, to in level:
            whose[array] = [None] * count
            for i in range(count):
                whose[array][to[i]] = whose[source][i]
            for i in range(count):
                if all(whose[array][i] != origin for _, origin in seen[i]):
                    seen[i].append((array, whose[array][i]))
    origins = [[seen[i][j][1] for i in range(count)] for j in range(count)]
    places = [[seen[i][j][0] for i in range(count)] for j in range(count)]
    return levels, origins, places


class Line:
    def __init__(self, block, axis):
        self.axis = axis
        self.levels, _, self.places = line_plan(lax.axis_size(axis))
        self.held = {0: block}
        self.at = 0

    def step(self):
        for array, source, to in self.levels[self.at]:
            self.held[array] = lax.ppermute(self.held[source], self.axis, list(enumerate(to)))
        self.at += 1
        return self.at < len(self.levels)

    def fenced(self, *values):
        last = [array for array, _, _ in self.levels[self.at - 1]]
        out = fence(*values, *(self.held[array] for array in last))
        self.held.update(zip(last, out[len(values):]))
        return out[: len(values)]

    def taken(self):
        kinds = sorted({kind for row in self.places for kind in row})
        return kinds, [self.held[kind] for kind in kinds]


def among(index, members):
    found = index == members[0]
    for member in members[1:]:
        found = jnp.logical_or(found, index == member)
    return found


def looked_up(index, table):
    value = jnp.int32(table[0])
    for i, entry in enumerate(table[1:], 1):
        value = jnp.where(index == i, jnp.int32(entry), value)
    return value


def fence_kernel(*refs):
    pass


def fence(*values):
    place = pl.BlockSpec(memory_space=pl.ANY)
    return pl.pallas_call(
        fence_kernel,
        out_shape=[jax.ShapeDtypeStruct(v.shape, v.dtype) for v in values],
        in_specs=[place] * len(values),
        out_specs=[place] * len(values),
        input_output_aliases={n: n for n in range(len(values))},
        compiler_params=pltpu.CompilerParams(vmem_limit_bytes=1 << 20),
    )(*values)


def found_at(map_ref, child, place, wanted, child_count):
    at = jnp.int32(0)
    found = jnp.float32(0)
    for k in range(child_count):
        same = map_ref[child, place, k] == wanted
        at = jnp.where(same, jnp.int32(k), at)
        found = jnp.where(same, jnp.float32(1), found)
    return at, found


def block_places(map_ref, child, columns, slot_count, child_count):
    sub_index, row_index, col_index = (lax.axis_index(name) for name in ("sub", "row", "col"))
    rows = [
        found_at(map_ref, child, row_index, 2 * a + sub_index, child_count) for a in range(slot_count)
    ]
    cols = [found_at(map_ref, child, col_index, b, child_count) for b in columns]
    return rows, cols


def child_block(ref, row, col):
    return ref[row[0], col[0]].astype(jnp.float32) * (row[1] * col[1])


def line_tiles(count, share, lanes):
    return [(col, tile) for col in range(count) for tile in range(-(-(col + 1) * share // lanes))]


def pack_line(share_refs, out_ref, first, tiles):
    col_index = lax.axis_index("col")
    count = len(share_refs)
    rows, lanes = share_refs[0].shape[0], out_ref.shape[1]
    for apart, ref in enumerate(share_refs):
        for col in range(count):

            @pl.when(lax.rem(col_index + count - apart, count) == col)
            def _():
                for n, (home, tile) in enumerate(tiles):
                    if home == col:
                        out_ref[pl.ds(first + n * rows, rows), :] = ref[:, tile * lanes:(tile + 1) * lanes]


def panel_kernel(part, tiles, map_ref, pattern_ref, entries_ref, own_ref, received_ref, *refs):
    row_size, col_size = lax.axis_size("row"), lax.axis_size("col")
    share_refs, (piece_ref, *part_refs) = refs[: -1 - row_size], refs[-1 - row_size:]
    slot_count, groups, size, _ = entries_ref.shape
    child_count = own_ref.shape[0]
    sub_index, row_index = lax.axis_index("sub"), lax.axis_index("row")
    places = [
        block_places(map_ref, child, range(groups), slot_count, child_count)
        for child in (sub_index, 1 - sub_index)
    ]
    for a in range(slot_count):
        for b in range(groups):
            total = entries_ref[a, b].astype(jnp.float32) * pattern_ref[a, 0, b].astype(jnp.float32)
            for (rows, cols), ref in zip(places, (own_ref, received_ref)):
                total = total + child_block(ref, rows[a], cols[b])
            piece_ref[pl.ds(a * size, size), pl.ds(b * size, size)] = total.astype(jnp.bfloat16)
    used = slot_count * size
    if used < piece_ref.shape[0]:
        piece_ref[pl.ds(used, piece_ref.shape[0] - used), :] = jnp.zeros(
            (piece_ref.shape[0] - used, piece_ref.shape[1]), piece_ref.dtype
        )
    for mask, ref in enumerate(part_refs):
        ref[pl.ds(0, part), :] = piece_ref[
            pl.ds(pl.multiple_of((row_index ^ mask) * part, ROW_TILE), part), :
        ]
    if share_refs:
        pack_line(share_refs, part_refs[1], part, tiles)


def front_kernel(groups, map_ref, pattern_ref, entries_ref, own_ref, received_ref, piece_ref, out_ref):
    slot_count, column_count, size, _ = entries_ref.shape
    child_count = own_ref.shape[0]
    sub_index = lax.axis_index("sub")
    columns = range(groups, column_count)
    places = [
        block_places(map_ref, child, columns, slot_count, child_count)
        for child in (sub_index, 1 - sub_index)
    ]
    for a in range(slot_count):
        for b in range(groups):
            out_ref[a, b] = piece_ref[pl.ds(a * size, size), pl.ds(b * size, size)]
        for n, b in enumerate(columns):
            total = entries_ref[a, b].astype(jnp.float32) * pattern_ref[a, 0, b].astype(jnp.float32)
            for (rows, cols), ref in zip(places, (own_ref, received_ref)):
                total = total + child_block(ref, rows[a], cols[n])
            out_ref[a, b] = total.astype(jnp.bfloat16)


def inverse_kernel(rows, tiles, *refs):
    *in_refs, out_ref = refs
    sub_index, row_index = lax.axis_index("sub"), lax.axis_index("row")
    sub_size, row_size, col_size = (lax.axis_size(name) for name in ("sub", "row", "col"))
    width = out_ref.shape[0]
    lanes = in_refs[0].shape[1]
    share = width // col_size
    lines = [
        (ref, line * len(tiles) * rows) for ref in in_refs for line in range(2)
    ]
    for n, (ref, first) in enumerate(lines):
        sub_at = sub_index if n < row_size else 1 - sub_index
        inside = (sub_at * row_size + (row_index ^ (n % row_size))) * rows
        for m, (col, tile) in enumerate(tiles):
            top = pl.multiple_of(col * share + inside, ROW_TILE)
            block = ref[pl.ds(first + m * rows, rows), :]
            if (tile + 1) * lanes > col * share:
                row_at = top + lax.broadcasted_iota(jnp.int32, block.shape, 0)
                col_at = tile * lanes + lax.broadcasted_iota(jnp.int32, block.shape, 1)
                block = jnp.where(col_at <= row_at, block.astype(jnp.float32), 0.0).astype(jnp.bfloat16)
            out_ref[pl.ds(top, rows), pl.ds(tile * lanes, lanes)] = block
    for col in range(col_size):
        for tile in range(width // lanes):
            if (col, tile) not in tiles:
                out_ref[pl.ds(col * share, share), pl.ds(tile * lanes, lanes)] = jnp.zeros(
                    (share, lanes), out_ref.dtype
                )


def lower_kernel(in_ref, out_ref):
    row_at = lax.broadcasted_iota(jnp.int32, in_ref.shape, 0)
    col_at = lax.broadcasted_iota(jnp.int32, in_ref.shape, 1)
    out_ref[...] = jnp.where(col_at <= row_at, in_ref[...].astype(jnp.float32), 0.0).astype(jnp.bfloat16)


def join_kernel(*refs):
    *in_refs, out_ref = refs
    rows = in_refs[0].shape[0]
    for n, ref in enumerate(in_refs):
        out_ref[pl.ds(n * rows, rows), :] = ref[...]


def joined(blocks):
    rows, width = blocks[0].shape
    return call(join_kernel, bf16(rows * len(blocks), width), [ON_CHIP] * len(blocks))(*blocks)


def inverse_shares(diag_inverse):
    part = diag_inverse.shape[0] // (lax.axis_size("sub") * lax.axis_size("row"))
    if part % ROW_TILE:
        return []
    first = (lax.axis_index("sub") * lax.axis_size("row") + lax.axis_index("row")) * part
    mine = lax.dynamic_slice_in_dim(diag_inverse, first, part, 0)
    return [mine] + [shifted(mine, "col", apart) for apart in range(1, lax.axis_size("col"))]


def turn_kernel(part, *refs):
    row_size, count = lax.axis_size("row"), lax.axis_size("col")
    held, refs = refs[:row_size], refs[row_size:]
    if len(refs) > count:
        sent_ref, *outs, lines_ref = refs
        rows = sent_ref.shape[0] - part
        lines_ref[pl.ds(0, rows), :] = sent_ref[pl.ds(part, rows), :]
        lines_ref[pl.ds(rows, rows), :] = held[1][pl.ds(part, rows), :]
    else:
        outs = refs
    row_index, col_index = lax.axis_index("row"), lax.axis_index("col")
    for apart, out_ref in enumerate(outs):
        wanted = row_index ^ lax.rem(col_index + apart, count)
        for mask, ref in enumerate(held):

            @pl.when(wanted == mask)
            def _():
                out_ref[...] = ref[pl.ds(0, part), :]


def place_piece(panel_ref, rows, block, origin, count, size):
    for g in range(block.shape[1] // size):
        left = (g * count + origin) * size
        if not isinstance(origin, int):
            left = pl.multiple_of(left, size)
        panel_ref[rows, pl.ds(left, size)] = block[:, g * size:(g + 1) * size]


def factor_from(panel_ref, inverse_ref, out_ref, tile):
    rows, width = out_ref.shape
    for first in range(0, width, tile):
        out_ref[:, pl.ds(first, tile)] = lax.dot_general(
            panel_ref[pl.ds(0, rows), pl.ds(0, first + tile)],
            inverse_ref[pl.ds(first, tile), pl.ds(0, first + tile)],
            CONTRACT,
            preferred_element_type=jnp.float32,
        ).astype(jnp.bfloat16)


def row_factor_kernel(places, origins, kinds, size, tile, inverse_ref, *refs):
    arrays, out_ref, panel_ref = refs[: len(kinds)], refs[-2], refs[-1]
    col_index = lax.axis_index("col")
    count = len(origins)
    rows = out_ref.shape[0]
    for slot in range(count):
        origin = looked_up(col_index, origins[slot])
        for kind, ref in zip(kinds, arrays):
            members = tuple(i for i in range(count) if places[slot][i] == kind)
            if members:

                @pl.when(among(col_index, members))
                def _():
                    for top in range(0, rows, size):
                        at = pl.ds(top, size)
                        place_piece(panel_ref, at, ref[at, :], origin, count, size)

    factor_from(panel_ref, inverse_ref, out_ref, tile)


def column_factor_kernel(size, tile, inverse_ref, *refs):
    parts, out_ref, panel_ref = refs[:-2], refs[-2], refs[-1]
    row_index, col_index = lax.axis_index("row"), lax.axis_index("col")
    count = lax.axis_size("col")
    part = parts[0].shape[0] // count
    for mask, ref in enumerate(parts):
        at = pl.ds(pl.multiple_of((row_index ^ mask) * part, ROW_TILE), part)
        for apart in range(count):
            origin = lax.rem(col_index + count - apart, count)
            place_piece(panel_ref, at, ref[pl.ds(apart * part, part), :], origin, count, size)
    factor_from(panel_ref, inverse_ref, out_ref, tile)


def product_kernel(mine, rows_ref, columns_ref, front_ref, *refs):
    out_hbm, out_ref, sem = refs[-3:]
    sub_index = lax.axis_index("sub")
    half = sub_index if mine else 1 - sub_index
    slot_count, _, size, _ = out_ref.shape
    product = lax.dot_general(
        rows_ref[...], columns_ref[...], CONTRACT, preferred_element_type=jnp.float32
    )
    for m in range(slot_count):
        for a in range(slot_count):
            block = product[m * size:(m + 1) * size, a * size:(a + 1) * size]
            out_ref[m, a] = (front_ref[m, a, half].astype(jnp.float32) - block).astype(jnp.bfloat16)
    copy = pltpu.make_async_copy(out_ref, out_hbm.at[:, :, half], sem)
    copy.start()
    copy.wait()


def body(front_entries, block_pattern, child_update, child_map, diag_inverse):
    slot_count = front_entries.shape[0]
    size = front_entries.shape[3]
    column_count = front_entries.shape[4]
    child_count = child_update.shape[1]
    row_size = lax.axis_size("row")
    col_size = lax.axis_size("col")
    groups = -(-(PANEL // size) // col_size)
    tile = PANEL // 2
    rows = slot_count * size
    part = -(-rows // (row_size * ROW_TILE)) * ROW_TILE
    padded = part * row_size
    depth = groups * col_size * size
    in_hbm = pl.BlockSpec(memory_space=pltpu.HBM)
    entries = front_entries.reshape(slot_count, size, column_count, size).transpose(0, 2, 1, 3)
    pattern = block_pattern.reshape(slot_count, 1, column_count)
    slots = child_map.transpose(0, 2, 1)
    own = child_update.reshape(child_count, size, child_count, size).transpose(0, 2, 1, 3)

    received = flipped(own, "sub", 1)
    shares = inverse_shares(diag_inverse)
    lanes = groups * size
    tiles = line_tiles(col_size, diag_inverse.shape[0], lanes) if shares else []
    line_rows = len(tiles) * shares[0].shape[0] if shares else 0
    extra = [line_rows if mask == 1 else 0 for mask in range(row_size)]
    piece, *parts = call(
        functools.partial(panel_kernel, part, tiles),
        [bf16(padded, lanes)] + [bf16(part + more, lanes) for more in extra],
        [SCALARS, SCALARS] + [ON_CHIP] * (3 + len(shares)),
    )(slots, pattern, entries[:, :groups], own, received, *shares)

    _, origins, places = line_plan(col_size)
    pieces = Line(piece, "col")
    pieces.step()
    held = [parts[0]] + [flipped(parts[mask], "row", mask) for mask in range(1, row_size)]
    sent = parts[1:2] if shares else []
    turned = call(
        functools.partial(turn_kernel, part),
        [bf16(part, lanes)] * col_size + [bf16(2 * line_rows, lanes)] * len(sent),
        [ON_CHIP] * (row_size + len(sent)),
    )(*held, *sent)
    turned = pieces.fenced(*turned)
    near, sends, lines = turned[0], turned[1:col_size], list(turned[col_size:])
    if shares:
        for bit in range(1, row_size.bit_length() - 1):
            lines += [flipped(line, "row", 1 << bit) for line in lines]
    turned = joined(
        [near] + [shifted(block, "col", apart) for apart, block in enumerate(sends, 1)]
    )
    turned, *lines = pieces.fenced(turned, *lines)
    if shares:
        lines += [flipped(line, "sub", 1) for line in lines]
        inverse = call(
            functools.partial(inverse_kernel, shares[0].shape[0], tiles),
            bf16(PANEL, PANEL), [ON_CHIP] * len(lines), moved=4 << 20,
        )(*lines)
    else:
        whole = lax.all_gather(diag_inverse, "col", axis=0, tiled=True)
        inverse = call(lower_kernel, bf16(PANEL, PANEL), [ON_CHIP], moved=4 << 20)(whole)
    parts = [turned] + [flipped(turned, "row", mask) for mask in range(1, row_size)]
    while pieces.at < len(pieces.levels):
        pieces.step()
    front = call(
        functools.partial(front_kernel, groups),
        bf16(slot_count, column_count, size, size),
        [SCALARS, SCALARS] + [ON_CHIP] * 4,
        moved=6 << 20,
    )(slots, pattern, entries, own, received, piece)
    front, inverse, *parts = pieces.fenced(front, inverse, *parts)
    front = front.reshape(slot_count, slot_count, 2, size, size)

    kinds, arrays = pieces.taken()
    scratch = [pltpu.VMEM((padded, depth), jnp.bfloat16)]
    flops = 2 * rows * PANEL * PANEL * 3 // 4
    column_factor = call(
        functools.partial(column_factor_kernel, size, tile),
        bf16(rows, PANEL), [ON_CHIP] * (1 + row_size), flops=flops, scratch_shapes=scratch,
    )(inverse, *parts)
    other_factor = flipped(column_factor, "sub", 1)
    row_factor = call(
        functools.partial(row_factor_kernel, places, origins, kinds, size, tile),
        bf16(rows, PANEL), [ON_CHIP] * (1 + len(arrays)), flops=flops, scratch_shapes=scratch,
    )(inverse, *arrays)
    product = functools.partial(
        call,
        out_shape=bf16(slot_count, slot_count, 2, size, size),
        flops=2 * rows * rows * PANEL,
        out_specs=in_hbm,
        scratch_shapes=[
            pltpu.VMEM((slot_count, slot_count, size, size), jnp.bfloat16),
            pltpu.SemaphoreType.DMA,
        ],
    )
    trailing = product(functools.partial(product_kernel, True), in_specs=[ON_CHIP] * 3)(
        row_factor, column_factor, front
    )
    trailing = product(
        functools.partial(product_kernel, False), in_specs=[ON_CHIP] * 3 + [in_hbm],
        input_output_aliases={3: 0},
    )(row_factor, other_factor, front, trailing)
    return trailing.reshape(slot_count, column_count, size, size).transpose(0, 2, 1, 3).reshape(
        slot_count, 1, 1, size, column_count, 1, size
    )


def solution(mesh):
    return jax.shard_map(
        body,
        mesh=mesh,
        in_specs=(
            P(None, "sub", "row", None, None, "col", None),
            P(None, "sub", "row", None, "col"),
            P("sub", None, "row", None, None, "col", None),
            P(),
            P("col", None),
        ),
        out_specs=P(None, "sub", "row", None, None, "col", None),
        check_vma=False,
    )
```

```python
import functools

import jax
import jax.numpy as jnp
from jax import lax
from jax.experimental import pallas as pl
from jax.experimental.pallas import tpu as pltpu
from jax.sharding import PartitionSpec as P

PANEL = 1024
ROW_TILE = 16
VMEM_BYTES = 12 * 1024 * 1024
CONTRACT = (((1,), (1,)), ((), ()))
ON_CHIP = pl.BlockSpec(memory_space=pltpu.VMEM)
SCALARS = pl.BlockSpec(memory_space=pltpu.SMEM)


def call(kernel, out_shape, in_specs, flops=0, moved=1 << 19, **more):
    single = not isinstance(out_shape, (list, tuple))
    return pl.pallas_call(
        kernel,
        out_shape=out_shape,
        in_specs=in_specs,
        out_specs=more.pop("out_specs", ON_CHIP if single else [ON_CHIP] * len(out_shape)),
        compiler_params=pltpu.CompilerParams(vmem_limit_bytes=VMEM_BYTES),
        cost_estimate=pl.CostEstimate(flops=flops, bytes_accessed=moved, transcendentals=0),
        **more,
    )


def bf16(*shape):
    return jax.ShapeDtypeStruct(shape, jnp.bfloat16)


def f32(*shape):
    return jax.ShapeDtypeStruct(shape, jnp.float32)


def flipped(block, axis, mask):
    count = lax.axis_size(axis)
    return lax.ppermute(block, axis, [(i, i ^ mask) for i in range(count)])


def shifted(block, axis, apart):
    count = lax.axis_size(axis)
    return lax.ppermute(block, axis, [(i, (i + apart) % count) for i in range(count)])


def swap_even(i, count):
    return i ^ 1 if i ^ 1 < count else i


def swap_odd(i, count):
    j = ((i + 1) ^ 1) - 1
    return j if 0 <= j < count else i


@functools.cache
def line_plan(count):
    even = [swap_even(i, count) for i in range(count)]
    odd = [swap_odd(i, count) for i in range(count)]
    if count == 4:
        levels = [[(1, 0, even), (2, 0, odd)], [(3, 2, [2, 0, 3, 1]), (4, 1, [1, 3, 0, 2])]]
    else:
        levels, last = [], [0, 0]
        for step in range(count - 1):
            level = []
            for stream in (0, 1):
                level.append((1 + 2 * step + stream, last[stream], odd if (step + stream) % 2 else even))
                last[stream] = level[-1][0]
            levels.append(level)
    whose = {0: list(range(count))}
    seen = [[(0, i)] for i in range(count)]
    for level in levels:
        for array, source, to in level:
            whose[array] = [None] * count
            for i in range(count):
                whose[array][to[i]] = whose[source][i]
            for i in range(count):
                if all(whose[array][i] != origin for _, origin in seen[i]):
                    seen[i].append((array, whose[array][i]))
    origins = [[seen[i][j][1] for i in range(count)] for j in range(count)]
    places = [[seen[i][j][0] for i in range(count)] for j in range(count)]
    return levels, origins, places


class Line:
    def __init__(self, block, axis):
        self.axis = axis
        self.levels, _, self.places = line_plan(lax.axis_size(axis))
        self.held = {0: block}
        self.at = 0

    def step(self):
        for array, source, to in self.levels[self.at]:
            self.held[array] = lax.ppermute(self.held[source], self.axis, list(enumerate(to)))
        self.at += 1
        return self.at < len(self.levels)

    def fenced(self, *values):
        last = [array for array, _, _ in self.levels[self.at - 1]]
        out = fence(*values, *(self.held[array] for array in last))
        self.held.update(zip(last, out[len(values):]))
        return out[: len(values)]

    def taken(self):
        kinds = sorted({kind for row in self.places for kind in row})
        return kinds, [self.held[kind] for kind in kinds]


def among(index, members):
    found = index == members[0]
    for member in members[1:]:
        found = jnp.logical_or(found, index == member)
    return found


def looked_up(index, table):
    value = jnp.int32(table[0])
    for i, entry in enumerate(table[1:], 1):
        value = jnp.where(index == i, jnp.int32(entry), value)
    return value


def fence_kernel(*refs):
    pass


def fence(*values):
    place = pl.BlockSpec(memory_space=pl.ANY)
    return pl.pallas_call(
        fence_kernel,
        out_shape=[jax.ShapeDtypeStruct(v.shape, v.dtype) for v in values],
        in_specs=[place] * len(values),
        out_specs=[place] * len(values),
        input_output_aliases={n: n for n in range(len(values))},
        compiler_params=pltpu.CompilerParams(vmem_limit_bytes=1 << 20),
    )(*values)


def found_at(map_ref, child, place, wanted, child_count):
    at = jnp.int32(0)
    found = jnp.float32(0)
    for k in range(child_count):
        same = map_ref[child, place, k] == wanted
        at = jnp.where(same, jnp.int32(k), at)
        found = jnp.where(same, jnp.float32(1), found)
    return at, found


def block_places(map_ref, child, columns, slot_count, child_count):
    sub_index, row_index, col_index = (lax.axis_index(name) for name in ("sub", "row", "col"))
    rows = [
        found_at(map_ref, child, row_index, 2 * a + sub_index, child_count) for a in range(slot_count)
    ]
    cols = [found_at(map_ref, child, col_index, b, child_count) for b in columns]
    return rows, cols


def child_block(ref, row, col):
    return ref[row[0], col[0]].astype(jnp.float32) * (row[1] * col[1])


def line_tiles(count, share, lanes):
    return [(col, tile) for col in range(count) for tile in range(-(-(col + 1) * share // lanes))]


def pack_line(share_refs, out_ref, first, tiles):
    col_index = lax.axis_index("col")
    count = len(share_refs)
    rows, lanes = share_refs[0].shape[0], out_ref.shape[1]
    for apart, ref in enumerate(share_refs):
        for col in range(count):

            @pl.when(lax.rem(col_index + count - apart, count) == col)
            def _():
                for n, (home, tile) in enumerate(tiles):
                    if home == col:
                        out_ref[pl.ds(first + n * rows, rows), :] = ref[:, tile * lanes:(tile + 1) * lanes]


def pack_kernel(part, tiles, *refs):
    part_ref, *share_refs, out_ref = refs
    out_ref[pl.ds(0, part), :] = part_ref[...]
    pack_line(share_refs, out_ref, part, tiles)


def panel_kernel(part, groups, map_ref, pattern_ref, entries_ref, own_ref, received_ref, piece_ref, *part_refs):
    slot_count, _, size, _ = entries_ref.shape
    child_count = own_ref.shape[0]
    sub_index, row_index = lax.axis_index("sub"), lax.axis_index("row")
    places = [
        block_places(map_ref, child, range(groups), slot_count, child_count)
        for child in (sub_index, 1 - sub_index)
    ]
    for a in range(slot_count):
        for b in range(groups):
            total = entries_ref[a, b].astype(jnp.float32) * pattern_ref[a, 0, b].astype(jnp.float32)
            for (rows, cols), ref in zip(places, (own_ref, received_ref)):
                total = total + child_block(ref, rows[a], cols[b])
            piece_ref[pl.ds(a * size, size), pl.ds(b * size, size)] = total.astype(jnp.bfloat16)
    used = slot_count * size
    if used < piece_ref.shape[0]:
        piece_ref[pl.ds(used, piece_ref.shape[0] - used), :] = jnp.zeros(
            (piece_ref.shape[0] - used, piece_ref.shape[1]), piece_ref.dtype
        )
    for mask, ref in enumerate(part_refs):
        ref[...] = piece_ref[pl.ds(pl.multiple_of((row_index ^ mask) * part, ROW_TILE), part), :]


def front_kernel(groups, map_ref, pattern_ref, entries_ref, own_ref, received_ref, piece_ref, out_ref):
    slot_count, column_count, size, _ = entries_ref.shape
    child_count = own_ref.shape[0]
    sub_index = lax.axis_index("sub")
    columns = range(groups, column_count)
    places = [
        block_places(map_ref, child, columns, slot_count, child_count)
        for child in (sub_index, 1 - sub_index)
    ]
    for a in range(slot_count):
        for b in range(groups):
            out_ref[a, b] = piece_ref[pl.ds(a * size, size), pl.ds(b * size, size)]
        for n, b in enumerate(columns):
            total = entries_ref[a, b].astype(jnp.float32) * pattern_ref[a, 0, b].astype(jnp.float32)
            for (rows, cols), ref in zip(places, (own_ref, received_ref)):
                total = total + child_block(ref, rows[a], cols[n])
            out_ref[a, b] = total.astype(jnp.bfloat16)


def inverse_kernel(rows, tiles, *refs):
    *in_refs, out_ref = refs
    sub_index, row_index = lax.axis_index("sub"), lax.axis_index("row")
    sub_size, row_size, col_size = (lax.axis_size(name) for name in ("sub", "row", "col"))
    width = out_ref.shape[0]
    lanes = in_refs[0].shape[1]
    share = width // col_size
    lines = [
        (ref, line * len(tiles) * rows) for ref in in_refs for line in range(2)
    ]
    for n, (ref, first) in enumerate(lines):
        sub_at = sub_index if n < row_size else 1 - sub_index
        inside = (sub_at * row_size + (row_index ^ (n % row_size))) * rows
        for m, (col, tile) in enumerate(tiles):
            top = pl.multiple_of(col * share + inside, ROW_TILE)
            block = ref[pl.ds(first + m * rows, rows), :]
            if (tile + 1) * lanes > col * share:
                row_at = top + lax.broadcasted_iota(jnp.int32, block.shape, 0)
                col_at = tile * lanes + lax.broadcasted_iota(jnp.int32, block.shape, 1)
                block = jnp.where(col_at <= row_at, block.astype(jnp.float32), 0.0).astype(jnp.bfloat16)
            out_ref[pl.ds(top, rows), pl.ds(tile * lanes, lanes)] = block
    for col in range(col_size):
        for tile in range(width // lanes):
            if (col, tile) not in tiles:
                out_ref[pl.ds(col * share, share), pl.ds(tile * lanes, lanes)] = jnp.zeros(
                    (share, lanes), out_ref.dtype
                )


def lower_kernel(in_ref, out_ref):
    row_at = lax.broadcasted_iota(jnp.int32, in_ref.shape, 0)
    col_at = lax.broadcasted_iota(jnp.int32, in_ref.shape, 1)
    out_ref[...] = jnp.where(col_at <= row_at, in_ref[...].astype(jnp.float32), 0.0).astype(jnp.bfloat16)


def join_kernel(*refs):
    *in_refs, out_ref = refs
    rows = in_refs[0].shape[0]
    for n, ref in enumerate(in_refs):
        out_ref[pl.ds(n * rows, rows), :] = ref[...]


def joined(blocks):
    rows, width = blocks[0].shape
    return call(join_kernel, bf16(rows * len(blocks), width), [ON_CHIP] * len(blocks))(*blocks)


def inverse_shares(diag_inverse):
    part = diag_inverse.shape[0] // (lax.axis_size("sub") * lax.axis_size("row"))
    if part % ROW_TILE:
        return []
    first = (lax.axis_index("sub") * lax.axis_size("row") + lax.axis_index("row")) * part
    mine = lax.dynamic_slice_in_dim(diag_inverse, first, part, 0)
    return [mine] + [shifted(mine, "col", apart) for apart in range(1, lax.axis_size("col"))]


def turn_kernel(part, *refs):
    row_size, count = lax.axis_size("row"), lax.axis_size("col")
    held, refs = refs[:row_size], refs[row_size:]
    if len(refs) > count:
        sent_ref, *outs, lines_ref = refs
        rows = sent_ref.shape[0] - part
        lines_ref[pl.ds(0, rows), :] = sent_ref[pl.ds(part, rows), :]
        lines_ref[pl.ds(rows, rows), :] = held[1][pl.ds(part, rows), :]
    else:
        outs = refs
    row_index, col_index = lax.axis_index("row"), lax.axis_index("col")
    for apart, out_ref in enumerate(outs):
        wanted = row_index ^ lax.rem(col_index + apart, count)
        for mask, ref in enumerate(held):

            @pl.when(wanted == mask)
            def _():
                out_ref[...] = ref[pl.ds(0, part), :]


def place_piece(panel_ref, rows, block, origin, count, size):
    for g in range(block.shape[1] // size):
        left = (g * count + origin) * size
        if not isinstance(origin, int):
            left = pl.multiple_of(left, size)
        panel_ref[rows, pl.ds(left, size)] = block[:, g * size:(g + 1) * size]


def factor_from(panel_ref, inverse_ref, out_ref, tile):
    rows, width = out_ref.shape
    for first in range(0, width, tile):
        out_ref[:, pl.ds(first, tile)] = lax.dot_general(
            panel_ref[pl.ds(0, rows), pl.ds(0, first + tile)],
            inverse_ref[pl.ds(first, tile), pl.ds(0, first + tile)],
            CONTRACT,
            preferred_element_type=jnp.float32,
        ).astype(jnp.bfloat16)


def row_factor_kernel(places, origins, kinds, size, tile, inverse_ref, *refs):
    arrays, out_ref, panel_ref = refs[: len(kinds)], refs[-2], refs[-1]
    col_index = lax.axis_index("col")
    count = len(origins)
    rows = out_ref.shape[0]
    for slot in range(count):
        origin = looked_up(col_index, origins[slot])
        for kind, ref in zip(kinds, arrays):
            members = tuple(i for i in range(count) if places[slot][i] == kind)
            if members:

                @pl.when(among(col_index, members))
                def _():
                    for top in range(0, rows, size):
                        at = pl.ds(top, size)
                        place_piece(panel_ref, at, ref[at, :], origin, count, size)

    factor_from(panel_ref, inverse_ref, out_ref, tile)


def column_factor_kernel(size, tile, inverse_ref, *refs):
    parts, out_ref, panel_ref = refs[:-2], refs[-2], refs[-1]
    row_index, col_index = lax.axis_index("row"), lax.axis_index("col")
    count = lax.axis_size("col")
    part = parts[0].shape[0] // count
    for mask, ref in enumerate(parts):
        at = pl.ds(pl.multiple_of((row_index ^ mask) * part, ROW_TILE), part)
        for apart in range(count):
            origin = lax.rem(col_index + count - apart, count)
            place_piece(panel_ref, at, ref[pl.ds(apart * part, part), :], origin, count, size)
    factor_from(panel_ref, inverse_ref, out_ref, tile)


def product_kernel(mine, rows_ref, columns_ref, front_ref, *refs):
    out_hbm, out_ref, sems = refs[-3:]
    sub_index = lax.axis_index("sub")
    half = sub_index if mine else 1 - sub_index
    slot_count, _, size, _ = out_ref.shape
    copies = []
    for n, first in enumerate(range(0, slot_count, 2)):
        blocks = min(2, slot_count - first)
        product = lax.dot_general(
            rows_ref[...],
            columns_ref[pl.ds(first * size, blocks * size), :],
            CONTRACT,
            preferred_element_type=jnp.float32,
        )
        for m in range(slot_count):
            for a in range(blocks):
                block = product[m * size:(m + 1) * size, a * size:(a + 1) * size]
                out_ref[m, first + a] = (
                    front_ref[m, first + a, half].astype(jnp.float32) - block
                ).astype(jnp.bfloat16)
        done = pl.ds(first, blocks)
        copies.append(pltpu.make_async_copy(out_ref.at[:, done], out_hbm.at[:, done, half], sems.at[n]))
        copies[-1].start()
    for copy in copies:
        copy.wait()


def body(front_entries, block_pattern, child_update, child_map, diag_inverse):
    slot_count = front_entries.shape[0]
    size = front_entries.shape[3]
    column_count = front_entries.shape[4]
    child_count = child_update.shape[1]
    row_size = lax.axis_size("row")
    col_size = lax.axis_size("col")
    groups = -(-(PANEL // size) // col_size)
    tile = PANEL // 2
    rows = slot_count * size
    part = -(-rows // (row_size * ROW_TILE)) * ROW_TILE
    padded = part * row_size
    depth = groups * col_size * size
    in_hbm = pl.BlockSpec(memory_space=pltpu.HBM)
    entries = front_entries.reshape(slot_count, size, column_count, size).transpose(0, 2, 1, 3)
    pattern = block_pattern.reshape(slot_count, 1, column_count)
    slots = child_map.transpose(0, 2, 1)
    own = child_update.reshape(child_count, size, child_count, size).transpose(0, 2, 1, 3)

    received = flipped(own, "sub", 1)
    shares = inverse_shares(diag_inverse)
    lanes = groups * size
    tiles = line_tiles(col_size, diag_inverse.shape[0], lanes) if shares else []
    line_rows = len(tiles) * shares[0].shape[0] if shares else 0
    received, *shares = fence(received, *shares)
    piece, *parts = call(
        functools.partial(panel_kernel, part, groups),
        [bf16(padded, lanes)] + [bf16(part, lanes)] * row_size,
        [SCALARS, SCALARS] + [ON_CHIP] * 3,
    )(slots, pattern, entries, own, received)
    if shares:
        parts[1] = call(
            functools.partial(pack_kernel, part, tiles), bf16(part + line_rows, lanes), [ON_CHIP] * (1 + len(shares))
        )(parts[1], *shares)

    _, origins, places = line_plan(col_size)
    pieces = Line(piece, "col")
    pieces.step()
    held = [parts[0]] + [flipped(parts[mask], "row", mask) for mask in range(1, row_size)]
    sent = parts[1:2] if shares else []
    turned = call(
        functools.partial(turn_kernel, part),
        [bf16(part, lanes)] * col_size + [bf16(2 * line_rows, lanes)] * len(sent),
        [ON_CHIP] * (row_size + len(sent)),
    )(*held, *sent)
    turned = pieces.fenced(*turned)
    near, sends, lines = turned[0], turned[1:col_size], list(turned[col_size:])
    if shares:
        for bit in range(1, row_size.bit_length() - 1):
            lines += [flipped(line, "row", 1 << bit) for line in lines]
    turned = joined(
        [near] + [shifted(block, "col", apart) for apart, block in enumerate(sends, 1)]
    )
    turned, *lines = pieces.fenced(turned, *lines)
    if shares:
        lines += [flipped(line, "sub", 1) for line in lines]
        inverse = call(
            functools.partial(inverse_kernel, shares[0].shape[0], tiles),
            bf16(PANEL, PANEL), [ON_CHIP] * len(lines), moved=4 << 20,
        )(*lines)
    else:
        whole = lax.all_gather(diag_inverse, "col", axis=0, tiled=True)
        inverse = call(lower_kernel, bf16(PANEL, PANEL), [ON_CHIP], moved=4 << 20)(whole)
    parts = [turned] + [flipped(turned, "row", mask) for mask in range(1, row_size)]
    while pieces.at < len(pieces.levels):
        pieces.step()
    front = call(
        functools.partial(front_kernel, groups),
        bf16(slot_count, column_count, size, size),
        [SCALARS, SCALARS] + [ON_CHIP] * 4,
        moved=6 << 20,
    )(slots, pattern, entries, own, received, piece)
    front, inverse, *parts = pieces.fenced(front, inverse, *parts)
    front = front.reshape(slot_count, slot_count, 2, size, size)

    kinds, arrays = pieces.taken()
    scratch = [pltpu.VMEM((padded, depth), jnp.bfloat16)]
    flops = 2 * rows * PANEL * PANEL * 3 // 4
    column_factor = call(
        functools.partial(column_factor_kernel, size, tile),
        bf16(rows, PANEL), [ON_CHIP] * (1 + row_size), flops=flops, scratch_shapes=scratch,
    )(inverse, *parts)
    other_factor = flipped(column_factor, "sub", 1)
    row_factor = call(
        functools.partial(row_factor_kernel, places, origins, kinds, size, tile),
        bf16(rows, PANEL), [ON_CHIP] * (1 + len(arrays)), flops=flops, scratch_shapes=scratch,
    )(inverse, *arrays)
    product = functools.partial(
        call,
        out_shape=bf16(slot_count, slot_count, 2, size, size),
        flops=2 * rows * rows * PANEL,
        out_specs=in_hbm,
        scratch_shapes=[
            pltpu.VMEM((slot_count, slot_count, size, size), jnp.bfloat16),
            pltpu.SemaphoreType.DMA((-(-slot_count // 2),)),
        ],
    )
    trailing = product(functools.partial(product_kernel, True), in_specs=[ON_CHIP] * 3)(
        row_factor, column_factor, front
    )
    trailing = product(
        functools.partial(product_kernel, False), in_specs=[ON_CHIP] * 3 + [in_hbm],
        input_output_aliases={3: 0},
    )(row_factor, other_factor, front, trailing)
    return trailing.reshape(slot_count, column_count, size, size).transpose(0, 2, 1, 3).reshape(
        slot_count, 1, 1, size, column_count, 1, size
    )


def solution(mesh):
    return jax.shard_map(
        body,
        mesh=mesh,
        in_specs=(
            P(None, "sub", "row", None, None, "col", None),
            P(None, "sub", "row", None, "col"),
            P("sub", None, "row", None, None, "col", None),
            P(),
            P("col", None),
        ),
        out_specs=P(None, "sub", "row", None, None, "col", None),
        check_vma=False,
    )
```

```python
import functools

import jax
import jax.numpy as jnp
from jax import lax
from jax.experimental import pallas as pl
from jax.experimental.pallas import tpu as pltpu
from jax.sharding import PartitionSpec as P

PANEL = 1024
ROW_TILE = 16
VMEM_BYTES = 12 * 1024 * 1024
CONTRACT = (((1,), (1,)), ((), ()))
ON_CHIP = pl.BlockSpec(memory_space=pltpu.VMEM)
SCALARS = pl.BlockSpec(memory_space=pltpu.SMEM)


def call(kernel, out_shape, in_specs, flops=0, moved=1 << 19, **more):
    single = not isinstance(out_shape, (list, tuple))
    return pl.pallas_call(
        kernel,
        out_shape=out_shape,
        in_specs=in_specs,
        out_specs=more.pop("out_specs", ON_CHIP if single else [ON_CHIP] * len(out_shape)),
        compiler_params=pltpu.CompilerParams(vmem_limit_bytes=VMEM_BYTES),
        cost_estimate=pl.CostEstimate(flops=flops, bytes_accessed=moved, transcendentals=0),
        **more,
    )


def bf16(*shape):
    return jax.ShapeDtypeStruct(shape, jnp.bfloat16)


def f32(*shape):
    return jax.ShapeDtypeStruct(shape, jnp.float32)


def flipped(block, axis, mask):
    count = lax.axis_size(axis)
    return lax.ppermute(block, axis, [(i, i ^ mask) for i in range(count)])


def shifted(block, axis, apart):
    count = lax.axis_size(axis)
    return lax.ppermute(block, axis, [(i, (i + apart) % count) for i in range(count)])


def swap_even(i, count):
    return i ^ 1 if i ^ 1 < count else i


def swap_odd(i, count):
    j = ((i + 1) ^ 1) - 1
    return j if 0 <= j < count else i


@functools.cache
def line_plan(count):
    even = [swap_even(i, count) for i in range(count)]
    odd = [swap_odd(i, count) for i in range(count)]
    if count == 4:
        levels = [[(1, 0, even), (2, 0, odd)], [(3, 2, [2, 0, 3, 1]), (4, 1, [1, 3, 0, 2])]]
    else:
        levels, last = [], [0, 0]
        for step in range(count - 1):
            level = []
            for stream in (0, 1):
                level.append((1 + 2 * step + stream, last[stream], odd if (step + stream) % 2 else even))
                last[stream] = level[-1][0]
            levels.append(level)
    whose = {0: list(range(count))}
    seen = [[(0, i)] for i in range(count)]
    for level in levels:
        for array, source, to in level:
            whose[array] = [None] * count
            for i in range(count):
                whose[array][to[i]] = whose[source][i]
            for i in range(count):
                if all(whose[array][i] != origin for _, origin in seen[i]):
                    seen[i].append((array, whose[array][i]))
    origins = [[seen[i][j][1] for i in range(count)] for j in range(count)]
    places = [[seen[i][j][0] for i in range(count)] for j in range(count)]
    return levels, origins, places


class Line:
    def __init__(self, block, axis):
        self.axis = axis
        self.levels, _, self.places = line_plan(lax.axis_size(axis))
        self.held = {0: block}
        self.at = 0

    def step(self):
        for array, source, to in self.levels[self.at]:
            self.held[array] = lax.ppermute(self.held[source], self.axis, list(enumerate(to)))
        self.at += 1
        return self.at < len(self.levels)

    def fenced(self, *values):
        last = [array for array, _, _ in self.levels[self.at - 1]]
        out = fence(*values, *(self.held[array] for array in last))
        self.held.update(zip(last, out[len(values):]))
        return out[: len(values)]

    def taken(self):
        kinds = sorted({kind for row in self.places for kind in row})
        return kinds, [self.held[kind] for kind in kinds]


def among(index, members):
    found = index == members[0]
    for member in members[1:]:
        found = jnp.logical_or(found, index == member)
    return found


def looked_up(index, table):
    value = jnp.int32(table[0])
    for i, entry in enumerate(table[1:], 1):
        value = jnp.where(index == i, jnp.int32(entry), value)
    return value


def fence_kernel(*refs):
    pass


def fence(*values):
    place = pl.BlockSpec(memory_space=pl.ANY)
    return pl.pallas_call(
        fence_kernel,
        out_shape=[jax.ShapeDtypeStruct(v.shape, v.dtype) for v in values],
        in_specs=[place] * len(values),
        out_specs=[place] * len(values),
        input_output_aliases={n: n for n in range(len(values))},
        compiler_params=pltpu.CompilerParams(vmem_limit_bytes=1 << 20),
    )(*values)


def found_at(map_ref, child, place, wanted, child_count):
    at = jnp.int32(0)
    found = jnp.float32(0)
    for k in range(child_count):
        same = map_ref[child, place, k] == wanted
        at = jnp.where(same, jnp.int32(k), at)
        found = jnp.where(same, jnp.float32(1), found)
    return at, found


def block_places(map_ref, child, columns, slot_count, child_count):
    sub_index, row_index, col_index = (lax.axis_index(name) for name in ("sub", "row", "col"))
    rows = [
        found_at(map_ref, child, row_index, 2 * a + sub_index, child_count) for a in range(slot_count)
    ]
    cols = [found_at(map_ref, child, col_index, b, child_count) for b in columns]
    return rows, cols


def child_block(ref, row, col):
    return ref[row[0], col[0]].astype(jnp.float32) * (row[1] * col[1])


def line_tiles(count, share, lanes):
    return [(col, tile) for col in range(count) for tile in range(-(-(col + 1) * share // lanes))]


def pack_line(share_refs, out_ref, first, tiles):
    col_index = lax.axis_index("col")
    count = len(share_refs)
    rows, lanes = share_refs[0].shape[0], out_ref.shape[1]
    for apart, ref in enumerate(share_refs):
        for col in range(count):

            @pl.when(lax.rem(col_index + count - apart, count) == col)
            def _():
                for n, (home, tile) in enumerate(tiles):
                    if home == col:
                        out_ref[pl.ds(first + n * rows, rows), :] = ref[:, tile * lanes:(tile + 1) * lanes]


def pack_kernel(part, tiles, *refs):
    part_ref, *share_refs, out_ref = refs
    out_ref[pl.ds(0, part), :] = part_ref[...]
    pack_line(share_refs, out_ref, part, tiles)


def panel_kernel(part, groups, map_ref, pattern_ref, entries_ref, own_ref, received_ref, piece_ref, *part_refs):
    slot_count, _, size, _ = entries_ref.shape
    child_count = own_ref.shape[0]
    sub_index, row_index = lax.axis_index("sub"), lax.axis_index("row")
    places = [
        block_places(map_ref, child, range(groups), slot_count, child_count)
        for child in (sub_index, 1 - sub_index)
    ]
    for a in range(slot_count):
        for b in range(groups):
            total = entries_ref[a, b].astype(jnp.float32) * pattern_ref[a, 0, b].astype(jnp.float32)
            for (rows, cols), ref in zip(places, (own_ref, received_ref)):
                total = total + child_block(ref, rows[a], cols[b])
            piece_ref[pl.ds(a * size, size), pl.ds(b * size, size)] = total.astype(jnp.bfloat16)
    used = slot_count * size
    if used < piece_ref.shape[0]:
        piece_ref[pl.ds(used, piece_ref.shape[0] - used), :] = jnp.zeros(
            (piece_ref.shape[0] - used, piece_ref.shape[1]), piece_ref.dtype
        )
    for mask, ref in enumerate(part_refs):
        ref[...] = piece_ref[pl.ds(pl.multiple_of((row_index ^ mask) * part, ROW_TILE), part), :]


def front_kernel(groups, map_ref, pattern_ref, entries_ref, own_ref, received_ref, piece_ref, out_ref):
    slot_count, column_count, size, _ = entries_ref.shape
    child_count = own_ref.shape[0]
    sub_index = lax.axis_index("sub")
    columns = range(groups, column_count)
    places = [
        block_places(map_ref, child, columns, slot_count, child_count)
        for child in (sub_index, 1 - sub_index)
    ]
    for a in range(slot_count):
        for b in range(groups):
            out_ref[a, b] = piece_ref[pl.ds(a * size, size), pl.ds(b * size, size)]
        for n, b in enumerate(columns):
            total = entries_ref[a, b].astype(jnp.float32) * pattern_ref[a, 0, b].astype(jnp.float32)
            for (rows, cols), ref in zip(places, (own_ref, received_ref)):
                total = total + child_block(ref, rows[a], cols[n])
            out_ref[a, b] = total.astype(jnp.bfloat16)


def inverse_kernel(rows, tiles, *refs):
    *in_refs, out_ref = refs
    sub_index, row_index = lax.axis_index("sub"), lax.axis_index("row")
    sub_size, row_size, col_size = (lax.axis_size(name) for name in ("sub", "row", "col"))
    width = out_ref.shape[0]
    lanes = in_refs[0].shape[1]
    share = width // col_size
    lines = [
        (ref, line * len(tiles) * rows) for ref in in_refs for line in range(2)
    ]
    for n, (ref, first) in enumerate(lines):
        sub_at = sub_index if n < row_size else 1 - sub_index
        inside = (sub_at * row_size + (row_index ^ (n % row_size))) * rows
        for m, (col, tile) in enumerate(tiles):
            top = pl.multiple_of(col * share + inside, ROW_TILE)
            block = ref[pl.ds(first + m * rows, rows), :]
            if (tile + 1) * lanes > col * share:
                row_at = top + lax.broadcasted_iota(jnp.int32, block.shape, 0)
                col_at = tile * lanes + lax.broadcasted_iota(jnp.int32, block.shape, 1)
                block = jnp.where(col_at <= row_at, block.astype(jnp.float32), 0.0).astype(jnp.bfloat16)
            out_ref[pl.ds(top, rows), pl.ds(tile * lanes, lanes)] = block
    for col in range(col_size):
        for tile in range(width // lanes):
            if (col, tile) not in tiles:
                out_ref[pl.ds(col * share, share), pl.ds(tile * lanes, lanes)] = jnp.zeros(
                    (share, lanes), out_ref.dtype
                )


def lower_kernel(in_ref, out_ref):
    row_at = lax.broadcasted_iota(jnp.int32, in_ref.shape, 0)
    col_at = lax.broadcasted_iota(jnp.int32, in_ref.shape, 1)
    out_ref[...] = jnp.where(col_at <= row_at, in_ref[...].astype(jnp.float32), 0.0).astype(jnp.bfloat16)


def join_kernel(*refs):
    *in_refs, out_ref = refs
    rows = in_refs[0].shape[0]
    for n, ref in enumerate(in_refs):
        out_ref[pl.ds(n * rows, rows), :] = ref[...]


def joined(blocks):
    rows, width = blocks[0].shape
    return call(join_kernel, bf16(rows * len(blocks), width), [ON_CHIP] * len(blocks))(*blocks)


def inverse_shares(diag_inverse):
    part = diag_inverse.shape[0] // (lax.axis_size("sub") * lax.axis_size("row"))
    if part % ROW_TILE:
        return []
    first = (lax.axis_index("sub") * lax.axis_size("row") + lax.axis_index("row")) * part
    mine = lax.dynamic_slice_in_dim(diag_inverse, first, part, 0)
    return [mine] + [shifted(mine, "col", apart) for apart in range(1, lax.axis_size("col"))]


def turn_kernel(part, *refs):
    row_size, count = lax.axis_size("row"), lax.axis_size("col")
    held, refs = refs[:row_size], refs[row_size:]
    if len(refs) > count:
        sent_ref, *outs, lines_ref = refs
        rows = sent_ref.shape[0] - part
        lines_ref[pl.ds(0, rows), :] = sent_ref[pl.ds(part, rows), :]
        lines_ref[pl.ds(rows, rows), :] = held[1][pl.ds(part, rows), :]
    else:
        outs = refs
    row_index, col_index = lax.axis_index("row"), lax.axis_index("col")
    for apart, out_ref in enumerate(outs):
        wanted = row_index ^ lax.rem(col_index + apart, count)
        for mask, ref in enumerate(held):

            @pl.when(wanted == mask)
            def _():
                out_ref[...] = ref[pl.ds(0, part), :]


def place_piece(panel_ref, rows, block, origin, count, size):
    for g in range(block.shape[1] // size):
        left = (g * count + origin) * size
        if not isinstance(origin, int):
            left = pl.multiple_of(left, size)
        panel_ref[rows, pl.ds(left, size)] = block[:, g * size:(g + 1) * size]


def factor_from(panel_ref, inverse_ref, out_ref, tile):
    rows, width = out_ref.shape
    for first in range(0, width, tile):
        out_ref[:, pl.ds(first, tile)] = lax.dot_general(
            panel_ref[pl.ds(0, rows), pl.ds(0, first + tile)],
            inverse_ref[pl.ds(first, tile), pl.ds(0, first + tile)],
            CONTRACT,
            preferred_element_type=jnp.float32,
        ).astype(jnp.bfloat16)


def row_factor_kernel(places, origins, kinds, size, tile, inverse_ref, *refs):
    arrays, out_ref, panel_ref = refs[: len(kinds)], refs[-2], refs[-1]
    col_index = lax.axis_index("col")
    count = len(origins)
    rows = out_ref.shape[0]
    for slot in range(count):
        origin = looked_up(col_index, origins[slot])
        for kind, ref in zip(kinds, arrays):
            members = tuple(i for i in range(count) if places[slot][i] == kind)
            if members:

                @pl.when(among(col_index, members))
                def _():
                    for top in range(0, rows, size):
                        at = pl.ds(top, size)
                        place_piece(panel_ref, at, ref[at, :], origin, count, size)

    factor_from(panel_ref, inverse_ref, out_ref, tile)


def column_factor_kernel(size, tile, inverse_ref, *refs):
    parts, out_ref, panel_ref = refs[:-2], refs[-2], refs[-1]
    row_index, col_index = lax.axis_index("row"), lax.axis_index("col")
    count = lax.axis_size("col")
    part = parts[0].shape[0] // count
    for mask, ref in enumerate(parts):
        at = pl.ds(pl.multiple_of((row_index ^ mask) * part, ROW_TILE), part)
        for apart in range(count):
            origin = lax.rem(col_index + count - apart, count)
            place_piece(panel_ref, at, ref[pl.ds(apart * part, part), :], origin, count, size)
    factor_from(panel_ref, inverse_ref, out_ref, tile)


def product_kernel(mine, rows_ref, columns_ref, front_ref, *refs):
    out_hbm, out_ref, sems = refs[-3:]
    sub_index = lax.axis_index("sub")
    half = sub_index if mine else 1 - sub_index
    slot_count, _, size, _ = out_ref.shape
    product = lax.dot_general(
        rows_ref[...], columns_ref[...], CONTRACT, preferred_element_type=jnp.float32
    )
    copies = []
    for m in range(slot_count):
        for a in range(slot_count):
            block = product[m * size:(m + 1) * size, a * size:(a + 1) * size]
            out_ref[m, a] = (front_ref[m, a, half].astype(jnp.float32) - block).astype(jnp.bfloat16)
        copies.append(pltpu.make_async_copy(out_ref.at[m], out_hbm.at[m, :, half], sems.at[m]))
        copies[-1].start()
    for copy in copies:
        copy.wait()


def body(front_entries, block_pattern, child_update, child_map, diag_inverse):
    slot_count = front_entries.shape[0]
    size = front_entries.shape[3]
    column_count = front_entries.shape[4]
    child_count = child_update.shape[1]
    row_size = lax.axis_size("row")
    col_size = lax.axis_size("col")
    groups = -(-(PANEL // size) // col_size)
    tile = PANEL // 2
    rows = slot_count * size
    part = -(-rows // (row_size * ROW_TILE)) * ROW_TILE
    padded = part * row_size
    depth = groups * col_size * size
    in_hbm = pl.BlockSpec(memory_space=pltpu.HBM)
    entries = front_entries.reshape(slot_count, size, column_count, size).transpose(0, 2, 1, 3)
    pattern = block_pattern.reshape(slot_count, 1, column_count)
    slots = child_map.transpose(0, 2, 1)
    own = child_update.reshape(child_count, size, child_count, size).transpose(0, 2, 1, 3)

    received = flipped(own, "sub", 1)
    shares = inverse_shares(diag_inverse)
    lanes = groups * size
    tiles = line_tiles(col_size, diag_inverse.shape[0], lanes) if shares else []
    line_rows = len(tiles) * shares[0].shape[0] if shares else 0
    received, *shares = fence(received, *shares)
    piece, *parts = call(
        functools.partial(panel_kernel, part, groups),
        [bf16(padded, lanes)] + [bf16(part, lanes)] * row_size,
        [SCALARS, SCALARS] + [ON_CHIP] * 3,
    )(slots, pattern, entries[:, :groups], own, received)
    if shares:
        parts[1] = call(
            functools.partial(pack_kernel, part, tiles), bf16(part + line_rows, lanes), [ON_CHIP] * (1 + len(shares))
        )(parts[1], *shares)

    _, origins, places = line_plan(col_size)
    pieces = Line(piece, "col")
    pieces.step()
    held = [parts[0]] + [flipped(parts[mask], "row", mask) for mask in range(1, row_size)]
    sent = parts[1:2] if shares else []
    turned = call(
        functools.partial(turn_kernel, part),
        [bf16(part, lanes)] * col_size + [bf16(2 * line_rows, lanes)] * len(sent),
        [ON_CHIP] * (row_size + len(sent)),
    )(*held, *sent)
    turned = pieces.fenced(*turned)
    near, sends, lines = turned[0], turned[1:col_size], list(turned[col_size:])
    if shares:
        for bit in range(1, row_size.bit_length() - 1):
            lines += [flipped(line, "row", 1 << bit) for line in lines]
    turned = joined(
        [near] + [shifted(block, "col", apart) for apart, block in enumerate(sends, 1)]
    )
    turned, *lines = pieces.fenced(turned, *lines)
    if shares:
        lines += [flipped(line, "sub", 1) for line in lines]
        inverse = call(
            functools.partial(inverse_kernel, shares[0].shape[0], tiles),
            bf16(PANEL, PANEL), [ON_CHIP] * len(lines), moved=4 << 20,
        )(*lines)
    else:
        whole = lax.all_gather(diag_inverse, "col", axis=0, tiled=True)
        inverse = call(lower_kernel, bf16(PANEL, PANEL), [ON_CHIP], moved=4 << 20)(whole)
    parts = [turned] + [flipped(turned, "row", mask) for mask in range(1, row_size)]
    while pieces.at < len(pieces.levels):
        pieces.step()
    front = call(
        functools.partial(front_kernel, groups),
        bf16(slot_count, column_count, size, size),
        [SCALARS, SCALARS] + [ON_CHIP] * 4,
        moved=6 << 20,
    )(slots, pattern, entries, own, received, piece)
    front, inverse, *parts = pieces.fenced(front, inverse, *parts)
    front = front.reshape(slot_count, slot_count, 2, size, size)

    kinds, arrays = pieces.taken()
    scratch = [pltpu.VMEM((padded, depth), jnp.bfloat16)]
    flops = 2 * rows * PANEL * PANEL * 3 // 4
    column_factor = call(
        functools.partial(column_factor_kernel, size, tile),
        bf16(rows, PANEL), [ON_CHIP] * (1 + row_size), flops=flops, scratch_shapes=scratch,
    )(inverse, *parts)
    other_factor = flipped(column_factor, "sub", 1)
    row_factor = call(
        functools.partial(row_factor_kernel, places, origins, kinds, size, tile),
        bf16(rows, PANEL), [ON_CHIP] * (1 + len(arrays)), flops=flops, scratch_shapes=scratch,
    )(inverse, *arrays)
    product = functools.partial(
        call,
        out_shape=bf16(slot_count, slot_count, 2, size, size),
        flops=2 * rows * rows * PANEL,
        out_specs=in_hbm,
        scratch_shapes=[
            pltpu.VMEM((slot_count, slot_count, size, size), jnp.bfloat16),
            pltpu.SemaphoreType.DMA((slot_count,)),
        ],
    )
    trailing = product(functools.partial(product_kernel, True), in_specs=[ON_CHIP] * 3)(
        row_factor, column_factor, front
    )
    trailing = product(
        functools.partial(product_kernel, False), in_specs=[ON_CHIP] * 3 + [in_hbm],
        input_output_aliases={3: 0},
    )(row_factor, other_factor, front, trailing)
    return trailing.reshape(slot_count, column_count, size, size).transpose(0, 2, 1, 3).reshape(
        slot_count, 1, 1, size, column_count, 1, size
    )


def solution(mesh):
    return jax.shard_map(
        body,
        mesh=mesh,
        in_specs=(
            P(None, "sub", "row", None, None, "col", None),
            P(None, "sub", "row", None, "col"),
            P("sub", None, "row", None, None, "col", None),
            P(),
            P("col", None),
        ),
        out_specs=P(None, "sub", "row", None, None, "col", None),
        check_vma=False,
    )
```

```python
import functools

import jax
import jax.numpy as jnp
from jax import lax
from jax.experimental import pallas as pl
from jax.experimental.pallas import tpu as pltpu
from jax.sharding import PartitionSpec as P

PANEL = 1024
ROW_TILE = 16
VMEM_BYTES = 12 * 1024 * 1024
CONTRACT = (((1,), (1,)), ((), ()))
ON_CHIP = pl.BlockSpec(memory_space=pltpu.VMEM)
SCALARS = pl.BlockSpec(memory_space=pltpu.SMEM)


def call(kernel, out_shape, in_specs, flops=0, moved=1 << 19, **more):
    single = not isinstance(out_shape, (list, tuple))
    return pl.pallas_call(
        kernel,
        out_shape=out_shape,
        in_specs=in_specs,
        out_specs=more.pop("out_specs", ON_CHIP if single else [ON_CHIP] * len(out_shape)),
        compiler_params=pltpu.CompilerParams(vmem_limit_bytes=VMEM_BYTES),
        cost_estimate=pl.CostEstimate(flops=flops, bytes_accessed=moved, transcendentals=0),
        **more,
    )


def bf16(*shape):
    return jax.ShapeDtypeStruct(shape, jnp.bfloat16)


def f32(*shape):
    return jax.ShapeDtypeStruct(shape, jnp.float32)


def flipped(block, axis, mask):
    count = lax.axis_size(axis)
    return lax.ppermute(block, axis, [(i, i ^ mask) for i in range(count)])


def shifted(block, axis, apart):
    count = lax.axis_size(axis)
    return lax.ppermute(block, axis, [(i, (i + apart) % count) for i in range(count)])


def swap_even(i, count):
    return i ^ 1 if i ^ 1 < count else i


def swap_odd(i, count):
    j = ((i + 1) ^ 1) - 1
    return j if 0 <= j < count else i


@functools.cache
def line_plan(count):
    even = [swap_even(i, count) for i in range(count)]
    odd = [swap_odd(i, count) for i in range(count)]
    if count == 4:
        levels = [[(1, 0, even), (2, 0, odd)], [(3, 2, [2, 0, 3, 1]), (4, 1, [1, 3, 0, 2])]]
    else:
        levels, last = [], [0, 0]
        for step in range(count - 1):
            level = []
            for stream in (0, 1):
                level.append((1 + 2 * step + stream, last[stream], odd if (step + stream) % 2 else even))
                last[stream] = level[-1][0]
            levels.append(level)
    whose = {0: list(range(count))}
    seen = [[(0, i)] for i in range(count)]
    for level in levels:
        for array, source, to in level:
            whose[array] = [None] * count
            for i in range(count):
                whose[array][to[i]] = whose[source][i]
            for i in range(count):
                if all(whose[array][i] != origin for _, origin in seen[i]):
                    seen[i].append((array, whose[array][i]))
    origins = [[seen[i][j][1] for i in range(count)] for j in range(count)]
    places = [[seen[i][j][0] for i in range(count)] for j in range(count)]
    return levels, origins, places


class Line:
    def __init__(self, block, axis):
        self.axis = axis
        self.levels, _, self.places = line_plan(lax.axis_size(axis))
        self.held = {0: block}
        self.at = 0

    def step(self):
        for array, source, to in self.levels[self.at]:
            self.held[array] = lax.ppermute(self.held[source], self.axis, list(enumerate(to)))
        self.at += 1
        return self.at < len(self.levels)

    def fenced(self, *values):
        last = [array for array, _, _ in self.levels[self.at - 1]]
        out = fence(*values, *(self.held[array] for array in last))
        self.held.update(zip(last, out[len(values):]))
        return out[: len(values)]

    def taken(self):
        kinds = sorted({kind for row in self.places for kind in row})
        return kinds, [self.held[kind] for kind in kinds]


def among(index, members):
    found = index == members[0]
    for member in members[1:]:
        found = jnp.logical_or(found, index == member)
    return found


def looked_up(index, table):
    value = jnp.int32(table[0])
    for i, entry in enumerate(table[1:], 1):
        value = jnp.where(index == i, jnp.int32(entry), value)
    return value


def fence_kernel(*refs):
    pass


def fence(*values):
    place = pl.BlockSpec(memory_space=pl.ANY)
    return pl.pallas_call(
        fence_kernel,
        out_shape=[jax.ShapeDtypeStruct(v.shape, v.dtype) for v in values],
        in_specs=[place] * len(values),
        out_specs=[place] * len(values),
        input_output_aliases={n: n for n in range(len(values))},
        compiler_params=pltpu.CompilerParams(vmem_limit_bytes=1 << 20),
    )(*values)


def found_at(map_ref, child, place, wanted, child_count):
    at = jnp.int32(0)
    found = jnp.float32(0)
    for k in range(child_count):
        same = map_ref[child, place, k] == wanted
        at = jnp.where(same, jnp.int32(k), at)
        found = jnp.where(same, jnp.float32(1), found)
    return at, found


def block_places(map_ref, child, columns, slot_count, child_count):
    sub_index, row_index, col_index = (lax.axis_index(name) for name in ("sub", "row", "col"))
    rows = [
        found_at(map_ref, child, row_index, 2 * a + sub_index, child_count) for a in range(slot_count)
    ]
    cols = [found_at(map_ref, child, col_index, b, child_count) for b in columns]
    return rows, cols


def child_block(ref, row, col):
    return ref[row[0], col[0]].astype(jnp.float32) * (row[1] * col[1])


def line_tiles(count, share, lanes):
    return [(col, tile) for col in range(count) for tile in range(-(-(col + 1) * share // lanes))]


def pack_line(share_refs, out_ref, first, tiles):
    col_index = lax.axis_index("col")
    count = len(share_refs)
    rows, lanes = share_refs[0].shape[0], out_ref.shape[1]
    for apart, ref in enumerate(share_refs):
        for col in range(count):

            @pl.when(lax.rem(col_index + count - apart, count) == col)
            def _():
                for n, (home, tile) in enumerate(tiles):
                    if home == col:
                        out_ref[pl.ds(first + n * rows, rows), :] = ref[:, tile * lanes:(tile + 1) * lanes]


def pack_kernel(part, tiles, *refs):
    part_ref, *share_refs, out_ref = refs
    out_ref[pl.ds(0, part), :] = part_ref[...]
    pack_line(share_refs, out_ref, part, tiles)


def panel_kernel(part, groups, map_ref, pattern_ref, entries_ref, own_ref, received_ref, piece_ref, *part_refs):
    slot_count, _, size, _ = entries_ref.shape
    child_count = own_ref.shape[0]
    sub_index, row_index = lax.axis_index("sub"), lax.axis_index("row")
    places = [
        block_places(map_ref, child, range(groups), slot_count, child_count)
        for child in (sub_index, 1 - sub_index)
    ]
    for a in range(slot_count):
        for b in range(groups):
            total = entries_ref[a, b].astype(jnp.float32) * pattern_ref[a, 0, b].astype(jnp.float32)
            for (rows, cols), ref in zip(places, (own_ref, received_ref)):
                total = total + child_block(ref, rows[a], cols[b])
            piece_ref[pl.ds(a * size, size), pl.ds(b * size, size)] = total.astype(jnp.bfloat16)
    used = slot_count * size
    if used < piece_ref.shape[0]:
        piece_ref[pl.ds(used, piece_ref.shape[0] - used), :] = jnp.zeros(
            (piece_ref.shape[0] - used, piece_ref.shape[1]), piece_ref.dtype
        )
    for mask, ref in enumerate(part_refs):
        ref[...] = piece_ref[pl.ds(pl.multiple_of((row_index ^ mask) * part, ROW_TILE), part), :]


def front_kernel(groups, map_ref, pattern_ref, entries_ref, own_ref, received_ref, piece_ref, out_ref):
    slot_count, column_count, size, _ = entries_ref.shape
    child_count = own_ref.shape[0]
    sub_index = lax.axis_index("sub")
    columns = range(groups, column_count)
    places = [
        block_places(map_ref, child, columns, slot_count, child_count)
        for child in (sub_index, 1 - sub_index)
    ]
    for a in range(slot_count):
        for b in range(groups):
            out_ref[a, b] = piece_ref[pl.ds(a * size, size), pl.ds(b * size, size)]
        for n, b in enumerate(columns):
            total = entries_ref[a, b].astype(jnp.float32) * pattern_ref[a, 0, b].astype(jnp.float32)
            for (rows, cols), ref in zip(places, (own_ref, received_ref)):
                total = total + child_block(ref, rows[a], cols[n])
            out_ref[a, b] = total.astype(jnp.bfloat16)


def inverse_kernel(rows, tiles, *refs):
    *in_refs, out_ref = refs
    sub_index, row_index = lax.axis_index("sub"), lax.axis_index("row")
    sub_size, row_size, col_size = (lax.axis_size(name) for name in ("sub", "row", "col"))
    width = out_ref.shape[0]
    lanes = in_refs[0].shape[1]
    share = width // col_size
    lines = [
        (ref, line * len(tiles) * rows) for ref in in_refs for line in range(2)
    ]
    for n, (ref, first) in enumerate(lines):
        sub_at = sub_index if n < row_size else 1 - sub_index
        inside = (sub_at * row_size + (row_index ^ (n % row_size))) * rows
        for m, (col, tile) in enumerate(tiles):
            top = pl.multiple_of(col * share + inside, ROW_TILE)
            block = ref[pl.ds(first + m * rows, rows), :]
            if (tile + 1) * lanes > col * share:
                row_at = top + lax.broadcasted_iota(jnp.int32, block.shape, 0)
                col_at = tile * lanes + lax.broadcasted_iota(jnp.int32, block.shape, 1)
                block = jnp.where(col_at <= row_at, block.astype(jnp.float32), 0.0).astype(jnp.bfloat16)
            out_ref[pl.ds(top, rows), pl.ds(tile * lanes, lanes)] = block
    for col in range(col_size):
        for tile in range(width // lanes):
            if (col, tile) not in tiles:
                out_ref[pl.ds(col * share, share), pl.ds(tile * lanes, lanes)] = jnp.zeros(
                    (share, lanes), out_ref.dtype
                )


def lower_kernel(in_ref, out_ref):
    row_at = lax.broadcasted_iota(jnp.int32, in_ref.shape, 0)
    col_at = lax.broadcasted_iota(jnp.int32, in_ref.shape, 1)
    out_ref[...] = jnp.where(col_at <= row_at, in_ref[...].astype(jnp.float32), 0.0).astype(jnp.bfloat16)


def join_kernel(*refs):
    *in_refs, out_ref = refs
    rows = in_refs[0].shape[0]
    for n, ref in enumerate(in_refs):
        out_ref[pl.ds(n * rows, rows), :] = ref[...]


def joined(blocks):
    rows, width = blocks[0].shape
    return call(join_kernel, bf16(rows * len(blocks), width), [ON_CHIP] * len(blocks))(*blocks)


def inverse_shares(diag_inverse):
    part = diag_inverse.shape[0] // (lax.axis_size("sub") * lax.axis_size("row"))
    if part % ROW_TILE:
        return []
    first = (lax.axis_index("sub") * lax.axis_size("row") + lax.axis_index("row")) * part
    mine = lax.dynamic_slice_in_dim(diag_inverse, first, part, 0)
    return [mine] + [shifted(mine, "col", apart) for apart in range(1, lax.axis_size("col"))]


def turn_kernel(part, *refs):
    row_size, count = lax.axis_size("row"), lax.axis_size("col")
    held, refs = refs[:row_size], refs[row_size:]
    if len(refs) > count:
        sent_ref, *outs, lines_ref = refs
        rows = sent_ref.shape[0] - part
        lines_ref[pl.ds(0, rows), :] = sent_ref[pl.ds(part, rows), :]
        lines_ref[pl.ds(rows, rows), :] = held[1][pl.ds(part, rows), :]
    else:
        outs = refs
    row_index, col_index = lax.axis_index("row"), lax.axis_index("col")
    for apart, out_ref in enumerate(outs):
        wanted = row_index ^ lax.rem(col_index + apart, count)
        for mask, ref in enumerate(held):

            @pl.when(wanted == mask)
            def _():
                out_ref[...] = ref[pl.ds(0, part), :]


def place_piece(panel_ref, rows, block, origin, count, size):
    for g in range(block.shape[1] // size):
        left = (g * count + origin) * size
        if not isinstance(origin, int):
            left = pl.multiple_of(left, size)
        panel_ref[rows, pl.ds(left, size)] = block[:, g * size:(g + 1) * size]


def factor_from(panel_ref, inverse_ref, out_ref, tile):
    rows, width = out_ref.shape
    for first in range(0, width, tile):
        out_ref[:, pl.ds(first, tile)] = lax.dot_general(
            panel_ref[pl.ds(0, rows), pl.ds(0, first + tile)],
            inverse_ref[pl.ds(first, tile), pl.ds(0, first + tile)],
            CONTRACT,
            preferred_element_type=jnp.float32,
        ).astype(jnp.bfloat16)


def row_factor_kernel(places, origins, kinds, size, tile, inverse_ref, *refs):
    arrays, out_ref, panel_ref = refs[: len(kinds)], refs[-2], refs[-1]
    col_index = lax.axis_index("col")
    count = len(origins)
    rows = out_ref.shape[0]
    for slot in range(count):
        origin = looked_up(col_index, origins[slot])
        for kind, ref in zip(kinds, arrays):
            members = tuple(i for i in range(count) if places[slot][i] == kind)
            if members:

                @pl.when(among(col_index, members))
                def _():
                    for top in range(0, rows, size):
                        at = pl.ds(top, size)
                        place_piece(panel_ref, at, ref[at, :], origin, count, size)

    factor_from(panel_ref, inverse_ref, out_ref, tile)


def column_factor_kernel(size, tile, inverse_ref, *refs):
    parts, out_ref, panel_ref = refs[:-2], refs[-2], refs[-1]
    row_index, col_index = lax.axis_index("row"), lax.axis_index("col")
    count = lax.axis_size("col")
    part = parts[0].shape[0] // count
    for mask, ref in enumerate(parts):
        at = pl.ds(pl.multiple_of((row_index ^ mask) * part, ROW_TILE), part)
        for apart in range(count):
            origin = lax.rem(col_index + count - apart, count)
            place_piece(panel_ref, at, ref[pl.ds(apart * part, part), :], origin, count, size)
    factor_from(panel_ref, inverse_ref, out_ref, tile)


def product_kernel(mine, rows_ref, columns_ref, front_ref, *refs):
    out_hbm, out_ref, sems = refs[-3:]
    sub_index = lax.axis_index("sub")
    half = sub_index if mine else 1 - sub_index
    slot_count, _, size, _ = out_ref.shape
    product = lax.dot_general(
        rows_ref[...], columns_ref[...], CONTRACT, preferred_element_type=jnp.float32
    )
    copies = []
    for m in range(slot_count):
        for a in range(slot_count):
            block = product[m * size:(m + 1) * size, a * size:(a + 1) * size]
            out_ref[m, a] = (front_ref[m, a, half].astype(jnp.float32) - block).astype(jnp.bfloat16)
        copies.append(pltpu.make_async_copy(out_ref.at[m], out_hbm.at[m, :, half], sems.at[m]))
        copies[-1].start()
    for copy in copies:
        copy.wait()


def body(front_entries, block_pattern, child_update, child_map, diag_inverse):
    slot_count = front_entries.shape[0]
    size = front_entries.shape[3]
    column_count = front_entries.shape[4]
    child_count = child_update.shape[1]
    row_size = lax.axis_size("row")
    col_size = lax.axis_size("col")
    groups = -(-(PANEL // size) // col_size)
    tile = PANEL // 2
    rows = slot_count * size
    part = -(-rows // (row_size * ROW_TILE)) * ROW_TILE
    padded = part * row_size
    depth = groups * col_size * size
    in_hbm = pl.BlockSpec(memory_space=pltpu.HBM)
    entries = front_entries.reshape(slot_count, size, column_count, size).transpose(0, 2, 1, 3)
    pattern = block_pattern.reshape(slot_count, 1, column_count)
    slots = child_map.transpose(0, 2, 1)
    own = child_update.reshape(child_count, size, child_count, size).transpose(0, 2, 1, 3)

    received = flipped(own, "sub", 1)
    shares = inverse_shares(diag_inverse)
    lanes = groups * size
    tiles = line_tiles(col_size, diag_inverse.shape[0], lanes) if shares else []
    line_rows = len(tiles) * shares[0].shape[0] if shares else 0
    piece, *parts = call(
        functools.partial(panel_kernel, part, groups),
        [bf16(padded, lanes)] + [bf16(part, lanes)] * row_size,
        [SCALARS, SCALARS] + [ON_CHIP] * 3,
    )(slots, pattern, entries[:, :groups], own, received)
    if shares:
        parts[1] = call(
            functools.partial(pack_kernel, part, tiles), bf16(part + line_rows, lanes), [ON_CHIP] * (1 + len(shares))
        )(parts[1], *shares)
        piece, *parts = fence(piece, *parts)

    _, origins, places = line_plan(col_size)
    pieces = Line(piece, "col")
    pieces.step()
    held = [parts[0]] + [flipped(parts[mask], "row", mask) for mask in range(1, row_size)]
    sent = parts[1:2] if shares else []
    turned = call(
        functools.partial(turn_kernel, part),
        [bf16(part, lanes)] * col_size + [bf16(2 * line_rows, lanes)] * len(sent),
        [ON_CHIP] * (row_size + len(sent)),
    )(*held, *sent)
    turned = pieces.fenced(*turned)
    near, sends, lines = turned[0], turned[1:col_size], list(turned[col_size:])
    if shares:
        for bit in range(1, row_size.bit_length() - 1):
            lines += [flipped(line, "row", 1 << bit) for line in lines]
    sends = [shifted(block, "col", apart) for apart, block in enumerate(sends, 1)]
    near, *lines = pieces.fenced(near, *sends, *lines)
    sends, lines = lines[: len(sends)], lines[len(sends):]
    turned = joined([near, *sends])
    if shares:
        lines += [flipped(line, "sub", 1) for line in lines]
        inverse = call(
            functools.partial(inverse_kernel, shares[0].shape[0], tiles),
            bf16(PANEL, PANEL), [ON_CHIP] * len(lines), moved=4 << 20,
        )(*lines)
    else:
        whole = lax.all_gather(diag_inverse, "col", axis=0, tiled=True)
        inverse = call(lower_kernel, bf16(PANEL, PANEL), [ON_CHIP], moved=4 << 20)(whole)
    parts = [turned] + [flipped(turned, "row", mask) for mask in range(1, row_size)]
    while pieces.at < len(pieces.levels):
        pieces.step()
    front = call(
        functools.partial(front_kernel, groups),
        bf16(slot_count, column_count, size, size),
        [SCALARS, SCALARS] + [ON_CHIP] * 4,
        moved=6 << 20,
    )(slots, pattern, entries, own, received, piece)
    front, inverse, *parts = pieces.fenced(front, inverse, *parts)
    front = front.reshape(slot_count, slot_count, 2, size, size)

    kinds, arrays = pieces.taken()
    scratch = [pltpu.VMEM((padded, depth), jnp.bfloat16)]
    flops = 2 * rows * PANEL * PANEL * 3 // 4
    column_factor = call(
        functools.partial(column_factor_kernel, size, tile),
        bf16(rows, PANEL), [ON_CHIP] * (1 + row_size), flops=flops, scratch_shapes=scratch,
    )(inverse, *parts)
    other_factor = flipped(column_factor, "sub", 1)
    row_factor = call(
        functools.partial(row_factor_kernel, places, origins, kinds, size, tile),
        bf16(rows, PANEL), [ON_CHIP] * (1 + len(arrays)), flops=flops, scratch_shapes=scratch,
    )(inverse, *arrays)
    product = functools.partial(
        call,
        out_shape=bf16(slot_count, slot_count, 2, size, size),
        flops=2 * rows * rows * PANEL,
        out_specs=in_hbm,
        scratch_shapes=[
            pltpu.VMEM((slot_count, slot_count, size, size), jnp.bfloat16),
            pltpu.SemaphoreType.DMA((slot_count,)),
        ],
    )
    trailing = product(functools.partial(product_kernel, True), in_specs=[ON_CHIP] * 3)(
        row_factor, column_factor, front
    )
    trailing = product(
        functools.partial(product_kernel, False), in_specs=[ON_CHIP] * 3 + [in_hbm],
        input_output_aliases={3: 0},
    )(row_factor, other_factor, front, trailing)
    return trailing.reshape(slot_count, column_count, size, size).transpose(0, 2, 1, 3).reshape(
        slot_count, 1, 1, size, column_count, 1, size
    )


def solution(mesh):
    return jax.shard_map(
        body,
        mesh=mesh,
        in_specs=(
            P(None, "sub", "row", None, None, "col", None),
            P(None, "sub", "row", None, "col"),
            P("sub", None, "row", None, None, "col", None),
            P(),
            P("col", None),
        ),
        out_specs=P(None, "sub", "row", None, None, "col", None),
        check_vma=False,
    )
```

```python
import functools

import jax
import jax.numpy as jnp
from jax import lax
from jax.experimental import pallas as pl
from jax.experimental.pallas import tpu as pltpu
from jax.sharding import PartitionSpec as P

PANEL = 1024
ROW_TILE = 16
VMEM_BYTES = 12 * 1024 * 1024
CONTRACT = (((1,), (1,)), ((), ()))
ON_CHIP = pl.BlockSpec(memory_space=pltpu.VMEM)
SCALARS = pl.BlockSpec(memory_space=pltpu.SMEM)


def call(kernel, out_shape, in_specs, flops=0, moved=1 << 19, **more):
    single = not isinstance(out_shape, (list, tuple))
    return pl.pallas_call(
        kernel,
        out_shape=out_shape,
        in_specs=in_specs,
        out_specs=more.pop("out_specs", ON_CHIP if single else [ON_CHIP] * len(out_shape)),
        compiler_params=pltpu.CompilerParams(vmem_limit_bytes=VMEM_BYTES),
        cost_estimate=pl.CostEstimate(flops=flops, bytes_accessed=moved, transcendentals=0),
        **more,
    )


def bf16(*shape):
    return jax.ShapeDtypeStruct(shape, jnp.bfloat16)


def f32(*shape):
    return jax.ShapeDtypeStruct(shape, jnp.float32)


def flipped(block, axis, mask):
    count = lax.axis_size(axis)
    return lax.ppermute(block, axis, [(i, i ^ mask) for i in range(count)])


def shifted(block, axis, apart):
    count = lax.axis_size(axis)
    return lax.ppermute(block, axis, [(i, (i + apart) % count) for i in range(count)])


def swap_even(i, count):
    return i ^ 1 if i ^ 1 < count else i


def swap_odd(i, count):
    j = ((i + 1) ^ 1) - 1
    return j if 0 <= j < count else i


@functools.cache
def line_plan(count):
    even = [swap_even(i, count) for i in range(count)]
    odd = [swap_odd(i, count) for i in range(count)]
    if count == 4:
        levels = [[(1, 0, even), (2, 0, odd)], [(3, 2, [2, 0, 3, 1]), (4, 1, [1, 3, 0, 2])]]
    else:
        levels, last = [], [0, 0]
        for step in range(count - 1):
            level = []
            for stream in (0, 1):
                level.append((1 + 2 * step + stream, last[stream], odd if (step + stream) % 2 else even))
                last[stream] = level[-1][0]
            levels.append(level)
    whose = {0: list(range(count))}
    seen = [[(0, i)] for i in range(count)]
    for level in levels:
        for array, source, to in level:
            whose[array] = [None] * count
            for i in range(count):
                whose[array][to[i]] = whose[source][i]
            for i in range(count):
                if all(whose[array][i] != origin for _, origin in seen[i]):
                    seen[i].append((array, whose[array][i]))
    origins = [[seen[i][j][1] for i in range(count)] for j in range(count)]
    places = [[seen[i][j][0] for i in range(count)] for j in range(count)]
    return levels, origins, places


class Line:
    def __init__(self, block, axis):
        self.axis = axis
        self.levels, _, self.places = line_plan(lax.axis_size(axis))
        self.held = {0: block}
        self.at = 0

    def step(self):
        for array, source, to in self.levels[self.at]:
            self.held[array] = lax.ppermute(self.held[source], self.axis, list(enumerate(to)))
        self.at += 1
        return self.at < len(self.levels)

    def fenced(self, *values):
        last = [array for array, _, _ in self.levels[self.at - 1]]
        out = fence(*values, *(self.held[array] for array in last))
        self.held.update(zip(last, out[len(values):]))
        return out[: len(values)]

    def taken(self):
        kinds = sorted({kind for row in self.places for kind in row})
        return kinds, [self.held[kind] for kind in kinds]


def among(index, members):
    found = index == members[0]
    for member in members[1:]:
        found = jnp.logical_or(found, index == member)
    return found


def looked_up(index, table):
    value = jnp.int32(table[0])
    for i, entry in enumerate(table[1:], 1):
        value = jnp.where(index == i, jnp.int32(entry), value)
    return value


def fence_kernel(*refs):
    pass


def fence(*values):
    place = pl.BlockSpec(memory_space=pl.ANY)
    return pl.pallas_call(
        fence_kernel,
        out_shape=[jax.ShapeDtypeStruct(v.shape, v.dtype) for v in values],
        in_specs=[place] * len(values),
        out_specs=[place] * len(values),
        input_output_aliases={n: n for n in range(len(values))},
        compiler_params=pltpu.CompilerParams(vmem_limit_bytes=1 << 20),
    )(*values)


def found_at(map_ref, child, place, wanted, child_count):
    at = jnp.int32(0)
    found = jnp.float32(0)
    for k in range(child_count):
        same = map_ref[child, place, k] == wanted
        at = jnp.where(same, jnp.int32(k), at)
        found = jnp.where(same, jnp.float32(1), found)
    return at, found


def block_places(map_ref, child, columns, slot_count, child_count):
    sub_index, row_index, col_index = (lax.axis_index(name) for name in ("sub", "row", "col"))
    rows = [
        found_at(map_ref, child, row_index, 2 * a + sub_index, child_count) for a in range(slot_count)
    ]
    cols = [found_at(map_ref, child, col_index, b, child_count) for b in columns]
    return rows, cols


def child_block(ref, row, col):
    return ref[row[0], col[0]].astype(jnp.float32) * (row[1] * col[1])


def line_tiles(count, share, lanes):
    return [(col, tile) for col in range(count) for tile in range(-(-(col + 1) * share // lanes))]


def pack_line(share_refs, out_ref, first, tiles):
    col_index = lax.axis_index("col")
    count = len(share_refs)
    rows, lanes = share_refs[0].shape[0], out_ref.shape[1]
    for apart, ref in enumerate(share_refs):
        for col in range(count):

            @pl.when(lax.rem(col_index + count - apart, count) == col)
            def _():
                for n, (home, tile) in enumerate(tiles):
                    if home == col:
                        out_ref[pl.ds(first + n * rows, rows), :] = ref[:, tile * lanes:(tile + 1) * lanes]


def pack_kernel(part, tiles, *refs):
    part_ref, *share_refs, out_ref = refs
    out_ref[pl.ds(0, part), :] = part_ref[...]
    pack_line(share_refs, out_ref, part, tiles)


def panel_kernel(part, groups, map_ref, pattern_ref, entries_ref, own_ref, received_ref, piece_ref, *part_refs):
    slot_count, _, size, _ = entries_ref.shape
    child_count = own_ref.shape[0]
    sub_index, row_index = lax.axis_index("sub"), lax.axis_index("row")
    places = [
        block_places(map_ref, child, range(groups), slot_count, child_count)
        for child in (sub_index, 1 - sub_index)
    ]
    for a in range(slot_count):
        for b in range(groups):
            total = entries_ref[a, b].astype(jnp.float32) * pattern_ref[a, 0, b].astype(jnp.float32)
            for (rows, cols), ref in zip(places, (own_ref, received_ref)):
                total = total + child_block(ref, rows[a], cols[b])
            piece_ref[pl.ds(a * size, size), pl.ds(b * size, size)] = total.astype(jnp.bfloat16)
    used = slot_count * size
    if used < piece_ref.shape[0]:
        piece_ref[pl.ds(used, piece_ref.shape[0] - used), :] = jnp.zeros(
            (piece_ref.shape[0] - used, piece_ref.shape[1]), piece_ref.dtype
        )
    for mask, ref in enumerate(part_refs):
        ref[...] = piece_ref[pl.ds(pl.multiple_of((row_index ^ mask) * part, ROW_TILE), part), :]


def front_kernel(groups, map_ref, pattern_ref, entries_ref, own_ref, received_ref, piece_ref, out_ref):
    slot_count, column_count, size, _ = entries_ref.shape
    child_count = own_ref.shape[0]
    sub_index = lax.axis_index("sub")
    columns = range(groups, column_count)
    places = [
        block_places(map_ref, child, columns, slot_count, child_count)
        for child in (sub_index, 1 - sub_index)
    ]
    for a in range(slot_count):
        for b in range(groups):
            out_ref[a, b] = piece_ref[pl.ds(a * size, size), pl.ds(b * size, size)]
        for n, b in enumerate(columns):
            total = entries_ref[a, b].astype(jnp.float32) * pattern_ref[a, 0, b].astype(jnp.float32)
            for (rows, cols), ref in zip(places, (own_ref, received_ref)):
                total = total + child_block(ref, rows[a], cols[n])
            out_ref[a, b] = total.astype(jnp.bfloat16)


def inverse_kernel(rows, tiles, *refs):
    *in_refs, out_ref = refs
    sub_index, row_index = lax.axis_index("sub"), lax.axis_index("row")
    sub_size, row_size, col_size = (lax.axis_size(name) for name in ("sub", "row", "col"))
    width = out_ref.shape[0]
    lanes = in_refs[0].shape[1]
    share = width // col_size
    lines = [
        (ref, line * len(tiles) * rows) for ref in in_refs for line in range(2)
    ]
    for n, (ref, first) in enumerate(lines):
        sub_at = sub_index if n < row_size else 1 - sub_index
        inside = (sub_at * row_size + (row_index ^ (n % row_size))) * rows
        for m, (col, tile) in enumerate(tiles):
            top = pl.multiple_of(col * share + inside, ROW_TILE)
            block = ref[pl.ds(first + m * rows, rows), :]
            if (tile + 1) * lanes > col * share:
                row_at = top + lax.broadcasted_iota(jnp.int32, block.shape, 0)
                col_at = tile * lanes + lax.broadcasted_iota(jnp.int32, block.shape, 1)
                block = jnp.where(col_at <= row_at, block.astype(jnp.float32), 0.0).astype(jnp.bfloat16)
            out_ref[pl.ds(top, rows), pl.ds(tile * lanes, lanes)] = block
    for col in range(col_size):
        for tile in range(width // lanes):
            if (col, tile) not in tiles:
                out_ref[pl.ds(col * share, share), pl.ds(tile * lanes, lanes)] = jnp.zeros(
                    (share, lanes), out_ref.dtype
                )


def lower_kernel(in_ref, out_ref):
    row_at = lax.broadcasted_iota(jnp.int32, in_ref.shape, 0)
    col_at = lax.broadcasted_iota(jnp.int32, in_ref.shape, 1)
    out_ref[...] = jnp.where(col_at <= row_at, in_ref[...].astype(jnp.float32), 0.0).astype(jnp.bfloat16)


def join_kernel(*refs):
    *in_refs, out_ref = refs
    rows = in_refs[0].shape[0]
    for n, ref in enumerate(in_refs):
        out_ref[pl.ds(n * rows, rows), :] = ref[...]


def joined(blocks):
    rows, width = blocks[0].shape
    return call(join_kernel, bf16(rows * len(blocks), width), [ON_CHIP] * len(blocks))(*blocks)


def inverse_shares(diag_inverse):
    part = diag_inverse.shape[0] // (lax.axis_size("sub") * lax.axis_size("row"))
    if part % ROW_TILE:
        return []
    first = (lax.axis_index("sub") * lax.axis_size("row") + lax.axis_index("row")) * part
    mine = lax.dynamic_slice_in_dim(diag_inverse, first, part, 0)
    return [mine] + [shifted(mine, "col", apart) for apart in range(1, lax.axis_size("col"))]


def turn_kernel(part, *refs):
    row_size, count = lax.axis_size("row"), lax.axis_size("col")
    held, refs = refs[:row_size], refs[row_size:]
    if len(refs) > count:
        sent_ref, *outs, lines_ref = refs
        rows = sent_ref.shape[0] - part
        lines_ref[pl.ds(0, rows), :] = sent_ref[pl.ds(part, rows), :]
        lines_ref[pl.ds(rows, rows), :] = held[1][pl.ds(part, rows), :]
    else:
        outs = refs
    row_index, col_index = lax.axis_index("row"), lax.axis_index("col")
    for apart, out_ref in enumerate(outs):
        wanted = row_index ^ lax.rem(col_index + apart, count)
        for mask, ref in enumerate(held):

            @pl.when(wanted == mask)
            def _():
                out_ref[...] = ref[pl.ds(0, part), :]


def place_piece(panel_ref, rows, block, origin, count, size):
    for g in range(block.shape[1] // size):
        left = (g * count + origin) * size
        if not isinstance(origin, int):
            left = pl.multiple_of(left, size)
        panel_ref[rows, pl.ds(left, size)] = block[:, g * size:(g + 1) * size]


def factor_from(panel_ref, inverse_ref, out_ref, tile):
    rows, width = out_ref.shape
    for first in range(0, width, tile):
        out_ref[:, pl.ds(first, tile)] = lax.dot_general(
            panel_ref[pl.ds(0, rows), pl.ds(0, first + tile)],
            inverse_ref[pl.ds(first, tile), pl.ds(0, first + tile)],
            CONTRACT,
            preferred_element_type=jnp.float32,
        ).astype(jnp.bfloat16)


def row_factor_kernel(places, origins, kinds, size, tile, inverse_ref, *refs):
    arrays, out_ref, panel_ref = refs[: len(kinds)], refs[-2], refs[-1]
    col_index = lax.axis_index("col")
    count = len(origins)
    rows = out_ref.shape[0]
    for slot in range(count):
        origin = looked_up(col_index, origins[slot])
        for kind, ref in zip(kinds, arrays):
            members = tuple(i for i in range(count) if places[slot][i] == kind)
            if members:

                @pl.when(among(col_index, members))
                def _():
                    for top in range(0, rows, size):
                        at = pl.ds(top, size)
                        place_piece(panel_ref, at, ref[at, :], origin, count, size)

    factor_from(panel_ref, inverse_ref, out_ref, tile)


def column_factor_kernel(size, tile, inverse_ref, *refs):
    parts, out_ref, panel_ref = refs[:-2], refs[-2], refs[-1]
    row_index, col_index = lax.axis_index("row"), lax.axis_index("col")
    count = lax.axis_size("col")
    part = parts[0].shape[0] // count
    for mask, ref in enumerate(parts):
        at = pl.ds(pl.multiple_of((row_index ^ mask) * part, ROW_TILE), part)
        for apart in range(count):
            origin = lax.rem(col_index + count - apart, count)
            place_piece(panel_ref, at, ref[pl.ds(apart * part, part), :], origin, count, size)
    factor_from(panel_ref, inverse_ref, out_ref, tile)


def product_kernel(mine, rows_ref, columns_ref, front_ref, *refs):
    out_hbm, out_ref, sems = refs[-3:]
    sub_index = lax.axis_index("sub")
    half = sub_index if mine else 1 - sub_index
    slot_count, _, size, _ = out_ref.shape
    product = lax.dot_general(
        rows_ref[...], columns_ref[...], CONTRACT, preferred_element_type=jnp.float32
    )
    copies = []
    for m in range(slot_count):
        for a in range(slot_count):
            block = product[m * size:(m + 1) * size, a * size:(a + 1) * size]
            out_ref[m, a] = (front_ref[m, a, half].astype(jnp.float32) - block).astype(jnp.bfloat16)
        copies.append(pltpu.make_async_copy(out_ref.at[m], out_hbm.at[m, :, half], sems.at[m]))
        copies[-1].start()
    for copy in copies:
        copy.wait()


def body(front_entries, block_pattern, child_update, child_map, diag_inverse):
    slot_count = front_entries.shape[0]
    size = front_entries.shape[3]
    column_count = front_entries.shape[4]
    child_count = child_update.shape[1]
    row_size = lax.axis_size("row")
    col_size = lax.axis_size("col")
    groups = -(-(PANEL // size) // col_size)
    tile = PANEL // 2
    rows = slot_count * size
    part = -(-rows // (row_size * ROW_TILE)) * ROW_TILE
    padded = part * row_size
    depth = groups * col_size * size
    in_hbm = pl.BlockSpec(memory_space=pltpu.HBM)
    entries = front_entries.reshape(slot_count, size, column_count, size).transpose(0, 2, 1, 3)
    pattern = block_pattern.reshape(slot_count, 1, column_count)
    slots = child_map.transpose(0, 2, 1)
    own = child_update.reshape(child_count, size, child_count, size).transpose(0, 2, 1, 3)

    received = flipped(own, "sub", 1)
    shares = inverse_shares(diag_inverse)
    lanes = groups * size
    tiles = line_tiles(col_size, diag_inverse.shape[0], lanes) if shares else []
    line_rows = len(tiles) * shares[0].shape[0] if shares else 0
    piece, *parts = call(
        functools.partial(panel_kernel, part, groups),
        [bf16(padded, lanes)] + [bf16(part, lanes)] * row_size,
        [SCALARS, SCALARS] + [ON_CHIP] * 3,
    )(slots, pattern, entries[:, :groups], own, received)
    if shares:
        parts[1] = call(
            functools.partial(pack_kernel, part, tiles), bf16(part + line_rows, lanes), [ON_CHIP] * (1 + len(shares))
        )(parts[1], *shares)
        piece, *parts = fence(piece, *parts)

    _, origins, places = line_plan(col_size)
    pieces = Line(piece, "col")
    pieces.step()
    held = [parts[0]] + [flipped(parts[mask], "row", mask) for mask in range(1, row_size)]
    sent = parts[1:2] if shares else []
    turned = call(
        functools.partial(turn_kernel, part),
        [bf16(part, lanes)] * col_size + [bf16(2 * line_rows, lanes)] * len(sent),
        [ON_CHIP] * (row_size + len(sent)),
    )(*held, *sent)
    turned = pieces.fenced(*turned)
    near, sends, lines = turned[0], turned[1:col_size], list(turned[col_size:])
    if shares:
        for bit in range(1, row_size.bit_length() - 1):
            lines += [flipped(line, "row", 1 << bit) for line in lines]
    sends = [shifted(block, "col", apart) for apart, block in enumerate(sends, 1)]
    (sends[0],) = pieces.fenced(sends[0])
    turned, *lines = fence(joined([near, *sends]), *lines)
    if shares:
        lines += [flipped(line, "sub", 1) for line in lines]
        inverse = call(
            functools.partial(inverse_kernel, shares[0].shape[0], tiles),
            bf16(PANEL, PANEL), [ON_CHIP] * len(lines), moved=4 << 20,
        )(*lines)
    else:
        whole = lax.all_gather(diag_inverse, "col", axis=0, tiled=True)
        inverse = call(lower_kernel, bf16(PANEL, PANEL), [ON_CHIP], moved=4 << 20)(whole)
    parts = [turned] + [flipped(turned, "row", mask) for mask in range(1, row_size)]
    while pieces.at < len(pieces.levels):
        pieces.step()
    front = call(
        functools.partial(front_kernel, groups),
        bf16(slot_count, column_count, size, size),
        [SCALARS, SCALARS] + [ON_CHIP] * 4,
        moved=6 << 20,
    )(slots, pattern, entries, own, received, piece)
    front, inverse, *parts = pieces.fenced(front, inverse, *parts)
    front = front.reshape(slot_count, slot_count, 2, size, size)

    kinds, arrays = pieces.taken()
    scratch = [pltpu.VMEM((padded, depth), jnp.bfloat16)]
    flops = 2 * rows * PANEL * PANEL * 3 // 4
    column_factor = call(
        functools.partial(column_factor_kernel, size, tile),
        bf16(rows, PANEL), [ON_CHIP] * (1 + row_size), flops=flops, scratch_shapes=scratch,
    )(inverse, *parts)
    other_factor = flipped(column_factor, "sub", 1)
    row_factor = call(
        functools.partial(row_factor_kernel, places, origins, kinds, size, tile),
        bf16(rows, PANEL), [ON_CHIP] * (1 + len(arrays)), flops=flops, scratch_shapes=scratch,
    )(inverse, *arrays)
    product = functools.partial(
        call,
        out_shape=bf16(slot_count, slot_count, 2, size, size),
        flops=2 * rows * rows * PANEL,
        out_specs=in_hbm,
        scratch_shapes=[
            pltpu.VMEM((slot_count, slot_count, size, size), jnp.bfloat16),
            pltpu.SemaphoreType.DMA((slot_count,)),
        ],
    )
    trailing = product(functools.partial(product_kernel, True), in_specs=[ON_CHIP] * 3)(
        row_factor, column_factor, front
    )
    trailing = product(
        functools.partial(product_kernel, False), in_specs=[ON_CHIP] * 3 + [in_hbm],
        input_output_aliases={3: 0},
    )(row_factor, other_factor, front, trailing)
    return trailing.reshape(slot_count, column_count, size, size).transpose(0, 2, 1, 3).reshape(
        slot_count, 1, 1, size, column_count, 1, size
    )


def solution(mesh):
    return jax.shard_map(
        body,
        mesh=mesh,
        in_specs=(
            P(None, "sub", "row", None, None, "col", None),
            P(None, "sub", "row", None, "col"),
            P("sub", None, "row", None, None, "col", None),
            P(),
            P("col", None),
        ),
        out_specs=P(None, "sub", "row", None, None, "col", None),
        check_vma=False,
    )
```

```python
import functools

import jax
import jax.numpy as jnp
from jax import lax
from jax.experimental import pallas as pl
from jax.experimental.pallas import tpu as pltpu
from jax.sharding import PartitionSpec as P

PANEL = 1024
ROW_TILE = 16
VMEM_BYTES = 12 * 1024 * 1024
CONTRACT = (((1,), (1,)), ((), ()))
ON_CHIP = pl.BlockSpec(memory_space=pltpu.VMEM)
SCALARS = pl.BlockSpec(memory_space=pltpu.SMEM)


def call(kernel, out_shape, in_specs, flops=0, moved=1 << 19, **more):
    single = not isinstance(out_shape, (list, tuple))
    return pl.pallas_call(
        kernel,
        out_shape=out_shape,
        in_specs=in_specs,
        out_specs=more.pop("out_specs", ON_CHIP if single else [ON_CHIP] * len(out_shape)),
        compiler_params=pltpu.CompilerParams(vmem_limit_bytes=VMEM_BYTES),
        cost_estimate=pl.CostEstimate(flops=flops, bytes_accessed=moved, transcendentals=0),
        **more,
    )


def bf16(*shape):
    return jax.ShapeDtypeStruct(shape, jnp.bfloat16)


def f32(*shape):
    return jax.ShapeDtypeStruct(shape, jnp.float32)


def flipped(block, axis, mask):
    count = lax.axis_size(axis)
    return lax.ppermute(block, axis, [(i, i ^ mask) for i in range(count)])


def shifted(block, axis, apart):
    count = lax.axis_size(axis)
    return lax.ppermute(block, axis, [(i, (i + apart) % count) for i in range(count)])


def swap_even(i, count):
    return i ^ 1 if i ^ 1 < count else i


def swap_odd(i, count):
    j = ((i + 1) ^ 1) - 1
    return j if 0 <= j < count else i


@functools.cache
def line_plan(count):
    even = [swap_even(i, count) for i in range(count)]
    odd = [swap_odd(i, count) for i in range(count)]
    if count == 4:
        levels = [[(1, 0, even), (2, 0, odd)], [(3, 2, [2, 0, 3, 1]), (4, 1, [1, 3, 0, 2])]]
    else:
        levels, last = [], [0, 0]
        for step in range(count - 1):
            level = []
            for stream in (0, 1):
                level.append((1 + 2 * step + stream, last[stream], odd if (step + stream) % 2 else even))
                last[stream] = level[-1][0]
            levels.append(level)
    whose = {0: list(range(count))}
    seen = [[(0, i)] for i in range(count)]
    for level in levels:
        for array, source, to in level:
            whose[array] = [None] * count
            for i in range(count):
                whose[array][to[i]] = whose[source][i]
            for i in range(count):
                if all(whose[array][i] != origin for _, origin in seen[i]):
                    seen[i].append((array, whose[array][i]))
    origins = [[seen[i][j][1] for i in range(count)] for j in range(count)]
    places = [[seen[i][j][0] for i in range(count)] for j in range(count)]
    return levels, origins, places


class Line:
    def __init__(self, block, axis):
        self.axis = axis
        self.levels, _, self.places = line_plan(lax.axis_size(axis))
        self.held = {0: block}
        self.at = 0

    def step(self):
        for array, source, to in self.levels[self.at]:
            self.held[array] = lax.ppermute(self.held[source], self.axis, list(enumerate(to)))
        self.at += 1
        return self.at < len(self.levels)

    def fenced(self, *values):
        last = [array for array, _, _ in self.levels[self.at - 1]]
        out = fence(*values, *(self.held[array] for array in last))
        self.held.update(zip(last, out[len(values):]))
        return out[: len(values)]

    def taken(self):
        kinds = sorted({kind for row in self.places for kind in row})
        return kinds, [self.held[kind] for kind in kinds]


def among(index, members):
    found = index == members[0]
    for member in members[1:]:
        found = jnp.logical_or(found, index == member)
    return found


def looked_up(index, table):
    value = jnp.int32(table[0])
    for i, entry in enumerate(table[1:], 1):
        value = jnp.where(index == i, jnp.int32(entry), value)
    return value


def fence_kernel(*refs):
    pass


def fence(*values):
    place = pl.BlockSpec(memory_space=pl.ANY)
    return pl.pallas_call(
        fence_kernel,
        out_shape=[jax.ShapeDtypeStruct(v.shape, v.dtype) for v in values],
        in_specs=[place] * len(values),
        out_specs=[place] * len(values),
        input_output_aliases={n: n for n in range(len(values))},
        compiler_params=pltpu.CompilerParams(vmem_limit_bytes=1 << 20),
    )(*values)


def found_at(map_ref, child, place, wanted, child_count):
    at = jnp.int32(0)
    found = jnp.float32(0)
    for k in range(child_count):
        same = map_ref[child, place, k] == wanted
        at = jnp.where(same, jnp.int32(k), at)
        found = jnp.where(same, jnp.float32(1), found)
    return at, found


def block_places(map_ref, child, columns, slot_count, child_count):
    sub_index, row_index, col_index = (lax.axis_index(name) for name in ("sub", "row", "col"))
    rows = [
        found_at(map_ref, child, row_index, 2 * a + sub_index, child_count) for a in range(slot_count)
    ]
    cols = [found_at(map_ref, child, col_index, b, child_count) for b in columns]
    return rows, cols


def child_block(ref, row, col):
    return ref[row[0], col[0]].astype(jnp.float32) * (row[1] * col[1])


def line_tiles(count, share, lanes):
    return [(col, tile) for col in range(count) for tile in range(-(-(col + 1) * share // lanes))]


def pack_line(share_refs, out_ref, first, tiles):
    col_index = lax.axis_index("col")
    count = len(share_refs)
    rows, lanes = share_refs[0].shape[0], out_ref.shape[1]
    for apart, ref in enumerate(share_refs):
        for col in range(count):

            @pl.when(lax.rem(col_index + count - apart, count) == col)
            def _():
                for n, (home, tile) in enumerate(tiles):
                    if home == col:
                        out_ref[pl.ds(first + n * rows, rows), :] = ref[:, tile * lanes:(tile + 1) * lanes]


def pack_kernel(part, tiles, *refs):
    part_ref, *share_refs, out_ref = refs
    out_ref[pl.ds(0, part), :] = part_ref[...]
    pack_line(share_refs, out_ref, part, tiles)


def panel_kernel(part, groups, map_ref, pattern_ref, entries_ref, own_ref, received_ref, piece_ref, *part_refs):
    slot_count, _, size, _ = entries_ref.shape
    child_count = own_ref.shape[0]
    sub_index, row_index = lax.axis_index("sub"), lax.axis_index("row")
    places = [
        block_places(map_ref, child, range(groups), slot_count, child_count)
        for child in (sub_index, 1 - sub_index)
    ]
    for a in range(slot_count):
        for b in range(groups):
            total = entries_ref[a, b].astype(jnp.float32) * pattern_ref[a, 0, b].astype(jnp.float32)
            for (rows, cols), ref in zip(places, (own_ref, received_ref)):
                total = total + child_block(ref, rows[a], cols[b])
            piece_ref[pl.ds(a * size, size), pl.ds(b * size, size)] = total.astype(jnp.bfloat16)
    used = slot_count * size
    if used < piece_ref.shape[0]:
        piece_ref[pl.ds(used, piece_ref.shape[0] - used), :] = jnp.zeros(
            (piece_ref.shape[0] - used, piece_ref.shape[1]), piece_ref.dtype
        )
    for mask, ref in enumerate(part_refs):
        ref[...] = piece_ref[pl.ds(pl.multiple_of((row_index ^ mask) * part, ROW_TILE), part), :]


def front_kernel(groups, map_ref, pattern_ref, entries_ref, own_ref, received_ref, piece_ref, out_ref):
    slot_count, column_count, size, _ = entries_ref.shape
    child_count = own_ref.shape[0]
    sub_index = lax.axis_index("sub")
    columns = range(groups, column_count)
    places = [
        block_places(map_ref, child, columns, slot_count, child_count)
        for child in (sub_index, 1 - sub_index)
    ]
    for a in range(slot_count):
        for b in range(groups):
            out_ref[a, b] = piece_ref[pl.ds(a * size, size), pl.ds(b * size, size)]
        for n, b in enumerate(columns):
            total = entries_ref[a, b].astype(jnp.float32) * pattern_ref[a, 0, b].astype(jnp.float32)
            for (rows, cols), ref in zip(places, (own_ref, received_ref)):
                total = total + child_block(ref, rows[a], cols[n])
            out_ref[a, b] = total.astype(jnp.bfloat16)


def inverse_kernel(rows, tiles, *refs):
    *in_refs, turned_ref, out_ref = refs
    sub_index, row_index = lax.axis_index("sub"), lax.axis_index("row")
    sub_size, row_size, col_size = (lax.axis_size(name) for name in ("sub", "row", "col"))
    width = out_ref.shape[0]
    lanes = in_refs[0].shape[1]
    share = width // col_size
    lines = [
        (ref, line * len(tiles) * rows) for ref in in_refs for line in range(2)
    ]
    for n, (ref, first) in enumerate(lines):
        sub_at = sub_index if n < row_size else 1 - sub_index
        inside = (sub_at * row_size + (row_index ^ (n % row_size))) * rows
        for m, (col, tile) in enumerate(tiles):
            top = pl.multiple_of(col * share + inside, ROW_TILE)
            block = ref[pl.ds(first + m * rows, rows), :]
            if (tile + 1) * lanes > col * share:
                row_at = top + lax.broadcasted_iota(jnp.int32, block.shape, 0)
                col_at = tile * lanes + lax.broadcasted_iota(jnp.int32, block.shape, 1)
                block = jnp.where(col_at <= row_at, block.astype(jnp.float32), 0.0).astype(jnp.bfloat16)
            out_ref[pl.ds(top, rows), pl.ds(tile * lanes, lanes)] = block
    for col in range(col_size):
        for tile in range(width // lanes):
            if (col, tile) not in tiles:
                out_ref[pl.ds(col * share, share), pl.ds(tile * lanes, lanes)] = jnp.zeros(
                    (share, lanes), out_ref.dtype
                )
    turn_over(out_ref, turned_ref)


def turn_over(in_ref, out_ref, tile=256):
    for top in range(0, in_ref.shape[0], tile):
        for left in range(0, in_ref.shape[1], tile):
            out_ref[pl.ds(left, tile), pl.ds(top, tile)] = in_ref[pl.ds(top, tile), pl.ds(left, tile)].T


def lower_kernel(in_ref, turned_ref, out_ref):
    row_at = lax.broadcasted_iota(jnp.int32, in_ref.shape, 0)
    col_at = lax.broadcasted_iota(jnp.int32, in_ref.shape, 1)
    out_ref[...] = jnp.where(col_at <= row_at, in_ref[...].astype(jnp.float32), 0.0).astype(jnp.bfloat16)
    turn_over(out_ref, turned_ref)


def join_kernel(*refs):
    *in_refs, out_ref = refs
    rows = in_refs[0].shape[0]
    for n, ref in enumerate(in_refs):
        out_ref[pl.ds(n * rows, rows), :] = ref[...]


def joined(blocks):
    rows, width = blocks[0].shape
    return call(join_kernel, bf16(rows * len(blocks), width), [ON_CHIP] * len(blocks))(*blocks)


def inverse_shares(diag_inverse):
    part = diag_inverse.shape[0] // (lax.axis_size("sub") * lax.axis_size("row"))
    if part % ROW_TILE:
        return []
    first = (lax.axis_index("sub") * lax.axis_size("row") + lax.axis_index("row")) * part
    mine = lax.dynamic_slice_in_dim(diag_inverse, first, part, 0)
    return [mine] + [shifted(mine, "col", apart) for apart in range(1, lax.axis_size("col"))]


def turn_kernel(part, *refs):
    row_size, count = lax.axis_size("row"), lax.axis_size("col")
    held, refs = refs[:row_size], refs[row_size:]
    if len(refs) > count:
        sent_ref, *outs, lines_ref = refs
        rows = sent_ref.shape[0] - part
        lines_ref[pl.ds(0, rows), :] = sent_ref[pl.ds(part, rows), :]
        lines_ref[pl.ds(rows, rows), :] = held[1][pl.ds(part, rows), :]
    else:
        outs = refs
    row_index, col_index = lax.axis_index("row"), lax.axis_index("col")
    for apart, out_ref in enumerate(outs):
        wanted = row_index ^ lax.rem(col_index + apart, count)
        for mask, ref in enumerate(held):

            @pl.when(wanted == mask)
            def _():
                out_ref[...] = ref[pl.ds(0, part), :]


def place_piece(panel_ref, rows, block, origin, count, size):
    for g in range(block.shape[1] // size):
        left = (g * count + origin) * size
        if not isinstance(origin, int):
            left = pl.multiple_of(left, size)
        panel_ref[rows, pl.ds(left, size)] = block[:, g * size:(g + 1) * size]


def factor_from(panel_ref, inverse_ref, out_ref, tile):
    rows, width = out_ref.shape
    for first in range(0, width, tile):
        out_ref[:, pl.ds(first, tile)] = lax.dot_general(
            panel_ref[pl.ds(0, rows), pl.ds(0, first + tile)],
            inverse_ref[pl.ds(0, first + tile), pl.ds(first, tile)],
            (((1,), (0,)), ((), ())),
            preferred_element_type=jnp.float32,
        ).astype(jnp.bfloat16)


def row_factor_kernel(places, origins, kinds, size, tile, inverse_ref, *refs):
    arrays, out_ref, panel_ref = refs[: len(kinds)], refs[-2], refs[-1]
    col_index = lax.axis_index("col")
    count = len(origins)
    rows = out_ref.shape[0]
    for slot in range(count):
        origin = looked_up(col_index, origins[slot])
        for kind, ref in zip(kinds, arrays):
            members = tuple(i for i in range(count) if places[slot][i] == kind)
            if members:

                @pl.when(among(col_index, members))
                def _():
                    for top in range(0, rows, size):
                        at = pl.ds(top, size)
                        place_piece(panel_ref, at, ref[at, :], origin, count, size)

    factor_from(panel_ref, inverse_ref, out_ref, tile)


def column_factor_kernel(size, tile, inverse_ref, *refs):
    parts, out_ref, panel_ref = refs[:-2], refs[-2], refs[-1]
    row_index, col_index = lax.axis_index("row"), lax.axis_index("col")
    count = lax.axis_size("col")
    part = parts[0].shape[0] // count
    for mask, ref in enumerate(parts):
        at = pl.ds(pl.multiple_of((row_index ^ mask) * part, ROW_TILE), part)
        for apart in range(count):
            origin = lax.rem(col_index + count - apart, count)
            place_piece(panel_ref, at, ref[pl.ds(apart * part, part), :], origin, count, size)
    factor_from(panel_ref, inverse_ref, out_ref, tile)


def product_kernel(mine, step, rows_ref, columns_ref, front_ref, *refs):
    out_hbm, out_ref, sems = refs[-3:]
    sub_index = lax.axis_index("sub")
    half = sub_index if mine else 1 - sub_index
    slot_count, _, size, _ = out_ref.shape
    copies = []
    for first in range(0, slot_count, step):
        blocks = min(step, slot_count - first)
        product = lax.dot_general(
            rows_ref[pl.ds(first * size, blocks * size), :], columns_ref[...], CONTRACT,
            preferred_element_type=jnp.float32,
        )
        for m in range(first, first + blocks):
            for a in range(slot_count):
                block = product[(m - first) * size:(m - first + 1) * size, a * size:(a + 1) * size]
                out_ref[m, a] = (front_ref[m, a, half].astype(jnp.float32) - block).astype(jnp.bfloat16)
            copies.append(pltpu.make_async_copy(out_ref.at[m], out_hbm.at[m, :, half], sems.at[m]))
            copies[-1].start()
    for copy in copies:
        copy.wait()


def body(front_entries, block_pattern, child_update, child_map, diag_inverse):
    slot_count = front_entries.shape[0]
    size = front_entries.shape[3]
    column_count = front_entries.shape[4]
    child_count = child_update.shape[1]
    row_size = lax.axis_size("row")
    col_size = lax.axis_size("col")
    groups = -(-(PANEL // size) // col_size)
    tile = PANEL // 2
    rows = slot_count * size
    part = -(-rows // (row_size * ROW_TILE)) * ROW_TILE
    padded = part * row_size
    depth = groups * col_size * size
    in_hbm = pl.BlockSpec(memory_space=pltpu.HBM)
    entries = front_entries.reshape(slot_count, size, column_count, size).transpose(0, 2, 1, 3)
    pattern = block_pattern.reshape(slot_count, 1, column_count)
    slots = child_map.transpose(0, 2, 1)
    own = child_update.reshape(child_count, size, child_count, size).transpose(0, 2, 1, 3)

    received = flipped(own, "sub", 1)
    shares = inverse_shares(diag_inverse)
    lanes = groups * size
    tiles = line_tiles(col_size, diag_inverse.shape[0], lanes) if shares else []
    line_rows = len(tiles) * shares[0].shape[0] if shares else 0
    piece, *parts = call(
        functools.partial(panel_kernel, part, groups),
        [bf16(padded, lanes)] + [bf16(part, lanes)] * row_size,
        [SCALARS, SCALARS] + [ON_CHIP] * 3,
    )(slots, pattern, entries[:, :groups], own, received)
    if shares:
        parts[1] = call(
            functools.partial(pack_kernel, part, tiles), bf16(part + line_rows, lanes), [ON_CHIP] * (1 + len(shares))
        )(parts[1], *shares)
        piece, *parts = fence(piece, *parts)

    _, origins, places = line_plan(col_size)
    pieces = Line(piece, "col")
    pieces.step()
    held = [parts[0]] + [flipped(parts[mask], "row", mask) for mask in range(1, row_size)]
    sent = parts[1:2] if shares else []
    turned = call(
        functools.partial(turn_kernel, part),
        [bf16(part, lanes)] * col_size + [bf16(2 * line_rows, lanes)] * len(sent),
        [ON_CHIP] * (row_size + len(sent)),
    )(*held, *sent)
    turned = pieces.fenced(*turned)
    near, sends, lines = turned[0], turned[1:col_size], list(turned[col_size:])
    if shares:
        for bit in range(1, row_size.bit_length() - 1):
            lines += [flipped(line, "row", 1 << bit) for line in lines]
    sends = [shifted(block, "col", apart) for apart, block in enumerate(sends, 1)]
    (sends[0],) = pieces.fenced(sends[0])
    turned, *lines = fence(joined([near, *sends]), *lines)
    if shares:
        lines += [flipped(line, "sub", 1) for line in lines]
        inverse = call(
            functools.partial(inverse_kernel, shares[0].shape[0], tiles),
            bf16(PANEL, PANEL), [ON_CHIP] * len(lines), moved=4 << 20,
            scratch_shapes=[pltpu.VMEM((PANEL, PANEL), jnp.bfloat16)],
        )(*lines)
    else:
        whole = lax.all_gather(diag_inverse, "col", axis=0, tiled=True)
        inverse = call(
            lower_kernel, bf16(PANEL, PANEL), [ON_CHIP], moved=4 << 20,
            scratch_shapes=[pltpu.VMEM((PANEL, PANEL), jnp.bfloat16)],
        )(whole)
    parts = [turned] + [flipped(turned, "row", mask) for mask in range(1, row_size)]
    while pieces.at < len(pieces.levels):
        pieces.step()
    front = call(
        functools.partial(front_kernel, groups),
        bf16(slot_count, column_count, size, size),
        [SCALARS, SCALARS] + [ON_CHIP] * 4,
        moved=6 << 20,
    )(slots, pattern, entries, own, received, piece)
    front, inverse, *parts = pieces.fenced(front, inverse, *parts)
    front = front.reshape(slot_count, slot_count, 2, size, size)

    kinds, arrays = pieces.taken()
    scratch = [pltpu.VMEM((padded, depth), jnp.bfloat16)]
    flops = 2 * rows * PANEL * PANEL * 3 // 4
    column_factor = call(
        functools.partial(column_factor_kernel, size, tile),
        bf16(rows, PANEL), [ON_CHIP] * (1 + row_size), flops=flops, scratch_shapes=scratch,
    )(inverse, *parts)
    other_factor = flipped(column_factor, "sub", 1)
    row_factor = call(
        functools.partial(row_factor_kernel, places, origins, kinds, size, tile),
        bf16(rows, PANEL), [ON_CHIP] * (1 + len(arrays)), flops=flops, scratch_shapes=scratch,
    )(inverse, *arrays)
    product = functools.partial(
        call,
        out_shape=bf16(slot_count, slot_count, 2, size, size),
        flops=2 * rows * rows * PANEL,
        out_specs=in_hbm,
        scratch_shapes=[
            pltpu.VMEM((slot_count, slot_count, size, size), jnp.bfloat16),
            pltpu.SemaphoreType.DMA((slot_count,)),
        ],
    )
    trailing = product(functools.partial(product_kernel, True, (slot_count + 1) // 2), in_specs=[ON_CHIP] * 3)(
        row_factor, column_factor, front
    )
    trailing = product(
        functools.partial(product_kernel, False, slot_count), in_specs=[ON_CHIP] * 3 + [in_hbm],
        input_output_aliases={3: 0},
    )(row_factor, other_factor, front, trailing)
    return trailing.reshape(slot_count, column_count, size, size).transpose(0, 2, 1, 3).reshape(
        slot_count, 1, 1, size, column_count, 1, size
    )


def solution(mesh):
    return jax.shard_map(
        body,
        mesh=mesh,
        in_specs=(
            P(None, "sub", "row", None, None, "col", None),
            P(None, "sub", "row", None, "col"),
            P("sub", None, "row", None, None, "col", None),
            P(),
            P("col", None),
        ),
        out_specs=P(None, "sub", "row", None, None, "col", None),
        check_vma=False,
    )
```

```python
import functools

import jax
import jax.numpy as jnp
from jax import lax
from jax.experimental import pallas as pl
from jax.experimental.pallas import tpu as pltpu
from jax.sharding import PartitionSpec as P

PANEL = 1024
ROW_TILE = 16
VMEM_BYTES = 12 * 1024 * 1024
CONTRACT = (((1,), (1,)), ((), ()))
ON_CHIP = pl.BlockSpec(memory_space=pltpu.VMEM)
SCALARS = pl.BlockSpec(memory_space=pltpu.SMEM)


def call(kernel, out_shape, in_specs, flops=0, moved=1 << 19, **more):
    single = not isinstance(out_shape, (list, tuple))
    return pl.pallas_call(
        kernel,
        out_shape=out_shape,
        in_specs=in_specs,
        out_specs=more.pop("out_specs", ON_CHIP if single else [ON_CHIP] * len(out_shape)),
        compiler_params=pltpu.CompilerParams(vmem_limit_bytes=VMEM_BYTES),
        cost_estimate=pl.CostEstimate(flops=flops, bytes_accessed=moved, transcendentals=0),
        **more,
    )


def bf16(*shape):
    return jax.ShapeDtypeStruct(shape, jnp.bfloat16)


def f32(*shape):
    return jax.ShapeDtypeStruct(shape, jnp.float32)


def flipped(block, axis, mask):
    count = lax.axis_size(axis)
    return lax.ppermute(block, axis, [(i, i ^ mask) for i in range(count)])


def shifted(block, axis, apart):
    count = lax.axis_size(axis)
    return lax.ppermute(block, axis, [(i, (i + apart) % count) for i in range(count)])


def crossed(block, apart):
    row_size, col_size = lax.axis_size("row"), lax.axis_size("col")
    route = [
        (row * col_size + col, (col ^ apart) * col_size + row)
        for row in range(row_size)
        for col in range(col_size)
    ]
    return lax.ppermute(block, ("row", "col"), route)


def swap_even(i, count):
    return i ^ 1 if i ^ 1 < count else i


def swap_odd(i, count):
    j = ((i + 1) ^ 1) - 1
    return j if 0 <= j < count else i


@functools.cache
def line_plan(count):
    even = [swap_even(i, count) for i in range(count)]
    odd = [swap_odd(i, count) for i in range(count)]
    if count == 4:
        levels = [[(1, 0, even), (2, 0, odd)], [(3, 2, [2, 0, 3, 1]), (4, 1, [1, 3, 0, 2])]]
    else:
        levels, last = [], [0, 0]
        for step in range(count - 1):
            level = []
            for stream in (0, 1):
                level.append((1 + 2 * step + stream, last[stream], odd if (step + stream) % 2 else even))
                last[stream] = level[-1][0]
            levels.append(level)
    whose = {0: list(range(count))}
    seen = [[(0, i)] for i in range(count)]
    for level in levels:
        for array, source, to in level:
            whose[array] = [None] * count
            for i in range(count):
                whose[array][to[i]] = whose[source][i]
            for i in range(count):
                if all(whose[array][i] != origin for _, origin in seen[i]):
                    seen[i].append((array, whose[array][i]))
    origins = [[seen[i][j][1] for i in range(count)] for j in range(count)]
    places = [[seen[i][j][0] for i in range(count)] for j in range(count)]
    return levels, origins, places


class Line:
    def __init__(self, block, axis):
        self.axis = axis
        self.levels, _, self.places = line_plan(lax.axis_size(axis))
        self.held = {0: block}
        self.at = 0

    def step(self):
        for array, source, to in self.levels[self.at]:
            self.held[array] = lax.ppermute(self.held[source], self.axis, list(enumerate(to)))
        self.at += 1
        return self.at < len(self.levels)

    def fenced(self, *values):
        last = [array for array, _, _ in self.levels[self.at - 1]]
        out = fence(*values, *(self.held[array] for array in last))
        self.held.update(zip(last, out[len(values):]))
        return out[: len(values)]

    def taken(self):
        kinds = sorted({kind for row in self.places for kind in row})
        return kinds, [self.held[kind] for kind in kinds]


def among(index, members):
    found = index == members[0]
    for member in members[1:]:
        found = jnp.logical_or(found, index == member)
    return found


def looked_up(index, table):
    value = jnp.int32(table[0])
    for i, entry in enumerate(table[1:], 1):
        value = jnp.where(index == i, jnp.int32(entry), value)
    return value


def fence_kernel(*refs):
    pass


def fence(*values):
    place = pl.BlockSpec(memory_space=pl.ANY)
    return pl.pallas_call(
        fence_kernel,
        out_shape=[jax.ShapeDtypeStruct(v.shape, v.dtype) for v in values],
        in_specs=[place] * len(values),
        out_specs=[place] * len(values),
        input_output_aliases={n: n for n in range(len(values))},
        compiler_params=pltpu.CompilerParams(vmem_limit_bytes=1 << 20),
    )(*values)


def found_at(map_ref, child, place, wanted, child_count):
    at = jnp.int32(0)
    found = jnp.float32(0)
    for k in range(child_count):
        same = map_ref[child, place, k] == wanted
        at = jnp.where(same, jnp.int32(k), at)
        found = jnp.where(same, jnp.float32(1), found)
    return at, found


def block_places(map_ref, child, columns, slot_count, child_count):
    sub_index, row_index, col_index = (lax.axis_index(name) for name in ("sub", "row", "col"))
    rows = [
        found_at(map_ref, child, row_index, 2 * a + sub_index, child_count) for a in range(slot_count)
    ]
    cols = [found_at(map_ref, child, col_index, b, child_count) for b in columns]
    return rows, cols


def child_block(ref, row, col):
    return ref[row[0], col[0]].astype(jnp.float32) * (row[1] * col[1])


def line_tiles(count, share, lanes):
    return [(col, tile) for col in range(count) for tile in range(-(-(col + 1) * share // lanes))]


def pack_line(share_refs, out_ref, first, tiles):
    col_index = lax.axis_index("col")
    count = len(share_refs)
    rows, lanes = share_refs[0].shape[0], out_ref.shape[1]
    for apart, ref in enumerate(share_refs):
        for col in range(count):

            @pl.when(lax.rem(col_index + count - apart, count) == col)
            def _():
                for n, (home, tile) in enumerate(tiles):
                    if home == col:
                        out_ref[pl.ds(first + n * rows, rows), :] = ref[:, tile * lanes:(tile + 1) * lanes]


def pack_kernel(tiles, *refs):
    *share_refs, out_ref = refs
    pack_line(share_refs, out_ref, 0, tiles)


def panel_kernel(part, groups, map_ref, pattern_ref, entries_ref, own_ref, received_ref, piece_ref, *part_refs):
    slot_count, _, size, _ = entries_ref.shape
    child_count = own_ref.shape[0]
    sub_index, row_index = lax.axis_index("sub"), lax.axis_index("row")
    places = [
        block_places(map_ref, child, range(groups), slot_count, child_count)
        for child in (sub_index, 1 - sub_index)
    ]
    for a in range(slot_count):
        for b in range(groups):
            total = entries_ref[a, b].astype(jnp.float32) * pattern_ref[a, 0, b].astype(jnp.float32)
            for (rows, cols), ref in zip(places, (own_ref, received_ref)):
                total = total + child_block(ref, rows[a], cols[b])
            piece_ref[pl.ds(a * size, size), pl.ds(b * size, size)] = total.astype(jnp.bfloat16)
    used = slot_count * size
    if used < piece_ref.shape[0]:
        piece_ref[pl.ds(used, piece_ref.shape[0] - used), :] = jnp.zeros(
            (piece_ref.shape[0] - used, piece_ref.shape[1]), piece_ref.dtype
        )
    col_index = lax.axis_index("col")
    for apart, ref in enumerate(part_refs):
        ref[...] = piece_ref[pl.ds(pl.multiple_of((col_index ^ apart) * part, ROW_TILE), part), :]


def front_kernel(groups, map_ref, pattern_ref, entries_ref, own_ref, received_ref, piece_ref, out_ref):
    slot_count, column_count, size, _ = entries_ref.shape
    child_count = own_ref.shape[0]
    sub_index = lax.axis_index("sub")
    columns = range(groups, column_count)
    places = [
        block_places(map_ref, child, columns, slot_count, child_count)
        for child in (sub_index, 1 - sub_index)
    ]
    for a in range(slot_count):
        for b in range(groups):
            out_ref[a, b] = piece_ref[pl.ds(a * size, size), pl.ds(b * size, size)]
        for n, b in enumerate(columns):
            total = entries_ref[a, b].astype(jnp.float32) * pattern_ref[a, 0, b].astype(jnp.float32)
            for (rows, cols), ref in zip(places, (own_ref, received_ref)):
                total = total + child_block(ref, rows[a], cols[n])
            out_ref[a, b] = total.astype(jnp.bfloat16)


def inverse_kernel(rows, tiles, *refs):
    *in_refs, turned_ref, out_ref = refs
    sub_index, row_index = lax.axis_index("sub"), lax.axis_index("row")
    sub_size, row_size, col_size = (lax.axis_size(name) for name in ("sub", "row", "col"))
    width = out_ref.shape[0]
    lanes = in_refs[0].shape[1]
    share = width // col_size
    for n, ref in enumerate(in_refs):
        sub_at = sub_index if n < row_size else 1 - sub_index
        inside = (sub_at * row_size + (row_index ^ (n % row_size))) * rows
        for m, (col, tile) in enumerate(tiles):
            top = pl.multiple_of(col * share + inside, ROW_TILE)
            block = ref[pl.ds(m * rows, rows), :]
            if (tile + 1) * lanes > col * share:
                row_at = top + lax.broadcasted_iota(jnp.int32, block.shape, 0)
                col_at = tile * lanes + lax.broadcasted_iota(jnp.int32, block.shape, 1)
                block = jnp.where(col_at <= row_at, block.astype(jnp.float32), 0.0).astype(jnp.bfloat16)
            out_ref[pl.ds(top, rows), pl.ds(tile * lanes, lanes)] = block
    for col in range(col_size):
        for tile in range(width // lanes):
            if (col, tile) not in tiles:
                out_ref[pl.ds(col * share, share), pl.ds(tile * lanes, lanes)] = jnp.zeros(
                    (share, lanes), out_ref.dtype
                )
    turn_over(out_ref, turned_ref)


def turn_over(in_ref, out_ref, tile=256):
    for top in range(0, in_ref.shape[0], tile):
        for left in range(0, in_ref.shape[1], tile):
            out_ref[pl.ds(left, tile), pl.ds(top, tile)] = in_ref[pl.ds(top, tile), pl.ds(left, tile)].T


def lower_kernel(in_ref, turned_ref, out_ref):
    row_at = lax.broadcasted_iota(jnp.int32, in_ref.shape, 0)
    col_at = lax.broadcasted_iota(jnp.int32, in_ref.shape, 1)
    out_ref[...] = jnp.where(col_at <= row_at, in_ref[...].astype(jnp.float32), 0.0).astype(jnp.bfloat16)
    turn_over(out_ref, turned_ref)


def join_kernel(*refs):
    *in_refs, out_ref = refs
    rows = in_refs[0].shape[0]
    for n, ref in enumerate(in_refs):
        out_ref[pl.ds(n * rows, rows), :] = ref[...]


def joined(blocks):
    rows, width = blocks[0].shape
    return call(join_kernel, bf16(rows * len(blocks), width), [ON_CHIP] * len(blocks))(*blocks)


def inverse_shares(diag_inverse):
    part = diag_inverse.shape[0] // (lax.axis_size("sub") * lax.axis_size("row"))
    if part % ROW_TILE:
        return []
    first = (lax.axis_index("sub") * lax.axis_size("row") + lax.axis_index("row")) * part
    mine = lax.dynamic_slice_in_dim(diag_inverse, first, part, 0)
    return [mine] + [shifted(mine, "col", apart) for apart in range(1, lax.axis_size("col"))]


def place_piece(panel_ref, rows, block, origin, count, size):
    for g in range(block.shape[1] // size):
        left = (g * count + origin) * size
        if not isinstance(origin, int):
            left = pl.multiple_of(left, size)
        panel_ref[rows, pl.ds(left, size)] = block[:, g * size:(g + 1) * size]


def factor_from(panel_ref, inverse_ref, out_ref, tile):
    rows, width = out_ref.shape
    for first in range(0, width, tile):
        out_ref[:, pl.ds(first, tile)] = lax.dot_general(
            panel_ref[pl.ds(0, rows), pl.ds(0, first + tile)],
            inverse_ref[pl.ds(0, first + tile), pl.ds(first, tile)],
            (((1,), (0,)), ((), ())),
            preferred_element_type=jnp.float32,
        ).astype(jnp.bfloat16)


def row_factor_kernel(places, origins, kinds, size, tile, inverse_ref, *refs):
    arrays, out_ref, panel_ref = refs[: len(kinds)], refs[-2], refs[-1]
    col_index = lax.axis_index("col")
    count = len(origins)
    rows = out_ref.shape[0]
    for slot in range(count):
        origin = looked_up(col_index, origins[slot])
        for kind, ref in zip(kinds, arrays):
            members = tuple(i for i in range(count) if places[slot][i] == kind)
            if members:

                @pl.when(among(col_index, members))
                def _():
                    for top in range(0, rows, size):
                        at = pl.ds(top, size)
                        place_piece(panel_ref, at, ref[at, :], origin, count, size)

    factor_from(panel_ref, inverse_ref, out_ref, tile)


def column_factor_kernel(size, tile, inverse_ref, *refs):
    parts, out_ref, panel_ref = refs[:-2], refs[-2], refs[-1]
    row_index = lax.axis_index("row")
    count = lax.axis_size("col")
    part = parts[0].shape[0] // count
    for mask, ref in enumerate(parts):
        at = pl.ds(pl.multiple_of((row_index ^ mask) * part, ROW_TILE), part)
        for apart in range(count):
            origin = row_index ^ mask ^ apart
            place_piece(panel_ref, at, ref[pl.ds(apart * part, part), :], origin, count, size)
    factor_from(panel_ref, inverse_ref, out_ref, tile)


def product_kernel(mine, step, rows_ref, columns_ref, front_ref, *refs):
    out_hbm, out_ref, sems = refs[-3:]
    sub_index = lax.axis_index("sub")
    half = sub_index if mine else 1 - sub_index
    slot_count, _, size, _ = out_ref.shape
    copies = []
    for first in range(0, slot_count, step):
        blocks = min(step, slot_count - first)
        product = lax.dot_general(
            rows_ref[pl.ds(first * size, blocks * size), :], columns_ref[...], CONTRACT,
            preferred_element_type=jnp.float32,
        )
        for m in range(first, first + blocks):
            for a in range(slot_count):
                block = product[(m - first) * size:(m - first + 1) * size, a * size:(a + 1) * size]
                out_ref[m, a] = (front_ref[m, a, half].astype(jnp.float32) - block).astype(jnp.bfloat16)
            copies.append(pltpu.make_async_copy(out_ref.at[m], out_hbm.at[m, :, half], sems.at[m]))
            copies[-1].start()
    for copy in copies:
        copy.wait()


def body(front_entries, block_pattern, child_update, child_map, diag_inverse):
    slot_count = front_entries.shape[0]
    size = front_entries.shape[3]
    column_count = front_entries.shape[4]
    child_count = child_update.shape[1]
    row_size = lax.axis_size("row")
    col_size = lax.axis_size("col")
    groups = -(-(PANEL // size) // col_size)
    tile = PANEL // 2
    rows = slot_count * size
    part = -(-rows // (row_size * ROW_TILE)) * ROW_TILE
    padded = part * row_size
    depth = groups * col_size * size
    in_hbm = pl.BlockSpec(memory_space=pltpu.HBM)
    entries = front_entries.reshape(slot_count, size, column_count, size).transpose(0, 2, 1, 3)
    pattern = block_pattern.reshape(slot_count, 1, column_count)
    slots = child_map.transpose(0, 2, 1)
    own = child_update.reshape(child_count, size, child_count, size).transpose(0, 2, 1, 3)

    received = flipped(own, "sub", 1)
    shares = inverse_shares(diag_inverse)
    lanes = groups * size
    tiles = line_tiles(col_size, diag_inverse.shape[0], lanes) if shares else []
    piece, *parts = call(
        functools.partial(panel_kernel, part, groups),
        [bf16(padded, lanes)] + [bf16(part, lanes)] * col_size,
        [SCALARS, SCALARS] + [ON_CHIP] * 3,
    )(slots, pattern, entries[:, :groups], own, received)
    lines = []
    if shares:
        line = call(
            functools.partial(pack_kernel, tiles),
            bf16(len(tiles) * shares[0].shape[0], lanes), [ON_CHIP] * len(shares),
        )(*shares)
        piece, line, *parts = fence(piece, line, *parts)

    _, origins, places = line_plan(col_size)
    pieces = Line(piece, "col")
    pieces.step()
    if shares:
        lines = [line] + [flipped(line, "row", mask) for mask in range(1, row_size)]
    crossing = [crossed(block, apart) for apart, block in enumerate(parts)]
    turned, *lines = pieces.fenced(joined(crossing), *lines)
    if shares:
        lines += [flipped(line, "sub", 1) for line in lines]
        inverse = call(
            functools.partial(inverse_kernel, shares[0].shape[0], tiles),
            bf16(PANEL, PANEL), [ON_CHIP] * len(lines), moved=4 << 20,
            scratch_shapes=[pltpu.VMEM((PANEL, PANEL), jnp.bfloat16)],
        )(*lines)
    else:
        whole = lax.all_gather(diag_inverse, "col", axis=0, tiled=True)
        inverse = call(
            lower_kernel, bf16(PANEL, PANEL), [ON_CHIP], moved=4 << 20,
            scratch_shapes=[pltpu.VMEM((PANEL, PANEL), jnp.bfloat16)],
        )(whole)
    parts = [turned] + [flipped(turned, "row", mask) for mask in range(1, row_size)]
    while pieces.at < len(pieces.levels):
        pieces.step()
    front = call(
        functools.partial(front_kernel, groups),
        bf16(slot_count, column_count, size, size),
        [SCALARS, SCALARS] + [ON_CHIP] * 4,
        moved=6 << 20,
    )(slots, pattern, entries, own, received, piece)
    front, inverse, *parts = pieces.fenced(front, inverse, *parts)
    front = front.reshape(slot_count, slot_count, 2, size, size)

    kinds, arrays = pieces.taken()
    scratch = [pltpu.VMEM((padded, depth), jnp.bfloat16)]
    flops = 2 * rows * PANEL * PANEL * 3 // 4
    column_factor = call(
        functools.partial(column_factor_kernel, size, tile),
        bf16(rows, PANEL), [ON_CHIP] * (1 + row_size), flops=flops, scratch_shapes=scratch,
    )(inverse, *parts)
    other_factor = flipped(column_factor, "sub", 1)
    row_factor = call(
        functools.partial(row_factor_kernel, places, origins, kinds, size, tile),
        bf16(rows, PANEL), [ON_CHIP] * (1 + len(arrays)), flops=flops, scratch_shapes=scratch,
    )(inverse, *arrays)
    product = functools.partial(
        call,
        out_shape=bf16(slot_count, slot_count, 2, size, size),
        flops=2 * rows * rows * PANEL,
        out_specs=in_hbm,
        scratch_shapes=[
            pltpu.VMEM((slot_count, slot_count, size, size), jnp.bfloat16),
            pltpu.SemaphoreType.DMA((slot_count,)),
        ],
    )
    trailing = product(functools.partial(product_kernel, True, (slot_count + 1) // 2), in_specs=[ON_CHIP] * 3)(
        row_factor, column_factor, front
    )
    trailing = product(
        functools.partial(product_kernel, False, slot_count), in_specs=[ON_CHIP] * 3 + [in_hbm],
        input_output_aliases={3: 0},
    )(row_factor, other_factor, front, trailing)
    return trailing.reshape(slot_count, column_count, size, size).transpose(0, 2, 1, 3).reshape(
        slot_count, 1, 1, size, column_count, 1, size
    )


def solution(mesh):
    return jax.shard_map(
        body,
        mesh=mesh,
        in_specs=(
            P(None, "sub", "row", None, None, "col", None),
            P(None, "sub", "row", None, "col"),
            P("sub", None, "row", None, None, "col", None),
            P(),
            P("col", None),
        ),
        out_specs=P(None, "sub", "row", None, None, "col", None),
        check_vma=False,
    )
```

```python
import functools

import jax
import jax.numpy as jnp
from jax import lax
from jax.experimental import pallas as pl
from jax.experimental.pallas import tpu as pltpu
from jax.sharding import PartitionSpec as P

PANEL = 1024
ROW_TILE = 16
VMEM_BYTES = 12 * 1024 * 1024
CONTRACT = (((1,), (1,)), ((), ()))
ON_CHIP = pl.BlockSpec(memory_space=pltpu.VMEM)
SCALARS = pl.BlockSpec(memory_space=pltpu.SMEM)


def call(kernel, out_shape, in_specs, flops=0, moved=1 << 19, **more):
    single = not isinstance(out_shape, (list, tuple))
    return pl.pallas_call(
        kernel,
        out_shape=out_shape,
        in_specs=in_specs,
        out_specs=more.pop("out_specs", ON_CHIP if single else [ON_CHIP] * len(out_shape)),
        compiler_params=pltpu.CompilerParams(vmem_limit_bytes=VMEM_BYTES),
        cost_estimate=pl.CostEstimate(flops=flops, bytes_accessed=moved, transcendentals=0),
        **more,
    )


def bf16(*shape):
    return jax.ShapeDtypeStruct(shape, jnp.bfloat16)


def f32(*shape):
    return jax.ShapeDtypeStruct(shape, jnp.float32)


def flipped(block, axis, mask):
    count = lax.axis_size(axis)
    return lax.ppermute(block, axis, [(i, i ^ mask) for i in range(count)])


def shifted(block, axis, apart):
    count = lax.axis_size(axis)
    return lax.ppermute(block, axis, [(i, (i + apart) % count) for i in range(count)])


def far_last(count):
    return sorted(range(1, count), key=lambda apart: (min(apart, count - apart), apart))


def swap_even(i, count):
    return i ^ 1 if i ^ 1 < count else i


def swap_odd(i, count):
    j = ((i + 1) ^ 1) - 1
    return j if 0 <= j < count else i


@functools.cache
def line_plan(count):
    even = [swap_even(i, count) for i in range(count)]
    odd = [swap_odd(i, count) for i in range(count)]
    if count == 4:
        levels = [[(1, 0, even), (2, 0, odd)], [(3, 2, [2, 0, 3, 1]), (4, 1, [1, 3, 0, 2])]]
    else:
        levels, last = [], [0, 0]
        for step in range(count - 1):
            level = []
            for stream in (0, 1):
                level.append((1 + 2 * step + stream, last[stream], odd if (step + stream) % 2 else even))
                last[stream] = level[-1][0]
            levels.append(level)
    whose = {0: list(range(count))}
    seen = [[(0, i)] for i in range(count)]
    for level in levels:
        for array, source, to in level:
            whose[array] = [None] * count
            for i in range(count):
                whose[array][to[i]] = whose[source][i]
            for i in range(count):
                if all(whose[array][i] != origin for _, origin in seen[i]):
                    seen[i].append((array, whose[array][i]))
    origins = [[seen[i][j][1] for i in range(count)] for j in range(count)]
    places = [[seen[i][j][0] for i in range(count)] for j in range(count)]
    return levels, origins, places


class Line:
    def __init__(self, block, axis):
        self.axis = axis
        self.levels, _, self.places = line_plan(lax.axis_size(axis))
        self.held = {0: block}
        self.at = 0

    def step(self):
        for array, source, to in self.levels[self.at]:
            self.held[array] = lax.ppermute(self.held[source], self.axis, list(enumerate(to)))
        self.at += 1
        return self.at < len(self.levels)

    def fenced(self, *values):
        last = [array for array, _, _ in self.levels[self.at - 1]]
        out = fence(*values, *(self.held[array] for array in last))
        self.held.update(zip(last, out[len(values):]))
        return out[: len(values)]

    def taken(self):
        kinds = sorted({kind for row in self.places for kind in row})
        return kinds, [self.held[kind] for kind in kinds]


def among(index, members):
    found = index == members[0]
    for member in members[1:]:
        found = jnp.logical_or(found, index == member)
    return found


def looked_up(index, table):
    value = jnp.int32(table[0])
    for i, entry in enumerate(table[1:], 1):
        value = jnp.where(index == i, jnp.int32(entry), value)
    return value


def fence_kernel(*refs):
    pass


def fence(*values):
    place = pl.BlockSpec(memory_space=pl.ANY)
    return pl.pallas_call(
        fence_kernel,
        out_shape=[jax.ShapeDtypeStruct(v.shape, v.dtype) for v in values],
        in_specs=[place] * len(values),
        out_specs=[place] * len(values),
        input_output_aliases={n: n for n in range(len(values))},
        compiler_params=pltpu.CompilerParams(vmem_limit_bytes=1 << 20),
    )(*values)


def found_at(map_ref, child, place, wanted, child_count):
    at = jnp.int32(0)
    found = jnp.float32(0)
    for k in range(child_count):
        same = map_ref[child, place, k] == wanted
        at = jnp.where(same, jnp.int32(k), at)
        found = jnp.where(same, jnp.float32(1), found)
    return at, found


def block_places(map_ref, child, columns, slot_count, child_count):
    sub_index, row_index, col_index = (lax.axis_index(name) for name in ("sub", "row", "col"))
    rows = [
        found_at(map_ref, child, row_index, 2 * a + sub_index, child_count) for a in range(slot_count)
    ]
    cols = [found_at(map_ref, child, col_index, b, child_count) for b in columns]
    return rows, cols


def child_block(ref, row, col):
    return ref[row[0], col[0]].astype(jnp.float32) * (row[1] * col[1])


def line_tiles(count, share, lanes):
    return [(col, tile) for col in range(count) for tile in range(-(-(col + 1) * share // lanes))]


def pack_line(share_refs, out_ref, first, tiles):
    col_index = lax.axis_index("col")
    count = len(share_refs)
    rows, lanes = share_refs[0].shape[0], out_ref.shape[1]
    for apart, ref in zip([0, *far_last(count)], share_refs):
        for col in range(count):

            @pl.when(lax.rem(col_index + count - apart, count) == col)
            def _():
                for n, (home, tile) in enumerate(tiles):
                    if home == col:
                        out_ref[pl.ds(first + n * rows, rows), :] = ref[:, tile * lanes:(tile + 1) * lanes]


def pack_kernel(part, tiles, *refs):
    part_ref, *share_refs, out_ref = refs
    out_ref[pl.ds(0, part), :] = part_ref[...]
    pack_line(share_refs, out_ref, part, tiles)


def panel_kernel(part, groups, map_ref, pattern_ref, entries_ref, own_ref, received_ref, piece_ref, *part_refs):
    slot_count, _, size, _ = entries_ref.shape
    child_count = own_ref.shape[0]
    sub_index, row_index = lax.axis_index("sub"), lax.axis_index("row")
    places = [
        block_places(map_ref, child, range(groups), slot_count, child_count)
        for child in (sub_index, 1 - sub_index)
    ]
    for a in range(slot_count):
        for b in range(groups):
            total = entries_ref[a, b].astype(jnp.float32) * pattern_ref[a, 0, b].astype(jnp.float32)
            for (rows, cols), ref in zip(places, (own_ref, received_ref)):
                total = total + child_block(ref, rows[a], cols[b])
            piece_ref[pl.ds(a * size, size), pl.ds(b * size, size)] = total.astype(jnp.bfloat16)
    used = slot_count * size
    if used < piece_ref.shape[0]:
        piece_ref[pl.ds(used, piece_ref.shape[0] - used), :] = jnp.zeros(
            (piece_ref.shape[0] - used, piece_ref.shape[1]), piece_ref.dtype
        )
    for mask, ref in enumerate(part_refs):
        ref[...] = piece_ref[pl.ds(pl.multiple_of((row_index ^ mask) * part, ROW_TILE), part), :]


def front_kernel(groups, map_ref, pattern_ref, entries_ref, own_ref, received_ref, piece_ref, out_ref):
    slot_count, column_count, size, _ = entries_ref.shape
    child_count = own_ref.shape[0]
    sub_index = lax.axis_index("sub")
    columns = range(groups, column_count)
    places = [
        block_places(map_ref, child, columns, slot_count, child_count)
        for child in (sub_index, 1 - sub_index)
    ]
    for a in range(slot_count):
        for b in range(groups):
            out_ref[a, b] = piece_ref[pl.ds(a * size, size), pl.ds(b * size, size)]
        for n, b in enumerate(columns):
            total = entries_ref[a, b].astype(jnp.float32) * pattern_ref[a, 0, b].astype(jnp.float32)
            for (rows, cols), ref in zip(places, (own_ref, received_ref)):
                total = total + child_block(ref, rows[a], cols[n])
            out_ref[a, b] = total.astype(jnp.bfloat16)


def inverse_kernel(rows, tiles, *refs):
    *in_refs, turned_ref, out_ref = refs
    sub_index, row_index = lax.axis_index("sub"), lax.axis_index("row")
    sub_size, row_size, col_size = (lax.axis_size(name) for name in ("sub", "row", "col"))
    width = out_ref.shape[0]
    lanes = in_refs[0].shape[1]
    share = width // col_size
    lines = [
        (ref, line * len(tiles) * rows) for ref in in_refs for line in range(row_size)
    ]
    for n, (ref, first) in enumerate(lines):
        sub_at = sub_index if n < row_size else 1 - sub_index
        inside = (sub_at * row_size + (row_index ^ (n % row_size))) * rows
        for m, (col, tile) in enumerate(tiles):
            top = pl.multiple_of(col * share + inside, ROW_TILE)
            block = ref[pl.ds(first + m * rows, rows), :]
            if (tile + 1) * lanes > col * share:
                row_at = top + lax.broadcasted_iota(jnp.int32, block.shape, 0)
                col_at = tile * lanes + lax.broadcasted_iota(jnp.int32, block.shape, 1)
                block = jnp.where(col_at <= row_at, block.astype(jnp.float32), 0.0).astype(jnp.bfloat16)
            out_ref[pl.ds(top, rows), pl.ds(tile * lanes, lanes)] = block
    for col in range(col_size):
        for tile in range(width // lanes):
            if (col, tile) not in tiles:
                out_ref[pl.ds(col * share, share), pl.ds(tile * lanes, lanes)] = jnp.zeros(
                    (share, lanes), out_ref.dtype
                )
    turn_over(out_ref, turned_ref)


def turn_over(in_ref, out_ref, tile=256):
    for top in range(0, in_ref.shape[0], tile):
        for left in range(0, in_ref.shape[1], tile):
            out_ref[pl.ds(left, tile), pl.ds(top, tile)] = in_ref[pl.ds(top, tile), pl.ds(left, tile)].T


def lower_kernel(in_ref, turned_ref, out_ref):
    row_at = lax.broadcasted_iota(jnp.int32, in_ref.shape, 0)
    col_at = lax.broadcasted_iota(jnp.int32, in_ref.shape, 1)
    out_ref[...] = jnp.where(col_at <= row_at, in_ref[...].astype(jnp.float32), 0.0).astype(jnp.bfloat16)
    turn_over(out_ref, turned_ref)


def join_kernel(*refs):
    *in_refs, out_ref = refs
    rows = in_refs[0].shape[0]
    for n, ref in enumerate(in_refs):
        out_ref[pl.ds(n * rows, rows), :] = ref[...]


def joined(blocks):
    rows, width = blocks[0].shape
    return call(join_kernel, bf16(rows * len(blocks), width), [ON_CHIP] * len(blocks))(*blocks)


def inverse_shares(diag_inverse):
    part = diag_inverse.shape[0] // (lax.axis_size("sub") * lax.axis_size("row"))
    if part % ROW_TILE:
        return []
    first = (lax.axis_index("sub") * lax.axis_size("row") + lax.axis_index("row")) * part
    mine = lax.dynamic_slice_in_dim(diag_inverse, first, part, 0)
    return [mine] + [shifted(mine, "col", apart) for apart in far_last(lax.axis_size("col"))]


def turn_kernel(part, *refs):
    row_size, count = lax.axis_size("row"), lax.axis_size("col")
    held, refs = refs[:row_size], refs[row_size:]
    if len(refs) > count:
        sent_ref, *outs, lines_ref = refs
        rows = sent_ref.shape[0] - part
        lines_ref[pl.ds(0, rows), :] = sent_ref[pl.ds(part, rows), :]
        lines_ref[pl.ds(rows, rows), :] = held[1][pl.ds(part, rows), :]
    else:
        outs = refs
    row_index, col_index = lax.axis_index("row"), lax.axis_index("col")
    for apart, out_ref in enumerate(outs):
        wanted = row_index ^ lax.rem(col_index + apart, count)
        for mask, ref in enumerate(held):

            @pl.when(wanted == mask)
            def _():
                out_ref[...] = ref[pl.ds(0, part), :]


def place_piece(panel_ref, rows, block, origin, count, size):
    for g in range(block.shape[1] // size):
        left = (g * count + origin) * size
        if not isinstance(origin, int):
            left = pl.multiple_of(left, size)
        panel_ref[rows, pl.ds(left, size)] = block[:, g * size:(g + 1) * size]


def factor_from(panel_ref, inverse_ref, out_ref, tile):
    rows, width = out_ref.shape
    for first in range(0, width, tile):
        out_ref[:, pl.ds(first, tile)] = lax.dot_general(
            panel_ref[pl.ds(0, rows), pl.ds(0, first + tile)],
            inverse_ref[pl.ds(0, first + tile), pl.ds(first, tile)],
            (((1,), (0,)), ((), ())),
            preferred_element_type=jnp.float32,
        ).astype(jnp.bfloat16)


def row_factor_kernel(places, origins, kinds, size, tile, inverse_ref, *refs):
    arrays, out_ref, panel_ref = refs[: len(kinds)], refs[-2], refs[-1]
    col_index = lax.axis_index("col")
    count = len(origins)
    rows = out_ref.shape[0]
    for slot in range(count):
        origin = looked_up(col_index, origins[slot])
        for kind, ref in zip(kinds, arrays):
            members = tuple(i for i in range(count) if places[slot][i] == kind)
            if members:

                @pl.when(among(col_index, members))
                def _():
                    for top in range(0, rows, size):
                        at = pl.ds(top, size)
                        place_piece(panel_ref, at, ref[at, :], origin, count, size)

    factor_from(panel_ref, inverse_ref, out_ref, tile)


def column_factor_kernel(size, tile, inverse_ref, *refs):
    parts, out_ref, panel_ref = refs[:-2], refs[-2], refs[-1]
    row_index, col_index = lax.axis_index("row"), lax.axis_index("col")
    count = lax.axis_size("col")
    part = parts[0].shape[0] // count
    for mask, ref in enumerate(parts):
        at = pl.ds(pl.multiple_of((row_index ^ mask) * part, ROW_TILE), part)
        for apart in range(count):
            origin = lax.rem(col_index + count - apart, count)
            place_piece(panel_ref, at, ref[pl.ds(apart * part, part), :], origin, count, size)
    factor_from(panel_ref, inverse_ref, out_ref, tile)


def product_kernel(mine, step, rows_ref, columns_ref, front_ref, *refs):
    out_hbm, out_ref, sems = refs[-3:]
    sub_index = lax.axis_index("sub")
    half = sub_index if mine else 1 - sub_index
    slot_count, _, size, _ = out_ref.shape
    copies = []
    for first in range(0, slot_count, step):
        blocks = min(step, slot_count - first)
        product = lax.dot_general(
            rows_ref[pl.ds(first * size, blocks * size), :], columns_ref[...], CONTRACT,
            preferred_element_type=jnp.float32,
        )
        for m in range(first, first + blocks):
            for a in range(slot_count):
                block = product[(m - first) * size:(m - first + 1) * size, a * size:(a + 1) * size]
                out_ref[m, a] = (front_ref[m, a, half].astype(jnp.float32) - block).astype(jnp.bfloat16)
            copies.append(pltpu.make_async_copy(out_ref.at[m], out_hbm.at[m, :, half], sems.at[m]))
            copies[-1].start()
    for copy in copies:
        copy.wait()


def body(front_entries, block_pattern, child_update, child_map, diag_inverse):
    slot_count = front_entries.shape[0]
    size = front_entries.shape[3]
    column_count = front_entries.shape[4]
    child_count = child_update.shape[1]
    row_size = lax.axis_size("row")
    col_size = lax.axis_size("col")
    groups = -(-(PANEL // size) // col_size)
    tile = PANEL // 2
    rows = slot_count * size
    part = -(-rows // (row_size * ROW_TILE)) * ROW_TILE
    padded = part * row_size
    depth = groups * col_size * size
    in_hbm = pl.BlockSpec(memory_space=pltpu.HBM)
    entries = front_entries.reshape(slot_count, size, column_count, size).transpose(0, 2, 1, 3)
    pattern = block_pattern.reshape(slot_count, 1, column_count)
    slots = child_map.transpose(0, 2, 1)
    own = child_update.reshape(child_count, size, child_count, size).transpose(0, 2, 1, 3)

    received = flipped(own, "sub", 1)
    shares = inverse_shares(diag_inverse)
    lanes = groups * size
    tiles = line_tiles(col_size, diag_inverse.shape[0], lanes) if shares else []
    line_rows = len(tiles) * shares[0].shape[0] if shares else 0
    piece, *parts = call(
        functools.partial(panel_kernel, part, groups),
        [bf16(padded, lanes)] + [bf16(part, lanes)] * row_size,
        [SCALARS, SCALARS] + [ON_CHIP] * 3,
    )(slots, pattern, entries[:, :groups], own, received)
    if shares:
        parts[1] = call(
            functools.partial(pack_kernel, part, tiles), bf16(part + line_rows, lanes), [ON_CHIP] * (1 + len(shares))
        )(parts[1], *shares)
        piece, *parts = fence(piece, *parts)

    _, origins, places = line_plan(col_size)
    pieces = Line(piece, "col")
    pieces.step()
    held = [parts[0]] + [flipped(parts[mask], "row", mask) for mask in range(1, row_size)]
    sent = parts[1:2] if shares else []
    turned = call(
        functools.partial(turn_kernel, part),
        [bf16(part, lanes)] * col_size + [bf16(2 * line_rows, lanes)] * len(sent),
        [ON_CHIP] * (row_size + len(sent)),
    )(*held, *sent)
    turned = pieces.fenced(*turned)
    near, sends, lines = turned[0], turned[1:col_size], list(turned[col_size:])
    if shares:
        for bit in range(1, row_size.bit_length() - 1):
            lines += [flipped(line, "row", 1 << bit) for line in lines]
    come = {apart: shifted(sends[apart - 1], "col", apart) for apart in reversed(far_last(col_size))}
    first = far_last(col_size)[-1]
    (come[first],) = pieces.fenced(come[first])
    turned = joined([near] + [come[apart] for apart in range(1, col_size)])
    if shares:
        lines = [joined(lines)]
    turned, *lines = fence(turned, *lines)
    if shares:
        lines += [flipped(line, "sub", 1) for line in lines]
        inverse = call(
            functools.partial(inverse_kernel, shares[0].shape[0], tiles),
            bf16(PANEL, PANEL), [ON_CHIP] * len(lines), moved=4 << 20,
            scratch_shapes=[pltpu.VMEM((PANEL, PANEL), jnp.bfloat16)],
        )(*lines)
    else:
        whole = lax.all_gather(diag_inverse, "col", axis=0, tiled=True)
        inverse = call(
            lower_kernel, bf16(PANEL, PANEL), [ON_CHIP], moved=4 << 20,
            scratch_shapes=[pltpu.VMEM((PANEL, PANEL), jnp.bfloat16)],
        )(whole)
    parts = [turned] + [flipped(turned, "row", mask) for mask in range(1, row_size)]
    while pieces.at < len(pieces.levels):
        pieces.step()
    front = call(
        functools.partial(front_kernel, groups),
        bf16(slot_count, column_count, size, size),
        [SCALARS, SCALARS] + [ON_CHIP] * 4,
        moved=6 << 20,
    )(slots, pattern, entries, own, received, piece)
    front, inverse, *parts = pieces.fenced(front, inverse, *parts)
    front = front.reshape(slot_count, slot_count, 2, size, size)

    kinds, arrays = pieces.taken()
    scratch = [pltpu.VMEM((padded, depth), jnp.bfloat16)]
    flops = 2 * rows * PANEL * PANEL * 3 // 4
    column_factor = call(
        functools.partial(column_factor_kernel, size, tile),
        bf16(rows, PANEL), [ON_CHIP] * (1 + row_size), flops=flops, scratch_shapes=scratch,
    )(inverse, *parts)
    other_factor = flipped(column_factor, "sub", 1)
    row_factor = call(
        functools.partial(row_factor_kernel, places, origins, kinds, size, tile),
        bf16(rows, PANEL), [ON_CHIP] * (1 + len(arrays)), flops=flops, scratch_shapes=scratch,
    )(inverse, *arrays)
    product = functools.partial(
        call,
        out_shape=bf16(slot_count, slot_count, 2, size, size),
        flops=2 * rows * rows * PANEL,
        out_specs=in_hbm,
        scratch_shapes=[
            pltpu.VMEM((slot_count, slot_count, size, size), jnp.bfloat16),
            pltpu.SemaphoreType.DMA((slot_count,)),
        ],
    )
    trailing = product(functools.partial(product_kernel, True, (slot_count + 1) // 2), in_specs=[ON_CHIP] * 3)(
        row_factor, column_factor, front
    )
    trailing = product(
        functools.partial(product_kernel, False, slot_count), in_specs=[ON_CHIP] * 3 + [in_hbm],
        input_output_aliases={3: 0},
    )(row_factor, other_factor, front, trailing)
    return trailing.reshape(slot_count, column_count, size, size).transpose(0, 2, 1, 3).reshape(
        slot_count, 1, 1, size, column_count, 1, size
    )


def solution(mesh):
    return jax.shard_map(
        body,
        mesh=mesh,
        in_specs=(
            P(None, "sub", "row", None, None, "col", None),
            P(None, "sub", "row", None, "col"),
            P("sub", None, "row", None, None, "col", None),
            P(),
            P("col", None),
        ),
        out_specs=P(None, "sub", "row", None, None, "col", None),
        check_vma=False,
    )
```

```python
import functools

import jax
import jax.numpy as jnp
from jax import lax
from jax.experimental import pallas as pl
from jax.experimental.pallas import tpu as pltpu
from jax.sharding import PartitionSpec as P

PANEL = 1024
ROW_TILE = 16
VMEM_BYTES = 12 * 1024 * 1024
CONTRACT = (((1,), (1,)), ((), ()))
ON_CHIP = pl.BlockSpec(memory_space=pltpu.VMEM)
SCALARS = pl.BlockSpec(memory_space=pltpu.SMEM)


def call(kernel, out_shape, in_specs, flops=0, moved=1 << 19, **more):
    single = not isinstance(out_shape, (list, tuple))
    return pl.pallas_call(
        kernel,
        out_shape=out_shape,
        in_specs=in_specs,
        out_specs=more.pop("out_specs", ON_CHIP if single else [ON_CHIP] * len(out_shape)),
        compiler_params=pltpu.CompilerParams(vmem_limit_bytes=VMEM_BYTES),
        cost_estimate=pl.CostEstimate(flops=flops, bytes_accessed=moved, transcendentals=0),
        **more,
    )


def bf16(*shape):
    return jax.ShapeDtypeStruct(shape, jnp.bfloat16)


def f32(*shape):
    return jax.ShapeDtypeStruct(shape, jnp.float32)


def flipped(block, axis, mask):
    count = lax.axis_size(axis)
    return lax.ppermute(block, axis, [(i, i ^ mask) for i in range(count)])


def shifted(block, axis, apart):
    count = lax.axis_size(axis)
    return lax.ppermute(block, axis, [(i, (i + apart) % count) for i in range(count)])


def far_last(count):
    return sorted(range(1, count), key=lambda apart: (min(apart, count - apart), apart))


def swap_even(i, count):
    return i ^ 1 if i ^ 1 < count else i


def swap_odd(i, count):
    j = ((i + 1) ^ 1) - 1
    return j if 0 <= j < count else i


@functools.cache
def line_plan(count):
    even = [swap_even(i, count) for i in range(count)]
    odd = [swap_odd(i, count) for i in range(count)]
    if count == 4:
        levels = [[(1, 0, even), (2, 0, [i ^ 2 for i in range(count)])], [(3, 2, even)]]
    else:
        levels, last = [], [0, 0]
        for step in range(count - 1):
            level = []
            for stream in (0, 1):
                level.append((1 + 2 * step + stream, last[stream], odd if (step + stream) % 2 else even))
                last[stream] = level[-1][0]
            levels.append(level)
    whose = {0: list(range(count))}
    seen = [[(0, i)] for i in range(count)]
    for level in levels:
        for array, source, to in level:
            whose[array] = [None] * count
            for i in range(count):
                whose[array][to[i]] = whose[source][i]
            for i in range(count):
                if all(whose[array][i] != origin for _, origin in seen[i]):
                    seen[i].append((array, whose[array][i]))
    origins = [[seen[i][j][1] for i in range(count)] for j in range(count)]
    places = [[seen[i][j][0] for i in range(count)] for j in range(count)]
    return levels, origins, places


class Line:
    def __init__(self, block, axis):
        self.axis = axis
        self.levels, _, self.places = line_plan(lax.axis_size(axis))
        self.held = {0: block}
        self.at = 0

    def step(self):
        for array, source, to in self.levels[self.at]:
            self.held[array] = lax.ppermute(self.held[source], self.axis, list(enumerate(to)))
        self.at += 1
        return self.at < len(self.levels)

    def fenced(self, *values):
        last = [array for array, _, _ in self.levels[self.at - 1]]
        out = fence(*values, *(self.held[array] for array in last))
        self.held.update(zip(last, out[len(values):]))
        return out[: len(values)]

    def taken(self):
        kinds = sorted({kind for row in self.places for kind in row})
        return kinds, [self.held[kind] for kind in kinds]


def among(index, members):
    found = index == members[0]
    for member in members[1:]:
        found = jnp.logical_or(found, index == member)
    return found


def looked_up(index, table):
    value = jnp.int32(table[0])
    for i, entry in enumerate(table[1:], 1):
        value = jnp.where(index == i, jnp.int32(entry), value)
    return value


def fence_kernel(*refs):
    pass


def fence(*values):
    place = pl.BlockSpec(memory_space=pl.ANY)
    return pl.pallas_call(
        fence_kernel,
        out_shape=[jax.ShapeDtypeStruct(v.shape, v.dtype) for v in values],
        in_specs=[place] * len(values),
        out_specs=[place] * len(values),
        input_output_aliases={n: n for n in range(len(values))},
        compiler_params=pltpu.CompilerParams(vmem_limit_bytes=1 << 20),
    )(*values)


def found_at(map_ref, child, place, wanted, child_count):
    at = jnp.int32(0)
    found = jnp.float32(0)
    for k in range(child_count):
        same = map_ref[child, place, k] == wanted
        at = jnp.where(same, jnp.int32(k), at)
        found = jnp.where(same, jnp.float32(1), found)
    return at, found


def block_places(map_ref, child, columns, slot_count, child_count):
    sub_index, row_index, col_index = (lax.axis_index(name) for name in ("sub", "row", "col"))
    rows = [
        found_at(map_ref, child, row_index, 2 * a + sub_index, child_count) for a in range(slot_count)
    ]
    cols = [found_at(map_ref, child, col_index, b, child_count) for b in columns]
    return rows, cols


def child_block(ref, row, col):
    return ref[row[0], col[0]].astype(jnp.float32) * (row[1] * col[1])


def line_tiles(count, share, lanes):
    return [(col, tile) for col in range(count) for tile in range(-(-(col + 1) * share // lanes))]


def pack_line(share_refs, out_ref, first, tiles):
    col_index = lax.axis_index("col")
    count = len(share_refs)
    rows, lanes = share_refs[0].shape[0], out_ref.shape[1]
    for apart, ref in zip([0, *far_last(count)], share_refs):
        for col in range(count):

            @pl.when(lax.rem(col_index + count - apart, count) == col)
            def _():
                for n, (home, tile) in enumerate(tiles):
                    if home == col:
                        out_ref[pl.ds(first + n * rows, rows), :] = ref[:, tile * lanes:(tile + 1) * lanes]


def pack_kernel(part, tiles, *refs):
    part_ref, *share_refs, out_ref = refs
    out_ref[pl.ds(0, part), :] = part_ref[...]
    pack_line(share_refs, out_ref, part, tiles)


def panel_kernel(part, groups, map_ref, pattern_ref, entries_ref, own_ref, received_ref, piece_ref, *part_refs):
    slot_count, _, size, _ = entries_ref.shape
    child_count = own_ref.shape[0]
    sub_index, row_index = lax.axis_index("sub"), lax.axis_index("row")
    places = [
        block_places(map_ref, child, range(groups), slot_count, child_count)
        for child in (sub_index, 1 - sub_index)
    ]
    for a in range(slot_count):
        for b in range(groups):
            total = entries_ref[a, b].astype(jnp.float32) * pattern_ref[a, 0, b].astype(jnp.float32)
            for (rows, cols), ref in zip(places, (own_ref, received_ref)):
                total = total + child_block(ref, rows[a], cols[b])
            piece_ref[pl.ds(a * size, size), pl.ds(b * size, size)] = total.astype(jnp.bfloat16)
    used = slot_count * size
    if used < piece_ref.shape[0]:
        piece_ref[pl.ds(used, piece_ref.shape[0] - used), :] = jnp.zeros(
            (piece_ref.shape[0] - used, piece_ref.shape[1]), piece_ref.dtype
        )
    for mask, ref in enumerate(part_refs):
        ref[...] = piece_ref[pl.ds(pl.multiple_of((row_index ^ mask) * part, ROW_TILE), part), :]


def front_kernel(groups, map_ref, pattern_ref, entries_ref, own_ref, received_ref, piece_ref, out_ref):
    slot_count, column_count, size, _ = entries_ref.shape
    child_count = own_ref.shape[0]
    sub_index = lax.axis_index("sub")
    columns = range(groups, column_count)
    places = [
        block_places(map_ref, child, columns, slot_count, child_count)
        for child in (sub_index, 1 - sub_index)
    ]
    for a in range(slot_count):
        for b in range(groups):
            out_ref[a, b] = piece_ref[pl.ds(a * size, size), pl.ds(b * size, size)]
        for n, b in enumerate(columns):
            total = entries_ref[a, b].astype(jnp.float32) * pattern_ref[a, 0, b].astype(jnp.float32)
            for (rows, cols), ref in zip(places, (own_ref, received_ref)):
                total = total + child_block(ref, rows[a], cols[n])
            out_ref[a, b] = total.astype(jnp.bfloat16)


def inverse_kernel(rows, tiles, *refs):
    *in_refs, turned_ref, out_ref = refs
    sub_index, row_index = lax.axis_index("sub"), lax.axis_index("row")
    sub_size, row_size, col_size = (lax.axis_size(name) for name in ("sub", "row", "col"))
    width = out_ref.shape[0]
    lanes = in_refs[0].shape[1]
    share = width // col_size
    lines = [
        (ref, line * len(tiles) * rows) for ref in in_refs for line in range(row_size)
    ]
    for n, (ref, first) in enumerate(lines):
        sub_at = sub_index if n < row_size else 1 - sub_index
        inside = (sub_at * row_size + (row_index ^ (n % row_size))) * rows
        for m, (col, tile) in enumerate(tiles):
            top = pl.multiple_of(col * share + inside, ROW_TILE)
            block = ref[pl.ds(first + m * rows, rows), :]
            if (tile + 1) * lanes > col * share:
                row_at = top + lax.broadcasted_iota(jnp.int32, block.shape, 0)
                col_at = tile * lanes + lax.broadcasted_iota(jnp.int32, block.shape, 1)
                block = jnp.where(col_at <= row_at, block.astype(jnp.float32), 0.0).astype(jnp.bfloat16)
            out_ref[pl.ds(top, rows), pl.ds(tile * lanes, lanes)] = block
    for col in range(col_size):
        for tile in range(width // lanes):
            if (col, tile) not in tiles:
                out_ref[pl.ds(col * share, share), pl.ds(tile * lanes, lanes)] = jnp.zeros(
                    (share, lanes), out_ref.dtype
                )
    turn_over(out_ref, turned_ref)


def turn_over(in_ref, out_ref, tile=256):
    for top in range(0, in_ref.shape[0], tile):
        for left in range(0, in_ref.shape[1], tile):
            out_ref[pl.ds(left, tile), pl.ds(top, tile)] = in_ref[pl.ds(top, tile), pl.ds(left, tile)].T


def lower_kernel(in_ref, turned_ref, out_ref):
    row_at = lax.broadcasted_iota(jnp.int32, in_ref.shape, 0)
    col_at = lax.broadcasted_iota(jnp.int32, in_ref.shape, 1)
    out_ref[...] = jnp.where(col_at <= row_at, in_ref[...].astype(jnp.float32), 0.0).astype(jnp.bfloat16)
    turn_over(out_ref, turned_ref)


def join_kernel(*refs):
    *in_refs, out_ref = refs
    rows = in_refs[0].shape[0]
    for n, ref in enumerate(in_refs):
        out_ref[pl.ds(n * rows, rows), :] = ref[...]


def joined(blocks):
    rows, width = blocks[0].shape
    return call(join_kernel, bf16(rows * len(blocks), width), [ON_CHIP] * len(blocks))(*blocks)


def inverse_shares(diag_inverse):
    part = diag_inverse.shape[0] // (lax.axis_size("sub") * lax.axis_size("row"))
    if part % ROW_TILE:
        return []
    first = (lax.axis_index("sub") * lax.axis_size("row") + lax.axis_index("row")) * part
    mine = lax.dynamic_slice_in_dim(diag_inverse, first, part, 0)
    return [mine] + [shifted(mine, "col", apart) for apart in far_last(lax.axis_size("col"))]


def turn_kernel(part, *refs):
    row_size, count = lax.axis_size("row"), lax.axis_size("col")
    held, refs = refs[:row_size], refs[row_size:]
    if len(refs) > count:
        sent_ref, *outs, lines_ref = refs
        rows = sent_ref.shape[0] - part
        lines_ref[pl.ds(0, rows), :] = sent_ref[pl.ds(part, rows), :]
        lines_ref[pl.ds(rows, rows), :] = held[1][pl.ds(part, rows), :]
    else:
        outs = refs
    row_index, col_index = lax.axis_index("row"), lax.axis_index("col")
    for apart, out_ref in enumerate(outs):
        wanted = row_index ^ lax.rem(col_index + apart, count)
        for mask, ref in enumerate(held):

            @pl.when(wanted == mask)
            def _():
                out_ref[...] = ref[pl.ds(0, part), :]


def place_piece(panel_ref, rows, block, origin, count, size):
    for g in range(block.shape[1] // size):
        left = (g * count + origin) * size
        if not isinstance(origin, int):
            left = pl.multiple_of(left, size)
        panel_ref[rows, pl.ds(left, size)] = block[:, g * size:(g + 1) * size]


def factor_from(panel_ref, inverse_ref, out_ref, tile):
    rows, width = out_ref.shape
    for first in range(0, width, tile):
        out_ref[:, pl.ds(first, tile)] = lax.dot_general(
            panel_ref[pl.ds(0, rows), pl.ds(0, first + tile)],
            inverse_ref[pl.ds(0, first + tile), pl.ds(first, tile)],
            (((1,), (0,)), ((), ())),
            preferred_element_type=jnp.float32,
        ).astype(jnp.bfloat16)


def row_factor_kernel(places, origins, kinds, size, tile, inverse_ref, *refs):
    arrays, out_ref, panel_ref = refs[: len(kinds)], refs[-2], refs[-1]
    col_index = lax.axis_index("col")
    count = len(origins)
    rows = out_ref.shape[0]
    for slot in range(count):
        origin = looked_up(col_index, origins[slot])
        for kind, ref in zip(kinds, arrays):
            members = tuple(i for i in range(count) if places[slot][i] == kind)
            if members:

                @pl.when(among(col_index, members))
                def _():
                    for top in range(0, rows, size):
                        at = pl.ds(top, size)
                        place_piece(panel_ref, at, ref[at, :], origin, count, size)

    factor_from(panel_ref, inverse_ref, out_ref, tile)


def column_factor_kernel(size, tile, inverse_ref, *refs):
    parts, out_ref, panel_ref = refs[:-2], refs[-2], refs[-1]
    row_index, col_index = lax.axis_index("row"), lax.axis_index("col")
    count = lax.axis_size("col")
    part = parts[0].shape[0] // count
    for mask, ref in enumerate(parts):
        at = pl.ds(pl.multiple_of((row_index ^ mask) * part, ROW_TILE), part)
        for apart in range(count):
            origin = lax.rem(col_index + count - apart, count)
            place_piece(panel_ref, at, ref[pl.ds(apart * part, part), :], origin, count, size)
    factor_from(panel_ref, inverse_ref, out_ref, tile)


def product_kernel(mine, step, rows_ref, columns_ref, front_ref, *refs):
    out_hbm, out_ref, sems = refs[-3:]
    sub_index = lax.axis_index("sub")
    half = sub_index if mine else 1 - sub_index
    slot_count, _, size, _ = out_ref.shape
    copies = []
    for first in range(0, slot_count, step):
        blocks = min(step, slot_count - first)
        product = lax.dot_general(
            rows_ref[pl.ds(first * size, blocks * size), :], columns_ref[...], CONTRACT,
            preferred_element_type=jnp.float32,
        )
        for m in range(first, first + blocks):
            for a in range(slot_count):
                block = product[(m - first) * size:(m - first + 1) * size, a * size:(a + 1) * size]
                out_ref[m, a] = (front_ref[m, a, half].astype(jnp.float32) - block).astype(jnp.bfloat16)
            copies.append(pltpu.make_async_copy(out_ref.at[m], out_hbm.at[m, :, half], sems.at[m]))
            copies[-1].start()
    for copy in copies:
        copy.wait()


def body(front_entries, block_pattern, child_update, child_map, diag_inverse):
    slot_count = front_entries.shape[0]
    size = front_entries.shape[3]
    column_count = front_entries.shape[4]
    child_count = child_update.shape[1]
    row_size = lax.axis_size("row")
    col_size = lax.axis_size("col")
    groups = -(-(PANEL // size) // col_size)
    tile = PANEL // 2
    rows = slot_count * size
    part = -(-rows // (row_size * ROW_TILE)) * ROW_TILE
    padded = part * row_size
    depth = groups * col_size * size
    in_hbm = pl.BlockSpec(memory_space=pltpu.HBM)
    entries = front_entries.reshape(slot_count, size, column_count, size).transpose(0, 2, 1, 3)
    pattern = block_pattern.reshape(slot_count, 1, column_count)
    slots = child_map.transpose(0, 2, 1)
    own = child_update.reshape(child_count, size, child_count, size).transpose(0, 2, 1, 3)

    received = flipped(own, "sub", 1)
    shares = inverse_shares(diag_inverse)
    lanes = groups * size
    tiles = line_tiles(col_size, diag_inverse.shape[0], lanes) if shares else []
    line_rows = len(tiles) * shares[0].shape[0] if shares else 0
    piece, *parts = call(
        functools.partial(panel_kernel, part, groups),
        [bf16(padded, lanes)] + [bf16(part, lanes)] * row_size,
        [SCALARS, SCALARS] + [ON_CHIP] * 3,
    )(slots, pattern, entries[:, :groups], own, received)
    if shares:
        parts[1] = call(
            functools.partial(pack_kernel, part, tiles), bf16(part + line_rows, lanes), [ON_CHIP] * (1 + len(shares))
        )(parts[1], *shares)
        piece, *parts = fence(piece, *parts)

    _, origins, places = line_plan(col_size)
    pieces = Line(piece, "col")
    pieces.step()
    held = [parts[0]] + [flipped(parts[mask], "row", mask) for mask in range(1, row_size)]
    sent = parts[1:2] if shares else []
    turned = call(
        functools.partial(turn_kernel, part),
        [bf16(part, lanes)] * col_size + [bf16(2 * line_rows, lanes)] * len(sent),
        [ON_CHIP] * (row_size + len(sent)),
    )(*held, *sent)
    pieces.held[1], *turned = fence(pieces.held[1], *turned)
    near, sends, lines = turned[0], turned[1:col_size], list(turned[col_size:])
    if shares:
        for bit in range(1, row_size.bit_length() - 1):
            lines += [flipped(line, "row", 1 << bit) for line in lines]
    come = {apart: shifted(sends[apart - 1], "col", apart) for apart in reversed(far_last(col_size))}
    first = far_last(col_size)[-1]
    (come[first],) = pieces.fenced(come[first])
    turned = joined([near] + [come[apart] for apart in range(1, col_size)])
    if shares:
        lines = [joined(lines)]
    turned, *lines = fence(turned, *lines)
    if shares:
        lines += [flipped(line, "sub", 1) for line in lines]
        inverse = call(
            functools.partial(inverse_kernel, shares[0].shape[0], tiles),
            bf16(PANEL, PANEL), [ON_CHIP] * len(lines), moved=4 << 20,
            scratch_shapes=[pltpu.VMEM((PANEL, PANEL), jnp.bfloat16)],
        )(*lines)
    else:
        whole = lax.all_gather(diag_inverse, "col", axis=0, tiled=True)
        inverse = call(
            lower_kernel, bf16(PANEL, PANEL), [ON_CHIP], moved=4 << 20,
            scratch_shapes=[pltpu.VMEM((PANEL, PANEL), jnp.bfloat16)],
        )(whole)
    parts = [turned] + [flipped(turned, "row", mask) for mask in range(1, row_size)]
    while pieces.at < len(pieces.levels):
        pieces.step()
    front = call(
        functools.partial(front_kernel, groups),
        bf16(slot_count, column_count, size, size),
        [SCALARS, SCALARS] + [ON_CHIP] * 4,
        moved=6 << 20,
    )(slots, pattern, entries, own, received, piece)
    kinds, arrays = pieces.taken()
    scratch = [pltpu.VMEM((padded, depth), jnp.bfloat16)]
    flops = 2 * rows * PANEL * PANEL * 3 // 4
    row_factor = call(
        functools.partial(row_factor_kernel, places, origins, kinds, size, tile),
        bf16(rows, PANEL), [ON_CHIP] * (1 + len(arrays)), flops=flops, scratch_shapes=scratch,
    )(inverse, *arrays)
    row_factor, front, inverse, *parts = fence(row_factor, front, inverse, *parts)
    front = front.reshape(slot_count, slot_count, 2, size, size)

    column_factor = call(
        functools.partial(column_factor_kernel, size, tile),
        bf16(rows, PANEL), [ON_CHIP] * (1 + row_size), flops=flops, scratch_shapes=scratch,
    )(inverse, *parts)
    other_factor = flipped(column_factor, "sub", 1)
    product = functools.partial(
        call,
        out_shape=bf16(slot_count, slot_count, 2, size, size),
        flops=2 * rows * rows * PANEL,
        out_specs=in_hbm,
        scratch_shapes=[
            pltpu.VMEM((slot_count, slot_count, size, size), jnp.bfloat16),
            pltpu.SemaphoreType.DMA((slot_count,)),
        ],
    )
    trailing = product(functools.partial(product_kernel, True, (slot_count + 1) // 2), in_specs=[ON_CHIP] * 3)(
        row_factor, column_factor, front
    )
    trailing = product(
        functools.partial(product_kernel, False, slot_count), in_specs=[ON_CHIP] * 3 + [in_hbm],
        input_output_aliases={3: 0},
    )(row_factor, other_factor, front, trailing)
    return trailing.reshape(slot_count, column_count, size, size).transpose(0, 2, 1, 3).reshape(
        slot_count, 1, 1, size, column_count, 1, size
    )


def solution(mesh):
    return jax.shard_map(
        body,
        mesh=mesh,
        in_specs=(
            P(None, "sub", "row", None, None, "col", None),
            P(None, "sub", "row", None, "col"),
            P("sub", None, "row", None, None, "col", None),
            P(),
            P("col", None),
        ),
        out_specs=P(None, "sub", "row", None, None, "col", None),
        check_vma=False,
    )
```

```python
import functools

import jax
import jax.numpy as jnp
from jax import lax
from jax.experimental import pallas as pl
from jax.experimental.pallas import tpu as pltpu
from jax.sharding import PartitionSpec as P

PANEL = 1024
ROW_TILE = 16
VMEM_BYTES = 12 * 1024 * 1024
CONTRACT = (((1,), (1,)), ((), ()))
ON_CHIP = pl.BlockSpec(memory_space=pltpu.VMEM)
SCALARS = pl.BlockSpec(memory_space=pltpu.SMEM)


def call(kernel, out_shape, in_specs, flops=0, moved=1 << 19, **more):
    single = not isinstance(out_shape, (list, tuple))
    return pl.pallas_call(
        kernel,
        out_shape=out_shape,
        in_specs=in_specs,
        out_specs=more.pop("out_specs", ON_CHIP if single else [ON_CHIP] * len(out_shape)),
        compiler_params=pltpu.CompilerParams(vmem_limit_bytes=VMEM_BYTES),
        cost_estimate=pl.CostEstimate(flops=flops, bytes_accessed=moved, transcendentals=0),
        **more,
    )


def bf16(*shape):
    return jax.ShapeDtypeStruct(shape, jnp.bfloat16)


def f32(*shape):
    return jax.ShapeDtypeStruct(shape, jnp.float32)


def flipped(block, axis, mask):
    count = lax.axis_size(axis)
    return lax.ppermute(block, axis, [(i, i ^ mask) for i in range(count)])


def shifted(block, axis, apart):
    count = lax.axis_size(axis)
    return lax.ppermute(block, axis, [(i, (i + apart) % count) for i in range(count)])


def far_last(count):
    return sorted(range(1, count), key=lambda apart: (min(apart, count - apart), apart))


def swap_even(i, count):
    return i ^ 1 if i ^ 1 < count else i


def swap_odd(i, count):
    j = ((i + 1) ^ 1) - 1
    return j if 0 <= j < count else i


@functools.cache
def line_plan(count):
    even = [swap_even(i, count) for i in range(count)]
    odd = [swap_odd(i, count) for i in range(count)]
    if count == 4:
        levels = [[(1, 0, even), (2, 0, odd)], [(3, 2, [2, 0, 3, 1]), (4, 1, [1, 3, 0, 2])]]
    else:
        levels, last = [], [0, 0]
        for step in range(count - 1):
            level = []
            for stream in (0, 1):
                level.append((1 + 2 * step + stream, last[stream], odd if (step + stream) % 2 else even))
                last[stream] = level[-1][0]
            levels.append(level)
    whose = {0: list(range(count))}
    seen = [[(0, i)] for i in range(count)]
    for level in levels:
        for array, source, to in level:
            whose[array] = [None] * count
            for i in range(count):
                whose[array][to[i]] = whose[source][i]
            for i in range(count):
                if all(whose[array][i] != origin for _, origin in seen[i]):
                    seen[i].append((array, whose[array][i]))
    origins = [[seen[i][j][1] for i in range(count)] for j in range(count)]
    places = [[seen[i][j][0] for i in range(count)] for j in range(count)]
    return levels, origins, places


class Line:
    def __init__(self, block, axis):
        self.axis = axis
        self.levels, _, self.places = line_plan(lax.axis_size(axis))
        self.held = {0: block}
        self.at = 0

    def step(self):
        for array, source, to in self.levels[self.at]:
            self.held[array] = lax.ppermute(self.held[source], self.axis, list(enumerate(to)))
        self.at += 1
        return self.at < len(self.levels)

    def fenced(self, *values):
        last = [array for array, _, _ in self.levels[self.at - 1]]
        out = fence(*values, *(self.held[array] for array in last))
        self.held.update(zip(last, out[len(values):]))
        return out[: len(values)]

    def taken(self):
        kinds = sorted({kind for row in self.places for kind in row})
        return kinds, [self.held[kind] for kind in kinds]


def among(index, members):
    found = index == members[0]
    for member in members[1:]:
        found = jnp.logical_or(found, index == member)
    return found


def looked_up(index, table):
    value = jnp.int32(table[0])
    for i, entry in enumerate(table[1:], 1):
        value = jnp.where(index == i, jnp.int32(entry), value)
    return value


def fence_kernel(*refs):
    pass


def fence(*values):
    place = pl.BlockSpec(memory_space=pl.ANY)
    return pl.pallas_call(
        fence_kernel,
        out_shape=[jax.ShapeDtypeStruct(v.shape, v.dtype) for v in values],
        in_specs=[place] * len(values),
        out_specs=[place] * len(values),
        input_output_aliases={n: n for n in range(len(values))},
        compiler_params=pltpu.CompilerParams(vmem_limit_bytes=1 << 20),
    )(*values)


def found_at(map_ref, child, place, wanted, child_count):
    at = jnp.int32(0)
    found = jnp.float32(0)
    for k in range(child_count):
        same = map_ref[child, place, k] == wanted
        at = jnp.where(same, jnp.int32(k), at)
        found = jnp.where(same, jnp.float32(1), found)
    return at, found


def block_places(map_ref, child, columns, slot_count, child_count):
    sub_index, row_index, col_index = (lax.axis_index(name) for name in ("sub", "row", "col"))
    rows = [
        found_at(map_ref, child, row_index, 2 * a + sub_index, child_count) for a in range(slot_count)
    ]
    cols = [found_at(map_ref, child, col_index, b, child_count) for b in columns]
    return rows, cols


def child_block(ref, row, col):
    return ref[row[0], col[0]].astype(jnp.float32) * (row[1] * col[1])


def line_tiles(count, share, lanes):
    return [(col, tile) for col in range(count) for tile in range(-(-(col + 1) * share // lanes))]


def pack_line(share_refs, out_ref, first, tiles):
    col_index = lax.axis_index("col")
    count = len(share_refs)
    rows, lanes = share_refs[0].shape[0], out_ref.shape[1]
    for apart, ref in zip([0, *far_last(count)], share_refs):
        for col in range(count):

            @pl.when(lax.rem(col_index + count - apart, count) == col)
            def _():
                for n, (home, tile) in enumerate(tiles):
                    if home == col:
                        out_ref[pl.ds(first + n * rows, rows), :] = ref[:, tile * lanes:(tile + 1) * lanes]


def pack_kernel(part, tiles, *refs):
    part_ref, *share_refs, out_ref = refs
    out_ref[pl.ds(0, part), :] = part_ref[...]
    pack_line(share_refs, out_ref, part, tiles)


def panel_kernel(part, groups, map_ref, pattern_ref, entries_ref, own_ref, received_ref, piece_ref, *part_refs):
    slot_count, _, size, _ = entries_ref.shape
    child_count = own_ref.shape[0]
    sub_index, row_index = lax.axis_index("sub"), lax.axis_index("row")
    places = [
        block_places(map_ref, child, range(groups), slot_count, child_count)
        for child in (sub_index, 1 - sub_index)
    ]
    for a in range(slot_count):
        for b in range(groups):
            total = entries_ref[a, b].astype(jnp.float32) * pattern_ref[a, 0, b].astype(jnp.float32)
            for (rows, cols), ref in zip(places, (own_ref, received_ref)):
                total = total + child_block(ref, rows[a], cols[b])
            piece_ref[pl.ds(a * size, size), pl.ds(b * size, size)] = total.astype(jnp.bfloat16)
    used = slot_count * size
    if used < piece_ref.shape[0]:
        piece_ref[pl.ds(used, piece_ref.shape[0] - used), :] = jnp.zeros(
            (piece_ref.shape[0] - used, piece_ref.shape[1]), piece_ref.dtype
        )
    for mask, ref in enumerate(part_refs):
        ref[...] = piece_ref[pl.ds(pl.multiple_of((row_index ^ mask) * part, ROW_TILE), part), :]


def front_kernel(groups, map_ref, pattern_ref, entries_ref, own_ref, received_ref, piece_ref, out_ref):
    slot_count, column_count, size, _ = entries_ref.shape
    child_count = own_ref.shape[0]
    sub_index = lax.axis_index("sub")
    columns = range(groups, column_count)
    places = [
        block_places(map_ref, child, columns, slot_count, child_count)
        for child in (sub_index, 1 - sub_index)
    ]
    for a in range(slot_count):
        for b in range(groups):
            out_ref[a, b] = piece_ref[pl.ds(a * size, size), pl.ds(b * size, size)]
        for n, b in enumerate(columns):
            total = entries_ref[a, b].astype(jnp.float32) * pattern_ref[a, 0, b].astype(jnp.float32)
            for (rows, cols), ref in zip(places, (own_ref, received_ref)):
                total = total + child_block(ref, rows[a], cols[n])
            out_ref[a, b] = total.astype(jnp.bfloat16)


def inverse_kernel(rows, tiles, *refs):
    *in_refs, turned_ref, out_ref = refs
    sub_index, row_index = lax.axis_index("sub"), lax.axis_index("row")
    sub_size, row_size, col_size = (lax.axis_size(name) for name in ("sub", "row", "col"))
    width = out_ref.shape[0]
    lanes = in_refs[0].shape[1]
    share = width // col_size
    lines = [
        (ref, line * len(tiles) * rows) for ref in in_refs for line in range(row_size)
    ]
    for n, (ref, first) in enumerate(lines):
        sub_at = sub_index if n < row_size else 1 - sub_index
        inside = (sub_at * row_size + (row_index ^ (n % row_size))) * rows
        for m, (col, tile) in enumerate(tiles):
            top = pl.multiple_of(col * share + inside, ROW_TILE)
            block = ref[pl.ds(first + m * rows, rows), :]
            if (tile + 1) * lanes > col * share:
                row_at = top + lax.broadcasted_iota(jnp.int32, block.shape, 0)
                col_at = tile * lanes + lax.broadcasted_iota(jnp.int32, block.shape, 1)
                block = jnp.where(col_at <= row_at, block.astype(jnp.float32), 0.0).astype(jnp.bfloat16)
            out_ref[pl.ds(top, rows), pl.ds(tile * lanes, lanes)] = block
    for col in range(col_size):
        for tile in range(width // lanes):
            if (col, tile) not in tiles:
                out_ref[pl.ds(col * share, share), pl.ds(tile * lanes, lanes)] = jnp.zeros(
                    (share, lanes), out_ref.dtype
                )
    turn_over(out_ref, turned_ref)


def turn_over(in_ref, out_ref, tile=256):
    for top in range(0, in_ref.shape[0], tile):
        for left in range(0, in_ref.shape[1], tile):
            out_ref[pl.ds(left, tile), pl.ds(top, tile)] = in_ref[pl.ds(top, tile), pl.ds(left, tile)].T


def lower_kernel(in_ref, turned_ref, out_ref):
    row_at = lax.broadcasted_iota(jnp.int32, in_ref.shape, 0)
    col_at = lax.broadcasted_iota(jnp.int32, in_ref.shape, 1)
    out_ref[...] = jnp.where(col_at <= row_at, in_ref[...].astype(jnp.float32), 0.0).astype(jnp.bfloat16)
    turn_over(out_ref, turned_ref)


def join_kernel(*refs):
    *in_refs, out_ref = refs
    rows = in_refs[0].shape[0]
    for n, ref in enumerate(in_refs):
        out_ref[pl.ds(n * rows, rows), :] = ref[...]


def joined(blocks):
    rows, width = blocks[0].shape
    return call(join_kernel, bf16(rows * len(blocks), width), [ON_CHIP] * len(blocks))(*blocks)


def inverse_shares(diag_inverse):
    part = diag_inverse.shape[0] // (lax.axis_size("sub") * lax.axis_size("row"))
    if part % ROW_TILE:
        return []
    first = (lax.axis_index("sub") * lax.axis_size("row") + lax.axis_index("row")) * part
    mine = lax.dynamic_slice_in_dim(diag_inverse, first, part, 0)
    return [mine] + [shifted(mine, "col", apart) for apart in far_last(lax.axis_size("col"))]


def turn_kernel(part, *refs):
    row_size, count = lax.axis_size("row"), lax.axis_size("col")
    held, refs = refs[:row_size], refs[row_size:]
    if len(refs) > count:
        sent_ref, *outs, lines_ref = refs
        rows = sent_ref.shape[0] - part
        lines_ref[pl.ds(0, rows), :] = sent_ref[pl.ds(part, rows), :]
        lines_ref[pl.ds(rows, rows), :] = held[1][pl.ds(part, rows), :]
    else:
        outs = refs
    row_index, col_index = lax.axis_index("row"), lax.axis_index("col")
    for apart, out_ref in enumerate(outs):
        wanted = row_index ^ lax.rem(col_index + apart, count)
        for mask, ref in enumerate(held):

            @pl.when(wanted == mask)
            def _():
                out_ref[...] = ref[pl.ds(0, part), :]


def place_piece(panel_ref, rows, block, origin, count, size):
    for g in range(block.shape[1] // size):
        left = (g * count + origin) * size
        if not isinstance(origin, int):
            left = pl.multiple_of(left, size)
        panel_ref[rows, pl.ds(left, size)] = block[:, g * size:(g + 1) * size]


def factor_from(panel_ref, inverse_ref, out_ref, tile):
    rows, width = out_ref.shape
    for first in range(0, width, tile):
        out_ref[:, pl.ds(first, tile)] = lax.dot_general(
            panel_ref[pl.ds(0, rows), pl.ds(0, first + tile)],
            inverse_ref[pl.ds(0, first + tile), pl.ds(first, tile)],
            (((1,), (0,)), ((), ())),
            preferred_element_type=jnp.float32,
        ).astype(jnp.bfloat16)


def row_factor_kernel(places, origins, kinds, size, tile, inverse_ref, *refs):
    arrays, out_ref, panel_ref = refs[: len(kinds)], refs[-2], refs[-1]
    col_index = lax.axis_index("col")
    count = len(origins)
    rows = out_ref.shape[0]
    for slot in range(count):
        origin = looked_up(col_index, origins[slot])
        for kind, ref in zip(kinds, arrays):
            members = tuple(i for i in range(count) if places[slot][i] == kind)
            if members:

                @pl.when(among(col_index, members))
                def _():
                    for top in range(0, rows, size):
                        at = pl.ds(top, size)
                        place_piece(panel_ref, at, ref[at, :], origin, count, size)

    factor_from(panel_ref, inverse_ref, out_ref, tile)


def column_factor_kernel(size, tile, inverse_ref, *refs):
    parts, out_ref, panel_ref = refs[:-2], refs[-2], refs[-1]
    row_index, col_index = lax.axis_index("row"), lax.axis_index("col")
    count = lax.axis_size("col")
    part = parts[0].shape[0] // count
    for mask, ref in enumerate(parts):
        at = pl.ds(pl.multiple_of((row_index ^ mask) * part, ROW_TILE), part)
        for apart in range(count):
            origin = lax.rem(col_index + count - apart, count)
            place_piece(panel_ref, at, ref[pl.ds(apart * part, part), :], origin, count, size)
    factor_from(panel_ref, inverse_ref, out_ref, tile)


def product_kernel(mine, step, rows_ref, columns_ref, front_ref, *refs):
    out_hbm, out_ref, sems = refs[-3:]
    sub_index = lax.axis_index("sub")
    half = sub_index if mine else 1 - sub_index
    slot_count, _, size, _ = out_ref.shape
    copies = []
    for first in range(0, slot_count, step):
        blocks = min(step, slot_count - first)
        product = lax.dot_general(
            rows_ref[pl.ds(first * size, blocks * size), :], columns_ref[...], CONTRACT,
            preferred_element_type=jnp.float32,
        )
        for m in range(first, first + blocks):
            for a in range(slot_count):
                block = product[(m - first) * size:(m - first + 1) * size, a * size:(a + 1) * size]
                out_ref[m, a] = (front_ref[m, a, half].astype(jnp.float32) - block).astype(jnp.bfloat16)
            copies.append(pltpu.make_async_copy(out_ref.at[m], out_hbm.at[m, :, half], sems.at[m]))
            copies[-1].start()
    for copy in copies:
        copy.wait()


def body(front_entries, block_pattern, child_update, child_map, diag_inverse):
    slot_count = front_entries.shape[0]
    size = front_entries.shape[3]
    column_count = front_entries.shape[4]
    child_count = child_update.shape[1]
    row_size = lax.axis_size("row")
    col_size = lax.axis_size("col")
    groups = -(-(PANEL // size) // col_size)
    tile = PANEL // 2
    rows = slot_count * size
    part = -(-rows // (row_size * ROW_TILE)) * ROW_TILE
    padded = part * row_size
    depth = groups * col_size * size
    in_hbm = pl.BlockSpec(memory_space=pltpu.HBM)
    entries = front_entries.reshape(slot_count, size, column_count, size).transpose(0, 2, 1, 3)
    pattern = block_pattern.reshape(slot_count, 1, column_count)
    slots = child_map.transpose(0, 2, 1)
    own = child_update.reshape(child_count, size, child_count, size).transpose(0, 2, 1, 3)

    received = flipped(own, "sub", 1)
    shares = inverse_shares(diag_inverse)
    lanes = groups * size
    tiles = line_tiles(col_size, diag_inverse.shape[0], lanes) if shares else []
    line_rows = len(tiles) * shares[0].shape[0] if shares else 0
    piece, *parts = call(
        functools.partial(panel_kernel, part, groups),
        [bf16(padded, lanes)] + [bf16(part, lanes)] * row_size,
        [SCALARS, SCALARS] + [ON_CHIP] * 3,
    )(slots, pattern, entries[:, :groups], own, received)
    if shares:
        parts[1] = call(
            functools.partial(pack_kernel, part, tiles), bf16(part + line_rows, lanes), [ON_CHIP] * (1 + len(shares))
        )(parts[1], *shares)
        piece, *parts = fence(piece, *parts)

    _, origins, places = line_plan(col_size)
    pieces = Line(piece, "col")
    pieces.step()
    held = [parts[0]] + [flipped(parts[mask], "row", mask) for mask in range(1, row_size)]
    sent = parts[1:2] if shares else []
    turned = call(
        functools.partial(turn_kernel, part),
        [bf16(part, lanes)] * col_size + [bf16(2 * line_rows, lanes)] * len(sent),
        [ON_CHIP] * (row_size + len(sent)),
    )(*held, *sent)
    pieces.held[1], *turned = fence(pieces.held[1], *turned)
    near, sends, lines = turned[0], turned[1:col_size], list(turned[col_size:])
    if shares:
        for bit in range(1, row_size.bit_length() - 1):
            lines += [flipped(line, "row", 1 << bit) for line in lines]
    come = {apart: shifted(sends[apart - 1], "col", apart) for apart in reversed(far_last(col_size))}
    first = far_last(col_size)[-1]
    (come[first],) = pieces.fenced(come[first])
    turned = joined([near] + [come[apart] for apart in range(1, col_size)])
    if shares:
        lines = [joined(lines)]
    turned, *lines = fence(turned, *lines)
    if shares:
        lines += [flipped(line, "sub", 1) for line in lines]
        inverse = call(
            functools.partial(inverse_kernel, shares[0].shape[0], tiles),
            bf16(PANEL, PANEL), [ON_CHIP] * len(lines), moved=4 << 20,
            scratch_shapes=[pltpu.VMEM((PANEL, PANEL), jnp.bfloat16)],
        )(*lines)
    else:
        whole = lax.all_gather(diag_inverse, "col", axis=0, tiled=True)
        inverse = call(
            lower_kernel, bf16(PANEL, PANEL), [ON_CHIP], moved=4 << 20,
            scratch_shapes=[pltpu.VMEM((PANEL, PANEL), jnp.bfloat16)],
        )(whole)
    parts = [turned] + [flipped(turned, "row", mask) for mask in range(1, row_size)]
    while pieces.at < len(pieces.levels):
        pieces.step()
    front = call(
        functools.partial(front_kernel, groups),
        bf16(slot_count, column_count, size, size),
        [SCALARS, SCALARS] + [ON_CHIP] * 4,
        moved=6 << 20,
    )(slots, pattern, entries, own, received, piece)
    front, inverse, *parts = pieces.fenced(front, inverse, *parts)
    front = front.reshape(slot_count, slot_count, 2, size, size)

    kinds, arrays = pieces.taken()
    scratch = [pltpu.VMEM((padded, depth), jnp.bfloat16)]
    flops = 2 * rows * PANEL * PANEL * 3 // 4
    column_factor = call(
        functools.partial(column_factor_kernel, size, tile),
        bf16(rows, PANEL), [ON_CHIP] * (1 + row_size), flops=flops, scratch_shapes=scratch,
    )(inverse, *parts)
    other_factor = flipped(column_factor, "sub", 1)
    row_factor = call(
        functools.partial(row_factor_kernel, places, origins, kinds, size, tile),
        bf16(rows, PANEL), [ON_CHIP] * (1 + len(arrays)), flops=flops, scratch_shapes=scratch,
    )(inverse, *arrays)
    product = functools.partial(
        call,
        out_shape=bf16(slot_count, slot_count, 2, size, size),
        flops=2 * rows * rows * PANEL,
        out_specs=in_hbm,
        scratch_shapes=[
            pltpu.VMEM((slot_count, slot_count, size, size), jnp.bfloat16),
            pltpu.SemaphoreType.DMA((slot_count,)),
        ],
    )
    trailing = product(functools.partial(product_kernel, True, (slot_count + 1) // 2), in_specs=[ON_CHIP] * 3)(
        row_factor, column_factor, front
    )
    trailing = product(
        functools.partial(product_kernel, False, slot_count), in_specs=[ON_CHIP] * 3 + [in_hbm],
        input_output_aliases={3: 0},
    )(row_factor, other_factor, front, trailing)
    return trailing.reshape(slot_count, column_count, size, size).transpose(0, 2, 1, 3).reshape(
        slot_count, 1, 1, size, column_count, 1, size
    )


def solution(mesh):
    return jax.shard_map(
        body,
        mesh=mesh,
        in_specs=(
            P(None, "sub", "row", None, None, "col", None),
            P(None, "sub", "row", None, "col"),
            P("sub", None, "row", None, None, "col", None),
            P(),
            P("col", None),
        ),
        out_specs=P(None, "sub", "row", None, None, "col", None),
        check_vma=False,
    )
```

```python
import functools

import jax
import jax.numpy as jnp
from jax import lax
from jax.experimental import pallas as pl
from jax.experimental.pallas import tpu as pltpu
from jax.sharding import PartitionSpec as P

PANEL = 1024
ROW_TILE = 16
VMEM_BYTES = 12 * 1024 * 1024
CONTRACT = (((1,), (1,)), ((), ()))
ON_CHIP = pl.BlockSpec(memory_space=pltpu.VMEM)
SCALARS = pl.BlockSpec(memory_space=pltpu.SMEM)


def call(kernel, out_shape, in_specs, flops=0, moved=1 << 19, **more):
    single = not isinstance(out_shape, (list, tuple))
    return pl.pallas_call(
        kernel,
        out_shape=out_shape,
        in_specs=in_specs,
        out_specs=more.pop("out_specs", ON_CHIP if single else [ON_CHIP] * len(out_shape)),
        compiler_params=pltpu.CompilerParams(vmem_limit_bytes=VMEM_BYTES),
        cost_estimate=pl.CostEstimate(flops=flops, bytes_accessed=moved, transcendentals=0),
        **more,
    )


def bf16(*shape):
    return jax.ShapeDtypeStruct(shape, jnp.bfloat16)


def f32(*shape):
    return jax.ShapeDtypeStruct(shape, jnp.float32)


def flipped(block, axis, mask):
    count = lax.axis_size(axis)
    return lax.ppermute(block, axis, [(i, i ^ mask) for i in range(count)])


def shifted(block, axis, apart):
    count = lax.axis_size(axis)
    return lax.ppermute(block, axis, [(i, (i + apart) % count) for i in range(count)])


def far_last(count):
    return sorted(range(1, count), key=lambda apart: (min(apart, count - apart), apart))


def swap_even(i, count):
    return i ^ 1 if i ^ 1 < count else i


def swap_odd(i, count):
    j = ((i + 1) ^ 1) - 1
    return j if 0 <= j < count else i


@functools.cache
def line_plan(count):
    even = [swap_even(i, count) for i in range(count)]
    odd = [swap_odd(i, count) for i in range(count)]
    if count == 4:
        levels = [[(1, 0, even), (2, 0, odd)], [(3, 2, [2, 0, 3, 1]), (4, 1, [1, 3, 0, 2])]]
    else:
        levels, last = [], [0, 0]
        for step in range(count - 1):
            level = []
            for stream in (0, 1):
                level.append((1 + 2 * step + stream, last[stream], odd if (step + stream) % 2 else even))
                last[stream] = level[-1][0]
            levels.append(level)
    whose = {0: list(range(count))}
    seen = [[(0, i)] for i in range(count)]
    for level in levels:
        for array, source, to in level:
            whose[array] = [None] * count
            for i in range(count):
                whose[array][to[i]] = whose[source][i]
            for i in range(count):
                if all(whose[array][i] != origin for _, origin in seen[i]):
                    seen[i].append((array, whose[array][i]))
    origins = [[seen[i][j][1] for i in range(count)] for j in range(count)]
    places = [[seen[i][j][0] for i in range(count)] for j in range(count)]
    return levels, origins, places


class Line:
    def __init__(self, block, axis):
        self.axis = axis
        self.levels, _, self.places = line_plan(lax.axis_size(axis))
        self.held = {0: block}
        self.at = 0

    def step(self):
        for array, source, to in self.levels[self.at]:
            self.held[array] = lax.ppermute(self.held[source], self.axis, list(enumerate(to)))
        self.at += 1
        return self.at < len(self.levels)

    def fenced(self, *values):
        last = [array for array, _, _ in self.levels[self.at - 1]]
        out = fence(*values, *(self.held[array] for array in last))
        self.held.update(zip(last, out[len(values):]))
        return out[: len(values)]

    def taken(self):
        kinds = sorted({kind for row in self.places for kind in row})
        return kinds, [self.held[kind] for kind in kinds]


def among(index, members):
    found = index == members[0]
    for member in members[1:]:
        found = jnp.logical_or(found, index == member)
    return found


def looked_up(index, table):
    value = jnp.int32(table[0])
    for i, entry in enumerate(table[1:], 1):
        value = jnp.where(index == i, jnp.int32(entry), value)
    return value


def fence_kernel(*refs):
    pass


def fence(*values):
    place = pl.BlockSpec(memory_space=pl.ANY)
    return pl.pallas_call(
        fence_kernel,
        out_shape=[jax.ShapeDtypeStruct(v.shape, v.dtype) for v in values],
        in_specs=[place] * len(values),
        out_specs=[place] * len(values),
        input_output_aliases={n: n for n in range(len(values))},
        compiler_params=pltpu.CompilerParams(vmem_limit_bytes=1 << 20),
    )(*values)


def found_at(map_ref, child, place, wanted, child_count):
    at = jnp.int32(0)
    found = jnp.float32(0)
    for k in range(child_count):
        same = map_ref[child, place, k] == wanted
        at = jnp.where(same, jnp.int32(k), at)
        found = jnp.where(same, jnp.float32(1), found)
    return at, found


def block_places(map_ref, child, columns, slot_count, child_count):
    sub_index, row_index, col_index = (lax.axis_index(name) for name in ("sub", "row", "col"))
    rows = [
        found_at(map_ref, child, row_index, 2 * a + sub_index, child_count) for a in range(slot_count)
    ]
    cols = [found_at(map_ref, child, col_index, b, child_count) for b in columns]
    return rows, cols


def child_block(ref, row, col):
    return ref[row[0], col[0]].astype(jnp.float32) * (row[1] * col[1])


def line_tiles(count, share, lanes):
    return [(col, tile) for col in range(count) for tile in range(-(-(col + 1) * share // lanes))]


def pack_line(share_refs, out_ref, first, tiles):
    col_index = lax.axis_index("col")
    count = len(share_refs)
    rows, lanes = share_refs[0].shape[0], out_ref.shape[1]
    for apart, ref in zip([0, *far_last(count)], share_refs):
        for col in range(count):

            @pl.when(lax.rem(col_index + count - apart, count) == col)
            def _():
                for n, (home, tile) in enumerate(tiles):
                    if home == col:
                        out_ref[pl.ds(first + n * rows, rows), :] = ref[:, tile * lanes:(tile + 1) * lanes]


def pack_kernel(part, tiles, *refs):
    part_ref, *share_refs, out_ref = refs
    out_ref[pl.ds(0, part), :] = part_ref[...]
    pack_line(share_refs, out_ref, part, tiles)


def panel_kernel(part, groups, map_ref, pattern_ref, entries_ref, own_ref, received_ref, piece_ref, *part_refs):
    slot_count, _, size, _ = entries_ref.shape
    child_count = own_ref.shape[0]
    sub_index, row_index = lax.axis_index("sub"), lax.axis_index("row")
    places = [
        block_places(map_ref, child, range(groups), slot_count, child_count)
        for child in (sub_index, 1 - sub_index)
    ]
    for a in range(slot_count):
        for b in range(groups):
            total = entries_ref[a, b].astype(jnp.float32) * pattern_ref[a, 0, b].astype(jnp.float32)
            for (rows, cols), ref in zip(places, (own_ref, received_ref)):
                total = total + child_block(ref, rows[a], cols[b])
            piece_ref[pl.ds(a * size, size), pl.ds(b * size, size)] = total.astype(jnp.bfloat16)
    used = slot_count * size
    if used < piece_ref.shape[0]:
        piece_ref[pl.ds(used, piece_ref.shape[0] - used), :] = jnp.zeros(
            (piece_ref.shape[0] - used, piece_ref.shape[1]), piece_ref.dtype
        )
    for mask, ref in enumerate(part_refs):
        ref[...] = piece_ref[pl.ds(pl.multiple_of((row_index ^ mask) * part, ROW_TILE), part), :]


def front_kernel(groups, map_ref, pattern_ref, entries_ref, own_ref, received_ref, piece_ref, out_ref):
    slot_count, column_count, size, _ = entries_ref.shape
    child_count = own_ref.shape[0]
    sub_index = lax.axis_index("sub")
    columns = range(groups, column_count)
    places = [
        block_places(map_ref, child, columns, slot_count, child_count)
        for child in (sub_index, 1 - sub_index)
    ]
    for a in range(slot_count):
        for b in range(groups):
            out_ref[a, b] = piece_ref[pl.ds(a * size, size), pl.ds(b * size, size)]
        for n, b in enumerate(columns):
            total = entries_ref[a, b].astype(jnp.float32) * pattern_ref[a, 0, b].astype(jnp.float32)
            for (rows, cols), ref in zip(places, (own_ref, received_ref)):
                total = total + child_block(ref, rows[a], cols[n])
            out_ref[a, b] = total.astype(jnp.bfloat16)


def inverse_kernel(rows, tiles, *refs):
    *in_refs, turned_ref, out_ref = refs
    sub_index, row_index = lax.axis_index("sub"), lax.axis_index("row")
    sub_size, row_size, col_size = (lax.axis_size(name) for name in ("sub", "row", "col"))
    width = out_ref.shape[0]
    lanes = in_refs[0].shape[1]
    share = width // col_size
    lines = [
        (ref, line * len(tiles) * rows) for ref in in_refs for line in range(row_size)
    ]
    for n, (ref, first) in enumerate(lines):
        sub_at = sub_index if n < row_size else 1 - sub_index
        inside = (sub_at * row_size + (row_index ^ (n % row_size))) * rows
        for m, (col, tile) in enumerate(tiles):
            top = pl.multiple_of(col * share + inside, ROW_TILE)
            block = ref[pl.ds(first + m * rows, rows), :]
            if (tile + 1) * lanes > col * share:
                row_at = top + lax.broadcasted_iota(jnp.int32, block.shape, 0)
                col_at = tile * lanes + lax.broadcasted_iota(jnp.int32, block.shape, 1)
                block = jnp.where(col_at <= row_at, block.astype(jnp.float32), 0.0).astype(jnp.bfloat16)
            out_ref[pl.ds(top, rows), pl.ds(tile * lanes, lanes)] = block
    for col in range(col_size):
        for tile in range(width // lanes):
            if (col, tile) not in tiles:
                out_ref[pl.ds(col * share, share), pl.ds(tile * lanes, lanes)] = jnp.zeros(
                    (share, lanes), out_ref.dtype
                )
    turn_over(out_ref, turned_ref)


def turn_over(in_ref, out_ref, tile=256):
    for top in range(0, in_ref.shape[0], tile):
        for left in range(0, in_ref.shape[1], tile):
            out_ref[pl.ds(left, tile), pl.ds(top, tile)] = in_ref[pl.ds(top, tile), pl.ds(left, tile)].T


def lower_kernel(in_ref, turned_ref, out_ref):
    row_at = lax.broadcasted_iota(jnp.int32, in_ref.shape, 0)
    col_at = lax.broadcasted_iota(jnp.int32, in_ref.shape, 1)
    out_ref[...] = jnp.where(col_at <= row_at, in_ref[...].astype(jnp.float32), 0.0).astype(jnp.bfloat16)
    turn_over(out_ref, turned_ref)


def join_kernel(*refs):
    *in_refs, out_ref = refs
    rows = in_refs[0].shape[0]
    for n, ref in enumerate(in_refs):
        out_ref[pl.ds(n * rows, rows), :] = ref[...]


def joined(blocks):
    rows, width = blocks[0].shape
    return call(join_kernel, bf16(rows * len(blocks), width), [ON_CHIP] * len(blocks))(*blocks)


def inverse_shares(diag_inverse):
    part = diag_inverse.shape[0] // (lax.axis_size("sub") * lax.axis_size("row"))
    if part % ROW_TILE:
        return []
    first = (lax.axis_index("sub") * lax.axis_size("row") + lax.axis_index("row")) * part
    mine = lax.dynamic_slice_in_dim(diag_inverse, first, part, 0)
    return [mine] + [shifted(mine, "col", apart) for apart in far_last(lax.axis_size("col"))]


def turn_kernel(part, *refs):
    row_size, count = lax.axis_size("row"), lax.axis_size("col")
    held, refs = refs[:row_size], refs[row_size:]
    if len(refs) > count:
        sent_ref, *outs, lines_ref = refs
        rows = sent_ref.shape[0] - part
        lines_ref[pl.ds(0, rows), :] = sent_ref[pl.ds(part, rows), :]
        lines_ref[pl.ds(rows, rows), :] = held[1][pl.ds(part, rows), :]
    else:
        outs = refs
    row_index, col_index = lax.axis_index("row"), lax.axis_index("col")
    for apart, out_ref in enumerate(outs):
        wanted = row_index ^ lax.rem(col_index + apart, count)
        for mask, ref in enumerate(held):

            @pl.when(wanted == mask)
            def _():
                out_ref[...] = ref[pl.ds(0, part), :]


def place_piece(panel_ref, rows, block, origin, count, size):
    for g in range(block.shape[1] // size):
        left = (g * count + origin) * size
        if not isinstance(origin, int):
            left = pl.multiple_of(left, size)
        panel_ref[rows, pl.ds(left, size)] = block[:, g * size:(g + 1) * size]


def factor_from(panel_ref, inverse_ref, out_ref, tile):
    rows, width = out_ref.shape
    for first in range(0, width, tile):
        out_ref[:, pl.ds(first, tile)] = lax.dot_general(
            panel_ref[pl.ds(0, rows), pl.ds(0, first + tile)],
            inverse_ref[pl.ds(0, first + tile), pl.ds(first, tile)],
            (((1,), (0,)), ((), ())),
            preferred_element_type=jnp.float32,
        ).astype(jnp.bfloat16)


def row_factor_kernel(places, origins, kinds, size, tile, inverse_ref, *refs):
    arrays, out_ref, panel_ref = refs[: len(kinds)], refs[-2], refs[-1]
    col_index = lax.axis_index("col")
    count = len(origins)
    rows = out_ref.shape[0]
    for slot in range(count):
        origin = looked_up(col_index, origins[slot])
        for kind, ref in zip(kinds, arrays):
            members = tuple(i for i in range(count) if places[slot][i] == kind)
            if members:

                @pl.when(among(col_index, members))
                def _():
                    for top in range(0, rows, size):
                        at = pl.ds(top, size)
                        place_piece(panel_ref, at, ref[at, :], origin, count, size)

    factor_from(panel_ref, inverse_ref, out_ref, tile)


def column_factor_kernel(size, tile, inverse_ref, *refs):
    parts, out_ref, panel_ref = refs[:-2], refs[-2], refs[-1]
    row_index, col_index = lax.axis_index("row"), lax.axis_index("col")
    count = lax.axis_size("col")
    part = parts[0].shape[0] // count
    for mask, ref in enumerate(parts):
        at = pl.ds(pl.multiple_of((row_index ^ mask) * part, ROW_TILE), part)
        for apart in range(count):
            origin = lax.rem(col_index + count - apart, count)
            place_piece(panel_ref, at, ref[pl.ds(apart * part, part), :], origin, count, size)
    factor_from(panel_ref, inverse_ref, out_ref, tile)


def product_kernel(mine, step, rows_ref, columns_ref, front_ref, *refs):
    out_hbm, out_ref, sems = refs[-3:]
    sub_index = lax.axis_index("sub")
    half = sub_index if mine else 1 - sub_index
    slot_count, _, size, _ = out_ref.shape
    copies = []
    for first in range(0, slot_count, step):
        blocks = min(step, slot_count - first)
        product = lax.dot_general(
            rows_ref[pl.ds(first * size, blocks * size), :], columns_ref[...], CONTRACT,
            preferred_element_type=jnp.float32,
        )
        for m in range(first, first + blocks):
            for a in range(slot_count):
                block = product[(m - first) * size:(m - first + 1) * size, a * size:(a + 1) * size]
                out_ref[m, a] = (front_ref[m, a, half].astype(jnp.float32) - block).astype(jnp.bfloat16)
            copies.append(pltpu.make_async_copy(out_ref.at[m], out_hbm.at[m, :, half], sems.at[m]))
            copies[-1].start()
    for copy in copies:
        copy.wait()


def body(front_entries, block_pattern, child_update, child_map, diag_inverse):
    slot_count = front_entries.shape[0]
    size = front_entries.shape[3]
    column_count = front_entries.shape[4]
    child_count = child_update.shape[1]
    row_size = lax.axis_size("row")
    col_size = lax.axis_size("col")
    groups = -(-(PANEL // size) // col_size)
    tile = PANEL // 2
    rows = slot_count * size
    part = -(-rows // (row_size * ROW_TILE)) * ROW_TILE
    padded = part * row_size
    depth = groups * col_size * size
    in_hbm = pl.BlockSpec(memory_space=pltpu.HBM)
    entries = front_entries.reshape(slot_count, size, column_count, size).transpose(0, 2, 1, 3)
    pattern = block_pattern.reshape(slot_count, 1, column_count)
    slots = child_map.transpose(0, 2, 1)
    own = child_update.reshape(child_count, size, child_count, size).transpose(0, 2, 1, 3)

    received = flipped(own, "sub", 1)
    shares = inverse_shares(diag_inverse)
    lanes = groups * size
    tiles = line_tiles(col_size, diag_inverse.shape[0], lanes) if shares else []
    line_rows = len(tiles) * shares[0].shape[0] if shares else 0
    piece, *parts = call(
        functools.partial(panel_kernel, part, groups),
        [bf16(padded, lanes)] + [bf16(part, lanes)] * row_size,
        [SCALARS, SCALARS] + [ON_CHIP] * 3,
    )(slots, pattern, entries[:, :groups], own, received)
    if shares:
        parts[1] = call(
            functools.partial(pack_kernel, part, tiles), bf16(part + line_rows, lanes), [ON_CHIP] * (1 + len(shares))
        )(parts[1], *shares)
        piece, *parts = fence(piece, *parts)

    _, origins, places = line_plan(col_size)
    pieces = Line(piece, "col")
    pieces.step()
    held = [parts[0]] + [flipped(parts[mask], "row", mask) for mask in range(1, row_size)]
    sent = parts[1:2] if shares else []
    turned = call(
        functools.partial(turn_kernel, part),
        [bf16(part, lanes)] * col_size + [bf16(2 * line_rows, lanes)] * len(sent),
        [ON_CHIP] * (row_size + len(sent)),
    )(*held, *sent)
    pieces.held[1], *turned = fence(pieces.held[1], *turned)
    near, sends, lines = turned[0], turned[1:col_size], list(turned[col_size:])
    if shares:
        for bit in range(1, row_size.bit_length() - 1):
            lines += [flipped(line, "row", 1 << bit) for line in lines]
    come = {apart: shifted(sends[apart - 1], "col", apart) for apart in reversed(far_last(col_size))}
    first = far_last(col_size)[-1]
    (come[first],) = pieces.fenced(come[first])
    turned = joined([near] + [come[apart] for apart in range(1, col_size)])
    if shares:
        lines = [joined(lines)]
    turned, *lines = fence(turned, *lines)
    if shares:
        lines += [flipped(line, "sub", 1) for line in lines]
        inverse = call(
            functools.partial(inverse_kernel, shares[0].shape[0], tiles),
            bf16(PANEL, PANEL), [ON_CHIP] * len(lines), moved=4 << 20,
            scratch_shapes=[pltpu.VMEM((PANEL, PANEL), jnp.bfloat16)],
        )(*lines)
    else:
        whole = lax.all_gather(diag_inverse, "col", axis=0, tiled=True)
        inverse = call(
            lower_kernel, bf16(PANEL, PANEL), [ON_CHIP], moved=4 << 20,
            scratch_shapes=[pltpu.VMEM((PANEL, PANEL), jnp.bfloat16)],
        )(whole)
    parts = [turned] + [flipped(turned, "row", mask) for mask in range(1, row_size)]
    while pieces.at < len(pieces.levels):
        pieces.step()
    front = call(
        functools.partial(front_kernel, groups),
        bf16(slot_count, column_count, size, size),
        [SCALARS, SCALARS] + [ON_CHIP] * 4,
        moved=6 << 20,
    )(slots, pattern, entries, own, received, piece)
    kinds, arrays = pieces.taken()
    scratch = [pltpu.VMEM((padded, depth), jnp.bfloat16)]
    flops = 2 * rows * PANEL * PANEL * 3 // 4
    row_factor = call(
        functools.partial(row_factor_kernel, places, origins, kinds, size, tile),
        bf16(rows, PANEL), [ON_CHIP] * (1 + len(arrays)), flops=flops, scratch_shapes=scratch,
    )(inverse, *arrays)
    row_factor, front, inverse, *parts = fence(row_factor, front, inverse, *parts)
    front = front.reshape(slot_count, slot_count, 2, size, size)

    column_factor = call(
        functools.partial(column_factor_kernel, size, tile),
        bf16(rows, PANEL), [ON_CHIP] * (1 + row_size), flops=flops, scratch_shapes=scratch,
    )(inverse, *parts)
    other_factor = flipped(column_factor, "sub", 1)
    product = functools.partial(
        call,
        out_shape=bf16(slot_count, slot_count, 2, size, size),
        flops=2 * rows * rows * PANEL,
        out_specs=in_hbm,
        scratch_shapes=[
            pltpu.VMEM((slot_count, slot_count, size, size), jnp.bfloat16),
            pltpu.SemaphoreType.DMA((slot_count,)),
        ],
    )
    trailing = product(functools.partial(product_kernel, True, (slot_count + 1) // 2), in_specs=[ON_CHIP] * 3)(
        row_factor, column_factor, front
    )
    trailing = product(
        functools.partial(product_kernel, False, slot_count), in_specs=[ON_CHIP] * 3 + [in_hbm],
        input_output_aliases={3: 0},
    )(row_factor, other_factor, front, trailing)
    return trailing.reshape(slot_count, column_count, size, size).transpose(0, 2, 1, 3).reshape(
        slot_count, 1, 1, size, column_count, 1, size
    )


def solution(mesh):
    return jax.shard_map(
        body,
        mesh=mesh,
        in_specs=(
            P(None, "sub", "row", None, None, "col", None),
            P(None, "sub", "row", None, "col"),
            P("sub", None, "row", None, None, "col", None),
            P(),
            P("col", None),
        ),
        out_specs=P(None, "sub", "row", None, None, "col", None),
        check_vma=False,
    )
```

```python
import functools

import jax
import jax.numpy as jnp
from jax import lax
from jax.experimental import pallas as pl
from jax.experimental.pallas import tpu as pltpu
from jax.sharding import PartitionSpec as P

PANEL = 1024
ROW_TILE = 16
VMEM_BYTES = 12 * 1024 * 1024
CONTRACT = (((1,), (1,)), ((), ()))
ON_CHIP = pl.BlockSpec(memory_space=pltpu.VMEM)
SCALARS = pl.BlockSpec(memory_space=pltpu.SMEM)


def call(kernel, out_shape, in_specs, flops=0, moved=1 << 19, **more):
    single = not isinstance(out_shape, (list, tuple))
    return pl.pallas_call(
        kernel,
        out_shape=out_shape,
        in_specs=in_specs,
        out_specs=more.pop("out_specs", ON_CHIP if single else [ON_CHIP] * len(out_shape)),
        compiler_params=pltpu.CompilerParams(vmem_limit_bytes=VMEM_BYTES),
        cost_estimate=pl.CostEstimate(flops=flops, bytes_accessed=moved, transcendentals=0),
        **more,
    )


def bf16(*shape):
    return jax.ShapeDtypeStruct(shape, jnp.bfloat16)


def f32(*shape):
    return jax.ShapeDtypeStruct(shape, jnp.float32)


def flipped(block, axis, mask):
    count = lax.axis_size(axis)
    return lax.ppermute(block, axis, [(i, i ^ mask) for i in range(count)])


def shifted(block, axis, apart):
    count = lax.axis_size(axis)
    return lax.ppermute(block, axis, [(i, (i + apart) % count) for i in range(count)])


def far_last(count):
    return sorted(range(1, count), key=lambda apart: (min(apart, count - apart), apart))


def swap_even(i, count):
    return i ^ 1 if i ^ 1 < count else i


def swap_odd(i, count):
    j = ((i + 1) ^ 1) - 1
    return j if 0 <= j < count else i


@functools.cache
def line_plan(count):
    even = [swap_even(i, count) for i in range(count)]
    odd = [swap_odd(i, count) for i in range(count)]
    if count == 4:
        levels = [[(1, 0, even), (2, 0, odd)], [(3, 2, [2, 0, 3, 1]), (4, 1, [1, 3, 0, 2])]]
    else:
        levels, last = [], [0, 0]
        for step in range(count - 1):
            level = []
            for stream in (0, 1):
                level.append((1 + 2 * step + stream, last[stream], odd if (step + stream) % 2 else even))
                last[stream] = level[-1][0]
            levels.append(level)
    whose = {0: list(range(count))}
    seen = [[(0, i)] for i in range(count)]
    for level in levels:
        for array, source, to in level:
            whose[array] = [None] * count
            for i in range(count):
                whose[array][to[i]] = whose[source][i]
            for i in range(count):
                if all(whose[array][i] != origin for _, origin in seen[i]):
                    seen[i].append((array, whose[array][i]))
    origins = [[seen[i][j][1] for i in range(count)] for j in range(count)]
    places = [[seen[i][j][0] for i in range(count)] for j in range(count)]
    return levels, origins, places


class Line:
    def __init__(self, block, axis):
        self.axis = axis
        self.levels, _, self.places = line_plan(lax.axis_size(axis))
        self.held = {0: block}
        self.at = 0

    def step(self):
        for array, source, to in self.levels[self.at]:
            self.held[array] = lax.ppermute(self.held[source], self.axis, list(enumerate(to)))
        self.at += 1
        return self.at < len(self.levels)

    def fenced(self, *values):
        last = [array for array, _, _ in self.levels[self.at - 1]]
        out = fence(*values, *(self.held[array] for array in last))
        self.held.update(zip(last, out[len(values):]))
        return out[: len(values)]

    def taken(self):
        kinds = sorted({kind for row in self.places for kind in row})
        return kinds, [self.held[kind] for kind in kinds]


def among(index, members):
    found = index == members[0]
    for member in members[1:]:
        found = jnp.logical_or(found, index == member)
    return found


def looked_up(index, table):
    value = jnp.int32(table[0])
    for i, entry in enumerate(table[1:], 1):
        value = jnp.where(index == i, jnp.int32(entry), value)
    return value


def fence_kernel(*refs):
    pass


def fence(*values):
    place = pl.BlockSpec(memory_space=pl.ANY)
    return pl.pallas_call(
        fence_kernel,
        out_shape=[jax.ShapeDtypeStruct(v.shape, v.dtype) for v in values],
        in_specs=[place] * len(values),
        out_specs=[place] * len(values),
        input_output_aliases={n: n for n in range(len(values))},
        compiler_params=pltpu.CompilerParams(vmem_limit_bytes=1 << 20),
    )(*values)


def found_at(map_ref, child, place, wanted, child_count):
    at = jnp.int32(0)
    found = jnp.float32(0)
    for k in range(child_count):
        same = map_ref[child, place, k] == wanted
        at = jnp.where(same, jnp.int32(k), at)
        found = jnp.where(same, jnp.float32(1), found)
    return at, found


def block_places(map_ref, child, columns, slot_count, child_count):
    sub_index, row_index, col_index = (lax.axis_index(name) for name in ("sub", "row", "col"))
    rows = [
        found_at(map_ref, child, row_index, 2 * a + sub_index, child_count) for a in range(slot_count)
    ]
    cols = [found_at(map_ref, child, col_index, b, child_count) for b in columns]
    return rows, cols


def child_block(ref, row, col):
    return ref[row[0], col[0]].astype(jnp.float32) * (row[1] * col[1])


def line_tiles(count, share, lanes):
    return [(col, tile) for col in range(count) for tile in range(-(-(col + 1) * share // lanes))]


def pack_line(share_refs, out_ref, first, tiles):
    col_index = lax.axis_index("col")
    count = len(share_refs)
    rows, lanes = share_refs[0].shape[0], out_ref.shape[1]
    for apart, ref in zip([0, *far_last(count)], share_refs):
        for col in range(count):

            @pl.when(lax.rem(col_index + count - apart, count) == col)
            def _():
                for n, (home, tile) in enumerate(tiles):
                    if home == col:
                        out_ref[pl.ds(first + n * rows, rows), :] = ref[:, tile * lanes:(tile + 1) * lanes]


def pack_kernel(part, tiles, *refs):
    part_ref, *share_refs, out_ref = refs
    out_ref[pl.ds(0, part), :] = part_ref[...]
    pack_line(share_refs, out_ref, part, tiles)


def panel_kernel(part, groups, map_ref, pattern_ref, entries_ref, own_ref, received_ref, piece_ref, *part_refs):
    slot_count, _, size, _ = entries_ref.shape
    child_count = own_ref.shape[0]
    sub_index, row_index = lax.axis_index("sub"), lax.axis_index("row")
    places = [
        block_places(map_ref, child, range(groups), slot_count, child_count)
        for child in (sub_index, 1 - sub_index)
    ]
    for a in range(slot_count):
        for b in range(groups):
            total = entries_ref[a, b].astype(jnp.float32) * pattern_ref[a, 0, b].astype(jnp.float32)
            for (rows, cols), ref in zip(places, (own_ref, received_ref)):
                total = total + child_block(ref, rows[a], cols[b])
            piece_ref[pl.ds(a * size, size), pl.ds(b * size, size)] = total.astype(jnp.bfloat16)
    used = slot_count * size
    if used < piece_ref.shape[0]:
        piece_ref[pl.ds(used, piece_ref.shape[0] - used), :] = jnp.zeros(
            (piece_ref.shape[0] - used, piece_ref.shape[1]), piece_ref.dtype
        )
    for mask, ref in enumerate(part_refs):
        ref[...] = piece_ref[pl.ds(pl.multiple_of((row_index ^ mask) * part, ROW_TILE), part), :]


def front_kernel(groups, map_ref, pattern_ref, entries_ref, own_ref, received_ref, piece_ref, out_ref):
    slot_count, column_count, size, _ = entries_ref.shape
    child_count = own_ref.shape[0]
    sub_index = lax.axis_index("sub")
    columns = range(groups, column_count)
    places = [
        block_places(map_ref, child, columns, slot_count, child_count)
        for child in (sub_index, 1 - sub_index)
    ]
    for a in range(slot_count):
        for b in range(groups):
            out_ref[a, b] = piece_ref[pl.ds(a * size, size), pl.ds(b * size, size)]
        for n, b in enumerate(columns):
            total = entries_ref[a, b].astype(jnp.float32) * pattern_ref[a, 0, b].astype(jnp.float32)
            for (rows, cols), ref in zip(places, (own_ref, received_ref)):
                total = total + child_block(ref, rows[a], cols[n])
            out_ref[a, b] = total.astype(jnp.bfloat16)


def inverse_kernel(rows, tiles, *refs):
    *in_refs, turned_ref, out_ref = refs
    sub_index, row_index = lax.axis_index("sub"), lax.axis_index("row")
    sub_size, row_size, col_size = (lax.axis_size(name) for name in ("sub", "row", "col"))
    width = out_ref.shape[0]
    lanes = in_refs[0].shape[1]
    share = width // col_size
    lines = [
        (ref, line * len(tiles) * rows) for ref in in_refs for line in range(row_size)
    ]
    for n, (ref, first) in enumerate(lines):
        sub_at = sub_index if n < row_size else 1 - sub_index
        inside = (sub_at * row_size + (row_index ^ (n % row_size))) * rows
        for m, (col, tile) in enumerate(tiles):
            top = pl.multiple_of(col * share + inside, ROW_TILE)
            block = ref[pl.ds(first + m * rows, rows), :]
            if (tile + 1) * lanes > col * share:
                row_at = top + lax.broadcasted_iota(jnp.int32, block.shape, 0)
                col_at = tile * lanes + lax.broadcasted_iota(jnp.int32, block.shape, 1)
                block = jnp.where(col_at <= row_at, block.astype(jnp.float32), 0.0).astype(jnp.bfloat16)
            out_ref[pl.ds(top, rows), pl.ds(tile * lanes, lanes)] = block
    for col in range(col_size):
        for tile in range(width // lanes):
            if (col, tile) not in tiles:
                out_ref[pl.ds(col * share, share), pl.ds(tile * lanes, lanes)] = jnp.zeros(
                    (share, lanes), out_ref.dtype
                )
    turn_over(out_ref, turned_ref)


def turn_over(in_ref, out_ref, tile=256):
    for top in range(0, in_ref.shape[0], tile):
        for left in range(0, in_ref.shape[1], tile):
            out_ref[pl.ds(left, tile), pl.ds(top, tile)] = in_ref[pl.ds(top, tile), pl.ds(left, tile)].T


def lower_kernel(in_ref, turned_ref, out_ref):
    row_at = lax.broadcasted_iota(jnp.int32, in_ref.shape, 0)
    col_at = lax.broadcasted_iota(jnp.int32, in_ref.shape, 1)
    out_ref[...] = jnp.where(col_at <= row_at, in_ref[...].astype(jnp.float32), 0.0).astype(jnp.bfloat16)
    turn_over(out_ref, turned_ref)


def join_kernel(*refs):
    *in_refs, out_ref = refs
    rows = in_refs[0].shape[0]
    for n, ref in enumerate(in_refs):
        out_ref[pl.ds(n * rows, rows), :] = ref[...]


def joined(blocks):
    rows, width = blocks[0].shape
    return call(join_kernel, bf16(rows * len(blocks), width), [ON_CHIP] * len(blocks))(*blocks)


def inverse_shares(diag_inverse):
    part = diag_inverse.shape[0] // (lax.axis_size("sub") * lax.axis_size("row"))
    if part % ROW_TILE:
        return []
    first = (lax.axis_index("sub") * lax.axis_size("row") + lax.axis_index("row")) * part
    mine = lax.dynamic_slice_in_dim(diag_inverse, first, part, 0)
    return [mine] + [shifted(mine, "col", apart) for apart in far_last(lax.axis_size("col"))]


def turn_kernel(part, *refs):
    row_size, count = lax.axis_size("row"), lax.axis_size("col")
    held, refs = refs[:row_size], refs[row_size:]
    if len(refs) > count:
        sent_ref, *outs, lines_ref = refs
        rows = sent_ref.shape[0] - part
        lines_ref[pl.ds(0, rows), :] = sent_ref[pl.ds(part, rows), :]
        lines_ref[pl.ds(rows, rows), :] = held[1][pl.ds(part, rows), :]
    else:
        outs = refs
    row_index, col_index = lax.axis_index("row"), lax.axis_index("col")
    for apart, out_ref in enumerate(outs):
        wanted = row_index ^ lax.rem(col_index + apart, count)
        for mask, ref in enumerate(held):

            @pl.when(wanted == mask)
            def _():
                out_ref[...] = ref[pl.ds(0, part), :]


def place_piece(panel_ref, rows, block, origin, count, size):
    for g in range(block.shape[1] // size):
        left = (g * count + origin) * size
        if not isinstance(origin, int):
            left = pl.multiple_of(left, size)
        panel_ref[rows, pl.ds(left, size)] = block[:, g * size:(g + 1) * size]


def factor_from(panel_ref, inverse_ref, out_ref, tile):
    rows, width = out_ref.shape
    for first in range(0, width, tile):
        out_ref[:, pl.ds(first, tile)] = lax.dot_general(
            panel_ref[pl.ds(0, rows), pl.ds(0, first + tile)],
            inverse_ref[pl.ds(0, first + tile), pl.ds(first, tile)],
            (((1,), (0,)), ((), ())),
            preferred_element_type=jnp.float32,
        ).astype(jnp.bfloat16)


def row_factor_kernel(places, origins, kinds, size, tile, inverse_ref, *refs):
    arrays, out_ref, panel_ref = refs[: len(kinds)], refs[-2], refs[-1]
    col_index = lax.axis_index("col")
    count = len(origins)
    rows = out_ref.shape[0]
    for slot in range(count):
        origin = looked_up(col_index, origins[slot])
        for kind, ref in zip(kinds, arrays):
            members = tuple(i for i in range(count) if places[slot][i] == kind)
            if members:

                @pl.when(among(col_index, members))
                def _():
                    for top in range(0, rows, size):
                        at = pl.ds(top, size)
                        place_piece(panel_ref, at, ref[at, :], origin, count, size)

    factor_from(panel_ref, inverse_ref, out_ref, tile)


def column_factor_kernel(size, count, inverse_ref, *refs):
    parts, outs, panel_ref = refs[: -1 - count], refs[-1 - count:-1], refs[-1]
    row_index, col_index = lax.axis_index("row"), lax.axis_index("col")
    col_size = lax.axis_size("col")
    part = parts[0].shape[0] // col_size
    rows, tile = outs[0].shape
    for mask, ref in enumerate(parts):
        at = pl.ds(pl.multiple_of((row_index ^ mask) * part, ROW_TILE), part)
        for apart in range(col_size):
            origin = lax.rem(col_index + col_size - apart, col_size)
            place_piece(panel_ref, at, ref[pl.ds(apart * part, part), :], origin, col_size, size)
    for n, out_ref in enumerate(outs):
        first = n * tile
        out_ref[...] = lax.dot_general(
            panel_ref[pl.ds(0, rows), pl.ds(0, first + tile)],
            inverse_ref[pl.ds(0, first + tile), pl.ds(first, tile)],
            (((1,), (0,)), ((), ())),
            preferred_element_type=jnp.float32,
        ).astype(jnp.bfloat16)


def product_kernel(mine, halves, rows_ref, front_ref, *refs):
    columns_refs = refs[:halves]
    out_hbm, out_ref, sems = refs[-3:]
    sub_index = lax.axis_index("sub")
    half = sub_index if mine else 1 - sub_index
    slot_count, _, size, _ = out_ref.shape
    copies = []
    product = None
    for n, ref in enumerate(columns_refs):
        width = ref.shape[1]
        share = lax.dot_general(
            rows_ref[:, pl.ds(n * width, width)], ref[...], CONTRACT, preferred_element_type=jnp.float32
        )
        product = share if product is None else product + share
    for m in range(slot_count):
        for a in range(slot_count):
            block = product[m * size:(m + 1) * size, a * size:(a + 1) * size]
            out_ref[m, a] = (front_ref[m, a, half].astype(jnp.float32) - block).astype(jnp.bfloat16)
        copies.append(pltpu.make_async_copy(out_ref.at[m], out_hbm.at[m, :, half], sems.at[m]))
        copies[-1].start()
    for copy in copies:
        copy.wait()


def body(front_entries, block_pattern, child_update, child_map, diag_inverse):
    slot_count = front_entries.shape[0]
    size = front_entries.shape[3]
    column_count = front_entries.shape[4]
    child_count = child_update.shape[1]
    row_size = lax.axis_size("row")
    col_size = lax.axis_size("col")
    groups = -(-(PANEL // size) // col_size)
    tile = PANEL // 2
    rows = slot_count * size
    part = -(-rows // (row_size * ROW_TILE)) * ROW_TILE
    padded = part * row_size
    depth = groups * col_size * size
    in_hbm = pl.BlockSpec(memory_space=pltpu.HBM)
    entries = front_entries.reshape(slot_count, size, column_count, size).transpose(0, 2, 1, 3)
    pattern = block_pattern.reshape(slot_count, 1, column_count)
    slots = child_map.transpose(0, 2, 1)
    own = child_update.reshape(child_count, size, child_count, size).transpose(0, 2, 1, 3)

    received = flipped(own, "sub", 1)
    shares = inverse_shares(diag_inverse)
    lanes = groups * size
    tiles = line_tiles(col_size, diag_inverse.shape[0], lanes) if shares else []
    line_rows = len(tiles) * shares[0].shape[0] if shares else 0
    piece, *parts = call(
        functools.partial(panel_kernel, part, groups),
        [bf16(padded, lanes)] + [bf16(part, lanes)] * row_size,
        [SCALARS, SCALARS] + [ON_CHIP] * 3,
    )(slots, pattern, entries[:, :groups], own, received)
    if shares:
        parts[1] = call(
            functools.partial(pack_kernel, part, tiles), bf16(part + line_rows, lanes), [ON_CHIP] * (1 + len(shares))
        )(parts[1], *shares)
        piece, *parts = fence(piece, *parts)

    _, origins, places = line_plan(col_size)
    pieces = Line(piece, "col")
    pieces.step()
    held = [parts[0]] + [flipped(parts[mask], "row", mask) for mask in range(1, row_size)]
    sent = parts[1:2] if shares else []
    turned = call(
        functools.partial(turn_kernel, part),
        [bf16(part, lanes)] * col_size + [bf16(2 * line_rows, lanes)] * len(sent),
        [ON_CHIP] * (row_size + len(sent)),
    )(*held, *sent)
    pieces.held[1], *turned = fence(pieces.held[1], *turned)
    near, sends, lines = turned[0], turned[1:col_size], list(turned[col_size:])
    if shares:
        for bit in range(1, row_size.bit_length() - 1):
            lines += [flipped(line, "row", 1 << bit) for line in lines]
    come = {apart: shifted(sends[apart - 1], "col", apart) for apart in reversed(far_last(col_size))}
    first = far_last(col_size)[-1]
    (come[first],) = pieces.fenced(come[first])
    turned = joined([near] + [come[apart] for apart in range(1, col_size)])
    if shares:
        lines = [joined(lines)]
    turned, *lines = fence(turned, *lines)
    if shares:
        lines += [flipped(line, "sub", 1) for line in lines]
        inverse = call(
            functools.partial(inverse_kernel, shares[0].shape[0], tiles),
            bf16(PANEL, PANEL), [ON_CHIP] * len(lines), moved=4 << 20,
            scratch_shapes=[pltpu.VMEM((PANEL, PANEL), jnp.bfloat16)],
        )(*lines)
    else:
        whole = lax.all_gather(diag_inverse, "col", axis=0, tiled=True)
        inverse = call(
            lower_kernel, bf16(PANEL, PANEL), [ON_CHIP], moved=4 << 20,
            scratch_shapes=[pltpu.VMEM((PANEL, PANEL), jnp.bfloat16)],
        )(whole)
    parts = [turned] + [flipped(turned, "row", mask) for mask in range(1, row_size)]
    while pieces.at < len(pieces.levels):
        pieces.step()
    front = call(
        functools.partial(front_kernel, groups),
        bf16(slot_count, column_count, size, size),
        [SCALARS, SCALARS] + [ON_CHIP] * 4,
        moved=6 << 20,
    )(slots, pattern, entries, own, received, piece)
    kinds, arrays = pieces.taken()
    scratch = [pltpu.VMEM((padded, depth), jnp.bfloat16)]
    flops = 2 * rows * PANEL * PANEL * 3 // 4
    row_factor = call(
        functools.partial(row_factor_kernel, places, origins, kinds, size, tile),
        bf16(rows, PANEL), [ON_CHIP] * (1 + len(arrays)), flops=flops, scratch_shapes=scratch,
    )(inverse, *arrays)
    row_factor, front, inverse, *parts = fence(row_factor, front, inverse, *parts)
    front = front.reshape(slot_count, slot_count, 2, size, size)

    halves = PANEL // tile
    column_factor = call(
        functools.partial(column_factor_kernel, size, halves),
        [bf16(rows, tile)] * halves, [ON_CHIP] * (1 + row_size), flops=flops, scratch_shapes=scratch,
    )(inverse, *parts)
    other_factor = [flipped(share, "sub", 1) for share in column_factor]
    product = functools.partial(
        call,
        out_shape=bf16(slot_count, slot_count, 2, size, size),
        flops=2 * rows * rows * PANEL,
        out_specs=in_hbm,
        scratch_shapes=[
            pltpu.VMEM((slot_count, slot_count, size, size), jnp.bfloat16),
            pltpu.SemaphoreType.DMA((slot_count,)),
        ],
    )
    trailing = product(
        functools.partial(product_kernel, True, halves), in_specs=[ON_CHIP] * (2 + halves)
    )(row_factor, front, *column_factor)
    trailing = product(
        functools.partial(product_kernel, False, halves), in_specs=[ON_CHIP] * (2 + halves) + [in_hbm],
        input_output_aliases={2 + halves: 0},
    )(row_factor, front, *other_factor, trailing)
    return trailing.reshape(slot_count, column_count, size, size).transpose(0, 2, 1, 3).reshape(
        slot_count, 1, 1, size, column_count, 1, size
    )


def solution(mesh):
    return jax.shard_map(
        body,
        mesh=mesh,
        in_specs=(
            P(None, "sub", "row", None, None, "col", None),
            P(None, "sub", "row", None, "col"),
            P("sub", None, "row", None, None, "col", None),
            P(),
            P("col", None),
        ),
        out_specs=P(None, "sub", "row", None, None, "col", None),
        check_vma=False,
    )
```

```python
import functools

import jax
import jax.numpy as jnp
from jax import lax
from jax.experimental import pallas as pl
from jax.experimental.pallas import tpu as pltpu
from jax.sharding import PartitionSpec as P

PANEL = 1024
ROW_TILE = 16
VMEM_BYTES = 12 * 1024 * 1024
CONTRACT = (((1,), (1,)), ((), ()))
ON_CHIP = pl.BlockSpec(memory_space=pltpu.VMEM)
SCALARS = pl.BlockSpec(memory_space=pltpu.SMEM)


def call(kernel, out_shape, in_specs, flops=0, moved=1 << 19, **more):
    single = not isinstance(out_shape, (list, tuple))
    return pl.pallas_call(
        kernel,
        out_shape=out_shape,
        in_specs=in_specs,
        out_specs=more.pop("out_specs", ON_CHIP if single else [ON_CHIP] * len(out_shape)),
        compiler_params=pltpu.CompilerParams(vmem_limit_bytes=VMEM_BYTES),
        cost_estimate=pl.CostEstimate(flops=flops, bytes_accessed=moved, transcendentals=0),
        **more,
    )


def bf16(*shape):
    return jax.ShapeDtypeStruct(shape, jnp.bfloat16)


def f32(*shape):
    return jax.ShapeDtypeStruct(shape, jnp.float32)


def flipped(block, axis, mask):
    count = lax.axis_size(axis)
    return lax.ppermute(block, axis, [(i, i ^ mask) for i in range(count)])


def shifted(block, axis, apart):
    count = lax.axis_size(axis)
    return lax.ppermute(block, axis, [(i, (i + apart) % count) for i in range(count)])


def far_last(count):
    return sorted(range(1, count), key=lambda apart: (min(apart, count - apart), apart))


def swap_even(i, count):
    return i ^ 1 if i ^ 1 < count else i


def swap_odd(i, count):
    j = ((i + 1) ^ 1) - 1
    return j if 0 <= j < count else i


@functools.cache
def line_plan(count):
    even = [swap_even(i, count) for i in range(count)]
    odd = [swap_odd(i, count) for i in range(count)]
    if count == 4:
        levels = [[(1, 0, even), (2, 0, odd)], [(3, 2, [2, 0, 3, 1]), (4, 1, [1, 3, 0, 2])]]
    else:
        levels, last = [], [0, 0]
        for step in range(count - 1):
            level = []
            for stream in (0, 1):
                level.append((1 + 2 * step + stream, last[stream], odd if (step + stream) % 2 else even))
                last[stream] = level[-1][0]
            levels.append(level)
    whose = {0: list(range(count))}
    seen = [[(0, i)] for i in range(count)]
    for level in levels:
        for array, source, to in level:
            whose[array] = [None] * count
            for i in range(count):
                whose[array][to[i]] = whose[source][i]
            for i in range(count):
                if all(whose[array][i] != origin for _, origin in seen[i]):
                    seen[i].append((array, whose[array][i]))
    origins = [[seen[i][j][1] for i in range(count)] for j in range(count)]
    places = [[seen[i][j][0] for i in range(count)] for j in range(count)]
    return levels, origins, places


class Line:
    def __init__(self, block, axis):
        self.axis = axis
        self.levels, _, self.places = line_plan(lax.axis_size(axis))
        self.held = {0: block}
        self.at = 0

    def step(self):
        for array, source, to in self.levels[self.at]:
            self.held[array] = lax.ppermute(self.held[source], self.axis, list(enumerate(to)))
        self.at += 1
        return self.at < len(self.levels)

    def fenced(self, *values):
        last = [array for array, _, _ in self.levels[self.at - 1]]
        out = fence(*values, *(self.held[array] for array in last))
        self.held.update(zip(last, out[len(values):]))
        return out[: len(values)]

    def taken(self):
        kinds = sorted({kind for row in self.places for kind in row})
        return kinds, [self.held[kind] for kind in kinds]


def among(index, members):
    found = index == members[0]
    for member in members[1:]:
        found = jnp.logical_or(found, index == member)
    return found


def looked_up(index, table):
    value = jnp.int32(table[0])
    for i, entry in enumerate(table[1:], 1):
        value = jnp.where(index == i, jnp.int32(entry), value)
    return value


def fence_kernel(*refs):
    pass


def fence(*values):
    place = pl.BlockSpec(memory_space=pl.ANY)
    return pl.pallas_call(
        fence_kernel,
        out_shape=[jax.ShapeDtypeStruct(v.shape, v.dtype) for v in values],
        in_specs=[place] * len(values),
        out_specs=[place] * len(values),
        input_output_aliases={n: n for n in range(len(values))},
        compiler_params=pltpu.CompilerParams(vmem_limit_bytes=1 << 20),
    )(*values)


def found_at(map_ref, child, place, wanted, child_count):
    at = jnp.int32(0)
    found = jnp.float32(0)
    for k in range(child_count):
        same = map_ref[child, place, k] == wanted
        at = jnp.where(same, jnp.int32(k), at)
        found = jnp.where(same, jnp.float32(1), found)
    return at, found


def block_places(map_ref, child, columns, slot_count, child_count):
    sub_index, row_index, col_index = (lax.axis_index(name) for name in ("sub", "row", "col"))
    rows = [
        found_at(map_ref, child, row_index, 2 * a + sub_index, child_count) for a in range(slot_count)
    ]
    cols = [found_at(map_ref, child, col_index, b, child_count) for b in columns]
    return rows, cols


def child_block(ref, row, col):
    return ref[row[0], col[0]].astype(jnp.float32) * (row[1] * col[1])


def line_tiles(count, share, lanes):
    return [(col, tile) for col in range(count) for tile in range(-(-(col + 1) * share // lanes))]


def pack_line(share_refs, out_ref, first, tiles):
    col_index = lax.axis_index("col")
    count = len(share_refs)
    rows, lanes = share_refs[0].shape[0], out_ref.shape[1]
    for apart, ref in zip([0, *far_last(count)], share_refs):
        for col in range(count):

            @pl.when(lax.rem(col_index + count - apart, count) == col)
            def _():
                for n, (home, tile) in enumerate(tiles):
                    if home == col:
                        out_ref[pl.ds(first + n * rows, rows), :] = ref[:, tile * lanes:(tile + 1) * lanes]


def pack_kernel(part, tiles, *refs):
    part_ref, *share_refs, out_ref = refs
    out_ref[pl.ds(0, part), :] = part_ref[...]
    pack_line(share_refs, out_ref, part, tiles)


def panel_kernel(part, groups, map_ref, pattern_ref, entries_ref, own_ref, received_ref, piece_ref, *part_refs):
    slot_count, _, size, _ = entries_ref.shape
    child_count = own_ref.shape[0]
    sub_index, row_index = lax.axis_index("sub"), lax.axis_index("row")
    places = [
        block_places(map_ref, child, range(groups), slot_count, child_count)
        for child in (sub_index, 1 - sub_index)
    ]
    for a in range(slot_count):
        for b in range(groups):
            total = entries_ref[a, b].astype(jnp.float32) * pattern_ref[a, 0, b].astype(jnp.float32)
            for (rows, cols), ref in zip(places, (own_ref, received_ref)):
                total = total + child_block(ref, rows[a], cols[b])
            piece_ref[pl.ds(a * size, size), pl.ds(b * size, size)] = total.astype(jnp.bfloat16)
    used = slot_count * size
    if used < piece_ref.shape[0]:
        piece_ref[pl.ds(used, piece_ref.shape[0] - used), :] = jnp.zeros(
            (piece_ref.shape[0] - used, piece_ref.shape[1]), piece_ref.dtype
        )
    for mask, ref in enumerate(part_refs):
        ref[...] = piece_ref[pl.ds(pl.multiple_of((row_index ^ mask) * part, ROW_TILE), part), :]


def front_kernel(groups, map_ref, pattern_ref, entries_ref, own_ref, received_ref, piece_ref, out_ref):
    slot_count, column_count, size, _ = entries_ref.shape
    child_count = own_ref.shape[0]
    sub_index = lax.axis_index("sub")
    columns = range(groups, column_count)
    places = [
        block_places(map_ref, child, columns, slot_count, child_count)
        for child in (sub_index, 1 - sub_index)
    ]
    for a in range(slot_count):
        for b in range(groups):
            out_ref[a, b] = piece_ref[pl.ds(a * size, size), pl.ds(b * size, size)]
        for n, b in enumerate(columns):
            total = entries_ref[a, b].astype(jnp.float32) * pattern_ref[a, 0, b].astype(jnp.float32)
            for (rows, cols), ref in zip(places, (own_ref, received_ref)):
                total = total + child_block(ref, rows[a], cols[n])
            out_ref[a, b] = total.astype(jnp.bfloat16)


def inverse_kernel(rows, tiles, *refs):
    *in_refs, turned_ref, out_ref = refs
    sub_index, row_index = lax.axis_index("sub"), lax.axis_index("row")
    sub_size, row_size, col_size = (lax.axis_size(name) for name in ("sub", "row", "col"))
    width = out_ref.shape[0]
    lanes = in_refs[0].shape[1]
    share = width // col_size
    lines = [
        (ref, line * len(tiles) * rows) for ref in in_refs for line in range(row_size)
    ]
    for n, (ref, first) in enumerate(lines):
        sub_at = sub_index if n < row_size else 1 - sub_index
        inside = (sub_at * row_size + (row_index ^ (n % row_size))) * rows
        for m, (col, tile) in enumerate(tiles):
            top = pl.multiple_of(col * share + inside, ROW_TILE)
            block = ref[pl.ds(first + m * rows, rows), :]
            if (tile + 1) * lanes > col * share:
                row_at = top + lax.broadcasted_iota(jnp.int32, block.shape, 0)
                col_at = tile * lanes + lax.broadcasted_iota(jnp.int32, block.shape, 1)
                block = jnp.where(col_at <= row_at, block.astype(jnp.float32), 0.0).astype(jnp.bfloat16)
            out_ref[pl.ds(top, rows), pl.ds(tile * lanes, lanes)] = block
    for col in range(col_size):
        for tile in range(width // lanes):
            if (col, tile) not in tiles:
                out_ref[pl.ds(col * share, share), pl.ds(tile * lanes, lanes)] = jnp.zeros(
                    (share, lanes), out_ref.dtype
                )
    turn_over(out_ref, turned_ref)


def turn_over(in_ref, out_ref, tile=256):
    for top in range(0, in_ref.shape[0], tile):
        for left in range(0, in_ref.shape[1], tile):
            out_ref[pl.ds(left, tile), pl.ds(top, tile)] = in_ref[pl.ds(top, tile), pl.ds(left, tile)].T


def lower_kernel(in_ref, turned_ref, out_ref):
    row_at = lax.broadcasted_iota(jnp.int32, in_ref.shape, 0)
    col_at = lax.broadcasted_iota(jnp.int32, in_ref.shape, 1)
    out_ref[...] = jnp.where(col_at <= row_at, in_ref[...].astype(jnp.float32), 0.0).astype(jnp.bfloat16)
    turn_over(out_ref, turned_ref)


def join_kernel(*refs):
    *in_refs, out_ref = refs
    rows = in_refs[0].shape[0]
    for n, ref in enumerate(in_refs):
        out_ref[pl.ds(n * rows, rows), :] = ref[...]


def joined(blocks):
    rows, width = blocks[0].shape
    return call(join_kernel, bf16(rows * len(blocks), width), [ON_CHIP] * len(blocks))(*blocks)


def inverse_shares(diag_inverse):
    part = diag_inverse.shape[0] // (lax.axis_size("sub") * lax.axis_size("row"))
    if part % ROW_TILE:
        return []
    first = (lax.axis_index("sub") * lax.axis_size("row") + lax.axis_index("row")) * part
    mine = lax.dynamic_slice_in_dim(diag_inverse, first, part, 0)
    return [mine] + [shifted(mine, "col", apart) for apart in far_last(lax.axis_size("col"))]


def turn_kernel(part, *refs):
    row_size, count = lax.axis_size("row"), lax.axis_size("col")
    held, refs = refs[:row_size], refs[row_size:]
    if len(refs) > count:
        sent_ref, *outs, lines_ref = refs
        rows = sent_ref.shape[0] - part
        lines_ref[pl.ds(0, rows), :] = sent_ref[pl.ds(part, rows), :]
        lines_ref[pl.ds(rows, rows), :] = held[1][pl.ds(part, rows), :]
    else:
        outs = refs
    row_index, col_index = lax.axis_index("row"), lax.axis_index("col")
    for apart, out_ref in enumerate(outs):
        wanted = row_index ^ lax.rem(col_index + apart, count)
        for mask, ref in enumerate(held):

            @pl.when(wanted == mask)
            def _():
                out_ref[...] = ref[pl.ds(0, part), :]


def place_piece(panel_ref, rows, block, origin, count, size):
    for g in range(block.shape[1] // size):
        left = (g * count + origin) * size
        if not isinstance(origin, int):
            left = pl.multiple_of(left, size)
        panel_ref[rows, pl.ds(left, size)] = block[:, g * size:(g + 1) * size]


def factor_from(panel_ref, inverse_ref, out_ref, tile):
    rows, width = out_ref.shape
    for first in range(0, width, tile):
        out_ref[:, pl.ds(first, tile)] = lax.dot_general(
            panel_ref[pl.ds(0, rows), pl.ds(0, first + tile)],
            inverse_ref[pl.ds(0, first + tile), pl.ds(first, tile)],
            (((1,), (0,)), ((), ())),
            preferred_element_type=jnp.float32,
        ).astype(jnp.bfloat16)


def row_factor_kernel(places, origins, kinds, size, tile, inverse_ref, *refs):
    arrays, out_ref, panel_ref = refs[: len(kinds)], refs[-2], refs[-1]
    col_index = lax.axis_index("col")
    count = len(origins)
    rows = out_ref.shape[0]
    for slot in range(count):
        origin = looked_up(col_index, origins[slot])
        for kind, ref in zip(kinds, arrays):
            members = tuple(i for i in range(count) if places[slot][i] == kind)
            if members:

                @pl.when(among(col_index, members))
                def _():
                    for top in range(0, rows, size):
                        at = pl.ds(top, size)
                        place_piece(panel_ref, at, ref[at, :], origin, count, size)

    factor_from(panel_ref, inverse_ref, out_ref, tile)


def column_factor_kernel(size, tile, first, inverse_ref, *refs):
    row_index, col_index = lax.axis_index("row"), lax.axis_index("col")
    count = lax.axis_size("col")
    before_refs, refs = refs[:first], refs[first:]
    outs = refs[-1 - (2 if first else 1):-1]
    parts, panel_ref = refs[: -1 - len(outs)], refs[-1]
    part = parts[0].shape[0] // count
    for n, ref in enumerate(parts):
        at = pl.ds(n * part, part)
        for apart in range(count):
            origin = lax.rem(col_index + count - apart, count)
            place_piece(panel_ref, at, ref[pl.ds(apart * part, part), :], origin, count, size)
    factor_from(panel_ref, inverse_ref, outs[0], tile)
    if first:
        in_order(before_refs + (outs[0],), outs[1], part)


def in_order(refs, out_ref, part):
    row_index = lax.axis_index("row")
    mask = 0
    for ref in refs:
        for n in range(ref.shape[0] // part):
            at = pl.ds(pl.multiple_of((row_index ^ mask) * part, ROW_TILE), part)
            out_ref[at, :] = ref[pl.ds(n * part, part), :]
            mask += 1


def product_kernel(mine, part, rows_ref, front_ref, *refs):
    if mine:
        columns_ref, out_hbm, out_ref, sems = refs
    else:
        near_ref, far_ref, _, out_hbm, out_ref, sems, columns_ref = refs
        in_order((near_ref, far_ref), columns_ref, part)
    sub_index = lax.axis_index("sub")
    half = sub_index if mine else 1 - sub_index
    slot_count, _, size, _ = out_ref.shape
    copies = []
    product = lax.dot_general(
        rows_ref[...], columns_ref[pl.ds(0, rows_ref.shape[0]), :], CONTRACT, preferred_element_type=jnp.float32
    )
    for m in range(slot_count):
        for a in range(slot_count):
            block = product[m * size:(m + 1) * size, a * size:(a + 1) * size]
            out_ref[m, a] = (front_ref[m, a, half].astype(jnp.float32) - block).astype(jnp.bfloat16)
        copies.append(pltpu.make_async_copy(out_ref.at[m], out_hbm.at[m, :, half], sems.at[m]))
        copies[-1].start()
    for copy in copies:
        copy.wait()


def body(front_entries, block_pattern, child_update, child_map, diag_inverse):
    slot_count = front_entries.shape[0]
    size = front_entries.shape[3]
    column_count = front_entries.shape[4]
    child_count = child_update.shape[1]
    row_size = lax.axis_size("row")
    col_size = lax.axis_size("col")
    groups = -(-(PANEL // size) // col_size)
    tile = PANEL // 2
    rows = slot_count * size
    part = -(-rows // (row_size * ROW_TILE)) * ROW_TILE
    padded = part * row_size
    depth = groups * col_size * size
    in_hbm = pl.BlockSpec(memory_space=pltpu.HBM)
    entries = front_entries.reshape(slot_count, size, column_count, size).transpose(0, 2, 1, 3)
    pattern = block_pattern.reshape(slot_count, 1, column_count)
    slots = child_map.transpose(0, 2, 1)
    own = child_update.reshape(child_count, size, child_count, size).transpose(0, 2, 1, 3)

    received = flipped(own, "sub", 1)
    shares = inverse_shares(diag_inverse)
    lanes = groups * size
    tiles = line_tiles(col_size, diag_inverse.shape[0], lanes) if shares else []
    line_rows = len(tiles) * shares[0].shape[0] if shares else 0
    piece, *parts = call(
        functools.partial(panel_kernel, part, groups),
        [bf16(padded, lanes)] + [bf16(part, lanes)] * row_size,
        [SCALARS, SCALARS] + [ON_CHIP] * 3,
    )(slots, pattern, entries[:, :groups], own, received)
    if shares:
        parts[1] = call(
            functools.partial(pack_kernel, part, tiles), bf16(part + line_rows, lanes), [ON_CHIP] * (1 + len(shares))
        )(parts[1], *shares)
        piece, *parts = fence(piece, *parts)

    _, origins, places = line_plan(col_size)
    pieces = Line(piece, "col")
    pieces.step()
    held = [parts[0]] + [flipped(parts[mask], "row", mask) for mask in range(1, row_size)]
    sent = parts[1:2] if shares else []
    turned = call(
        functools.partial(turn_kernel, part),
        [bf16(part, lanes)] * col_size + [bf16(2 * line_rows, lanes)] * len(sent),
        [ON_CHIP] * (row_size + len(sent)),
    )(*held, *sent)
    pieces.held[1], *turned = fence(pieces.held[1], *turned)
    near, sends, lines = turned[0], turned[1:col_size], list(turned[col_size:])
    if shares:
        for bit in range(1, row_size.bit_length() - 1):
            lines += [flipped(line, "row", 1 << bit) for line in lines]
    come = {apart: shifted(sends[apart - 1], "col", apart) for apart in reversed(far_last(col_size))}
    first = far_last(col_size)[-1]
    (come[first],) = pieces.fenced(come[first])
    turned = joined([near] + [come[apart] for apart in range(1, col_size)])
    if shares:
        lines = [joined(lines)]
    turned, *lines = fence(turned, *lines)
    if shares:
        lines += [flipped(line, "sub", 1) for line in lines]
        inverse = call(
            functools.partial(inverse_kernel, shares[0].shape[0], tiles),
            bf16(PANEL, PANEL), [ON_CHIP] * len(lines), moved=4 << 20,
            scratch_shapes=[pltpu.VMEM((PANEL, PANEL), jnp.bfloat16)],
        )(*lines)
    else:
        whole = lax.all_gather(diag_inverse, "col", axis=0, tiled=True)
        inverse = call(
            lower_kernel, bf16(PANEL, PANEL), [ON_CHIP], moved=4 << 20,
            scratch_shapes=[pltpu.VMEM((PANEL, PANEL), jnp.bfloat16)],
        )(whole)
    parts = [turned] + [flipped(turned, "row", mask) for mask in range(1, row_size)]
    while pieces.at < len(pieces.levels):
        pieces.step()
    front = call(
        functools.partial(front_kernel, groups),
        bf16(slot_count, column_count, size, size),
        [SCALARS, SCALARS] + [ON_CHIP] * 4,
        moved=6 << 20,
    )(slots, pattern, entries, own, received, piece)
    kinds, arrays = pieces.taken()
    scratch = [pltpu.VMEM((padded, depth), jnp.bfloat16)]
    flops = 2 * rows * PANEL * PANEL * 3 // 4
    row_factor = call(
        functools.partial(row_factor_kernel, places, origins, kinds, size, tile),
        bf16(rows, PANEL), [ON_CHIP] * (1 + len(arrays)), flops=flops, scratch_shapes=scratch,
    )(inverse, *arrays)
    near_factor = call(
        functools.partial(column_factor_kernel, size, tile, 0),
        bf16(part, PANEL), [ON_CHIP] * 2, scratch_shapes=[pltpu.VMEM((part, depth), jnp.bfloat16)],
    )(inverse, parts[0])
    other_near = flipped(near_factor, "sub", 1)
    row_factor, front, inverse, near_factor, other_near, *parts = fence(
        row_factor, front, inverse, near_factor, other_near, *parts
    )
    front = front.reshape(slot_count, slot_count, 2, size, size)

    far_factor, column_factor = call(
        functools.partial(column_factor_kernel, size, tile, 1),
        [bf16(padded - part, PANEL), bf16(padded, PANEL)], [ON_CHIP] * (1 + row_size), flops=flops,
        scratch_shapes=[pltpu.VMEM((padded - part, depth), jnp.bfloat16)],
    )(inverse, near_factor, *parts[1:])
    other_far = flipped(far_factor, "sub", 1)
    product = functools.partial(
        call,
        out_shape=bf16(slot_count, slot_count, 2, size, size),
        flops=2 * rows * rows * PANEL,
        out_specs=in_hbm,
    )
    scratch = [
        pltpu.VMEM((slot_count, slot_count, size, size), jnp.bfloat16),
        pltpu.SemaphoreType.DMA((slot_count,)),
    ]
    trailing = product(
        functools.partial(product_kernel, True, part), in_specs=[ON_CHIP] * 3, scratch_shapes=scratch
    )(row_factor, front, column_factor)
    trailing = product(
        functools.partial(product_kernel, False, part), in_specs=[ON_CHIP] * 4 + [in_hbm],
        input_output_aliases={4: 0}, scratch_shapes=scratch + [pltpu.VMEM((padded, PANEL), jnp.bfloat16)],
    )(row_factor, front, other_near, other_far, trailing)
    return trailing.reshape(slot_count, column_count, size, size).transpose(0, 2, 1, 3).reshape(
        slot_count, 1, 1, size, column_count, 1, size
    )


def solution(mesh):
    return jax.shard_map(
        body,
        mesh=mesh,
        in_specs=(
            P(None, "sub", "row", None, None, "col", None),
            P(None, "sub", "row", None, "col"),
            P("sub", None, "row", None, None, "col", None),
            P(),
            P("col", None),
        ),
        out_specs=P(None, "sub", "row", None, None, "col", None),
        check_vma=False,
    )
```

```python
import functools

import jax
import jax.numpy as jnp
from jax import lax
from jax.experimental import pallas as pl
from jax.experimental.pallas import tpu as pltpu
from jax.sharding import PartitionSpec as P

PANEL = 1024
ROW_TILE = 16
VMEM_BYTES = 12 * 1024 * 1024
CONTRACT = (((1,), (1,)), ((), ()))
ON_CHIP = pl.BlockSpec(memory_space=pltpu.VMEM)
SCALARS = pl.BlockSpec(memory_space=pltpu.SMEM)


def call(kernel, out_shape, in_specs, flops=0, moved=1 << 19, **more):
    single = not isinstance(out_shape, (list, tuple))
    return pl.pallas_call(
        kernel,
        out_shape=out_shape,
        in_specs=in_specs,
        out_specs=more.pop("out_specs", ON_CHIP if single else [ON_CHIP] * len(out_shape)),
        compiler_params=pltpu.CompilerParams(vmem_limit_bytes=VMEM_BYTES),
        cost_estimate=pl.CostEstimate(flops=flops, bytes_accessed=moved, transcendentals=0),
        **more,
    )


def bf16(*shape):
    return jax.ShapeDtypeStruct(shape, jnp.bfloat16)


def f32(*shape):
    return jax.ShapeDtypeStruct(shape, jnp.float32)


def flipped(block, axis, mask):
    count = lax.axis_size(axis)
    return lax.ppermute(block, axis, [(i, i ^ mask) for i in range(count)])


def shifted(block, axis, apart):
    count = lax.axis_size(axis)
    return lax.ppermute(block, axis, [(i, (i + apart) % count) for i in range(count)])


def far_last(count):
    return sorted(range(1, count), key=lambda apart: (min(apart, count - apart), apart))


def swap_even(i, count):
    return i ^ 1 if i ^ 1 < count else i


def swap_odd(i, count):
    j = ((i + 1) ^ 1) - 1
    return j if 0 <= j < count else i


@functools.cache
def line_plan(count):
    even = [swap_even(i, count) for i in range(count)]
    odd = [swap_odd(i, count) for i in range(count)]
    if count == 4:
        levels = [[(1, 0, even), (2, 0, odd)], [(3, 2, [2, 0, 3, 1]), (4, 1, [1, 3, 0, 2])]]
    else:
        levels, last = [], [0, 0]
        for step in range(count - 1):
            level = []
            for stream in (0, 1):
                level.append((1 + 2 * step + stream, last[stream], odd if (step + stream) % 2 else even))
                last[stream] = level[-1][0]
            levels.append(level)
    whose = {0: list(range(count))}
    seen = [[(0, i)] for i in range(count)]
    for level in levels:
        for array, source, to in level:
            whose[array] = [None] * count
            for i in range(count):
                whose[array][to[i]] = whose[source][i]
            for i in range(count):
                if all(whose[array][i] != origin for _, origin in seen[i]):
                    seen[i].append((array, whose[array][i]))
    origins = [[seen[i][j][1] for i in range(count)] for j in range(count)]
    places = [[seen[i][j][0] for i in range(count)] for j in range(count)]
    return levels, origins, places


class Line:
    def __init__(self, block, axis):
        self.axis = axis
        self.levels, _, self.places = line_plan(lax.axis_size(axis))
        self.held = {0: block}
        self.at = 0

    def step(self):
        for array, source, to in self.levels[self.at]:
            self.held[array] = lax.ppermute(self.held[source], self.axis, list(enumerate(to)))
        self.at += 1
        return self.at < len(self.levels)

    def fenced(self, *values):
        last = [array for array, _, _ in self.levels[self.at - 1]]
        out = fence(*values, *(self.held[array] for array in last))
        self.held.update(zip(last, out[len(values):]))
        return out[: len(values)]

    def taken(self):
        kinds = sorted({kind for row in self.places for kind in row})
        return kinds, [self.held[kind] for kind in kinds]


def among(index, members):
    found = index == members[0]
    for member in members[1:]:
        found = jnp.logical_or(found, index == member)
    return found


def looked_up(index, table):
    value = jnp.int32(table[0])
    for i, entry in enumerate(table[1:], 1):
        value = jnp.where(index == i, jnp.int32(entry), value)
    return value


def fence_kernel(*refs):
    pass


def fence(*values):
    place = pl.BlockSpec(memory_space=pl.ANY)
    return pl.pallas_call(
        fence_kernel,
        out_shape=[jax.ShapeDtypeStruct(v.shape, v.dtype) for v in values],
        in_specs=[place] * len(values),
        out_specs=[place] * len(values),
        input_output_aliases={n: n for n in range(len(values))},
        compiler_params=pltpu.CompilerParams(vmem_limit_bytes=1 << 20),
    )(*values)


def found_at(map_ref, child, place, wanted, child_count):
    at = jnp.int32(0)
    found = jnp.float32(0)
    for k in range(child_count):
        same = map_ref[child, place, k] == wanted
        at = jnp.where(same, jnp.int32(k), at)
        found = jnp.where(same, jnp.float32(1), found)
    return at, found


def block_places(map_ref, child, columns, slot_count, child_count):
    sub_index, row_index, col_index = (lax.axis_index(name) for name in ("sub", "row", "col"))
    rows = [
        found_at(map_ref, child, row_index, 2 * a + sub_index, child_count) for a in range(slot_count)
    ]
    cols = [found_at(map_ref, child, col_index, b, child_count) for b in columns]
    return rows, cols


def child_block(ref, row, col):
    return ref[row[0], col[0]].astype(jnp.float32) * (row[1] * col[1])


def line_tiles(count, share, lanes):
    return [(col, tile) for col in range(count) for tile in range(-(-(col + 1) * share // lanes))]


def pack_line(share_refs, out_ref, first, tiles):
    col_index = lax.axis_index("col")
    count = len(share_refs)
    rows, lanes = share_refs[0].shape[0], out_ref.shape[1]
    for apart, ref in zip([0, *far_last(count)], share_refs):
        for col in range(count):

            @pl.when(lax.rem(col_index + count - apart, count) == col)
            def _():
                for n, (home, tile) in enumerate(tiles):
                    if home == col:
                        out_ref[pl.ds(first + n * rows, rows), :] = ref[:, tile * lanes:(tile + 1) * lanes]


def pack_kernel(part, tiles, *refs):
    part_ref, *share_refs, out_ref = refs
    out_ref[pl.ds(0, part), :] = part_ref[...]
    pack_line(share_refs, out_ref, part, tiles)


def panel_kernel(part, groups, map_ref, pattern_ref, entries_ref, own_ref, received_ref, piece_ref, *part_refs):
    slot_count, _, size, _ = entries_ref.shape
    child_count = own_ref.shape[0]
    sub_index, row_index = lax.axis_index("sub"), lax.axis_index("row")
    places = [
        block_places(map_ref, child, range(groups), slot_count, child_count)
        for child in (sub_index, 1 - sub_index)
    ]
    for a in range(slot_count):
        for b in range(groups):
            total = entries_ref[a, b].astype(jnp.float32) * pattern_ref[a, 0, b].astype(jnp.float32)
            for (rows, cols), ref in zip(places, (own_ref, received_ref)):
                total = total + child_block(ref, rows[a], cols[b])
            piece_ref[pl.ds(a * size, size), pl.ds(b * size, size)] = total.astype(jnp.bfloat16)
    used = slot_count * size
    if used < piece_ref.shape[0]:
        piece_ref[pl.ds(used, piece_ref.shape[0] - used), :] = jnp.zeros(
            (piece_ref.shape[0] - used, piece_ref.shape[1]), piece_ref.dtype
        )
    for mask, ref in enumerate(part_refs):
        ref[...] = piece_ref[pl.ds(pl.multiple_of((row_index ^ mask) * part, ROW_TILE), part), :]


def front_kernel(groups, map_ref, pattern_ref, entries_ref, own_ref, received_ref, piece_ref, out_ref):
    slot_count, column_count, size, _ = entries_ref.shape
    child_count = own_ref.shape[0]
    sub_index = lax.axis_index("sub")
    columns = range(groups, column_count)
    places = [
        block_places(map_ref, child, columns, slot_count, child_count)
        for child in (sub_index, 1 - sub_index)
    ]
    for a in range(slot_count):
        for b in range(groups):
            out_ref[a, b] = piece_ref[pl.ds(a * size, size), pl.ds(b * size, size)]
        for n, b in enumerate(columns):
            total = entries_ref[a, b].astype(jnp.float32) * pattern_ref[a, 0, b].astype(jnp.float32)
            for (rows, cols), ref in zip(places, (own_ref, received_ref)):
                total = total + child_block(ref, rows[a], cols[n])
            out_ref[a, b] = total.astype(jnp.bfloat16)


def inverse_kernel(rows, tiles, *refs):
    *in_refs, turned_ref, out_ref = refs
    sub_index, row_index = lax.axis_index("sub"), lax.axis_index("row")
    sub_size, row_size, col_size = (lax.axis_size(name) for name in ("sub", "row", "col"))
    width = out_ref.shape[0]
    lanes = in_refs[0].shape[1]
    share = width // col_size
    lines = [
        (ref, line * len(tiles) * rows) for ref in in_refs for line in range(row_size)
    ]
    for n, (ref, first) in enumerate(lines):
        sub_at = sub_index if n < row_size else 1 - sub_index
        inside = (sub_at * row_size + (row_index ^ (n % row_size))) * rows
        for m, (col, tile) in enumerate(tiles):
            top = pl.multiple_of(col * share + inside, ROW_TILE)
            block = ref[pl.ds(first + m * rows, rows), :]
            if (tile + 1) * lanes > col * share:
                row_at = top + lax.broadcasted_iota(jnp.int32, block.shape, 0)
                col_at = tile * lanes + lax.broadcasted_iota(jnp.int32, block.shape, 1)
                block = jnp.where(col_at <= row_at, block.astype(jnp.float32), 0.0).astype(jnp.bfloat16)
            out_ref[pl.ds(top, rows), pl.ds(tile * lanes, lanes)] = block
    for col in range(col_size):
        for tile in range(width // lanes):
            if (col, tile) not in tiles:
                out_ref[pl.ds(col * share, share), pl.ds(tile * lanes, lanes)] = jnp.zeros(
                    (share, lanes), out_ref.dtype
                )
    turn_over(out_ref, turned_ref)


def turn_over(in_ref, out_ref, tile=256):
    for top in range(0, in_ref.shape[0], tile):
        for left in range(0, in_ref.shape[1], tile):
            out_ref[pl.ds(left, tile), pl.ds(top, tile)] = in_ref[pl.ds(top, tile), pl.ds(left, tile)].T


def lower_kernel(in_ref, turned_ref, out_ref):
    row_at = lax.broadcasted_iota(jnp.int32, in_ref.shape, 0)
    col_at = lax.broadcasted_iota(jnp.int32, in_ref.shape, 1)
    out_ref[...] = jnp.where(col_at <= row_at, in_ref[...].astype(jnp.float32), 0.0).astype(jnp.bfloat16)
    turn_over(out_ref, turned_ref)


def join_kernel(*refs):
    *in_refs, out_ref = refs
    rows = in_refs[0].shape[0]
    for n, ref in enumerate(in_refs):
        out_ref[pl.ds(n * rows, rows), :] = ref[...]


def joined(blocks):
    rows, width = blocks[0].shape
    return call(join_kernel, bf16(rows * len(blocks), width), [ON_CHIP] * len(blocks))(*blocks)


def inverse_shares(diag_inverse):
    part = diag_inverse.shape[0] // (lax.axis_size("sub") * lax.axis_size("row"))
    if part % ROW_TILE:
        return []
    first = (lax.axis_index("sub") * lax.axis_size("row") + lax.axis_index("row")) * part
    mine = lax.dynamic_slice_in_dim(diag_inverse, first, part, 0)
    return [mine] + [shifted(mine, "col", apart) for apart in far_last(lax.axis_size("col"))]


def turn_kernel(part, *refs):
    row_size, count = lax.axis_size("row"), lax.axis_size("col")
    held, refs = refs[:row_size], refs[row_size:]
    if len(refs) > count:
        sent_ref, *outs, lines_ref = refs
        rows = sent_ref.shape[0] - part
        lines_ref[pl.ds(0, rows), :] = sent_ref[pl.ds(part, rows), :]
        lines_ref[pl.ds(rows, rows), :] = held[1][pl.ds(part, rows), :]
    else:
        outs = refs
    row_index, col_index = lax.axis_index("row"), lax.axis_index("col")
    for apart, out_ref in enumerate(outs):
        wanted = row_index ^ lax.rem(col_index + apart, count)
        for mask, ref in enumerate(held):

            @pl.when(wanted == mask)
            def _():
                out_ref[...] = ref[pl.ds(0, part), :]


def place_piece(panel_ref, rows, block, origin, count, size):
    for g in range(block.shape[1] // size):
        left = (g * count + origin) * size
        if not isinstance(origin, int):
            left = pl.multiple_of(left, size)
        panel_ref[rows, pl.ds(left, size)] = block[:, g * size:(g + 1) * size]


def factor_from(panel_ref, inverse_ref, out_ref, tile):
    rows, width = out_ref.shape
    for first in range(0, width, tile):
        out_ref[:, pl.ds(first, tile)] = lax.dot_general(
            panel_ref[pl.ds(0, rows), pl.ds(0, first + tile)],
            inverse_ref[pl.ds(0, first + tile), pl.ds(first, tile)],
            (((1,), (0,)), ((), ())),
            preferred_element_type=jnp.float32,
        ).astype(jnp.bfloat16)


def row_factor_kernel(places, origins, kinds, size, tile, inverse_ref, *refs):
    arrays, out_ref, panel_ref = refs[: len(kinds)], refs[-2], refs[-1]
    col_index = lax.axis_index("col")
    count = len(origins)
    rows = out_ref.shape[0]
    for slot in range(count):
        origin = looked_up(col_index, origins[slot])
        for kind, ref in zip(kinds, arrays):
            members = tuple(i for i in range(count) if places[slot][i] == kind)
            if members:

                @pl.when(among(col_index, members))
                def _():
                    for top in range(0, rows, size):
                        at = pl.ds(top, size)
                        place_piece(panel_ref, at, ref[at, :], origin, count, size)

    factor_from(panel_ref, inverse_ref, out_ref, tile)


def column_factor_kernel(size, tile, inverse_ref, *refs):
    col_index = lax.axis_index("col")
    count = lax.axis_size("col")
    *parts, out_ref, panel_ref = refs
    part = parts[0].shape[0] // count
    for n, ref in enumerate(parts):
        at = pl.ds(n * part, part)
        for apart in range(count):
            origin = lax.rem(col_index + count - apart, count)
            place_piece(panel_ref, at, ref[pl.ds(apart * part, part), :], origin, count, size)
    factor_from(panel_ref, inverse_ref, out_ref, tile)


def in_order(refs, out_ref, part):
    row_index = lax.axis_index("row")
    mask = 0
    for ref in refs:
        for n in range(ref.shape[0] // part):
            at = pl.ds(pl.multiple_of((row_index ^ mask) * part, ROW_TILE), part)
            out_ref[at, :] = ref[pl.ds(n * part, part), :]
            mask += 1


def product_kernel(mine, part, rows_ref, front_ref, *refs):
    near_ref, far_ref = refs[:2]
    out_hbm, out_ref, sems, columns_ref = refs[-4:]
    in_order((near_ref, far_ref), columns_ref, part)
    sub_index = lax.axis_index("sub")
    half = sub_index if mine else 1 - sub_index
    slot_count, _, size, _ = out_ref.shape
    copies = []
    product = lax.dot_general(
        rows_ref[...], columns_ref[pl.ds(0, rows_ref.shape[0]), :], CONTRACT, preferred_element_type=jnp.float32
    )
    for m in range(slot_count):
        for a in range(slot_count):
            block = product[m * size:(m + 1) * size, a * size:(a + 1) * size]
            out_ref[m, a] = (front_ref[m, a, half].astype(jnp.float32) - block).astype(jnp.bfloat16)
        copies.append(pltpu.make_async_copy(out_ref.at[m], out_hbm.at[m, :, half], sems.at[m]))
        copies[-1].start()
    for copy in copies:
        copy.wait()


def body(front_entries, block_pattern, child_update, child_map, diag_inverse):
    slot_count = front_entries.shape[0]
    size = front_entries.shape[3]
    column_count = front_entries.shape[4]
    child_count = child_update.shape[1]
    row_size = lax.axis_size("row")
    col_size = lax.axis_size("col")
    groups = -(-(PANEL // size) // col_size)
    tile = PANEL // 2
    rows = slot_count * size
    part = -(-rows // (row_size * ROW_TILE)) * ROW_TILE
    padded = part * row_size
    depth = groups * col_size * size
    in_hbm = pl.BlockSpec(memory_space=pltpu.HBM)
    entries = front_entries.reshape(slot_count, size, column_count, size).transpose(0, 2, 1, 3)
    pattern = block_pattern.reshape(slot_count, 1, column_count)
    slots = child_map.transpose(0, 2, 1)
    own = child_update.reshape(child_count, size, child_count, size).transpose(0, 2, 1, 3)

    received = flipped(own, "sub", 1)
    shares = inverse_shares(diag_inverse)
    lanes = groups * size
    tiles = line_tiles(col_size, diag_inverse.shape[0], lanes) if shares else []
    line_rows = len(tiles) * shares[0].shape[0] if shares else 0
    piece, *parts = call(
        functools.partial(panel_kernel, part, groups),
        [bf16(padded, lanes)] + [bf16(part, lanes)] * row_size,
        [SCALARS, SCALARS] + [ON_CHIP] * 3,
    )(slots, pattern, entries[:, :groups], own, received)
    if shares:
        parts[1] = call(
            functools.partial(pack_kernel, part, tiles), bf16(part + line_rows, lanes), [ON_CHIP] * (1 + len(shares))
        )(parts[1], *shares)
        piece, *parts = fence(piece, *parts)

    _, origins, places = line_plan(col_size)
    pieces = Line(piece, "col")
    pieces.step()
    held = [parts[0]] + [flipped(parts[mask], "row", mask) for mask in range(1, row_size)]
    sent = parts[1:2] if shares else []
    turned = call(
        functools.partial(turn_kernel, part),
        [bf16(part, lanes)] * col_size + [bf16(2 * line_rows, lanes)] * len(sent),
        [ON_CHIP] * (row_size + len(sent)),
    )(*held, *sent)
    pieces.held[1], *turned = fence(pieces.held[1], *turned)
    near, sends, lines = turned[0], turned[1:col_size], list(turned[col_size:])
    if shares:
        for bit in range(1, row_size.bit_length() - 1):
            lines += [flipped(line, "row", 1 << bit) for line in lines]
    come = {apart: shifted(sends[apart - 1], "col", apart) for apart in reversed(far_last(col_size))}
    first = far_last(col_size)[-1]
    (come[first],) = pieces.fenced(come[first])
    turned = joined([near] + [come[apart] for apart in range(1, col_size)])
    if shares:
        lines = [joined(lines)]
    turned, *lines = fence(turned, *lines)
    if shares:
        lines += [flipped(line, "sub", 1) for line in lines]
        inverse = call(
            functools.partial(inverse_kernel, shares[0].shape[0], tiles),
            bf16(PANEL, PANEL), [ON_CHIP] * len(lines), moved=4 << 20,
            scratch_shapes=[pltpu.VMEM((PANEL, PANEL), jnp.bfloat16)],
        )(*lines)
    else:
        whole = lax.all_gather(diag_inverse, "col", axis=0, tiled=True)
        inverse = call(
            lower_kernel, bf16(PANEL, PANEL), [ON_CHIP], moved=4 << 20,
            scratch_shapes=[pltpu.VMEM((PANEL, PANEL), jnp.bfloat16)],
        )(whole)
    parts = [turned] + [flipped(turned, "row", mask) for mask in range(1, row_size)]
    while pieces.at < len(pieces.levels):
        pieces.step()
    front = call(
        functools.partial(front_kernel, groups),
        bf16(slot_count, column_count, size, size),
        [SCALARS, SCALARS] + [ON_CHIP] * 4,
        moved=6 << 20,
    )(slots, pattern, entries, own, received, piece)
    kinds, arrays = pieces.taken()
    scratch = [pltpu.VMEM((padded, depth), jnp.bfloat16)]
    flops = 2 * rows * PANEL * PANEL * 3 // 4
    row_factor = call(
        functools.partial(row_factor_kernel, places, origins, kinds, size, tile),
        bf16(rows, PANEL), [ON_CHIP] * (1 + len(arrays)), flops=flops, scratch_shapes=scratch,
    )(inverse, *arrays)
    near_factor = call(
        functools.partial(column_factor_kernel, size, tile),
        bf16(part, PANEL), [ON_CHIP] * 2, scratch_shapes=[pltpu.VMEM((part, depth), jnp.bfloat16)],
    )(inverse, parts[0])
    other_near = flipped(near_factor, "sub", 1)
    row_factor, front, inverse, near_factor, other_near, *parts = fence(
        row_factor, front, inverse, near_factor, other_near, *parts
    )
    front = front.reshape(slot_count, slot_count, 2, size, size)

    far_factor = call(
        functools.partial(column_factor_kernel, size, tile),
        bf16(padded - part, PANEL), [ON_CHIP] * row_size, flops=flops,
        scratch_shapes=[pltpu.VMEM((padded - part, depth), jnp.bfloat16)],
    )(inverse, *parts[1:])
    other_far = flipped(far_factor, "sub", 1)
    product = functools.partial(
        call,
        out_shape=bf16(slot_count, slot_count, 2, size, size),
        flops=2 * rows * rows * PANEL,
        out_specs=in_hbm,
    )
    scratch = [
        pltpu.VMEM((slot_count, slot_count, size, size), jnp.bfloat16),
        pltpu.SemaphoreType.DMA((slot_count,)),
        pltpu.VMEM((padded, PANEL), jnp.bfloat16),
    ]
    trailing = product(
        functools.partial(product_kernel, True, part), in_specs=[ON_CHIP] * 4, scratch_shapes=scratch
    )(row_factor, front, near_factor, far_factor)
    trailing = product(
        functools.partial(product_kernel, False, part), in_specs=[ON_CHIP] * 4 + [in_hbm],
        input_output_aliases={4: 0}, scratch_shapes=scratch,
    )(row_factor, front, other_near, other_far, trailing)
    return trailing.reshape(slot_count, column_count, size, size).transpose(0, 2, 1, 3).reshape(
        slot_count, 1, 1, size, column_count, 1, size
    )


def solution(mesh):
    return jax.shard_map(
        body,
        mesh=mesh,
        in_specs=(
            P(None, "sub", "row", None, None, "col", None),
            P(None, "sub", "row", None, "col"),
            P("sub", None, "row", None, None, "col", None),
            P(),
            P("col", None),
        ),
        out_specs=P(None, "sub", "row", None, None, "col", None),
        check_vma=False,
    )
```
